32 devices in a mesh: shard: 4 (over z), ctx: 2 (over core), tp: 4 (over y, x).
Axes of the slice: x: 2, y: 2, z: 4, core: 2. Of those that a mesh axis runs over, the one named last changes fastest.
Arguments:
- hidden_in: bfloat16 [16384, 768], P(('shard', 'ctx', 'tp')), may hold values from -6 to 6
- cotangent: bfloat16 [16384, 768], P(('shard', 'ctx', 'tp')), may hold values from -6 to 6
- lengths: int32 [4], P('shard'), may hold values from 1024 to 4096, as said below
- routes: int32 [16384, 2], P(('shard', 'ctx')), may hold values from 0 to 11, all different within a row; in each aligned block of 2048 rows (0 to 2047, 2048 to 4095, ...) at most 512 rows name the same one
- prev_logits: float32 [16384, 12], P(('shard', 'ctx')), may hold values from -4 to 4
- norm_attn: bfloat16 [768], P('shard'), may hold values from 0.5 to 1.5
- w_query: bfloat16 [768, 768], P('shard', 'tp'), may hold values from -0.21875 to 0.21875
- w_key: bfloat16 [768, 768], P('shard', 'tp'), may hold values from -0.21875 to 0.21875
- w_value: bfloat16 [768, 768], P('shard', 'tp'), may hold values from -0.21875 to 0.21875
- w_out: bfloat16 [768, 768], P('tp', 'shard'), may hold values from -1.75 to 1.75
- norm_moe: bfloat16 [768], P('shard'), may hold values from 0.5 to 1.5
- w_router: bfloat16 [768, 12], P('shard'), may hold values from -0.109375 to 0.109375
- w_const: bfloat16 [768, 4], P('shard'), may hold values from -0.21875 to 0.21875
- const_vec: bfloat16 [2, 768], P(None, 'shard'), may hold values from -5 to 5
- w_gate: bfloat16 [8, 768, 2048], P(None, 'shard', 'tp'), may hold values from -0.21875 to 0.21875
- w_up: bfloat16 [8, 768, 2048], P(None, 'shard', 'tp'), may hold values from -0.21875 to 0.21875
- w_down: bfloat16 [8, 768, 2048], P(None, 'shard', 'tp'), may hold values from -0.125 to 0.125
- threshold: float32 [1], replicated, may hold values from 0.5 to 1.5
Outputs:
- output: bfloat16 [16384, 768], P(('shard', 'ctx', 'tp'))
- grad_input: float32 [16384, 768], P(('shard', 'ctx', 'tp'))
- grad_norm_attn: float32 [768], P('shard')
- grad_w_query: float32 [768, 768], P('shard', 'tp')
- grad_w_key: float32 [768, 768], P('shard', 'tp')
- grad_w_value: float32 [768, 768], P('shard', 'tp')
- grad_w_out: float32 [768, 768], P('tp', 'shard')
- grad_norm_moe: float32 [768], P('shard')
- grad_w_router: float32 [768, 12], P('shard')
- grad_w_const: float32 [768, 4], P('shard')
- grad_const_vec: float32 [2, 768], P(None, 'shard')
- grad_w_gate: float32 [8, 768, 2048], P(None, 'shard', 'tp')
- grad_w_up: float32 [8, 768, 2048], P(None, 'shard', 'tp')
- grad_w_down: float32 [8, 768, 2048], P(None, 'shard', 'tp')
- clip_factors: float32 [12], P('tp')
- clipped_query: bfloat16 [768, 768], P('shard', 'tp')
- clipped_key: bfloat16 [768, 768], P('shard', 'tp')
The draws below stay inside these ranges and needn't reach their ends.
Inputs may be any that keep to these rules, and one draw needn't show every extreme that they name: `lengths`: valid length of each sequence; some sequence is full (4096) in every draw. `routes`: each row names two different experts; in each aligned block of 2048 rows no expert is named by more than 512 rows, a bound that some block reaches.
All inputs are finite; a program needn't handle non-finite values.
Results may differ from the reference program's by a relative error of at most 0.013.
Values may be sent and summed in bfloat16 or wider, within the bound.
A program may use at most 320 MiB of HBM per device.

```python
import math
import jax
import jax.numpy as jnp
import numpy as np
from jax import lax

D = 768
HEADS = 12
HEAD_DIM = 64
FF = 2048
EXPERTS = 12
FFN_EXPERTS = 8
TOK_DEV = 2048
SEQ = 4096
TOKENS = 16384
MIN_LEN = 1024
CAP = 512
QBLOCK = 512
N_SHARD = 4


def draw_lengths(key, part):
    key = jax.random.fold_in(key, 3)
    first, second = jax.random.split(key)
    values = jax.random.randint(first, (N_SHARD,), MIN_LEN, SEQ + 1)
    which = jax.random.randint(second, (), 0, N_SHARD)
    return jnp.where(jnp.arange(N_SHARD) == which, SEQ, values).astype(jnp.int32)


def shard_levels(own_key, dims, cuts, low, top_value):
    level, own = 1.0, jax.random.fold_in(own_key, 6)
    for axis_at, parts in cuts:
        draws = jnp.exp(jax.random.uniform(jax.random.fold_in(own, axis_at), (parts,), jnp.float32, low / len(cuts), top_value / len(cuts)))
        level = level * jnp.repeat(draws, dims[axis_at] // parts).reshape([-1 if axis == axis_at else 1 for axis in range(len(dims))])
    return level


def routed_block(stream_key, own, number, rows, number_of, top, limit, slope):
    sequence = jax.random.permutation(stream_key, number_of)
    crowded, ordinary = shares(number_of, rows * top, limit, slope, True), shares(number_of, rows * top, limit, slope, False)
    places = jnp.arange(number_of)

    def named(sizes, turn):
        used = int((sizes > 0).sum())
        fixed = max(1, used // 4)
        shifted = fixed + (places - fixed + turn * (used - fixed)) % max(1, number_of - fixed)
        return jnp.zeros((number_of,), jnp.int32).at[sequence[jnp.where(places < fixed, places, shifted)]].set(jnp.asarray(sizes, jnp.int32))

    sizes = jnp.where(number % 4 == 0, named(crowded, number // 4), named(ordinary, number - number // 4 - 1))
    mixed = jax.random.permutation(jax.random.fold_in(own, 3), number_of)
    source_of, sink = mixed[0:number_of // 2 * 2:2], mixed[1:number_of // 2 * 2:2]
    room = jnp.minimum(sizes[source_of] - 1, limit - sizes[sink]) // 2
    room = jnp.where((source_of == sequence[0]) | (sink == sequence[0]) | (sizes[sink] == 0), 0, jnp.maximum(room, 0))
    shifted = jax.random.randint(jax.random.fold_in(own, 4), (number_of // 2,), 0, 1 << 20) % (room + 1)
    sizes = sizes.at[source_of].add(-shifted).at[sink].add(shifted)
    members = jnp.searchsorted(jnp.cumsum(sizes), jnp.arange(rows * top), side="right").astype(jnp.int32)
    grid = members.reshape(top, rows).T
    grid = grid[jax.random.permutation(jax.random.fold_in(own, 1), rows)]
    turn = jax.random.randint(jax.random.fold_in(own, 2), (rows, 1), 0, top)
    return jnp.take_along_axis(grid, (jnp.arange(top)[None, :] + turn) % top, axis=1)


def shares(number_of, total, most, lean, full):
    weights = [(1 << 20) // math.isqrt(grade ** lean) + 1 for grade in range(1, number_of + 1)]
    largest = most if full else min(most, max(-(-total // number_of), total * weights[0] // sum(weights)))
    least = 1 if total - largest >= number_of - 1 else 0
    holding, surplus = [largest] + [least] * (number_of - 1), total - largest - least * (number_of - 1)
    while surplus > 0:
        free = [i for i in range(1, number_of) if holding[i] < largest] or [i for i in range(1, number_of) if holding[i] < most]
        mass, budget = sum([weights[i] for i in free]), surplus
        for i in free:
            extra = min(most - holding[i], max(1, budget * weights[i] // mass), surplus)
            holding[i] = holding[i] + extra
            surplus = surplus - extra
    return np.array(holding)


def noise(key, extent, deviation, bound, pieces=(), held_as=jnp.bfloat16):
    values = jax.random.normal(key, extent, jnp.float32) * deviation
    if len(pieces) > 0:
        values = shard_levels(key, extent, pieces, -0.22, 0.18) * values
    return jnp.clip(values, min=-bound, max=bound).astype(held_as)


def setup_inputs(seed: int = 0) -> dict:
    key_list = jax.random.split(jax.random.key(seed), 19)
    hidden_in = noise(key_list[0], (TOKENS, D), 1.0, 6.0, ((0, 32),))
    cotangent = noise(key_list[1], (TOKENS, D), 1.0, 6.0, ((0, 32),))
    lengths = draw_lengths(jax.random.fold_in(key_list[18], 71), 0)
    routes_keys = jax.random.split(jax.random.fold_in(key_list[3], 1), TOKENS // TOK_DEV)
    routes_turns = jax.random.permutation(jax.random.fold_in(key_list[3], 3), TOKENS // TOK_DEV)
    routes = jax.vmap(lambda own, number: routed_block(jax.random.fold_in(key_list[3], 2), own, number, TOK_DEV, EXPERTS, 2, CAP, 1))(routes_keys, routes_turns).reshape((TOKENS, 2))
    prev_logits = noise(key_list[4], (TOKENS, EXPERTS), 0.5, 4.0, ((0, 8),), jnp.float32)
    norm_attn = jnp.clip(1.0 + 0.1 * jax.random.normal(key_list[5], (D,), jnp.float32), 0.5, 1.5).astype(jnp.bfloat16)
    w_query = noise(key_list[6], (D, D), D ** -0.5, 0.21875, ((0, 4), (1, 4)))
    w_key = noise(key_list[7], (D, D), D ** -0.5, 0.21875, ((0, 4), (1, 4)))
    w_value = noise(key_list[8], (D, D), D ** -0.5, 0.21875, ((0, 4), (1, 4)))
    w_out = noise(key_list[9], (D, D), (max(D // 64, 8)) ** -0.5, 1.75, ((0, 4), (1, 4)))
    norm_moe = jnp.clip(1.0 + 0.1 * jax.random.normal(key_list[10], (D,), jnp.float32), 0.5, 1.5).astype(jnp.bfloat16)
    w_router = noise(key_list[11], (D, EXPERTS), (4 * D) ** -0.5, 0.109375, ((0, 4),))
    w_const = noise(key_list[12], (D, 4), D ** -0.5, 0.21875, ((0, 4),))
    const_vec = noise(key_list[13], (2, D), 1.0, 5.0, ((1, 4),))
    w_gate = noise(key_list[14], (FFN_EXPERTS, D, FF), D ** -0.5, 0.21875, ((1, 4), (2, 4)))
    w_up = noise(key_list[15], (FFN_EXPERTS, D, FF), D ** -0.5, 0.21875, ((1, 4), (2, 4)))
    w_down = noise(key_list[16], (FFN_EXPERTS, D, FF), FF ** -0.5, 0.125, ((1, 4), (2, 4)))
    threshold = jnp.clip(jax.random.uniform(key_list[17], (1,), jnp.float32, 0.5, 1.5), 0.5, 1.5)
    return {"hidden_in": hidden_in, "cotangent": cotangent, "lengths": lengths, "routes": routes, "prev_logits": prev_logits, "norm_attn": norm_attn, "w_query": w_query, "w_key": w_key, "w_value": w_value, "w_out": w_out, "norm_moe": norm_moe, "w_router": w_router, "w_const": w_const, "const_vec": const_vec, "w_gate": w_gate, "w_up": w_up, "w_down": w_down, "threshold": threshold}


@jax.custom_vjp
def low(v):
    return lax.optimization_barrier(v.astype(jnp.bfloat16)).astype(jnp.float32)

@jax.custom_vjp
def low_back(v):
    return v

def low_keep(v):
    return (low(v), None)

def low_pass(kept, grad):
    return (grad,)

def back_keep(v):
    return (v, None)

def back_low(kept, grad):
    return (low(grad),)
low.defvjp(low_keep, low_pass)
low_back.defvjp(back_keep, back_low)
epsilon = 1e-06
highest = lax.Precision.HIGHEST
rope_base = 10000.0

def product(left, right):
    return jnp.dot(left, right, precision=highest)

def rms_norm(values, gain):
    return values * lax.rsqrt(lax.optimization_barrier(jnp.mean(values * values, axis=-1, keepdims=True)) + epsilon) * gain

def rotate(values, positions):
    half = values.shape[-1] // 2
    freqs = rope_base ** (-2.0 * jnp.arange(half).astype(jnp.float32) / values.shape[-1])
    angles = positions.astype(jnp.float32)[:, None] * freqs[None, :]
    cosine = jnp.cos(angles)[:, None, :]
    sine = jnp.sin(angles)[:, None, :]
    first = values[..., :half]
    second = values[..., half:]
    return jnp.concatenate([first * cosine - second * sine, second * cosine + first * sine], axis=-1)

def mixture(normed, router, const_weights, const_vectors, previous, chosen):
    logits = product(normed, router) + previous
    picked = jnp.take_along_axis(logits, chosen, axis=1)
    gates = jax.nn.softmax(picked, axis=-1)
    experts = jnp.arange(EXPERTS)
    combine = lax.optimization_barrier(jnp.sum(gates[:, :, None] * (chosen[:, :, None] == experts[None, None, :]).astype(jnp.float32), axis=1))
    mixed = combine[:, FFN_EXPERTS + 1:FFN_EXPERTS + 2] * normed
    for which in range(2):
        alphas = jax.nn.softmax(product(normed, const_weights[:, 2 * which:2 * which + 2]), axis=-1)
        column = FFN_EXPERTS + 2 + which
        mixed = mixed + combine[:, column:column + 1] * (alphas[:, :1] * normed + alphas[:, 1:] * const_vectors[which][None, :])
    return (gates, combine, mixed)

def layer(params, hidden, length, chosen, previous):
    gain_attn, query_w, key_w, value_w, out_w, gain_moe, router, const_weights, const_vectors, gate_w, up_w, down_w = params
    positions = jnp.arange(SEQ)
    valid = positions < length
    lowered = low(rms_norm(hidden, gain_attn))
    head_shape = (SEQ, HEADS, HEAD_DIM)
    query = low(rotate(low_back(product(lowered, query_w)).reshape(head_shape), positions))
    key = low(rotate(low_back(product(lowered, key_w)).reshape(head_shape), positions))
    value = low(low_back(product(lowered, value_w))).reshape(head_shape)
    scale = HEAD_DIM ** (-0.5)

    def attend(start):
        block = lax.dynamic_slice_in_dim(query, start, QBLOCK, 0)
        raw = low_back(jnp.einsum('qhd,khd->hqk', block, key, precision=highest))
        scores = raw * scale
        rows_here = start + jnp.arange(QBLOCK)
        allowed = (positions[None, :] <= rows_here[:, None]) & valid[None, :]
        masked = jnp.where(allowed[None], scores, -1e+30)
        peak = lax.optimization_barrier(jnp.max(masked, axis=-1, keepdims=True))
        weights = jnp.exp(masked - peak)
        probs = low(weights / lax.optimization_barrier(jnp.sum(weights, axis=-1, keepdims=True)))
        mixed = jnp.einsum('hqk,khd->qhd', probs, value, precision=highest)
        counted = allowed & (rows_here < length)[:, None]
        largest = lax.optimization_barrier(jnp.max(jnp.where(counted[None], scores, -1e+30), axis=(1, 2)))
        return (mixed, largest)
    starts = (jnp.arange(SEQ // QBLOCK) * QBLOCK).astype(jnp.int32)
    blocks, largest = lax.map(jax.checkpoint(attend), starts)
    attended = low(low_back(blocks.reshape(SEQ, HEADS * HEAD_DIM)))
    residual = hidden + low_back(product(attended, out_w))
    normed_moe = rms_norm(residual, gain_moe)
    lowered_moe = low(normed_moe)
    gates, combine, others = mixture(normed_moe, router, const_weights, const_vectors, previous, chosen)

    def expert(index):
        gate = low_back(product(lowered_moe, gate_w[index]))
        upper = low_back(product(lowered_moe, up_w[index]))
        inner = low(jax.nn.silu(gate) * upper)
        return low_back(product(inner, down_w[index].T))
    outputs = lax.map(jax.checkpoint(expert), jnp.arange(FFN_EXPERTS))
    feed = jnp.einsum('te,etd->td', combine[:, :FFN_EXPERTS], outputs, precision=highest)
    result = valid[:, None].astype(jnp.float32) * (residual + feed + others)
    return (result, lax.optimization_barrier(jnp.max(largest, axis=0)))

def reference(hidden_in, cotangent, lengths, routes, prev_logits, norm_attn, w_query, w_key, w_value, w_out, norm_moe, w_router, w_const, const_vec, w_gate, w_up, w_down, threshold):
    params = tuple((item.astype(jnp.float32) for item in (norm_attn, w_query, w_key, w_value, w_out, norm_moe, w_router, w_const, const_vec, w_gate, w_up, w_down)))

    def one(carry, index):
        totals, largest = carry
        start = (index * SEQ).astype(jnp.int32)
        rows_in = lax.dynamic_slice_in_dim(hidden_in, start, SEQ, 0).astype(jnp.float32)
        rows_cot = lax.dynamic_slice_in_dim(cotangent, start, SEQ, 0).astype(jnp.float32)
        rows_route = lax.dynamic_slice_in_dim(routes, start, SEQ, 0)
        rows_prev = lax.dynamic_slice_in_dim(prev_logits, start, SEQ, 0)
        length = lengths[index]

        def apply(weights, rows):
            return layer(weights, rows, length, rows_route, rows_prev)
        result, back, head_max = jax.vjp(apply, params, rows_in, has_aux=True)
        grads, grad_rows = back(rows_cot)
        totals = jax.tree.map(jnp.add, totals, grads)
        return ((totals, jnp.maximum(largest, head_max)), (result, grad_rows))
    initial = (jax.tree.map(jnp.zeros_like, params), jnp.full((HEADS,), -1e+30, jnp.float32))
    (totals, largest), (results, grads_in) = lax.scan(one, initial, jnp.arange(N_SHARD))
    factors = threshold[0] / jnp.maximum(largest, threshold[0])
    root = jnp.repeat(jnp.sqrt(factors), HEAD_DIM)
    clipped_query = (w_query.astype(jnp.float32) * root[None, :]).astype(jnp.bfloat16)
    clipped_key = (w_key.astype(jnp.float32) * root[None, :]).astype(jnp.bfloat16)
    return (results.reshape(TOKENS, D).astype(jnp.bfloat16), grads_in.reshape(TOKENS, D), totals[0], totals[1], totals[2], totals[3], totals[4], totals[5], totals[6], totals[7], totals[8], totals[9], totals[10], totals[11], factors, clipped_query, clipped_key)
```

```python
import functools

import jax
import jax.numpy as jnp
from jax import lax
from jax.experimental import pallas as pl
from jax.experimental.pallas import tpu as pltpu
from jax.sharding import PartitionSpec as P

HEAD_DIM = 64
EXPERTS = 12
FFN_EXPERTS = 8
CAP = 512
BLOCK = 512
EXTRA = 128
SMALL = 32
MESH = pl.DeviceIdType.MESH

epsilon = 1e-06
rope_base = 10000.0
bf16 = jnp.bfloat16
f32 = jnp.float32

NN = (((1,), (0,)), ((), ()))
NT = (((1,), (1,)), ((), ()))
TN = (((0,), (0,)), ((), ()))


def mm(left, right, dims=NN, precision=None):
    return lax.dot_general(
        left, right, dims, preferred_element_type=f32, precision=precision
    )


def params(mib=56, **more):
    return pltpu.CompilerParams(vmem_limit_bytes=mib * 1024 * 1024, **more)


def full(shape):
    return pl.BlockSpec(shape, lambda *_: (0,) * len(shape))


def zig(core, i):
    return 4 * (i // 2) + (core if i % 2 == 0 else 3 - core)


def qkv_kernel(x_ref, gain_ref, wt_ref, cos_ref, sin_ref, a_ref, qt_ref, kt_ref, k_ref, v_ref, vt_ref):
    heads = qt_ref.shape[0]
    width = heads * HEAD_DIM
    half = HEAD_DIM // 2
    x = x_ref[...].astype(f32)
    inverse = lax.rsqrt(jnp.mean(x * x, axis=1, keepdims=True) + epsilon)
    a = (x * inverse * gain_ref[...]).astype(bf16)
    a_ref[...] = a
    y = mm(wt_ref[...], a, NT)
    c, s = cos_ref[...], sin_ref[...]

    def turned(first):
        u, w = y[first : first + half], y[first + half : first + HEAD_DIM]
        return jnp.concatenate([u * c - w * s, w * c + u * s], axis=0)

    for h in range(heads):
        at = h * HEAD_DIM
        qt_ref[h] = (turned(at) * HEAD_DIM**-0.5).astype(bf16)
        key = turned(width + at)
        kt_ref[h] = key.astype(bf16)
        k_ref[h] = key.T.astype(bf16)
        value = y[2 * width + at : 2 * width + at + HEAD_DIM]
        v_ref[h] = value.T.astype(bf16)
        vt_ref[h, :HEAD_DIM] = value.astype(bf16)
        vt_ref[h, HEAD_DIM:] = jnp.ones((16, value.shape[1]), bf16)


def project(rows, gain, wt, cosine, sine, heads):
    total, width = rows.shape
    tile = BLOCK
    out = heads * HEAD_DIM
    return pl.pallas_call(
        qkv_kernel,
        grid=(total // tile,),
        in_specs=[
            pl.BlockSpec((tile, width), lambda i: (i, 0)),
            full((1, width)),
            full((3 * out, width)),
            pl.BlockSpec((HEAD_DIM // 2, tile), lambda i: (0, i)),
            pl.BlockSpec((HEAD_DIM // 2, tile), lambda i: (0, i)),
        ],
        out_specs=[
            pl.BlockSpec((tile, width), lambda i: (i, 0)),
            pl.BlockSpec((heads, HEAD_DIM, tile), lambda i: (0, 0, i)),
            pl.BlockSpec((heads, HEAD_DIM, tile), lambda i: (0, 0, i)),
            pl.BlockSpec((heads, tile, HEAD_DIM), lambda i: (0, i, 0)),
            pl.BlockSpec((heads, tile, HEAD_DIM), lambda i: (0, i, 0)),
            pl.BlockSpec((heads, HEAD_DIM + 16, tile), lambda i: (0, 0, i)),
        ],
        out_shape=[
            jax.ShapeDtypeStruct((total, width), bf16),
            jax.ShapeDtypeStruct((heads, HEAD_DIM, total), bf16),
            jax.ShapeDtypeStruct((heads, HEAD_DIM, total), bf16),
            jax.ShapeDtypeStruct((heads, total, HEAD_DIM), bf16),
            jax.ShapeDtypeStruct((heads, total, HEAD_DIM), bf16),
            jax.ShapeDtypeStruct((heads, HEAD_DIM + 16, total), bf16),
        ],
        compiler_params=params(),
        name="project",
    )(rows, gain, wt, cosine, sine)


def attend_kernel(table, length, qt_ref, k_ref, vt_ref, ot_ref, lse_ref, top_ref):
    index = table[pl.program_id(1)]
    qt = qt_ref[0]
    columns = qt.shape[1]

    def step(at, carry, diagonal):
        peak, total = carry
        start = pl.multiple_of(at * BLOCK, BLOCK)
        scores = mm(k_ref[0, pl.ds(start, BLOCK), :], qt)
        if diagonal:
            keys = lax.broadcasted_iota(jnp.int32, scores.shape, 0)
            queries = lax.broadcasted_iota(jnp.int32, scores.shape, 1)
            scores = jnp.where(keys <= queries, scores, -1e30)
        higher = jnp.maximum(peak, jnp.max(scores, axis=0, keepdims=True))
        weights = jnp.exp(scores - higher).astype(bf16)
        total = total * jnp.exp(peak - higher) + mm(vt_ref[0, :, pl.ds(start, BLOCK)], weights)
        return higher, total

    start = (jnp.full((1, columns), -1e30, f32), jnp.zeros((HEAD_DIM + 16, columns), f32))
    carry = lax.fori_loop(0, index, lambda at, c: step(at, c, False), start)
    peak, total = step(index, carry, True)
    mass = total[HEAD_DIM : HEAD_DIM + 1]
    ot_ref[0] = (total[:HEAD_DIM] / mass).astype(bf16)
    lse_ref[0, 0] = peak + jnp.log(mass)
    position = index * BLOCK + lax.broadcasted_iota(jnp.int32, peak.shape, 1)
    top_ref[0, 0] = jnp.where(position < length[0], peak, -1e30)


def attend(table, length, qt, k, vt):
    heads, _, total = qt.shape
    count = table.shape[0]
    return pl.pallas_call(
        attend_kernel,
        grid_spec=pltpu.PrefetchScalarGridSpec(
            num_scalar_prefetch=2,
            grid=(heads, count),
            in_specs=[
                pl.BlockSpec((1, HEAD_DIM, BLOCK), lambda h, i, t, n: (h, 0, t[i])),
                pl.BlockSpec((1, total, HEAD_DIM), lambda h, i, t, n: (h, 0, 0)),
                pl.BlockSpec((1, HEAD_DIM + 16, total), lambda h, i, t, n: (h, 0, 0)),
            ],
            out_specs=[
                pl.BlockSpec((1, HEAD_DIM, BLOCK), lambda h, i, t, n: (i, h, 0)),
                pl.BlockSpec((1, 1, 1, BLOCK), lambda h, i, t, n: (h, i, 0, 0)),
                pl.BlockSpec((1, 1, 1, BLOCK), lambda h, i, t, n: (h, i, 0, 0)),
            ],
        ),
        out_shape=[
            jax.ShapeDtypeStruct((count, heads * HEAD_DIM, BLOCK), bf16),
            jax.ShapeDtypeStruct((heads, count, 1, BLOCK), f32),
            jax.ShapeDtypeStruct((heads, count, 1, BLOCK), f32),
        ],
        compiler_params=params(),
        name="attend",
    )(table, length, qt, k, vt)


def revisit_kernel(table, qt_ref, k_ref, kt_ref, v_ref, ot_ref, got_ref, lse_ref, dq_ref, dk_ref, dv_ref, sum_k, sum_v):
    i = pl.program_id(1)
    index = table[i]
    qt, got = qt_ref[0], got_ref[0]
    lse = lse_ref[0, 0]
    centre = jnp.sum(ot_ref[0].astype(f32) * got.astype(f32), axis=0, keepdims=True)

    @pl.when(i == 0)
    def _():
        sum_k[...] = jnp.zeros_like(sum_k)
        sum_v[...] = jnp.zeros_like(sum_v)

    def step(at, grad, diagonal):
        start = pl.multiple_of(at * BLOCK, BLOCK)
        here = pl.ds(start, BLOCK)
        scores = mm(k_ref[0, here, :], qt)
        probs = jnp.exp(scores - lse)
        if diagonal:
            keys = lax.broadcasted_iota(jnp.int32, scores.shape, 0)
            queries = lax.broadcasted_iota(jnp.int32, scores.shape, 1)
            probs = jnp.where(keys <= queries, probs, 0.0)
        grad_probs = mm(v_ref[0, here, :], got)
        grad_scores = (probs * (grad_probs - centre)).astype(bf16)
        sum_v[here, :] += mm(probs.astype(bf16), got, NT)
        sum_k[here, :] += mm(grad_scores, qt, NT)
        return grad + mm(kt_ref[0, :, here], grad_scores)

    grad = lax.fori_loop(0, index, lambda at, c: step(at, c, False), jnp.zeros(qt.shape, f32))
    dq_ref[0] = step(index, grad, True) * HEAD_DIM**-0.5

    @pl.when(i == pl.num_programs(1) - 1)
    def _():
        dk_ref[0] = sum_k[...].T
        dv_ref[0] = sum_v[...].T


def revisit(table, qt, k, kt, v, ot, got, lse):
    heads, _, total = qt.shape
    count = table.shape[0]
    whole = pl.BlockSpec((1, HEAD_DIM, total), lambda h, i, t: (h, 0, 0))
    tall = pl.BlockSpec((1, total, HEAD_DIM), lambda h, i, t: (h, 0, 0))
    dealt = pl.BlockSpec((1, HEAD_DIM, BLOCK), lambda h, i, t: (i, h, 0))
    placed = pl.BlockSpec((1, HEAD_DIM, BLOCK), lambda h, i, t: (h, 0, t[i]))
    return pl.pallas_call(
        revisit_kernel,
        grid_spec=pltpu.PrefetchScalarGridSpec(
            num_scalar_prefetch=1,
            grid=(heads, count),
            in_specs=[
                placed,
                tall,
                whole,
                tall,
                dealt,
                dealt,
                pl.BlockSpec((1, 1, 1, BLOCK), lambda h, i, t: (h, i, 0, 0)),
            ],
            out_specs=[placed, whole, whole],
            scratch_shapes=[
                pltpu.VMEM((total, HEAD_DIM), f32),
                pltpu.VMEM((total, HEAD_DIM), f32),
            ],
        ),
        out_shape=[jax.ShapeDtypeStruct((heads, HEAD_DIM, total), f32)] * 3,
        compiler_params=params(),
        name="revisit",
    )(table, qt, k, kt, v, ot, got, lse)


def unproject_kernel(owned, dq_ref, dk_ref, dv_ref, cos_ref, sin_ref, a_ref, wt_ref, part_ref, gw_ref, total):
    heads = dq_ref.shape[0]
    half = HEAD_DIM // 2
    i = pl.program_id(0)
    c, s = cos_ref[...], sin_ref[...]

    def turned(g):
        u, w = g[:half], g[half:]
        return jnp.concatenate([u * c + w * s, w * c - u * s], axis=0)

    mine = owned[i] > 0
    pieces = [turned(jnp.where(mine, dq_ref[h], 0.0)) for h in range(heads)]
    pieces += [turned(dk_ref[h]) for h in range(heads)]
    pieces += [dv_ref[h] for h in range(heads)]
    grads = jnp.concatenate(pieces, axis=0).astype(bf16)
    part_ref[...] = mm(grads, wt_ref[...], TN).astype(bf16)

    @pl.when(i == 0)
    def _():
        total[...] = jnp.zeros_like(total)

    total[...] += mm(grads, a_ref[...])

    @pl.when(i == pl.num_programs(0) - 1)
    def _():
        gw_ref[...] = total[...].astype(bf16)


def unproject(owned, dq, dk, dv, cosine, sine, a, wt):
    heads, _, rows = dq.shape
    width = a.shape[1]
    out = wt.shape[0]
    piece = pl.BlockSpec((heads, HEAD_DIM, BLOCK), lambda i, o: (0, 0, i))
    table = pl.BlockSpec((HEAD_DIM // 2, BLOCK), lambda i, o: (0, i))
    return pl.pallas_call(
        unproject_kernel,
        grid_spec=pltpu.PrefetchScalarGridSpec(
            num_scalar_prefetch=1,
            grid=(rows // BLOCK,),
            in_specs=[
                piece,
                piece,
                piece,
                table,
                table,
                pl.BlockSpec((BLOCK, width), lambda i, o: (i, 0)),
                full((out, width)),
            ],
            out_specs=[pl.BlockSpec((BLOCK, width), lambda i, o: (i, 0)), full((out, width))],
            scratch_shapes=[pltpu.VMEM((out, width), f32)],
        ),
        out_shape=[
            jax.ShapeDtypeStruct((rows, width), bf16),
            jax.ShapeDtypeStruct((out, width), bf16),
        ],
        compiler_params=params(),
        name="unproject",
    )(owned, dq, dk, dv, cosine, sine, a, wt)


def greet(me_c, me_t, nc, nt):
    barrier = pltpu.get_barrier_semaphore()
    for step in range(1, nc * nt):
        other = lax.rem(me_c * nt + me_t + step, nc * nt)
        pl.semaphore_signal(
            barrier,
            inc=1,
            device_id={"ctx": other // nt, "tp": lax.rem(other, nt)},
            device_id_type=MESH,
        )
    pl.semaphore_wait(barrier, nc * nt - 1)


def to_owner_kernel(nc, nt, o_ref, att_ref, send_sem, recv_sem, local_sem):
    c, t = lax.axis_index("ctx"), lax.axis_index("tp")
    own = c * nt + t
    count = o_ref.shape[0]
    greet(c, t, nc, nt)
    copies = []
    for i in range(count):
        block = zig(c, i)
        copy = pltpu.make_async_remote_copy(
            src_ref=o_ref.at[i],
            dst_ref=att_ref.at[t],
            send_sem=send_sem.at[i],
            recv_sem=recv_sem.at[t],
            device_id={"ctx": block // nt, "tp": lax.rem(block, nt)},
            device_id_type=MESH,
        )
        local = pltpu.make_async_copy(o_ref.at[i], att_ref.at[t], local_sem)
        copies.append((block, copy, local))
    for block, copy, local in copies:

        @pl.when(block != own)
        def _():
            copy.start()

        @pl.when(block == own)
        def _():
            local.start()

    for block, copy, local in copies:

        @pl.when(block != own)
        def _():
            copy.wait_send()

        @pl.when(block == own)
        def _():
            local.wait()

    mine = lax.rem((own + 1) // 2, 2) == c
    for source in range(nt):

        @pl.when(jnp.logical_or(jnp.logical_not(mine), source != t))
        def _():
            pltpu.make_async_remote_copy(
                src_ref=o_ref.at[0],
                dst_ref=att_ref.at[source],
                send_sem=send_sem.at[0],
                recv_sem=recv_sem.at[source],
                device_id={"ctx": c, "tp": t},
                device_id_type=MESH,
            ).wait_recv()


def to_heads_kernel(nc, nt, o_ref, got_ref, send_sem, recv_sem, local_sem):
    c, t = lax.axis_index("ctx"), lax.axis_index("tp")
    own = c * nt + t
    count = got_ref.shape[0]
    greet(c, t, nc, nt)
    core = lax.rem((own + 1) // 2, 2)
    slot = 2 * (own // 4) + lax.rem(own, 4) // 2
    for target in range(nt):
        here = jnp.logical_and(core == c, target == t)

        @pl.when(jnp.logical_not(here))
        def _():
            pltpu.make_async_remote_copy(
                src_ref=o_ref.at[target],
                dst_ref=got_ref.at[slot],
                send_sem=send_sem.at[target],
                recv_sem=recv_sem.at[slot],
                device_id={"ctx": core, "tp": target},
                device_id_type=MESH,
            ).start()

        @pl.when(here)
        def _():
            pltpu.make_async_copy(o_ref.at[target], got_ref.at[slot], local_sem).start()

    for target in range(nt):
        here = jnp.logical_and(core == c, target == t)

        @pl.when(jnp.logical_not(here))
        def _():
            pltpu.make_async_remote_copy(
                src_ref=o_ref.at[target],
                dst_ref=got_ref.at[slot],
                send_sem=send_sem.at[target],
                recv_sem=recv_sem.at[slot],
                device_id={"ctx": core, "tp": target},
                device_id_type=MESH,
            ).wait_send()

        @pl.when(here)
        def _():
            pltpu.make_async_copy(o_ref.at[target], got_ref.at[slot], local_sem).wait()

    for i in range(count):

        @pl.when(zig(c, i) != own)
        def _():
            pltpu.make_async_remote_copy(
                src_ref=o_ref.at[0],
                dst_ref=got_ref.at[i],
                send_sem=send_sem.at[0],
                recv_sem=recv_sem.at[i],
                device_id={"ctx": c, "tp": t},
                device_id_type=MESH,
            ).wait_recv()


def exchange(kernel, value, count, number, name):
    nc, nt = lax.axis_size("ctx"), lax.axis_size("tp")
    return pl.pallas_call(
        functools.partial(kernel, nc, nt),
        in_specs=[pl.BlockSpec(memory_space=pltpu.VMEM)],
        out_specs=pl.BlockSpec(memory_space=pltpu.VMEM),
        out_shape=jax.ShapeDtypeStruct((count,) + value.shape[1:], value.dtype),
        scratch_shapes=[
            pltpu.SemaphoreType.DMA((value.shape[0],)),
            pltpu.SemaphoreType.DMA((count,)),
            pltpu.SemaphoreType.DMA,
        ],
        compiler_params=params(collective_id=number, has_side_effects=True),
        name=name,
    )(value)


def mixing(n2, wrc, previous, routes):
    z = mm(n2, wrc, precision=lax.Precision.HIGHEST)
    lane = lax.broadcasted_iota(jnp.int32, z.shape, 1)
    logits = z + previous
    hot = [lane == routes[:, r : r + 1] for r in range(2)]
    picked = [jnp.sum(jnp.where(hot[r], logits, 0.0), axis=1, keepdims=True) for r in range(2)]
    most = jnp.maximum(picked[0], picked[1])
    e = [jnp.exp(p - most) for p in picked]
    gates = [v / (e[0] + e[1]) for v in e]
    combine = jnp.where(hot[0], gates[0], 0.0) + jnp.where(hot[1], gates[1], 0.0)

    def column(array, at):
        return jnp.sum(jnp.where(lane == at, array, 0.0), axis=1, keepdims=True)

    alphas = []
    for j in range(2):
        first, second = column(z, EXPERTS + 2 * j), column(z, EXPERTS + 2 * j + 1)
        most = jnp.maximum(first, second)
        a, b = jnp.exp(first - most), jnp.exp(second - most)
        alphas.append((a / (a + b), b / (a + b)))
    weights = [column(combine, FFN_EXPERTS + 1 + j) for j in range(3)]
    return hot, gates, combine, alphas, weights


def forward_kernel(place, x_ref, att_ref, wo_ref, gain_ref, wrc_ref, vec_ref, prev_ref, routes_ref, res_ref, base_ref, a_ref, comb_ref):
    heads_in = att_ref.shape[0] * att_ref.shape[1]
    att = att_ref[...].reshape(heads_in, att_ref.shape[2])
    res = x_ref[...].astype(f32) + mm(att, wo_ref[...], TN)
    res_ref[...] = res
    inverse = lax.rsqrt(jnp.mean(res * res, axis=1, keepdims=True) + epsilon)
    n2 = res * inverse * gain_ref[...]
    a_ref[...] = n2.astype(bf16)
    _, _, combine, alphas, weights = mixing(n2, wrc_ref[...], prev_ref[...], routes_ref[...])
    scale = weights[0] + weights[1] * alphas[0][0] + weights[2] * alphas[1][0]
    base_ref[...] = (
        res
        + scale * n2
        + (weights[1] * alphas[0][1]) * vec_ref[0:1]
        + (weights[2] * alphas[1][1]) * vec_ref[1:2]
    )
    comb_ref[...] = combine.T[:16]


def forward_rows(place, x, att, wo, gain, wrc, vec, prev, routes):
    rows, width = x.shape
    own = lambda i, p: (p[0], 0)
    return pl.pallas_call(
        forward_kernel,
        grid_spec=pltpu.PrefetchScalarGridSpec(
            num_scalar_prefetch=1,
            grid=(1,),
            in_specs=[
                full(x.shape),
                full(att.shape),
                full(wo.shape),
                full(gain.shape),
                full(wrc.shape),
                full(vec.shape),
                pl.BlockSpec((rows, prev.shape[1]), own),
                pl.BlockSpec((rows, 2), own),
            ],
            out_specs=[full((rows, width)), full((rows, width)), full((rows, width)), full((16, rows))],
        ),
        out_shape=[
            jax.ShapeDtypeStruct((rows, width), f32),
            jax.ShapeDtypeStruct((rows, width), f32),
            jax.ShapeDtypeStruct((rows, width), bf16),
            jax.ShapeDtypeStruct((16, rows), f32),
        ],
        compiler_params=params(),
        name="forward_rows",
    )(place, x, att, wo, gain, wrc, vec, prev, routes)


def backward_kernel(place, res_ref, dn_ref, cot_ref, valid_ref, att_ref, wo_ref, gain_ref, wrc_ref, vec_ref, prev_ref, routes_ref,
                    dres_ref, got_ref, gwo_ref, small_ref):
    width = res_ref.shape[1]
    res = res_ref[...]
    gain = gain_ref[...]
    inverse = lax.rsqrt(jnp.mean(res * res, axis=1, keepdims=True) + epsilon)
    m = res * inverse
    n2 = m * gain
    hot, gates, _, alphas, weights = mixing(n2, wrc_ref[...], prev_ref[...], routes_ref[...])
    g = cot_ref[...].astype(f32) * valid_ref[...]
    inner = jnp.sum(g * n2, axis=1, keepdims=True)
    onto = [jnp.sum(g * vec_ref[j : j + 1], axis=1, keepdims=True) for j in range(2)]
    named = dn_ref[:, width:].astype(f32)
    lane = lax.broadcasted_iota(jnp.int32, hot[0].shape, 1)
    wide = lax.broadcasted_iota(jnp.int32, named.shape, 1)
    local = {
        FFN_EXPERTS + 1: inner,
        FFN_EXPERTS + 2: alphas[0][0] * inner + alphas[0][1] * onto[0],
        FFN_EXPERTS + 3: alphas[1][0] * inner + alphas[1][1] * onto[1],
    }
    routes = routes_ref[...]
    dgates = []
    for r in range(2):
        name = routes[:, r : r + 1]
        there = jnp.where((wide == name) | (wide == name + 16), named, 0.0)
        there = jnp.where(name < FFN_EXPERTS, jnp.sum(there, axis=1, keepdims=True), 0.0)
        for e, value in local.items():
            there = there + jnp.where(name == e, value, 0.0)
        dgates.append(there)
    mean = gates[0] * dgates[0] + gates[1] * dgates[1]
    dz = jnp.where(hot[0], gates[0] * (dgates[0] - mean), 0.0)
    dz = dz + jnp.where(hot[1], gates[1] * (dgates[1] - mean), 0.0)
    for j in range(2):
        da = weights[1 + j] * inner
        db = weights[1 + j] * onto[j]
        centre = alphas[j][0] * da + alphas[j][1] * db
        dz = dz + jnp.where(lane == EXPERTS + 2 * j, alphas[j][0] * (da - centre), 0.0)
        dz = dz + jnp.where(lane == EXPERTS + 2 * j + 1, alphas[j][1] * (db - centre), 0.0)
    scale = weights[0] + weights[1] * alphas[0][0] + weights[2] * alphas[1][0]
    highest = lax.Precision.HIGHEST
    dn2 = dn_ref[:, :width].astype(f32) + scale * g + mm(dz, wrc_ref[...], NT, highest)
    small_ref[0:16] = mm(dz, n2, TN, highest)
    small_ref[16:24] = jnp.zeros((8, width), f32)
    small_ref[16:17] = jnp.sum((weights[1] * alphas[0][1]) * g, axis=0, keepdims=True)
    small_ref[17:18] = jnp.sum((weights[2] * alphas[1][1]) * g, axis=0, keepdims=True)
    small_ref[18:19] = jnp.sum(dn2 * m, axis=0, keepdims=True)
    q = dn2 * gain
    dres = g + inverse * (q - m * jnp.mean(q * m, axis=1, keepdims=True))
    dres_ref[...] = dres
    da = dres.astype(bf16)
    got = mm(wo_ref[...], da, NT).astype(bf16)
    got_ref[...] = got.reshape(got_ref.shape)
    att = att_ref[...].reshape(got.shape)
    gwo_ref[...] = mm(att, da).astype(bf16)


def backward_rows(place, res, dn, cot, valid, att, wo, gain, wrc, vec, prev, routes):
    rows, width = res.shape
    own = lambda i, p: (p[0], 0)
    return pl.pallas_call(
        backward_kernel,
        grid_spec=pltpu.PrefetchScalarGridSpec(
            num_scalar_prefetch=1,
            grid=(1,),
            in_specs=[
                full(res.shape),
                full(dn.shape),
                full(cot.shape),
                full(valid.shape),
                full(att.shape),
                full(wo.shape),
                full(gain.shape),
                full(wrc.shape),
                full(vec.shape),
                pl.BlockSpec((rows, prev.shape[1]), own),
                pl.BlockSpec((rows, 2), own),
            ],
            out_specs=[full((rows, width)), full(att.shape), full((wo.shape[0], width)), full((24, width))],
        ),
        out_shape=[
            jax.ShapeDtypeStruct((rows, width), f32),
            jax.ShapeDtypeStruct(att.shape, bf16),
            jax.ShapeDtypeStruct((wo.shape[0], width), bf16),
            jax.ShapeDtypeStruct((24, width), f32),
        ],
        compiler_params=params(),
        name="backward_rows",
    )(place, res, dn, cot, valid, att, wo, gain, wrc, vec, prev, routes)


def finish_kernel(x_ref, dn_ref, dres_ref, gain_ref, base_ref, feed_ref, valid_ref, gin_ref, out_ref, small_ref):
    x = x_ref[...].astype(f32)
    inverse = lax.rsqrt(jnp.mean(x * x, axis=1, keepdims=True) + epsilon)
    m = x * inverse
    dn = dn_ref[...].astype(f32)
    q = dn * gain_ref[...]
    gin_ref[...] = dres_ref[...] + inverse * (q - m * jnp.mean(q * m, axis=1, keepdims=True))
    small_ref[...] = jnp.sum(dn * m, axis=0, keepdims=True)
    out_ref[...] = (valid_ref[...] * (base_ref[...] + feed_ref[...].astype(f32))).astype(bf16)


def finish_rows(x, dn, dres, gain, base, feed, valid):
    rows, width = x.shape
    return pl.pallas_call(
        finish_kernel,
        out_shape=[
            jax.ShapeDtypeStruct((rows, width), f32),
            jax.ShapeDtypeStruct((rows, width), bf16),
            jax.ShapeDtypeStruct((1, width), f32),
        ],
        compiler_params=params(),
        name="finish_rows",
    )(x, dn, dres, gain, base, feed, valid)


def place_kernel(per, rt_ref, rc_ref, row_ref, col_ref):
    total = rt_ref.shape[1]
    one = lax.broadcasted_iota(jnp.int32, (BLOCK, BLOCK), 0)
    two = lax.broadcasted_iota(jnp.int32, (BLOCK, BLOCK), 1)
    before_row = (one < two).astype(bf16)
    before_col = (two < one).astype(bf16)
    row_carry = col_carry = None
    for at in range(0, total, BLOCK):
        if at % per == 0:
            row_carry = jnp.zeros((16, 1), f32)
            col_carry = jnp.zeros((1, 16), f32)
        here = slice(at, at + BLOCK)
        expert = lax.broadcasted_iota(jnp.int32, (16, BLOCK), 0)
        member = (rt_ref[0:1, here] == expert) | (rt_ref[1:2, here] == expert)
        rank = mm(member.astype(bf16), before_row) + row_carry
        row_ref[:, here] = jnp.where(member, rank, -1.0)
        row_carry = row_carry + jnp.sum(member.astype(f32), axis=1, keepdims=True)
        expert = lax.broadcasted_iota(jnp.int32, (BLOCK, 16), 1)
        member = (rc_ref[here, 0:1] == expert) | (rc_ref[here, 1:2] == expert)
        rank = mm(before_col, member.astype(bf16)) + col_carry
        col_ref[here, :] = jnp.where(member, rank, -1.0)
        col_carry = col_carry + jnp.sum(member.astype(f32), axis=0, keepdims=True)


def place_rows(routes, per):
    total = routes.shape[0]
    return pl.pallas_call(
        functools.partial(place_kernel, per),
        out_shape=[
            jax.ShapeDtypeStruct((16, total), f32),
            jax.ShapeDtypeStruct((total, 16), f32),
        ],
        compiler_params=params(),
        name="place_rows",
    )(routes.T, routes)


def fetch_kernel(first, row_ref, comb_ref, rows_ref, out_ref, gate_ref):
    expert = first[0] + pl.program_id(1)
    slot = lax.broadcasted_iota(jnp.int32, (CAP, row_ref.shape[1]), 0).astype(f32)
    hot = slot == row_ref[pl.ds(expert, 1), :]
    out_ref[0] = mm(hot.astype(bf16), rows_ref[...]).astype(bf16)
    if gate_ref is not None:
        gate_ref[0] = jnp.sum(jnp.where(hot, comb_ref[pl.ds(expert, 1), :], 0.0), axis=1, keepdims=True)


def fetch_rows(first, row, comb, rows, per, local, gated):
    total, width = rows.shape
    blocks = total // per
    outs = [jax.ShapeDtypeStruct((local, blocks * CAP, width), bf16)]
    specs = [pl.BlockSpec((1, CAP, width), lambda b, j, f: (j, b, 0))]
    ins = [
        pl.BlockSpec((16, per), lambda b, j, f: (0, b)),
        pl.BlockSpec((16, per), lambda b, j, f: (0, b)),
        pl.BlockSpec((per, width), lambda b, j, f: (b, 0)),
    ]
    args = (row, comb, rows)
    if gated:
        outs.append(jax.ShapeDtypeStruct((local, blocks * CAP, 1), f32))
        specs.append(pl.BlockSpec((1, CAP, 1), lambda b, j, f: (j, b, 0)))
        body = fetch_kernel
    else:
        body = lambda f, p, r, o: fetch_kernel(f, p, None, r, o, None)
        del ins[1]
        args = (row, rows)
    return pl.pallas_call(
        body,
        grid_spec=pltpu.PrefetchScalarGridSpec(
            num_scalar_prefetch=1, grid=(blocks, local), in_specs=ins, out_specs=specs
        ),
        out_shape=outs,
        compiler_params=params(),
        name="fetch_rows",
    )(first, *args)


def expert_kernel(j, first, x_ref, g_ref, gate_ref, w_ref, feed_ref, back_ref, gw_ref, total):
    i = pl.program_id(0)
    parts, _, depth, hidden = w_ref.shape
    width = parts * depth
    wg, wu, wd = [w_ref[:, k].reshape(width, hidden) for k in range(3)]
    x, g, gate = x_ref[0], g_ref[0], gate_ref[0]
    gate_pre = mm(x, wg)
    up = mm(x, wu)
    sigmoid = 1.0 / (1.0 + jnp.exp(-gate_pre))
    activated = gate_pre * sigmoid
    inner = (activated * up).astype(bf16)
    out = mm(inner, wd, NT)
    g32 = g.astype(f32)
    feed_ref[...] = (gate * out).astype(bf16)
    dgate = jnp.sum(g32 * out, axis=1, keepdims=True)
    dout = (gate * g32).astype(bf16)
    dinner = mm(dout, wd)
    dpre = (dinner * up * sigmoid * (1.0 + gate_pre * (1.0 - sigmoid))).astype(bf16)
    dup = (dinner * activated).astype(bf16)
    back_ref[:, :width] = (mm(dpre, wg, NT) + mm(dup, wu, NT)).astype(bf16)
    lane = lax.broadcasted_iota(jnp.int32, (dgate.shape[0], back_ref.shape[1] - width), 1)
    coarse = dgate.astype(bf16).astype(f32)
    at = first[0] + j
    extra = jnp.where(lane == at, coarse, jnp.where(lane == at + 16, dgate - coarse, 0.0))
    back_ref[:, width:] = extra.astype(bf16)

    @pl.when(i == 0)
    def _():
        total[...] = jnp.zeros_like(total)

    total[0] += mm(x, dpre, TN)
    total[1] += mm(x, dup, TN)
    total[2] += mm(dout, inner, TN)

    @pl.when(i == pl.num_programs(0) - 1)
    def _():
        for k in range(3):
            gw_ref[:, k] = total[k].reshape(parts, depth, hidden).astype(bf16)


def expert(j, first, x, g, gate, w):
    slots, width = x.shape[1:]
    parts, _, depth, hidden = w.shape
    pick = lambda i, f: (j, i, 0)
    return pl.pallas_call(
        functools.partial(expert_kernel, j),
        grid_spec=pltpu.PrefetchScalarGridSpec(
            num_scalar_prefetch=1,
            grid=(slots // CAP,),
            in_specs=[
                pl.BlockSpec((1, CAP, width), pick),
                pl.BlockSpec((1, CAP, width), pick),
                pl.BlockSpec((1, CAP, 1), pick),
                full(w.shape),
            ],
            out_specs=[
                pl.BlockSpec((CAP, width), lambda i, f: (i, 0)),
                pl.BlockSpec((CAP, width + EXTRA), lambda i, f: (i, 0)),
                full(w.shape),
            ],
            scratch_shapes=[pltpu.VMEM((3, width, hidden), f32)],
        ),
        out_shape=[
            jax.ShapeDtypeStruct((slots, width), bf16),
            jax.ShapeDtypeStruct((slots, width + EXTRA), bf16),
            jax.ShapeDtypeStruct(w.shape, bf16),
        ],
        compiler_params=params(),
        name="expert",
    )(first, x, g, gate, w)


def spread_kernel(local, first, col_ref, *refs):
    out_ref = refs[-1]
    lane = lax.broadcasted_iota(jnp.int32, col_ref.shape, 1)
    slot = lax.broadcasted_iota(jnp.int32, (col_ref.shape[0], CAP), 1).astype(f32)
    total = None
    for j in range(local):
        mine = jnp.sum(jnp.where(lane == first[0] + j, col_ref[...], 0.0), axis=1, keepdims=True)
        term = mm((slot == mine).astype(bf16), refs[j][...])
        total = term if total is None else total + term
    out_ref[...] = total.astype(bf16)


def spread_rows(first, col, values, per):
    total = col.shape[0]
    tile = BLOCK
    width = values[0].shape[1]
    return pl.pallas_call(
        functools.partial(spread_kernel, len(values)),
        grid_spec=pltpu.PrefetchScalarGridSpec(
            num_scalar_prefetch=1,
            grid=(total // tile,),
            in_specs=[pl.BlockSpec((tile, 16), lambda i, f: (i, 0))]
            + [pl.BlockSpec((CAP, width), lambda i, f: (i // (per // tile), 0)) for _ in values],
            out_specs=pl.BlockSpec((tile, width), lambda i, f: (i, 0)),
        ),
        out_shape=jax.ShapeDtypeStruct((total, width), bf16),
        compiler_params=params(),
        name="spread_rows",
    )(first, col, *values)


def shards(
    hidden_in,
    cotangent,
    lengths,
    routes,
    prev_logits,
    norm_attn,
    w_query,
    w_key,
    w_value,
    w_out,
    norm_moe,
    w_router,
    w_const,
    const_vec,
    w_gate,
    w_up,
    w_down,
    threshold,
):
    plane = ("ctx", "tp")
    core, lane = lax.axis_index("ctx"), lax.axis_index("tp")
    nc, nt, ns = lax.axis_size("ctx"), lax.axis_size("tp"), lax.axis_size("shard")
    own, width = hidden_in.shape
    per = own * nt
    total = per * nc
    depth = w_gate.shape[1]
    heads = w_query.shape[1] // HEAD_DIM
    head_width = heads * HEAD_DIM
    local = FFN_EXPERTS // nc
    count = total // BLOCK // nc
    first_row = core * per + lane * own
    length = lengths[0]
    valid = (first_row + jnp.arange(own, dtype=jnp.int32) < length).astype(f32)[:, None]
    place = lane.astype(jnp.int32)[None]
    first = (core * local).astype(jnp.int32)[None]

    pack = jnp.concatenate(
        [
            w_query,
            w_key,
            w_value,
            w_out.T,
            norm_attn[:, None],
            norm_moe[:, None],
            w_router,
            w_const,
            const_vec.T,
            jnp.zeros((depth, 12), bf16),
        ],
        axis=1,
    )
    rows_all = lax.all_gather(hidden_in, plane, axis=0, tiled=True)
    packed = lax.all_gather(pack, "shard", axis=0, tiled=True)
    expert_w = []
    for j in range(local):
        pieces = [
            lax.dynamic_index_in_dim(w, core * local + j, 0, keepdims=False)
            for w in (w_gate, w_up, w_down)
        ]
        gathered = lax.all_gather(jnp.stack(pieces), "shard", axis=0, tiled=False)
        expert_w.append(gathered)

    wt = packed[:, : 3 * head_width].T
    out_t = packed[:, 3 * head_width : 4 * head_width]
    wo = lax.all_gather(out_t, "tp", axis=0, tiled=False)
    wo = wo.transpose(0, 2, 1).reshape(nt * head_width, width)
    smalls = packed[:, 4 * head_width :].astype(f32)
    gain_attn = smalls[:, 0][None]
    gain_moe = smalls[:, 1][None]
    wrc = smalls[:, 2 : 2 + EXPERTS + 4]
    vec = smalls[:, 2 + EXPERTS + 4 : 4 + EXPERTS + 4].T
    prev = jnp.pad(prev_logits, ((0, 0), (0, 4)))

    freqs = rope_base ** (-2.0 * jnp.arange(HEAD_DIM // 2).astype(f32) / HEAD_DIM)
    angles = freqs[:, None] * jnp.arange(total).astype(f32)[None, :]
    cosine, sine = jnp.cos(angles), jnp.sin(angles)

    a1, qt, kt, k, v, vt = project(rows_all, gain_attn, wt, cosine, sine, heads)
    table = jnp.stack([zig(core, i) for i in range(count)]).astype(jnp.int32)
    blocks = jnp.arange(total // BLOCK, dtype=jnp.int32)
    owned = jnp.any(blocks[:, None] == table[None, :], axis=1).astype(jnp.int32)
    ot, lse, top = attend(table, lengths, qt, k, vt)
    att = exchange(to_owner_kernel, ot, nt, 0, "to_owner")
    head_max = lax.pmax(jnp.max(top, axis=(1, 2, 3)), ("shard", "ctx"))
    factors = threshold[0] / jnp.maximum(head_max, threshold[0])
    root = jnp.repeat(jnp.sqrt(factors), HEAD_DIM)
    clipped_query = (w_query.astype(f32) * root[None, :]).astype(bf16)
    clipped_key = (w_key.astype(f32) * root[None, :]).astype(bf16)

    res, base, a2, comb = forward_rows(place, hidden_in, att, wo, gain_moe, wrc, vec, prev, routes)

    routes_all = lax.all_gather(routes, "ctx", axis=0, tiled=True)
    row_at, col_at = place_rows(routes_all, per)
    cot = (cotangent.astype(f32) * valid).astype(bf16)
    cot_all = lax.all_gather(cot, plane, axis=0, tiled=True)
    (g_slots,) = fetch_rows(first, row_at, None, cot_all, per, local, False)
    a2_all = lax.all_gather(a2, plane, axis=0, tiled=True)
    comb_all = lax.all_gather(comb, plane, axis=0, tiled=False)
    comb_all = comb_all.transpose(1, 0, 2).reshape(16, total)
    x_slots, gate_slots = fetch_rows(first, row_at, comb_all, a2_all, per, local, True)
    feeds, backs, grads = [], [], []
    for j in range(local):
        feed, back, grad = expert(j, first, x_slots, g_slots, gate_slots, expert_w[j])
        feeds.append(feed)
        backs.append(back)
        grads.append(grad)
    back = spread_rows(first, col_at, backs, per)
    back = lax.psum_scatter(back, plane, scatter_dimension=0, tiled=True)
    feed = spread_rows(first, col_at, feeds, per)
    feed = lax.psum_scatter(feed, plane, scatter_dimension=0, tiled=True)
    grads = [lax.psum_scatter(g, "shard", scatter_dimension=0, tiled=True)[0] for g in grads]

    dres, got, grad_out, small = backward_rows(
        place, res, back, cotangent, valid, att, wo, gain_moe, wrc, vec, prev, routes
    )
    got = exchange(to_heads_kernel, got, count, 1, "to_heads")
    dq, dk, dv = revisit(table, qt, k, kt, v, ot, got, lse)
    part, grad_qkv = unproject(owned, dq, dk, dv, cosine, sine, a1, wt)
    part = lax.psum_scatter(part, plane, scatter_dimension=0, tiled=True)
    grad_input, output, gain_row = finish_rows(
        hidden_in, part, dres, gain_attn, base, feed, valid
    )

    grad_expert = lax.all_gather(jnp.stack(grads), "ctx", axis=0, tiled=True).astype(f32)
    grad_gate, grad_up, grad_down = [grad_expert[:, k] for k in range(3)]
    grad_qkv = lax.psum_scatter(
        lax.psum(grad_qkv, "ctx").reshape(3 * head_width, ns, depth).transpose(1, 0, 2),
        "shard",
        scatter_dimension=0,
        tiled=False,
    )
    grad_q, grad_k, grad_v = [
        grad_qkv[i * head_width : (i + 1) * head_width].T.astype(f32) for i in range(3)
    ]
    grad_out = lax.psum_scatter(grad_out, "tp", scatter_dimension=0, tiled=True)
    grad_out = lax.psum(grad_out, "ctx").reshape(head_width, ns, depth).transpose(1, 0, 2)
    grad_out = lax.psum_scatter(grad_out, "shard", scatter_dimension=0, tiled=False).astype(f32)
    small = jnp.concatenate([small[:19], gain_row], axis=0)
    small = lax.psum(small, ("shard", "ctx", "tp"))
    small = lax.dynamic_slice_in_dim(small, lax.axis_index("shard") * depth, depth, 1)
    return (
        output,
        grad_input,
        small[19],
        grad_q,
        grad_k,
        grad_v,
        grad_out,
        small[18],
        small[:EXPERTS].T,
        small[EXPERTS : EXPERTS + 4].T,
        small[16:18],
        grad_gate,
        grad_up,
        grad_down,
        factors,
        clipped_query,
        clipped_key,
    )


def solution(mesh):
    return jax.shard_map(
        shards,
        mesh=mesh,
        in_specs=(
            P(("shard", "ctx", "tp"), None),
            P(("shard", "ctx", "tp"), None),
            P("shard"),
            P(("shard", "ctx"), None),
            P(("shard", "ctx"), None),
            P("shard"),
            P("shard", "tp"),
            P("shard", "tp"),
            P("shard", "tp"),
            P("tp", "shard"),
            P("shard"),
            P("shard", None),
            P("shard", None),
            P(None, "shard"),
            P(None, "shard", "tp"),
            P(None, "shard", "tp"),
            P(None, "shard", "tp"),
            P(),
        ),
        out_specs=(
            P(("shard", "ctx", "tp"), None),
            P(("shard", "ctx", "tp"), None),
            P("shard"),
            P("shard", "tp"),
            P("shard", "tp"),
            P("shard", "tp"),
            P("tp", "shard"),
            P("shard"),
            P("shard", None),
            P("shard", None),
            P(None, "shard"),
            P(None, "shard", "tp"),
            P(None, "shard", "tp"),
            P(None, "shard", "tp"),
            P("tp"),
            P("shard", "tp"),
            P("shard", "tp"),
        ),
        check_vma=False,
    )
```

```python
import functools

import jax
import jax.numpy as jnp
from jax import lax
from jax.experimental import pallas as pl
from jax.experimental.pallas import tpu as pltpu
from jax.sharding import PartitionSpec as P

HEAD_DIM = 64
EXPERTS = 12
FFN_EXPERTS = 8
CAP = 512
BLOCK = 512
EXTRA = 128
SMALL = 32
MESH = pl.DeviceIdType.MESH

epsilon = 1e-06
rope_base = 10000.0
bf16 = jnp.bfloat16
f32 = jnp.float32

NN = (((1,), (0,)), ((), ()))
NT = (((1,), (1,)), ((), ()))
TN = (((0,), (0,)), ((), ()))


def mm(left, right, dims=NN, precision=None):
    return lax.dot_general(
        left, right, dims, preferred_element_type=f32, precision=precision
    )


def params(mib=56, **more):
    return pltpu.CompilerParams(vmem_limit_bytes=mib * 1024 * 1024, **more)


def cost(us):
    return pl.CostEstimate(flops=int(us * 1e9), bytes_accessed=int(us * 3e6), transcendentals=0)


def full(shape):
    return pl.BlockSpec(shape, lambda *_: (0,) * len(shape))


def zig(core, i):
    return 4 * (i // 2) + (core if i % 2 == 0 else 3 - core)


def qkv_kernel(x_ref, gain_ref, wt_ref, cos_ref, sin_ref, qt_ref, kt_ref, k_ref, v_ref, vt_ref):
    heads = qt_ref.shape[0]
    width = heads * HEAD_DIM
    half = HEAD_DIM // 2
    x = x_ref[...].astype(f32)
    inverse = lax.rsqrt(jnp.mean(x * x, axis=1, keepdims=True) + epsilon)
    a = (x * inverse * gain_ref[...]).astype(bf16)
    y = mm(wt_ref[...], a, NT)
    c, s = cos_ref[...], sin_ref[...]

    def turned(first):
        u, w = y[first : first + half], y[first + half : first + HEAD_DIM]
        return jnp.concatenate([u * c - w * s, w * c + u * s], axis=0)

    for h in range(heads):
        at = h * HEAD_DIM
        qt_ref[h] = (turned(at) * HEAD_DIM**-0.5).astype(bf16)
        key = turned(width + at)
        kt_ref[h] = key.astype(bf16)
        k_ref[h] = key.T.astype(bf16)
        value = y[2 * width + at : 2 * width + at + HEAD_DIM]
        v_ref[h] = value.T.astype(bf16)
        vt_ref[h, :HEAD_DIM] = value.astype(bf16)
        vt_ref[h, HEAD_DIM:] = jnp.ones((16, value.shape[1]), bf16)


def project(rows, gain, wt, cosine, sine, heads):
    total, width = rows.shape
    tile = BLOCK
    out = heads * HEAD_DIM
    return pl.pallas_call(
        qkv_kernel,
        grid=(total // tile,),
        in_specs=[
            pl.BlockSpec((tile, width), lambda i: (i, 0)),
            full((1, width)),
            full((3 * out, width)),
            pl.BlockSpec((HEAD_DIM // 2, tile), lambda i: (0, i)),
            pl.BlockSpec((HEAD_DIM // 2, tile), lambda i: (0, i)),
        ],
        out_specs=[
            pl.BlockSpec((heads, HEAD_DIM, tile), lambda i: (0, 0, i)),
            pl.BlockSpec((heads, HEAD_DIM, tile), lambda i: (0, 0, i)),
            pl.BlockSpec((heads, tile, HEAD_DIM), lambda i: (0, i, 0)),
            pl.BlockSpec((heads, tile, HEAD_DIM), lambda i: (0, i, 0)),
            pl.BlockSpec((heads, HEAD_DIM + 16, tile), lambda i: (0, 0, i)),
        ],
        out_shape=[
            jax.ShapeDtypeStruct((heads, HEAD_DIM, total), bf16),
            jax.ShapeDtypeStruct((heads, HEAD_DIM, total), bf16),
            jax.ShapeDtypeStruct((heads, total, HEAD_DIM), bf16),
            jax.ShapeDtypeStruct((heads, total, HEAD_DIM), bf16),
            jax.ShapeDtypeStruct((heads, HEAD_DIM + 16, total), bf16),
        ],
        compiler_params=params(),
        cost_estimate=cost(13),
        name="project",
    )(rows, gain, wt, cosine, sine)


def attend_kernel(table, length, qt_ref, k_ref, vt_ref, ot_ref, lse_ref, top_ref):
    index = table[pl.program_id(1)]
    qt = qt_ref[0]
    columns = qt.shape[1]

    def step(at, carry, diagonal):
        peak, total = carry
        start = pl.multiple_of(at * BLOCK, BLOCK)
        scores = mm(k_ref[0, pl.ds(start, BLOCK), :], qt)
        if diagonal:
            keys = lax.broadcasted_iota(jnp.int32, scores.shape, 0)
            queries = lax.broadcasted_iota(jnp.int32, scores.shape, 1)
            scores = jnp.where(keys <= queries, scores, -1e30)
        higher = jnp.maximum(peak, jnp.max(scores, axis=0, keepdims=True))
        weights = jnp.exp(scores - higher).astype(bf16)
        total = total * jnp.exp(peak - higher) + mm(vt_ref[0, :, pl.ds(start, BLOCK)], weights)
        return higher, total

    start = (jnp.full((1, columns), -1e30, f32), jnp.zeros((HEAD_DIM + 16, columns), f32))
    carry = lax.fori_loop(0, index, lambda at, c: step(at, c, False), start)
    peak, total = step(index, carry, True)
    mass = total[HEAD_DIM : HEAD_DIM + 1]
    ot_ref[0] = (total[:HEAD_DIM] / mass).astype(bf16)
    lse_ref[0, 0] = peak + jnp.log(mass)
    position = index * BLOCK + lax.broadcasted_iota(jnp.int32, peak.shape, 1)
    top_ref[0, 0] = jnp.where(position < length[0], peak, -1e30)


def attend(table, length, qt, k, vt):
    heads, _, total = qt.shape
    count = table.shape[0]
    return pl.pallas_call(
        attend_kernel,
        grid_spec=pltpu.PrefetchScalarGridSpec(
            num_scalar_prefetch=2,
            grid=(heads, count),
            in_specs=[
                pl.BlockSpec((1, HEAD_DIM, BLOCK), lambda h, i, t, n: (h, 0, t[i])),
                pl.BlockSpec((1, total, HEAD_DIM), lambda h, i, t, n: (h, 0, 0)),
                pl.BlockSpec((1, HEAD_DIM + 16, total), lambda h, i, t, n: (h, 0, 0)),
            ],
            out_specs=[
                pl.BlockSpec((1, HEAD_DIM, BLOCK), lambda h, i, t, n: (i, h, 0)),
                pl.BlockSpec((1, 1, 1, BLOCK), lambda h, i, t, n: (h, i, 0, 0)),
                pl.BlockSpec((1, 1, 1, BLOCK), lambda h, i, t, n: (h, i, 0, 0)),
            ],
        ),
        out_shape=[
            jax.ShapeDtypeStruct((count, heads * HEAD_DIM, BLOCK), bf16),
            jax.ShapeDtypeStruct((heads, count, 1, BLOCK), f32),
            jax.ShapeDtypeStruct((heads, count, 1, BLOCK), f32),
        ],
        compiler_params=params(),
        cost_estimate=cost(35),
        name="attend",
    )(table, length, qt, k, vt)


def revisit_kernel(table, qt_ref, k_ref, kt_ref, v_ref, ot_ref, got_ref, lse_ref, dq_ref, dk_ref, dv_ref, sum_k, sum_v):
    i = pl.program_id(1)
    index = table[i]
    qt, got = qt_ref[0], got_ref[0]
    lse = lse_ref[0, 0]
    centre = jnp.sum(ot_ref[0].astype(f32) * got.astype(f32), axis=0, keepdims=True)

    @pl.when(i == 0)
    def _():
        sum_k[...] = jnp.zeros_like(sum_k)
        sum_v[...] = jnp.zeros_like(sum_v)

    def step(at, grad, diagonal):
        start = pl.multiple_of(at * BLOCK, BLOCK)
        here = pl.ds(start, BLOCK)
        scores = mm(k_ref[0, here, :], qt)
        probs = jnp.exp(scores - lse)
        if diagonal:
            keys = lax.broadcasted_iota(jnp.int32, scores.shape, 0)
            queries = lax.broadcasted_iota(jnp.int32, scores.shape, 1)
            probs = jnp.where(keys <= queries, probs, 0.0)
        grad_probs = mm(v_ref[0, here, :], got)
        grad_scores = (probs * (grad_probs - centre)).astype(bf16)
        sum_v[here, :] += mm(probs.astype(bf16), got, NT)
        sum_k[here, :] += mm(grad_scores, qt, NT)
        return grad + mm(kt_ref[0, :, here], grad_scores)

    grad = lax.fori_loop(0, index, lambda at, c: step(at, c, False), jnp.zeros(qt.shape, f32))
    dq_ref[0] = step(index, grad, True) * HEAD_DIM**-0.5

    @pl.when(i == pl.num_programs(1) - 1)
    def _():
        dk_ref[0] = sum_k[...].T
        dv_ref[0] = sum_v[...].T


def revisit(table, qt, k, kt, v, ot, got, lse):
    heads, _, total = qt.shape
    count = table.shape[0]
    whole = pl.BlockSpec((1, HEAD_DIM, total), lambda h, i, t: (h, 0, 0))
    tall = pl.BlockSpec((1, total, HEAD_DIM), lambda h, i, t: (h, 0, 0))
    dealt = pl.BlockSpec((1, HEAD_DIM, BLOCK), lambda h, i, t: (i, h, 0))
    placed = pl.BlockSpec((1, HEAD_DIM, BLOCK), lambda h, i, t: (h, 0, t[i]))
    return pl.pallas_call(
        revisit_kernel,
        grid_spec=pltpu.PrefetchScalarGridSpec(
            num_scalar_prefetch=1,
            grid=(heads, count),
            in_specs=[
                placed,
                tall,
                whole,
                tall,
                dealt,
                dealt,
                pl.BlockSpec((1, 1, 1, BLOCK), lambda h, i, t: (h, i, 0, 0)),
            ],
            out_specs=[placed, whole, whole],
            scratch_shapes=[
                pltpu.VMEM((total, HEAD_DIM), f32),
                pltpu.VMEM((total, HEAD_DIM), f32),
            ],
        ),
        out_shape=[jax.ShapeDtypeStruct((heads, HEAD_DIM, total), f32)] * 3,
        compiler_params=params(),
        cost_estimate=cost(50),
        name="revisit",
    )(table, qt, k, kt, v, ot, got, lse)


def unproject_kernel(owned, dq_ref, dk_ref, dv_ref, cos_ref, sin_ref, x_ref, gain_ref, wt_ref, go_ref, small_ref,
                     part_ref, gw_ref, smalls_ref, total, row):
    heads = dq_ref.shape[0]
    half = HEAD_DIM // 2
    i = pl.program_id(0)
    c, s = cos_ref[...], sin_ref[...]

    def turned(g):
        u, w = g[:half], g[half:]
        return jnp.concatenate([u * c + w * s, w * c - u * s], axis=0)

    @pl.when(i == 0)
    def _():
        total[...] = jnp.zeros_like(total)
        row[...] = jnp.zeros_like(row)

    x = x_ref[...].astype(f32)
    m = x * lax.rsqrt(jnp.mean(x * x, axis=1, keepdims=True) + epsilon)
    a = (m * gain_ref[...]).astype(bf16)
    mine = owned[i] > 0
    pieces = [turned(jnp.where(mine, dq_ref[h], 0.0)) for h in range(heads)]
    pieces += [turned(dk_ref[h]) for h in range(heads)]
    pieces += [dv_ref[h] for h in range(heads)]
    grads = jnp.concatenate(pieces, axis=0).astype(bf16)
    part = mm(grads, wt_ref[...], TN)
    part_ref[...] = part.astype(bf16)
    row[...] += jnp.sum(part * m, axis=0, keepdims=True)
    total[...] += mm(grads, a)

    @pl.when(i == pl.num_programs(0) - 1)
    def _():
        _, parts, rows, depth = gw_ref.shape
        mid = rows // 2
        at = lax.broadcasted_iota(jnp.int32, small_ref.shape, 0)
        smalls = small_ref[...] + jnp.where(at == 19, row[...], 0.0)
        for z in range(parts):
            here = slice(z * depth, (z + 1) * depth)
            gw_ref[0, z] = total[:rows, here].astype(bf16)
            gw_ref[1, z, :mid] = total[rows:, here].astype(bf16)
            gw_ref[1, z, mid:] = go_ref[:, here]
            smalls_ref[z] = smalls[:, here]


def unproject(owned, dq, dk, dv, cosine, sine, x, gain, wt, go, small, parts):
    heads, _, rows = dq.shape
    width = x.shape[1]
    out = wt.shape[0]
    depth = width // parts
    piece = pl.BlockSpec((heads, HEAD_DIM, BLOCK), lambda i, o: (0, 0, i))
    table = pl.BlockSpec((HEAD_DIM // 2, BLOCK), lambda i, o: (0, i))
    shapes = [
        jax.ShapeDtypeStruct((rows, width), bf16),
        jax.ShapeDtypeStruct((2, parts, 2 * heads * HEAD_DIM, depth), bf16),
        jax.ShapeDtypeStruct((parts,) + small.shape[:1] + (depth,), f32),
    ]
    return pl.pallas_call(
        unproject_kernel,
        grid_spec=pltpu.PrefetchScalarGridSpec(
            num_scalar_prefetch=1,
            grid=(rows // BLOCK,),
            in_specs=[
                piece,
                piece,
                piece,
                table,
                table,
                pl.BlockSpec((BLOCK, width), lambda i, o: (i, 0)),
                full(gain.shape),
                full(wt.shape),
                full(go.shape),
                full(small.shape),
            ],
            out_specs=[pl.BlockSpec((BLOCK, width), lambda i, o: (i, 0))] + [full(v.shape) for v in shapes[1:]],
            scratch_shapes=[pltpu.VMEM((out, width), f32), pltpu.VMEM((1, width), f32)],
        ),
        out_shape=shapes,
        compiler_params=params(),
        cost_estimate=cost(18),
        name="unproject",
    )(owned, dq, dk, dv, cosine, sine, x, gain, wt, go, small)


def spot():
    return lax.axis_index("shard"), lax.axis_index("ctx"), lax.axis_index("tp")


def across(t):
    return t + 1 - 2 * lax.rem(t, 2), lax.rem(t + 2, 4), 3 - t


def remote(source, target, sends, recvs, **where):
    return pltpu.make_async_remote_copy(
        src_ref=source,
        dst_ref=target,
        send_sem=sends,
        recv_sem=recvs,
        device_id=where,
        device_id_type=MESH,
    )


def greet(depth=True):
    z, c, t = spot()
    nc, nt, ns = lax.axis_size("ctx"), lax.axis_size("tp"), lax.axis_size("shard")
    barrier = pltpu.get_barrier_semaphore()
    for step in range(1, nc * nt):
        other = lax.rem(c * nt + t + step, nc * nt)
        pl.semaphore_signal(
            barrier,
            inc=1,
            device_id={"ctx": other // nt, "tp": lax.rem(other, nt)},
            device_id_type=MESH,
        )
    if depth:
        for step in range(1, ns):
            pl.semaphore_signal(
                barrier,
                inc=1,
                device_id={"shard": lax.rem(z + step, ns)},
                device_id_type=MESH,
            )
    pl.semaphore_wait(barrier, nc * nt - 1 + (ns - 1 if depth else 0))


class Gather:
    KINDS = 9

    def __init__(self, x, out, sends, recvs, own, cuts):
        z, c, t = spot()
        tx, ty, td = across(t)
        rows = x.shape[0] // cuts
        half = rows // 2
        self.cuts = cuts
        self.own = pltpu.make_async_copy(x, out.at[4 * c + t], own)
        sib = {"ctx": 1 - c}
        px, py = {"tp": tx}, {"tp": ty}

        def copies(s):
            whole = pl.ds(s * rows, rows)
            one, two = pl.ds(s * rows, half), pl.ds(s * rows + half, half)

            def at(k, source, target, where):
                return remote(source, target, sends.at[s, k], recvs.at[s, k], **where)

            def keep(k, slot, part, where):
                ref = out.at[4 * c + slot, part]
                return at(k, ref, ref, where)

            mine = [
                at(k, x.at[whole], out.at[4 * c + t, whole], where)
                for k, where in enumerate((px, py, sib))
            ]
            return mine + [
                keep(3, tx, whole, sib),
                keep(4, tx, one, py),
                keep(5, ty, whole, sib),
                keep(6, ty, two, px),
                keep(7, td, one, sib),
                keep(8, td, two, sib),
            ]

        self.copies = [copies(s) for s in range(cuts)]

        def arrivals(s):
            whole = pl.ds(s * rows, rows)
            one, two = pl.ds(s * rows, half), pl.ds(s * rows + half, half)
            where = [(c, tx, whole), (c, ty, whole), (1 - c, t, whole)]
            where += [(1 - c, tx, whole), (c, td, one), (1 - c, ty, whole), (c, td, two)]
            where += [(1 - c, td, one), (1 - c, td, two)]
            return [
                remote(out.at[4 * d + slot, part], out.at[4 * d + slot, part], sends.at[s, k], recvs.at[s, k], **sib)
                for k, (d, slot, part) in enumerate(where)
            ]

        self.arrivals = [arrivals(s) for s in range(cuts)]

    @staticmethod
    def scratch(cuts):
        return [
            pltpu.SemaphoreType.DMA((cuts, Gather.KINDS)),
            pltpu.SemaphoreType.DMA((cuts, Gather.KINDS)),
            pltpu.SemaphoreType.DMA,
        ]

    def first(self):
        for s in range(self.cuts):
            for k in (0, 1, 2):
                self.copies[s][k].start()
        self.own.start()

    def second(self):
        for s in range(self.cuts):
            self.arrivals[s][0].wait_recv()
            self.copies[s][4].start()
            self.copies[s][3].start()
            self.arrivals[s][1].wait_recv()
            self.copies[s][6].start()
            self.copies[s][5].start()

    def third(self):
        for s in range(self.cuts):
            for k in (4, 6):
                self.arrivals[s][k].wait_recv()
                self.copies[s][7 if k == 4 else 8].start()

    def last(self):
        for s in range(self.cuts):
            for k in (2, 3, 5, 7, 8):
                self.arrivals[s][k].wait_recv()
        for s in range(self.cuts):
            for k in range(self.KINDS):
                self.copies[s][k].wait_send()
        self.own.wait()


class Sum:
    def __init__(self, p, held, came, across_in, across_out, sends, recvs, loads):
        z, c, t = spot()
        self.t = t
        tx, ty, td = across(t)
        half = p.shape[1] // 2
        self.half = half
        self.one, self.two = pl.ds(0, half), pl.ds(half, half)
        self.order = (td, tx, ty, t)
        self.held, self.came, self.inn = held, came, across_in
        sib, px, py = {"ctx": 1 - c}, {"tp": tx}, {"tp": ty}
        self.loads = [pltpu.make_async_copy(p.at[4 * c + o], held.at[o], loads.at[k]) for k, o in enumerate(self.order)]
        self.core = []
        for k, o in enumerate(self.order):
            self.core.append(remote(p.at[4 * (1 - c) + o], came.at[o], sends.at[k], recvs.at[k], **sib))

        def send(k, source, slot, where):
            return remote(source, across_in.at[slot], sends.at[k], recvs.at[k], **where)

        self.side = {
            "dx": send(4, held.at[td, self.one], 0, px),
            "dy": send(5, held.at[td, self.two], 1, py),
            "x": send(6, held.at[tx, self.one], 2, px),
            "y": send(7, held.at[ty, self.two], 3, py),
            "cy": send(8, across_out.at[0], 4, py),
            "cx": send(9, across_out.at[1], 5, px),
        }
        self.out = across_out
        self.near = (tx, ty, td)

    @staticmethod
    def scratch(rows, width):
        return [
            pltpu.VMEM((4, rows, width), bf16),
            pltpu.VMEM((4, rows, width), bf16),
            pltpu.VMEM((6, rows // 2, width), bf16),
            pltpu.VMEM((2, rows // 2, width), bf16),
            pltpu.SemaphoreType.DMA((10,)),
            pltpu.SemaphoreType.DMA((10,)),
            pltpu.SemaphoreType.DMA((4,)),
        ]

    def first(self):
        for k in range(4):
            self.core[k].start()
            self.loads[k].start()

    def second(self):
        for k, o in enumerate(self.order):
            self.loads[k].wait()
            self.core[k].wait_recv()
            self.held[o] = (self.held[o].astype(f32) + self.came[o].astype(f32)).astype(bf16)
            if k == 0:
                self.side["dx"].start()
                self.side["dy"].start()
            if k == 1:
                self.side["x"].start()
            if k == 2:
                self.side["y"].start()

    def third(self):
        tx, ty, td = self.near
        self.side["dx"].wait_recv()
        self.out[0] = (self.held[ty, self.one].astype(f32) + self.inn[0].astype(f32)).astype(bf16)
        self.side["cy"].start()
        self.side["dy"].wait_recv()
        self.out[1] = (self.held[tx, self.two].astype(f32) + self.inn[1].astype(f32)).astype(bf16)
        self.side["cx"].start()

    def last(self):
        for k in ("x", "y", "cy", "cx"):
            self.side[k].wait_recv()
        for copy in self.core + list(self.side.values()):
            copy.wait_send()

    def total(self):
        def add(part, a, b):
            return self.held[self.t, part].astype(f32) + self.inn[a].astype(f32) + self.inn[b].astype(f32)

        return add(self.one, 2, 4), add(self.two, 3, 5)


def anywhere(count):
    return [pl.BlockSpec(memory_space=pl.ANY)] * count


def opening_kernel(cuts, x_ref, pack_ref, routes_ref, out_ref, packs_ref, all_routes_ref, *sems):
    gather = Gather(x_ref, out_ref, *sems[:3], cuts)
    sends, recvs, local = sems[3:]
    z, c, t = spot()
    ns = lax.axis_size("shard")
    greet()
    gather.first()
    pairs = []
    for step in range(1, ns):
        there, back = lax.rem(z + step, ns), lax.rem(z + ns - step, ns)
        copy = remote(pack_ref, packs_ref.at[z], sends.at[step], recvs.at[step], shard=there)
        copy.start()
        came = remote(pack_ref, packs_ref.at[back], sends.at[step], recvs.at[step], shard=there)
        pairs.append((copy, came))
    copy = remote(routes_ref, all_routes_ref.at[c], sends.at[0], recvs.at[0], ctx=1 - c)
    copy.start()
    pairs.append((copy, remote(routes_ref, all_routes_ref.at[1 - c], sends.at[0], recvs.at[0], ctx=1 - c)))
    mine = [
        pltpu.make_async_copy(pack_ref, packs_ref.at[z], local.at[0]),
        pltpu.make_async_copy(routes_ref, all_routes_ref.at[c], local.at[1]),
    ]
    for copy in mine:
        copy.start()
    gather.second()
    gather.third()
    gather.last()
    for copy, came in pairs:
        came.wait_recv()
        copy.wait_send()
    for copy in mine:
        copy.wait()


def opening(x, pack, routes, number):
    cuts = 2
    ns = lax.axis_size("shard")
    return pl.pallas_call(
        functools.partial(opening_kernel, cuts),
        in_specs=anywhere(3),
        out_specs=anywhere(3),
        out_shape=[
            jax.ShapeDtypeStruct((8,) + x.shape, x.dtype),
            jax.ShapeDtypeStruct((ns,) + pack.shape, pack.dtype),
            jax.ShapeDtypeStruct((2,) + routes.shape, routes.dtype),
        ],
        scratch_shapes=Gather.scratch(cuts)
        + [
            pltpu.SemaphoreType.DMA((ns,)),
            pltpu.SemaphoreType.DMA((ns,)),
            pltpu.SemaphoreType.DMA((2,)),
        ],
        compiler_params=params(16, collective_id=number, has_side_effects=True),
        cost_estimate=cost(30),
        name="opening",
    )(x, pack, routes)


def gather_kernel(cuts, count, *refs):
    xs, comb, outs, combs, sems = refs[:count], refs[count], refs[count + 1 : 2 * count + 1], refs[2 * count + 1], refs[2 * count + 2 :]
    gathers = [Gather(x, out, *sems[3 * i : 3 * i + 3], cuts) for i, (x, out) in enumerate(zip(xs, outs))]
    sends, recvs, local = sems[3 * count :]
    z, c, t = spot()
    own = 4 * c + t
    greet(False)
    for gather in gathers:
        gather.first()
    pairs = []
    for step in range(1, 8):
        other, back = lax.rem(own + step, 8), lax.rem(own + 8 - step, 8)
        where = {"ctx": other // 4, "tp": lax.rem(other, 4)}
        copy = remote(comb, combs.at[own], sends.at[step], recvs.at[step], **where)
        copy.start()
        pairs.append((copy, remote(comb, combs.at[back], sends.at[step], recvs.at[step], **where)))
    mine = pltpu.make_async_copy(comb, combs.at[own], local)
    mine.start()
    for gather in gathers:
        gather.second()
    for gather in gathers:
        gather.third()
    for gather in gathers:
        gather.last()
    for copy, came in pairs:
        came.wait_recv()
        copy.wait_send()
    mine.wait()


def gather_rows(xs, comb, number):
    cuts = 2
    return pl.pallas_call(
        functools.partial(gather_kernel, cuts, len(xs)),
        in_specs=anywhere(len(xs) + 1),
        out_specs=anywhere(len(xs) + 1),
        out_shape=[jax.ShapeDtypeStruct((8,) + x.shape, x.dtype) for x in (*xs, comb)],
        scratch_shapes=Gather.scratch(cuts) * len(xs)
        + [
            pltpu.SemaphoreType.DMA((8,)),
            pltpu.SemaphoreType.DMA((8,)),
            pltpu.SemaphoreType.DMA,
        ],
        compiler_params=params(16, collective_id=number, has_side_effects=True),
        cost_estimate=cost(30 * len(xs)),
        name="gather_rows",
    )(*xs, comb)


def sum_kernel(p_ref, out_ref, *scratch):
    job = Sum(p_ref, *scratch)
    greet(False)
    job.first()
    job.second()
    job.third()
    job.last()
    one, two = job.total()
    out_ref[: job.half] = one.astype(out_ref.dtype)
    out_ref[job.half :] = two.astype(out_ref.dtype)


def sum_rows(p, number):
    _, rows, width = p.shape
    return pl.pallas_call(
        sum_kernel,
        in_specs=anywhere(1),
        out_specs=pl.BlockSpec(memory_space=pltpu.VMEM),
        out_shape=jax.ShapeDtypeStruct((rows, width), f32),
        scratch_shapes=Sum.scratch(rows, width),
        compiler_params=params(40, collective_id=number, has_side_effects=True),
        cost_estimate=cost(35),
        name="sum_rows",
    )(p)


def to_owner_kernel(o_ref, w_ref, att_ref, all_w_ref, send_sem, recv_sem, w_send, w_recv, local_sem):
    z, c, t = spot()
    nt = lax.axis_size("tp")
    own = c * nt + t
    count = o_ref.shape[0]
    greet(False)
    copies = []
    for i in range(count):
        block = zig(c, i)
        copy = remote(o_ref.at[i], att_ref.at[t], send_sem.at[i], recv_sem.at[t], ctx=block // nt, tp=lax.rem(block, nt))
        local = pltpu.make_async_copy(o_ref.at[i], att_ref.at[t], local_sem.at[0])
        copies.append((block, copy, local))
    for block, copy, local in copies:

        @pl.when(block != own)
        def _():
            copy.start()

        @pl.when(block == own)
        def _():
            local.start()

    pairs = []
    for step in range(1, nt):
        there, back = lax.rem(t + step, nt), lax.rem(t + nt - step, nt)
        copy = remote(w_ref, all_w_ref.at[t], w_send.at[step], w_recv.at[step], tp=there)
        copy.start()
        pairs.append((copy, remote(w_ref, all_w_ref.at[back], w_send.at[step], w_recv.at[step], tp=there)))
    mine_w = pltpu.make_async_copy(w_ref, all_w_ref.at[t], local_sem.at[1])
    mine_w.start()
    for block, copy, local in copies:

        @pl.when(block != own)
        def _():
            copy.wait_send()

        @pl.when(block == own)
        def _():
            local.wait()

    mine = lax.rem((own + 1) // 2, 2) == c
    for source in range(nt):

        @pl.when(jnp.logical_or(jnp.logical_not(mine), source != t))
        def _():
            remote(o_ref.at[0], att_ref.at[source], send_sem.at[0], recv_sem.at[source], ctx=c, tp=t).wait_recv()

    for copy, came in pairs:
        came.wait_recv()
        copy.wait_send()
    mine_w.wait()


def to_owner(o, w, number):
    nt = lax.axis_size("tp")
    return pl.pallas_call(
        to_owner_kernel,
        in_specs=anywhere(2),
        out_specs=anywhere(2),
        out_shape=[
            jax.ShapeDtypeStruct((nt,) + o.shape[1:], o.dtype),
            jax.ShapeDtypeStruct((nt,) + w.shape, w.dtype),
        ],
        scratch_shapes=[
            pltpu.SemaphoreType.DMA((o.shape[0],)),
            pltpu.SemaphoreType.DMA((nt,)),
            pltpu.SemaphoreType.DMA((nt,)),
            pltpu.SemaphoreType.DMA((nt,)),
            pltpu.SemaphoreType.DMA((2,)),
        ],
        compiler_params=params(16, collective_id=number, has_side_effects=True),
        cost_estimate=cost(10),
        name="to_owner",
    )(o, w)


def to_heads_kernel(o_ref, w_ref, got_ref, sum_ref, came_ref, own_ref, send_sem, recv_sem, w_send, w_recv, local_sem):
    z, c, t = spot()
    nt = lax.axis_size("tp")
    own = c * nt + t
    count = got_ref.shape[0]
    greet(False)
    core = lax.rem((own + 1) // 2, 2)
    slot = 2 * (own // 4) + lax.rem(own, 4) // 2
    copies = []
    for target in range(nt):
        here = jnp.logical_and(core == c, target == t)
        copy = remote(o_ref.at[target], got_ref.at[slot], send_sem.at[target], recv_sem.at[slot], ctx=core, tp=target)
        local = pltpu.make_async_copy(o_ref.at[target], got_ref.at[slot], local_sem.at[0])
        copies.append((here, copy, local))
    for here, copy, local in copies:

        @pl.when(jnp.logical_not(here))
        def _():
            copy.start()

        @pl.when(here)
        def _():
            local.start()

    pairs = []
    for step in range(1, nt):
        there = lax.rem(t + step, nt)
        copy = remote(w_ref.at[there], came_ref.at[step], w_send.at[step], w_recv.at[step], tp=there)
        copy.start()
        pairs.append(copy)
    mine = pltpu.make_async_copy(w_ref.at[t], own_ref, local_sem.at[1])
    mine.start()
    for here, copy, local in copies:

        @pl.when(jnp.logical_not(here))
        def _():
            copy.wait_send()

        @pl.when(here)
        def _():
            local.wait()

    for i in range(count):

        @pl.when(zig(c, i) != own)
        def _():
            remote(o_ref.at[0], got_ref.at[i], send_sem.at[0], recv_sem.at[i], ctx=c, tp=t).wait_recv()

    mine.wait()
    total = own_ref[...].astype(f32)
    for step, copy in enumerate(pairs):
        copy.wait_recv()
        total = total + came_ref[step + 1].astype(f32)
        copy.wait_send()
    sum_ref[...] = total.astype(bf16)


def to_heads(o, w, count, number):
    nt = lax.axis_size("tp")
    return pl.pallas_call(
        to_heads_kernel,
        in_specs=anywhere(2),
        out_specs=anywhere(1) + [pl.BlockSpec(memory_space=pltpu.VMEM)],
        out_shape=[
            jax.ShapeDtypeStruct((count,) + o.shape[1:], o.dtype),
            jax.ShapeDtypeStruct(w.shape[1:], w.dtype),
        ],
        scratch_shapes=[
            pltpu.VMEM(w.shape, w.dtype),
            pltpu.VMEM(w.shape[1:], w.dtype),
            pltpu.SemaphoreType.DMA((nt,)),
            pltpu.SemaphoreType.DMA((count,)),
            pltpu.SemaphoreType.DMA((nt,)),
            pltpu.SemaphoreType.DMA((nt,)),
            pltpu.SemaphoreType.DMA((2,)),
        ],
        compiler_params=params(16, collective_id=number, has_side_effects=True),
        cost_estimate=cost(12),
        name="to_heads",
    )(o, w)


def closing_kernel(p_ref, gw_ref, small_ref, top_ref, ge_ref, out_ref, gsum_ref, ssum_ref, tmax_ref, gall_ref,
                   gcore, gline, gmine, sline, splane, tline, *sems):
    job = Sum(p_ref, *sems[:7])
    sends, recvs, local = sems[7:]
    z, c, t = spot()
    ns = lax.axis_size("shard")
    rows = gw_ref.shape[2]
    own = 4 * c + t
    greet()
    started = []

    def go(k, source, target, **where):
        copy = remote(source, target, sends.at[k], recvs.at[k], **where)
        copy.start()
        started.append(copy)
        return copy

    core = go(0, gw_ref.at[1 - c], gcore, ctx=1 - c)
    small = [go(3 + s, small_ref.at[lax.rem(z + s, ns)], sline.at[s], shard=lax.rem(z + s, ns)) for s in range(1, ns)]
    tops = [go(3 + ns + s, top_ref, tline.at[s], shard=lax.rem(z + s, ns)) for s in range(1, ns)]
    own_g = pltpu.make_async_copy(gw_ref.at[c], gmine, local.at[0])
    own_g.start()
    job.first()
    experts = go(1, ge_ref, gall_ref.at[c], ctx=1 - c)
    own_e = pltpu.make_async_copy(ge_ref, gall_ref.at[c], local.at[1])
    own_e.start()
    job.second()
    own_g.wait()
    core.wait_recv()
    gmine[...] = (gmine[...].astype(f32) + gcore[...].astype(f32)).astype(bf16)
    line = [go(3 + 2 * ns + s, gmine.at[lax.rem(z + s, ns)], gline.at[s], shard=lax.rem(z + s, ns)) for s in range(1, ns)]
    for copy in small:
        copy.wait_recv()
    total = small_ref[z]
    for s in range(1, ns):
        total = total + sline[s]
    splane[0] = total
    plane = []
    for s in range(1, 8):
        other = lax.rem(own + s, 8)
        plane.append(go(3 + 3 * ns + s, splane.at[0], splane.at[s], ctx=other // 4, tp=lax.rem(other, 4)))
    for copy in tops:
        copy.wait_recv()
    high = top_ref[...]
    for s in range(1, ns):
        high = jnp.maximum(high, tline[s])
    tline[0] = high
    pair = go(2, tline.at[0], tline.at[ns], ctx=1 - c)
    job.third()
    for copy in line:
        copy.wait_recv()
    total = gmine[z].astype(f32)
    for s in range(1, ns):
        total = total + gline[s].astype(f32)
    gsum_ref[c] = total
    final = go(3, gsum_ref.at[c], gsum_ref.at[c], ctx=1 - c)
    for copy in plane:
        copy.wait_recv()
    total = splane[0]
    for s in range(1, 8):
        total = total + splane[s]
    ssum_ref[...] = total
    pair.wait_recv()
    tmax_ref[...] = jnp.maximum(tline[0], tline[ns])
    job.last()
    one, two = job.total()
    out_ref[: job.half] = one
    out_ref[job.half :] = two
    remote(gsum_ref.at[1 - c], gsum_ref.at[1 - c], sends.at[3], recvs.at[3], ctx=1 - c).wait_recv()
    remote(ge_ref, gall_ref.at[1 - c], sends.at[1], recvs.at[1], ctx=1 - c).wait_recv()
    own_e.wait()
    for copy in started:
        copy.wait_send()


def closing(p, gw, small, top, ge, number):
    _, rows, width = p.shape
    ns = lax.axis_size("shard")
    vmem = pl.BlockSpec(memory_space=pltpu.VMEM)
    return pl.pallas_call(
        closing_kernel,
        in_specs=anywhere(2) + [vmem, vmem] + anywhere(1),
        out_specs=[vmem, vmem, vmem, vmem] + anywhere(1),
        out_shape=[
            jax.ShapeDtypeStruct((rows, width), f32),
            jax.ShapeDtypeStruct((2,) + gw.shape[2:], f32),
            jax.ShapeDtypeStruct(small.shape[1:], f32),
            jax.ShapeDtypeStruct(top.shape, f32),
            jax.ShapeDtypeStruct((2,) + ge.shape, ge.dtype),
        ],
        scratch_shapes=[
            pltpu.VMEM(gw.shape[1:], bf16),
            pltpu.VMEM(gw.shape[1:], bf16),
            pltpu.VMEM(gw.shape[1:], bf16),
            pltpu.VMEM(small.shape, f32),
            pltpu.VMEM((8,) + small.shape[1:], f32),
            pltpu.VMEM((ns + 1,) + top.shape, f32),
        ]
        + Sum.scratch(rows, width)
        + [
            pltpu.SemaphoreType.DMA((3 * ns + 11,)),
            pltpu.SemaphoreType.DMA((3 * ns + 11,)),
            pltpu.SemaphoreType.DMA((2,)),
        ],
        compiler_params=params(48, collective_id=number, has_side_effects=True),
        cost_estimate=cost(40),
        name="closing",
    )(p, gw, small, top, ge)


def mixing(n2, wrc, previous, routes):
    z = mm(n2, wrc, precision=lax.Precision.HIGHEST)
    lane = lax.broadcasted_iota(jnp.int32, z.shape, 1)
    logits = z + previous
    hot = [lane == routes[:, r : r + 1] for r in range(2)]
    picked = [jnp.sum(jnp.where(hot[r], logits, 0.0), axis=1, keepdims=True) for r in range(2)]
    most = jnp.maximum(picked[0], picked[1])
    e = [jnp.exp(p - most) for p in picked]
    gates = [v / (e[0] + e[1]) for v in e]
    combine = jnp.where(hot[0], gates[0], 0.0) + jnp.where(hot[1], gates[1], 0.0)

    def column(array, at):
        return jnp.sum(jnp.where(lane == at, array, 0.0), axis=1, keepdims=True)

    alphas = []
    for j in range(2):
        first, second = column(z, EXPERTS + 2 * j), column(z, EXPERTS + 2 * j + 1)
        most = jnp.maximum(first, second)
        a, b = jnp.exp(first - most), jnp.exp(second - most)
        alphas.append((a / (a + b), b / (a + b)))
    weights = [column(combine, FFN_EXPERTS + 1 + j) for j in range(3)]
    return hot, gates, combine, alphas, weights


def forward_kernel(place, x_ref, att_ref, wo_ref, gain_ref, wrc_ref, vec_ref, prev_ref, routes_ref, res_ref, base_ref, a_ref, comb_ref):
    heads_in = att_ref.shape[0] * att_ref.shape[1]
    att = att_ref[...].reshape(heads_in, att_ref.shape[2])
    res = x_ref[...].astype(f32) + mm(att, wo_ref[...], TN)
    res_ref[...] = res
    inverse = lax.rsqrt(jnp.mean(res * res, axis=1, keepdims=True) + epsilon)
    n2 = res * inverse * gain_ref[...]
    a_ref[...] = n2.astype(bf16)
    _, _, combine, alphas, weights = mixing(n2, wrc_ref[...], prev_ref[...], routes_ref[...])
    scale = weights[0] + weights[1] * alphas[0][0] + weights[2] * alphas[1][0]
    base_ref[...] = (
        res
        + scale * n2
        + (weights[1] * alphas[0][1]) * vec_ref[0:1]
        + (weights[2] * alphas[1][1]) * vec_ref[1:2]
    )
    comb_ref[...] = combine.T[:16]


def forward_rows(place, x, att, wo, gain, wrc, vec, prev, routes):
    rows, width = x.shape
    own = lambda i, p: (p[0], 0)
    return pl.pallas_call(
        forward_kernel,
        grid_spec=pltpu.PrefetchScalarGridSpec(
            num_scalar_prefetch=1,
            grid=(1,),
            in_specs=[
                full(x.shape),
                full(att.shape),
                full(wo.shape),
                full(gain.shape),
                full(wrc.shape),
                full(vec.shape),
                pl.BlockSpec((rows, prev.shape[1]), own),
                pl.BlockSpec((rows, 2), own),
            ],
            out_specs=[full((rows, width)), full((rows, width)), full((rows, width)), full((16, rows))],
        ),
        out_shape=[
            jax.ShapeDtypeStruct((rows, width), f32),
            jax.ShapeDtypeStruct((rows, width), f32),
            jax.ShapeDtypeStruct((rows, width), bf16),
            jax.ShapeDtypeStruct((16, rows), f32),
        ],
        compiler_params=params(),
        cost_estimate=cost(8),
        name="forward_rows",
    )(place, x, att, wo, gain, wrc, vec, prev, routes)


def backward_kernel(place, res_ref, dn_ref, cot_ref, valid_ref, att_ref, wo_ref, gain_ref, wrc_ref, vec_ref, prev_ref, routes_ref,
                    dres_ref, got_ref, gwo_ref, small_ref):
    width = res_ref.shape[1]
    res = res_ref[...]
    gain = gain_ref[...]
    inverse = lax.rsqrt(jnp.mean(res * res, axis=1, keepdims=True) + epsilon)
    m = res * inverse
    n2 = m * gain
    hot, gates, _, alphas, weights = mixing(n2, wrc_ref[...], prev_ref[...], routes_ref[...])
    g = cot_ref[...].astype(f32) * valid_ref[...]
    inner = jnp.sum(g * n2, axis=1, keepdims=True)
    onto = [jnp.sum(g * vec_ref[j : j + 1], axis=1, keepdims=True) for j in range(2)]
    named = dn_ref[:, width:].astype(f32)
    lane = lax.broadcasted_iota(jnp.int32, hot[0].shape, 1)
    wide = lax.broadcasted_iota(jnp.int32, named.shape, 1)
    local = {
        FFN_EXPERTS + 1: inner,
        FFN_EXPERTS + 2: alphas[0][0] * inner + alphas[0][1] * onto[0],
        FFN_EXPERTS + 3: alphas[1][0] * inner + alphas[1][1] * onto[1],
    }
    routes = routes_ref[...]
    dgates = []
    for r in range(2):
        name = routes[:, r : r + 1]
        there = jnp.where((wide == name) | (wide == name + 16), named, 0.0)
        there = jnp.where(name < FFN_EXPERTS, jnp.sum(there, axis=1, keepdims=True), 0.0)
        for e, value in local.items():
            there = there + jnp.where(name == e, value, 0.0)
        dgates.append(there)
    mean = gates[0] * dgates[0] + gates[1] * dgates[1]
    dz = jnp.where(hot[0], gates[0] * (dgates[0] - mean), 0.0)
    dz = dz + jnp.where(hot[1], gates[1] * (dgates[1] - mean), 0.0)
    for j in range(2):
        da = weights[1 + j] * inner
        db = weights[1 + j] * onto[j]
        centre = alphas[j][0] * da + alphas[j][1] * db
        dz = dz + jnp.where(lane == EXPERTS + 2 * j, alphas[j][0] * (da - centre), 0.0)
        dz = dz + jnp.where(lane == EXPERTS + 2 * j + 1, alphas[j][1] * (db - centre), 0.0)
    scale = weights[0] + weights[1] * alphas[0][0] + weights[2] * alphas[1][0]
    highest = lax.Precision.HIGHEST
    dn2 = dn_ref[:, :width].astype(f32) + scale * g + mm(dz, wrc_ref[...], NT, highest)
    small_ref[0:16] = mm(dz, n2, TN, highest)
    small_ref[16:24] = jnp.zeros((8, width), f32)
    small_ref[16:17] = jnp.sum((weights[1] * alphas[0][1]) * g, axis=0, keepdims=True)
    small_ref[17:18] = jnp.sum((weights[2] * alphas[1][1]) * g, axis=0, keepdims=True)
    small_ref[18:19] = jnp.sum(dn2 * m, axis=0, keepdims=True)
    q = dn2 * gain
    dres = g + inverse * (q - m * jnp.mean(q * m, axis=1, keepdims=True))
    dres_ref[...] = dres
    da = dres.astype(bf16)
    got = mm(wo_ref[...], da, NT).astype(bf16)
    got_ref[...] = got.reshape(got_ref.shape)
    att = att_ref[...].reshape(got.shape)
    gwo_ref[...] = mm(att, da).astype(bf16)


def backward_rows(place, res, dn, cot, valid, att, wo, gain, wrc, vec, prev, routes):
    rows, width = res.shape
    own = lambda i, p: (p[0], 0)
    return pl.pallas_call(
        backward_kernel,
        grid_spec=pltpu.PrefetchScalarGridSpec(
            num_scalar_prefetch=1,
            grid=(1,),
            in_specs=[
                full(res.shape),
                full(dn.shape),
                full(cot.shape),
                full(valid.shape),
                full(att.shape),
                full(wo.shape),
                full(gain.shape),
                full(wrc.shape),
                full(vec.shape),
                pl.BlockSpec((rows, prev.shape[1]), own),
                pl.BlockSpec((rows, 2), own),
            ],
            out_specs=[full((rows, width)), full(att.shape), full((wo.shape[0], width)), full((24, width))],
        ),
        out_shape=[
            jax.ShapeDtypeStruct((rows, width), f32),
            jax.ShapeDtypeStruct(att.shape, bf16),
            jax.ShapeDtypeStruct((wo.shape[0], width), bf16),
            jax.ShapeDtypeStruct((24, width), f32),
        ],
        compiler_params=params(),
        cost_estimate=cost(15),
        name="backward_rows",
    )(place, res, dn, cot, valid, att, wo, gain, wrc, vec, prev, routes)


def finish_kernel(x_ref, dn_ref, dres_ref, gain_ref, base_ref, feed_ref, valid_ref, gin_ref, out_ref):
    x = x_ref[...].astype(f32)
    inverse = lax.rsqrt(jnp.mean(x * x, axis=1, keepdims=True) + epsilon)
    m = x * inverse
    dn = dn_ref[...].astype(f32)
    q = dn * gain_ref[...]
    gin_ref[...] = dres_ref[...] + inverse * (q - m * jnp.mean(q * m, axis=1, keepdims=True))
    out_ref[...] = (valid_ref[...] * (base_ref[...] + feed_ref[...].astype(f32))).astype(bf16)


def finish_rows(x, dn, dres, gain, base, feed, valid):
    rows, width = x.shape
    return pl.pallas_call(
        finish_kernel,
        out_shape=[
            jax.ShapeDtypeStruct((rows, width), f32),
            jax.ShapeDtypeStruct((rows, width), bf16),
        ],
        compiler_params=params(),
        cost_estimate=cost(5),
        name="finish_rows",
    )(x, dn, dres, gain, base, feed, valid)


def place_kernel(per, rt_ref, rc_ref, row_ref, col_ref):
    total = rt_ref.shape[1]
    one = lax.broadcasted_iota(jnp.int32, (BLOCK, BLOCK), 0)
    two = lax.broadcasted_iota(jnp.int32, (BLOCK, BLOCK), 1)
    before_row = (one < two).astype(bf16)
    before_col = (two < one).astype(bf16)
    row_carry = col_carry = None
    for at in range(0, total, BLOCK):
        if at % per == 0:
            row_carry = jnp.zeros((16, 1), f32)
            col_carry = jnp.zeros((1, 16), f32)
        here = slice(at, at + BLOCK)
        expert = lax.broadcasted_iota(jnp.int32, (16, BLOCK), 0)
        member = (rt_ref[0:1, here] == expert) | (rt_ref[1:2, here] == expert)
        rank = mm(member.astype(bf16), before_row) + row_carry
        row_ref[:, here] = jnp.where(member, rank, -1.0)
        row_carry = row_carry + jnp.sum(member.astype(f32), axis=1, keepdims=True)
        expert = lax.broadcasted_iota(jnp.int32, (BLOCK, 16), 1)
        member = (rc_ref[here, 0:1] == expert) | (rc_ref[here, 1:2] == expert)
        rank = mm(before_col, member.astype(bf16)) + col_carry
        col_ref[here, :] = jnp.where(member, rank, -1.0)
        col_carry = col_carry + jnp.sum(member.astype(f32), axis=0, keepdims=True)


def place_rows(routes, per):
    total = routes.shape[0]
    return pl.pallas_call(
        functools.partial(place_kernel, per),
        out_shape=[
            jax.ShapeDtypeStruct((16, total), f32),
            jax.ShapeDtypeStruct((total, 16), f32),
        ],
        compiler_params=params(),
        cost_estimate=cost(5),
        name="place_rows",
    )(routes.T, routes)


def fetch_kernel(first, row_ref, comb_ref, rows_ref, out_ref, gate_ref):
    expert = first[0] + pl.program_id(1)
    slot = lax.broadcasted_iota(jnp.int32, (CAP, row_ref.shape[1]), 0).astype(f32)
    hot = slot == row_ref[pl.ds(expert, 1), :]
    out_ref[0] = mm(hot.astype(bf16), rows_ref[...]).astype(bf16)
    if gate_ref is not None:
        gate_ref[0] = jnp.sum(jnp.where(hot, comb_ref[pl.ds(expert, 1), :], 0.0), axis=1, keepdims=True)


def fetch_rows(first, row, comb, rows, per, local, gated):
    total, width = rows.shape
    blocks = total // per
    outs = [jax.ShapeDtypeStruct((local, blocks * CAP, width), bf16)]
    specs = [pl.BlockSpec((1, CAP, width), lambda b, j, f: (j, b, 0))]
    ins = [
        pl.BlockSpec((16, per), lambda b, j, f: (0, b)),
        pl.BlockSpec((16, per), lambda b, j, f: (0, b)),
        pl.BlockSpec((per, width), lambda b, j, f: (b, 0)),
    ]
    args = (row, comb, rows)
    if gated:
        outs.append(jax.ShapeDtypeStruct((local, blocks * CAP, 1), f32))
        specs.append(pl.BlockSpec((1, CAP, 1), lambda b, j, f: (j, b, 0)))
        body = fetch_kernel
    else:
        body = lambda f, p, r, o: fetch_kernel(f, p, None, r, o, None)
        del ins[1]
        args = (row, rows)
    return pl.pallas_call(
        body,
        grid_spec=pltpu.PrefetchScalarGridSpec(
            num_scalar_prefetch=1, grid=(blocks, local), in_specs=ins, out_specs=specs
        ),
        out_shape=outs,
        compiler_params=params(),
        cost_estimate=cost(18),
        name="fetch_rows",
    )(first, *args)


def expert_kernel(j, first, x_ref, g_ref, gate_ref, w_ref, feed_ref, back_ref, gw_ref, total):
    i = pl.program_id(0)
    parts, _, _, depth, hidden = w_ref.shape
    width = parts * depth
    wg, wu, wd = [w_ref[:, 0, k].reshape(width, hidden) for k in range(3)]
    x, g, gate = x_ref[0], g_ref[0], gate_ref[0]
    gate_pre = mm(x, wg)
    up = mm(x, wu)
    sigmoid = 1.0 / (1.0 + jnp.exp(-gate_pre))
    activated = gate_pre * sigmoid
    inner = (activated * up).astype(bf16)
    out = mm(inner, wd, NT)
    g32 = g.astype(f32)
    feed_ref[...] = (gate * out).astype(bf16)
    dgate = jnp.sum(g32 * out, axis=1, keepdims=True)
    dout = (gate * g32).astype(bf16)
    dinner = mm(dout, wd)
    dpre = (dinner * up * sigmoid * (1.0 + gate_pre * (1.0 - sigmoid))).astype(bf16)
    dup = (dinner * activated).astype(bf16)
    back_ref[:, :width] = (mm(dpre, wg, NT) + mm(dup, wu, NT)).astype(bf16)
    lane = lax.broadcasted_iota(jnp.int32, (dgate.shape[0], back_ref.shape[1] - width), 1)
    coarse = dgate.astype(bf16).astype(f32)
    at = first[0] + j
    extra = jnp.where(lane == at, coarse, jnp.where(lane == at + 16, dgate - coarse, 0.0))
    back_ref[:, width:] = extra.astype(bf16)

    @pl.when(i == 0)
    def _():
        total[...] = jnp.zeros_like(total)

    total[0] += mm(x, dpre, TN)
    total[1] += mm(x, dup, TN)
    total[2] += mm(dout, inner, TN)

    @pl.when(i == pl.num_programs(0) - 1)
    def _():
        for k in range(3):
            gw_ref[:, k] = total[k].reshape(parts, depth, hidden).astype(bf16)


def expert(j, first, x, g, gate, w):
    slots, width = x.shape[1:]
    parts, _, kinds, depth, hidden = w.shape
    grads = (parts, kinds, depth, hidden)
    pick = lambda i, f: (j, i, 0)
    return pl.pallas_call(
        functools.partial(expert_kernel, j),
        grid_spec=pltpu.PrefetchScalarGridSpec(
            num_scalar_prefetch=1,
            grid=(slots // CAP,),
            in_specs=[
                pl.BlockSpec((1, CAP, width), pick),
                pl.BlockSpec((1, CAP, width), pick),
                pl.BlockSpec((1, CAP, 1), pick),
                pl.BlockSpec((parts, 1, kinds, depth, hidden), lambda i, f: (0, j, 0, 0, 0)),
            ],
            out_specs=[
                pl.BlockSpec((CAP, width), lambda i, f: (i, 0)),
                pl.BlockSpec((CAP, width + EXTRA), lambda i, f: (i, 0)),
                full(grads),
            ],
            scratch_shapes=[pltpu.VMEM((3, width, hidden), f32)],
        ),
        out_shape=[
            jax.ShapeDtypeStruct((slots, width), bf16),
            jax.ShapeDtypeStruct((slots, width + EXTRA), bf16),
            jax.ShapeDtypeStruct(grads, bf16),
        ],
        compiler_params=params(),
        cost_estimate=cost(14),
        name="expert",
    )(first, x, g, gate, w)


def spread_kernel(local, first, col_ref, *refs):
    out_ref = refs[-1]
    lane = lax.broadcasted_iota(jnp.int32, col_ref.shape, 1)
    slot = lax.broadcasted_iota(jnp.int32, (col_ref.shape[0], CAP), 1).astype(f32)
    total = None
    for j in range(local):
        mine = jnp.sum(jnp.where(lane == first[0] + j, col_ref[...], 0.0), axis=1, keepdims=True)
        term = mm((slot == mine).astype(bf16), refs[j][...])
        total = term if total is None else total + term
    out_ref[...] = total.astype(bf16)


def spread_rows(first, col, values, per):
    total = col.shape[0]
    tile = BLOCK
    width = values[0].shape[1]
    return pl.pallas_call(
        functools.partial(spread_kernel, len(values)),
        grid_spec=pltpu.PrefetchScalarGridSpec(
            num_scalar_prefetch=1,
            grid=(total // tile,),
            in_specs=[pl.BlockSpec((tile, 16), lambda i, f: (i, 0))]
            + [pl.BlockSpec((CAP, width), lambda i, f: (i // (per // tile), 0)) for _ in values],
            out_specs=pl.BlockSpec((tile, width), lambda i, f: (i, 0)),
        ),
        out_shape=jax.ShapeDtypeStruct((total, width), bf16),
        compiler_params=params(),
        cost_estimate=cost(20),
        name="spread_rows",
    )(first, col, *values)


def shards(
    hidden_in,
    cotangent,
    lengths,
    routes,
    prev_logits,
    norm_attn,
    w_query,
    w_key,
    w_value,
    w_out,
    norm_moe,
    w_router,
    w_const,
    const_vec,
    w_gate,
    w_up,
    w_down,
    threshold,
):
    plane = ("ctx", "tp")
    core, lane = lax.axis_index("ctx"), lax.axis_index("tp")
    nc, nt, ns = lax.axis_size("ctx"), lax.axis_size("tp"), lax.axis_size("shard")
    own, width = hidden_in.shape
    per = own * nt
    total = per * nc
    depth = w_gate.shape[1]
    heads = w_query.shape[1] // HEAD_DIM
    head_width = heads * HEAD_DIM
    local = FFN_EXPERTS // nc
    count = total // BLOCK // nc
    first_row = core * per + lane * own
    length = lengths[0]
    valid = (first_row + jnp.arange(own, dtype=jnp.int32) < length).astype(f32)[:, None]
    place = lane.astype(jnp.int32)[None]
    first = (core * local).astype(jnp.int32)[None]

    pack = jnp.concatenate(
        [
            w_query,
            w_key,
            w_value,
            w_out.T,
            norm_attn[:, None],
            norm_moe[:, None],
            w_router,
            w_const,
            const_vec.T,
            jnp.zeros((depth, 12), bf16),
        ],
        axis=1,
    )
    pieces = [
        lax.dynamic_slice_in_dim(w, core * local, local, 0) for w in (w_gate, w_up, w_down)
    ]
    expert_w = lax.all_gather(jnp.stack(pieces, axis=1), "shard", axis=0, tiled=False)
    rows_all, packed, routes_all = opening(hidden_in, pack, routes, 0)
    rows_all = rows_all.reshape(total, width)
    packed = packed.reshape(width, pack.shape[1])
    routes_all = routes_all.reshape(total, 2)

    wt = packed[:, : 3 * head_width].T
    out_t = packed[:, 3 * head_width : 4 * head_width]
    smalls = packed[:, 4 * head_width :].astype(f32)
    gain_attn = smalls[:, 0][None]
    gain_moe = smalls[:, 1][None]
    wrc = smalls[:, 2 : 2 + EXPERTS + 4]
    vec = smalls[:, 2 + EXPERTS + 4 : 4 + EXPERTS + 4].T
    prev = jnp.pad(prev_logits, ((0, 0), (0, 4)))

    freqs = rope_base ** (-2.0 * jnp.arange(HEAD_DIM // 2).astype(f32) / HEAD_DIM)
    angles = freqs[:, None] * jnp.arange(total).astype(f32)[None, :]
    cosine, sine = jnp.cos(angles), jnp.sin(angles)

    qt, kt, k, v, vt = project(rows_all, gain_attn, wt, cosine, sine, heads)
    table = jnp.stack([zig(core, i) for i in range(count)]).astype(jnp.int32)
    blocks = jnp.arange(total // BLOCK, dtype=jnp.int32)
    owned = jnp.any(blocks[:, None] == table[None, :], axis=1).astype(jnp.int32)
    ot, lse, top = attend(table, lengths, qt, k, vt)
    top = jnp.pad(jnp.max(top, axis=(1, 2, 3))[:, None], ((0, 8 - heads), (0, 127)))
    att, wo = to_owner(ot, out_t.T, 1)
    wo = wo.reshape(nt * head_width, width)

    res, base, a2, comb = forward_rows(place, hidden_in, att, wo, gain_moe, wrc, vec, prev, routes)

    row_at, col_at = place_rows(routes_all, per)
    cot = (cotangent.astype(f32) * valid).astype(bf16)
    a2_all, cot_all, comb_all = gather_rows((a2, cot), comb, 2)
    a2_all, cot_all = a2_all.reshape(total, width), cot_all.reshape(total, width)
    (g_slots,) = fetch_rows(first, row_at, None, cot_all, per, local, False)
    comb_all = comb_all.transpose(1, 0, 2).reshape(16, total)
    x_slots, gate_slots = fetch_rows(first, row_at, comb_all, a2_all, per, local, True)
    feeds, backs, grads = [], [], []
    for j in range(local):
        feed, back, grad = expert(j, first, x_slots, g_slots, gate_slots, expert_w)
        feeds.append(feed)
        backs.append(back)
        grads.append(grad)
    back = spread_rows(first, col_at, backs, per).reshape(8, own, width + EXTRA)
    back = sum_rows(back, 3)
    feed = spread_rows(first, col_at, feeds, per).reshape(8, own, width)
    feed = sum_rows(feed, 4)
    grads = [lax.psum_scatter(g, "shard", scatter_dimension=0, tiled=True)[0] for g in grads]

    dres, got, grad_out, small = backward_rows(
        place, res, back, cotangent, valid, att, wo, gain_moe, wrc, vec, prev, routes
    )
    got, grad_out = to_heads(got, grad_out.reshape(nt, head_width, width), count, 5)
    dq, dk, dv = revisit(table, qt, k, kt, v, ot, got, lse)
    part, grad_w, small = unproject(
        owned, dq, dk, dv, cosine, sine, rows_all, gain_attn, wt, grad_out, small, ns
    )
    part, grad_w, small, top, grad_expert = closing(
        part.reshape(8, own, width), grad_w, small, top, jnp.stack(grads), 6
    )
    grad_input, output = finish_rows(hidden_in, part, dres, gain_attn, base, feed, valid)

    factors = threshold[0] / jnp.maximum(top[:heads, 0], threshold[0])
    root = jnp.repeat(jnp.sqrt(factors), HEAD_DIM)
    clipped_query = (w_query.astype(f32) * root[None, :]).astype(bf16)
    clipped_key = (w_key.astype(f32) * root[None, :]).astype(bf16)
    grad_expert = grad_expert.reshape((FFN_EXPERTS,) + grad_expert.shape[2:]).astype(f32)
    grad_gate, grad_up, grad_down = [grad_expert[:, k] for k in range(3)]
    grad_w = grad_w.reshape(4 * head_width, depth)
    grad_q, grad_k, grad_v = [grad_w[i * head_width : (i + 1) * head_width].T for i in range(3)]
    grad_out = grad_w[3 * head_width :]
    return (
        output,
        grad_input,
        small[19],
        grad_q,
        grad_k,
        grad_v,
        grad_out,
        small[18],
        small[:EXPERTS].T,
        small[EXPERTS : EXPERTS + 4].T,
        small[16:18],
        grad_gate,
        grad_up,
        grad_down,
        factors,
        clipped_query,
        clipped_key,
    )


def solution(mesh):
    return jax.shard_map(
        shards,
        mesh=mesh,
        in_specs=(
            P(("shard", "ctx", "tp"), None),
            P(("shard", "ctx", "tp"), None),
            P("shard"),
            P(("shard", "ctx"), None),
            P(("shard", "ctx"), None),
            P("shard"),
            P("shard", "tp"),
            P("shard", "tp"),
            P("shard", "tp"),
            P("tp", "shard"),
            P("shard"),
            P("shard", None),
            P("shard", None),
            P(None, "shard"),
            P(None, "shard", "tp"),
            P(None, "shard", "tp"),
            P(None, "shard", "tp"),
            P(),
        ),
        out_specs=(
            P(("shard", "ctx", "tp"), None),
            P(("shard", "ctx", "tp"), None),
            P("shard"),
            P("shard", "tp"),
            P("shard", "tp"),
            P("shard", "tp"),
            P("tp", "shard"),
            P("shard"),
            P("shard", None),
            P("shard", None),
            P(None, "shard"),
            P(None, "shard", "tp"),
            P(None, "shard", "tp"),
            P(None, "shard", "tp"),
            P("tp"),
            P("shard", "tp"),
            P("shard", "tp"),
        ),
        check_vma=False,
    )
```

```python
import functools

import jax
import jax.numpy as jnp
import numpy as np
from jax import lax
from jax.experimental import pallas as pl
from jax.experimental.pallas import tpu as pltpu
from jax.sharding import PartitionSpec as P

HEAD_DIM = 64
EXPERTS = 12
FFN_EXPERTS = 8
CAP = 512
BLOCK = 512
EXTRA = 128
SMALL = 32
SLOT = 256
MESH = pl.DeviceIdType.MESH

epsilon = 1e-06
rope_base = 10000.0
bf16 = jnp.bfloat16
f32 = jnp.float32

NN = (((1,), (0,)), ((), ()))
NT = (((1,), (1,)), ((), ()))
TN = (((0,), (0,)), ((), ()))


def mm(left, right, dims=NN, precision=None):
    return lax.dot_general(
        left, right, dims, preferred_element_type=f32, precision=precision
    )


def params(mib=56, **more):
    return pltpu.CompilerParams(vmem_limit_bytes=mib * 1024 * 1024, **more)


def cost(us):
    return pl.CostEstimate(flops=int(us * 1e9), bytes_accessed=int(us * 3e6), transcendentals=0)


def full(shape):
    return pl.BlockSpec(shape, lambda *_: (0,) * len(shape))


def rope_tables(total):
    half = HEAD_DIM // 2
    freqs = np.float32(rope_base) ** (np.float32(-2.0) * np.arange(half, dtype=np.float32) / np.float32(HEAD_DIM))
    angles = freqs.astype(np.float32)[:, None] * np.arange(total, dtype=np.float32)[None, :]
    angles = angles.astype(np.float64)
    return jnp.asarray(np.cos(angles), f32), jnp.asarray(np.sin(angles), f32)


def zig(core, i):
    return 4 * (i // 2) + (core if i % 2 == 0 else 3 - core)


def anywhere(count):
    return [pl.BlockSpec(memory_space=pl.ANY)] * count


def spot():
    return lax.axis_index("shard"), lax.axis_index("ctx"), lax.axis_index("tp")


def across(t):
    return t + 1 - 2 * lax.rem(t, 2), lax.rem(t + 2, 4), 3 - t


def remote(source, target, sends, recvs, **where):
    return pltpu.make_async_remote_copy(
        src_ref=source,
        dst_ref=target,
        send_sem=sends,
        recv_sem=recvs,
        device_id=where,
        device_id_type=MESH,
    )


def greet(depth=True):
    z, c, t = spot()
    nc, nt, ns = lax.axis_size("ctx"), lax.axis_size("tp"), lax.axis_size("shard")
    barrier = pltpu.get_barrier_semaphore()
    for step in range(1, nc * nt):
        other = lax.rem(c * nt + t + step, nc * nt)
        pl.semaphore_signal(
            barrier,
            inc=1,
            device_id={"ctx": other // nt, "tp": lax.rem(other, nt)},
            device_id_type=MESH,
        )
    if depth:
        for step in range(1, ns):
            pl.semaphore_signal(
                barrier,
                inc=1,
                device_id={"shard": lax.rem(z + step, ns)},
                device_id_type=MESH,
            )
    pl.semaphore_wait(barrier, nc * nt - 1 + (ns - 1 if depth else 0))


class Gather:
    KINDS = 9

    def __init__(self, x, out, sends, recvs, own, cuts):
        z, c, t = spot()
        tx, ty, td = across(t)
        rows = x.shape[0] // cuts
        half = rows // 2
        self.cuts = cuts
        self.own = pltpu.make_async_copy(x, out.at[4 * c + t], own)
        sib = {"ctx": 1 - c}
        px, py = {"tp": tx}, {"tp": ty}

        def copies(s):
            whole = pl.ds(s * rows, rows)
            one, two = pl.ds(s * rows, half), pl.ds(s * rows + half, half)

            def at(k, source, target, where):
                return remote(source, target, sends.at[s, k], recvs.at[s, k], **where)

            def keep(k, slot, part, where):
                ref = out.at[4 * c + slot, part]
                return at(k, ref, ref, where)

            mine = [
                at(k, x.at[whole], out.at[4 * c + t, whole], where)
                for k, where in enumerate((px, py, sib))
            ]
            return mine + [
                keep(3, tx, whole, sib),
                keep(4, tx, one, py),
                keep(5, ty, whole, sib),
                keep(6, ty, two, px),
                keep(7, td, one, sib),
                keep(8, td, two, sib),
            ]

        self.copies = [copies(s) for s in range(cuts)]

        def arrivals(s):
            whole = pl.ds(s * rows, rows)
            one, two = pl.ds(s * rows, half), pl.ds(s * rows + half, half)
            where = [(c, tx, whole), (c, ty, whole), (1 - c, t, whole)]
            where += [(1 - c, tx, whole), (c, td, one), (1 - c, ty, whole), (c, td, two)]
            where += [(1 - c, td, one), (1 - c, td, two)]
            return [
                remote(out.at[4 * d + slot, part], out.at[4 * d + slot, part], sends.at[s, k], recvs.at[s, k], **sib)
                for k, (d, slot, part) in enumerate(where)
            ]

        self.arrivals = [arrivals(s) for s in range(cuts)]

    @staticmethod
    def scratch(cuts):
        return [
            pltpu.SemaphoreType.DMA((cuts, Gather.KINDS)),
            pltpu.SemaphoreType.DMA((cuts, Gather.KINDS)),
            pltpu.SemaphoreType.DMA,
        ]

    def first(self):
        for s in range(self.cuts):
            for k in (0, 1, 2):
                self.copies[s][k].start()
        self.own.start()

    def second(self):
        for s in range(self.cuts):
            self.arrivals[s][0].wait_recv()
            self.copies[s][4].start()
            self.copies[s][3].start()
            self.arrivals[s][1].wait_recv()
            self.copies[s][6].start()
            self.copies[s][5].start()

    def third(self):
        for s in range(self.cuts):
            for k in (4, 6):
                self.arrivals[s][k].wait_recv()
                self.copies[s][7 if k == 4 else 8].start()

    def last(self):
        for s in range(self.cuts):
            for k in (2, 3, 5, 7, 8):
                self.arrivals[s][k].wait_recv()
        for s in range(self.cuts):
            for k in range(self.KINDS):
                self.copies[s][k].wait_send()
        self.own.wait()


class Sum:
    def __init__(self, p, held, came, across_in, across_out, sends, recvs, loads):
        z, c, t = spot()
        self.t = t
        tx, ty, td = across(t)
        half = p.shape[1] // 2
        self.half = half
        self.one, self.two = pl.ds(0, half), pl.ds(half, half)
        self.order = (td, tx, ty, t)
        self.held, self.came, self.inn = held, came, across_in
        sib, px, py = {"ctx": 1 - c}, {"tp": tx}, {"tp": ty}
        self.loads = [pltpu.make_async_copy(p.at[4 * c + o], held.at[o], loads.at[k]) for k, o in enumerate(self.order)]
        self.core = []
        for k, o in enumerate(self.order):
            self.core.append(remote(p.at[4 * (1 - c) + o], came.at[o], sends.at[k], recvs.at[k], **sib))

        def send(k, source, slot, where):
            return remote(source, across_in.at[slot], sends.at[k], recvs.at[k], **where)

        self.side = {
            "dx": send(4, held.at[td, self.one], 0, px),
            "dy": send(5, held.at[td, self.two], 1, py),
            "x": send(6, held.at[tx, self.one], 2, px),
            "y": send(7, held.at[ty, self.two], 3, py),
            "cy": send(8, across_out.at[0], 4, py),
            "cx": send(9, across_out.at[1], 5, px),
        }
        self.out = across_out
        self.near = (tx, ty, td)

    @staticmethod
    def scratch(rows, width):
        return [
            pltpu.VMEM((4, rows, width), bf16),
            pltpu.VMEM((4, rows, width), bf16),
            pltpu.VMEM((6, rows // 2, width), bf16),
            pltpu.VMEM((2, rows // 2, width), bf16),
            pltpu.SemaphoreType.DMA((10,)),
            pltpu.SemaphoreType.DMA((10,)),
            pltpu.SemaphoreType.DMA((4,)),
        ]

    def first(self):
        for k in range(4):
            self.core[k].start()
            self.loads[k].start()

    def second(self):
        for k, o in enumerate(self.order):
            self.loads[k].wait()
            self.core[k].wait_recv()
            self.held[o] = (self.held[o].astype(f32) + self.came[o].astype(f32)).astype(bf16)
            if k == 0:
                self.side["dx"].start()
                self.side["dy"].start()
            if k == 1:
                self.side["x"].start()
            if k == 2:
                self.side["y"].start()

    def third(self):
        tx, ty, td = self.near
        self.side["dx"].wait_recv()
        self.out[0] = (self.held[ty, self.one].astype(f32) + self.inn[0].astype(f32)).astype(bf16)
        self.side["cy"].start()
        self.side["dy"].wait_recv()
        self.out[1] = (self.held[tx, self.two].astype(f32) + self.inn[1].astype(f32)).astype(bf16)
        self.side["cx"].start()

    def last(self):
        for k in ("x", "y", "cy", "cx"):
            self.side[k].wait_recv()
        for copy in self.core + list(self.side.values()):
            copy.wait_send()

    def total(self):
        def add(part, a, b):
            return self.held[self.t, part].astype(f32) + self.inn[a].astype(f32) + self.inn[b].astype(f32)

        return add(self.one, 2, 4), add(self.two, 3, 5)


def qkv_kernel(x_ref, w_ref, cos_ref, sin_ref, qt_ref, kt_ref, k_ref, v_ref, vt_ref, wt_ref, wo_ref, small_ref):
    heads = qt_ref.shape[0]
    width = heads * HEAD_DIM
    half = HEAD_DIM // 2

    @pl.when(pl.program_id(0) == 0)
    def _():
        def whole(core, which, here):
            v = w_ref[core, :, which].astype(f32)
            return v.reshape(v.shape[0] * v.shape[1], SLOT)[:, here].T

        mine = slice(0, width)
        wt_ref[:width] = whole(0, 0, mine).astype(bf16)
        wt_ref[width : 2 * width] = whole(0, 1, mine).astype(bf16)
        wt_ref[2 * width :] = whole(1, 0, mine).astype(bf16)
        wo_ref[...] = whole(1, 1, mine).astype(bf16)
        small_ref[...] = whole(0, 0, slice(width, width + SMALL))

    x = x_ref[...].astype(f32)
    inverse = lax.rsqrt(jnp.mean(x * x, axis=1, keepdims=True) + epsilon)
    a = (x * inverse * small_ref[18:19]).astype(bf16)
    y = mm(wt_ref[...], a, NT)
    c, s = cos_ref[...], sin_ref[...]

    def turned(first):
        u, w = y[first : first + half], y[first + half : first + HEAD_DIM]
        return jnp.concatenate([u * c - w * s, w * c + u * s], axis=0)

    for h in range(heads):
        at = h * HEAD_DIM
        qt_ref[h] = (turned(at) * HEAD_DIM**-0.5).astype(bf16)
        key = turned(width + at)
        kt_ref[h] = key.astype(bf16)
        k_ref[h] = key.T.astype(bf16)
        value = y[2 * width + at : 2 * width + at + HEAD_DIM]
        v_ref[h] = value.T.astype(bf16)
        vt_ref[h, :HEAD_DIM] = value.astype(bf16)
        vt_ref[h, HEAD_DIM:] = jnp.ones((16, value.shape[1]), bf16)


def project(rows, w, cosine, sine, heads):
    total, width = rows.shape
    tile = BLOCK
    out = heads * HEAD_DIM
    shapes = [
        jax.ShapeDtypeStruct((heads, HEAD_DIM, total), bf16),
        jax.ShapeDtypeStruct((heads, HEAD_DIM, total), bf16),
        jax.ShapeDtypeStruct((heads, total, HEAD_DIM), bf16),
        jax.ShapeDtypeStruct((heads, total, HEAD_DIM), bf16),
        jax.ShapeDtypeStruct((heads, HEAD_DIM + 16, total), bf16),
        jax.ShapeDtypeStruct((3 * out, width), bf16),
        jax.ShapeDtypeStruct((out, width), bf16),
        jax.ShapeDtypeStruct((SMALL, width), f32),
    ]
    return pl.pallas_call(
        qkv_kernel,
        grid=(total // tile,),
        in_specs=[
            pl.BlockSpec((tile, width), lambda i: (i, 0)),
            full(w.shape),
            pl.BlockSpec((HEAD_DIM // 2, tile), lambda i: (0, i)),
            pl.BlockSpec((HEAD_DIM // 2, tile), lambda i: (0, i)),
        ],
        out_specs=[
            pl.BlockSpec((heads, HEAD_DIM, tile), lambda i: (0, 0, i)),
            pl.BlockSpec((heads, HEAD_DIM, tile), lambda i: (0, 0, i)),
            pl.BlockSpec((heads, tile, HEAD_DIM), lambda i: (0, i, 0)),
            pl.BlockSpec((heads, tile, HEAD_DIM), lambda i: (0, i, 0)),
            pl.BlockSpec((heads, HEAD_DIM + 16, tile), lambda i: (0, 0, i)),
        ]
        + [full(v.shape) for v in shapes[5:]],
        out_shape=shapes,
        compiler_params=params(),
        cost_estimate=cost(13),
        name="project",
    )(rows, w, cosine, sine)


def dealt(core, i):
    return 4 * (i // 2) + jnp.where(lax.rem(i, 2) == 0, core, 3 - core)


def attend_kernel(cuts, length, qt_ref, k_ref, vt_ref, cot_ref, w_ref, ot_ref, lse_ref, top_ref, cots_ref, ws_ref, mask_cot, w_send, w_recv, w_own, *sems):
    z, c, t = spot()
    nt = lax.axis_size("tp")
    h, i = pl.program_id(0), pl.program_id(1)
    count = pl.num_programs(1)
    at_step = h * count + i
    last = pl.num_programs(0) * count - 1
    gather = Gather(mask_cot, cots_ref, *sems, cuts)
    half = w_ref.shape[0] // 2
    mine = pl.ds(c * half, half)
    theirs = pl.ds((1 - c) * half, half)
    away, came = [], []
    for step in range(1, nt):
        there, back = lax.rem(t + step, nt), lax.rem(t + nt - step, nt)
        away.append(remote(w_ref.at[mine], ws_ref.at[t, mine], w_send.at[step], w_recv.at[step], tp=there))
        ref = ws_ref.at[back, mine]
        came.append(remote(ref, ref, w_send.at[nt + step], w_recv.at[step], ctx=1 - c))
        ref = ws_ref.at[back, theirs]
        came.append(remote(ref, ref, w_send.at[nt + step], w_recv.at[nt + step], ctx=1 - c))
    onward = [
        remote(ws_ref.at[lax.rem(t + nt - step, nt), mine], ws_ref.at[lax.rem(t + nt - step, nt), mine],
               w_send.at[nt + step], w_recv.at[nt + step], ctx=1 - c)
        for step in range(1, nt)
    ]
    own_w = pltpu.make_async_copy(w_ref, ws_ref.at[t], w_own)

    @pl.when(at_step == 0)
    def _():
        rows = cot_ref.shape[0]
        position = (c * nt + t) * rows + lax.broadcasted_iota(jnp.int32, cot_ref.shape, 0)
        mask_cot[...] = jnp.where(position < length[0], cot_ref[...].astype(f32), 0.0).astype(bf16)
        greet(False)
        gather.first()
        for copy in away:
            copy.start()
        own_w.start()

    index = dealt(c, i)
    columns = BLOCK
    qt = qt_ref[0, :, pl.ds(pl.multiple_of(index * BLOCK, BLOCK), BLOCK)]

    def step(at, carry, diagonal):
        peak, total = carry
        start = pl.multiple_of(at * BLOCK, BLOCK)
        scores = mm(k_ref[0, pl.ds(start, BLOCK), :], qt)
        if diagonal:
            keys = lax.broadcasted_iota(jnp.int32, scores.shape, 0)
            queries = lax.broadcasted_iota(jnp.int32, scores.shape, 1)
            scores = jnp.where(keys <= queries, scores, -1e30)
        higher = jnp.maximum(peak, jnp.max(scores, axis=0, keepdims=True))
        weights = jnp.exp(scores - higher).astype(bf16)
        total = total * jnp.exp(peak - higher) + mm(vt_ref[0, :, pl.ds(start, BLOCK)], weights)
        return higher, total

    start = (jnp.full((1, columns), -1e30, f32), jnp.zeros((HEAD_DIM + 16, columns), f32))
    carry = lax.fori_loop(0, index, lambda at, c: step(at, c, False), start)
    peak, total = step(index, carry, True)
    mass = total[HEAD_DIM : HEAD_DIM + 1]
    ot_ref[0] = (total[:HEAD_DIM] / mass).astype(bf16)
    lse_ref[0, 0] = peak + jnp.log(mass)
    position = index * BLOCK + lax.broadcasted_iota(jnp.int32, peak.shape, 1)
    top_ref[0, 0] = jnp.where(position < length[0], peak, -1e30)

    @pl.when(at_step == last // 2 + 1)
    def _():
        gather.second()
        for copy, forth in zip(came[0::2], onward):
            copy.wait_recv()
            forth.start()

    @pl.when(at_step == last - 1)
    def _():
        gather.third()

    @pl.when(at_step == last)
    def _():
        gather.last()
        for copy in came[1::2]:
            copy.wait_recv()
        for copy in away + onward:
            copy.wait_send()
        own_w.wait()


def attend(length, qt, k, vt, cot, w, count, number):
    cuts = 2
    heads, _, total = qt.shape
    nt = lax.axis_size("tp")
    return pl.pallas_call(
        functools.partial(attend_kernel, cuts),
        grid_spec=pltpu.PrefetchScalarGridSpec(
            num_scalar_prefetch=1,
            grid=(heads, count),
            in_specs=[
                pl.BlockSpec((1, HEAD_DIM, total), lambda h, i, n: (h, 0, 0)),
                pl.BlockSpec((1, total, HEAD_DIM), lambda h, i, n: (h, 0, 0)),
                pl.BlockSpec((1, HEAD_DIM + 16, total), lambda h, i, n: (h, 0, 0)),
                full(cot.shape),
                full(w.shape),
            ],
            out_specs=[
                pl.BlockSpec((1, HEAD_DIM, BLOCK), lambda h, i, n: (i, h, 0)),
                pl.BlockSpec((1, 1, 1, BLOCK), lambda h, i, n: (h, i, 0, 0)),
                pl.BlockSpec((1, 1, 1, BLOCK), lambda h, i, n: (h, i, 0, 0)),
            ]
            + anywhere(2),
            scratch_shapes=[
                pltpu.VMEM(cot.shape, bf16),
                pltpu.SemaphoreType.DMA((2 * nt,)),
                pltpu.SemaphoreType.DMA((2 * nt,)),
                pltpu.SemaphoreType.DMA,
            ]
            + Gather.scratch(cuts),
        ),
        out_shape=[
            jax.ShapeDtypeStruct((count, heads * HEAD_DIM, BLOCK), bf16),
            jax.ShapeDtypeStruct((heads, count, 1, BLOCK), f32),
            jax.ShapeDtypeStruct((heads, count, 1, BLOCK), f32),
            jax.ShapeDtypeStruct((8,) + cot.shape, bf16),
            jax.ShapeDtypeStruct((nt,) + w.shape, bf16),
        ],
        compiler_params=params(collective_id=number, has_side_effects=True),
        cost_estimate=cost(35),
        name="attend",
    )(length, qt, k, vt, cot, w)


def revisit_kernel(qt_ref, k_ref, kt_ref, v_ref, ot_ref, got_ref, lse_ref, go_ref, dq_ref, dk_ref, dv_ref, gos_ref, sum_k, sum_v, came_ref, w_send, w_recv):
    z, c, t = spot()
    nt = lax.axis_size("tp")
    h, i = pl.program_id(0), pl.program_id(1)
    count = pl.num_programs(1)
    index = dealt(c, i)
    here = pl.ds(pl.multiple_of(index * BLOCK, BLOCK), BLOCK)
    away = [
        remote(go_ref.at[lax.rem(t + step, nt)], came_ref.at[step], w_send.at[step], w_recv.at[step], tp=lax.rem(t + step, nt))
        for step in range(1, nt)
    ]

    @pl.when(h * count + i == 0)
    def _():
        greet(False)
        for copy in away:
            copy.start()

    qt, got = qt_ref[0, :, here], got_ref[0]
    lse = lse_ref[0, 0]
    centre = jnp.sum(ot_ref[0].astype(f32) * got.astype(f32), axis=0, keepdims=True)

    @pl.when(i == 0)
    def _():
        sum_k[...] = jnp.zeros_like(sum_k)
        sum_v[...] = jnp.zeros_like(sum_v)
        dq_ref[...] = jnp.zeros_like(dq_ref)

    def step(at, grad, diagonal):
        start = pl.multiple_of(at * BLOCK, BLOCK)
        here = pl.ds(start, BLOCK)
        scores = mm(k_ref[0, here, :], qt)
        probs = jnp.exp(scores - lse)
        if diagonal:
            keys = lax.broadcasted_iota(jnp.int32, scores.shape, 0)
            queries = lax.broadcasted_iota(jnp.int32, scores.shape, 1)
            probs = jnp.where(keys <= queries, probs, 0.0)
        grad_probs = mm(v_ref[0, here, :], got)
        grad_scores = (probs * (grad_probs - centre)).astype(bf16)
        sum_v[here, :] += mm(probs.astype(bf16), got, NT)
        sum_k[here, :] += mm(grad_scores, qt, NT)
        return grad + mm(kt_ref[0, :, here], grad_scores)

    grad = lax.fori_loop(0, index, lambda at, c: step(at, c, False), jnp.zeros(qt.shape, f32))
    dq_ref[0, :, here] = step(index, grad, True) * HEAD_DIM**-0.5

    @pl.when(i == count - 1)
    def _():
        dk_ref[0] = sum_k[...].T
        dv_ref[0] = sum_v[...].T

    @pl.when(h * count + i == pl.num_programs(0) * count - 1)
    def _():
        total = go_ref[t].astype(f32)
        for step, copy in enumerate(away):
            copy.wait_recv()
            total = total + came_ref[step + 1].astype(f32)
            copy.wait_send()
        gos_ref[...] = total.astype(bf16)


def revisit(qt, k, kt, v, ot, got, lse, go, number):
    heads, _, total = qt.shape
    count = ot.shape[0]
    nt = lax.axis_size("tp")
    whole = pl.BlockSpec((1, HEAD_DIM, total), lambda h, i: (h, 0, 0))
    tall = pl.BlockSpec((1, total, HEAD_DIM), lambda h, i: (h, 0, 0))
    some = pl.BlockSpec((1, HEAD_DIM, BLOCK), lambda h, i: (i, h, 0))
    return pl.pallas_call(
        revisit_kernel,
        grid=(heads, count),
        in_specs=[
            whole,
            tall,
            whole,
            tall,
            some,
            some,
            pl.BlockSpec((1, 1, 1, BLOCK), lambda h, i: (h, i, 0, 0)),
            full(go.shape),
        ],
        out_specs=[whole, whole, whole, full(go.shape[1:])],
        scratch_shapes=[
            pltpu.VMEM((total, HEAD_DIM), f32),
            pltpu.VMEM((total, HEAD_DIM), f32),
            pltpu.VMEM(go.shape, bf16),
            pltpu.SemaphoreType.DMA((nt,)),
            pltpu.SemaphoreType.DMA((nt,)),
        ],
        out_shape=[jax.ShapeDtypeStruct((heads, HEAD_DIM, total), f32)] * 3 + [jax.ShapeDtypeStruct(go.shape[1:], bf16)],
        compiler_params=params(collective_id=number, has_side_effects=True),
        cost_estimate=cost(50),
        name="revisit",
    )(qt, k, kt, v, ot, got, lse, go)


def unproject_kernel(dq_ref, dk_ref, dv_ref, cos_ref, sin_ref, x_ref, gain_ref, wt_ref, go_ref, small_ref,
                     part_ref, gw_ref, smalls_ref, total, row):
    heads = dq_ref.shape[0]
    half = HEAD_DIM // 2
    i = pl.program_id(0)
    c, s = cos_ref[...], sin_ref[...]

    def turned(g):
        u, w = g[:half], g[half:]
        return jnp.concatenate([u * c + w * s, w * c - u * s], axis=0)

    @pl.when(i == 0)
    def _():
        total[...] = jnp.zeros_like(total)
        row[...] = jnp.zeros_like(row)

    x = x_ref[...].astype(f32)
    m = x * lax.rsqrt(jnp.mean(x * x, axis=1, keepdims=True) + epsilon)
    a = (m * gain_ref[18:19]).astype(bf16)
    pieces = [turned(dq_ref[h]) for h in range(heads)]
    pieces += [turned(dk_ref[h]) for h in range(heads)]
    pieces += [dv_ref[h] for h in range(heads)]
    grads = jnp.concatenate(pieces, axis=0).astype(bf16)
    part = mm(grads, wt_ref[...], TN)
    part_ref[...] = part.astype(bf16)
    row[...] += jnp.sum(part * m, axis=0, keepdims=True)
    total[...] += mm(grads, a)

    @pl.when(i == pl.num_programs(0) - 1)
    def _():
        _, parts, rows, depth = gw_ref.shape
        mid = rows // 2
        at = lax.broadcasted_iota(jnp.int32, small_ref.shape, 0)
        smalls = small_ref[...] + jnp.where(at == 19, row[...], 0.0)
        for z in range(parts):
            here = slice(z * depth, (z + 1) * depth)
            gw_ref[0, z] = total[:rows, here].astype(bf16)
            gw_ref[1, z, :mid] = total[rows:, here].astype(bf16)
            gw_ref[1, z, mid:] = go_ref[:, here]
            smalls_ref[z] = smalls[:, here]


def unproject(dq, dk, dv, cosine, sine, x, gain, wt, go, small, parts):
    heads, _, rows = dq.shape
    width = x.shape[1]
    out = wt.shape[0]
    depth = width // parts
    piece = pl.BlockSpec((heads, HEAD_DIM, BLOCK), lambda i: (0, 0, i))
    table = pl.BlockSpec((HEAD_DIM // 2, BLOCK), lambda i: (0, i))
    shapes = [
        jax.ShapeDtypeStruct((rows, width), bf16),
        jax.ShapeDtypeStruct((2, parts, 2 * heads * HEAD_DIM, depth), bf16),
        jax.ShapeDtypeStruct((parts,) + small.shape[:1] + (depth,), f32),
    ]
    return pl.pallas_call(
        unproject_kernel,
        grid_spec=pl.GridSpec(
            grid=(rows // BLOCK,),
            in_specs=[
                piece,
                piece,
                piece,
                table,
                table,
                pl.BlockSpec((BLOCK, width), lambda i: (i, 0)),
                full(gain.shape),
                full(wt.shape),
                full(go.shape),
                full(small.shape),
            ],
            out_specs=[pl.BlockSpec((BLOCK, width), lambda i: (i, 0))] + [full(v.shape) for v in shapes[1:]],
            scratch_shapes=[pltpu.VMEM((out, width), f32), pltpu.VMEM((1, width), f32)],
        ),
        out_shape=shapes,
        compiler_params=params(),
        cost_estimate=cost(18),
        name="unproject",
    )(dq, dk, dv, cosine, sine, x, gain, wt, go, small)


def opening_kernel(cuts, x_ref, wq_ref, wk_ref, wv_ref, wo_ref, small_ref, routes_ref, out_ref, ws_ref, all_routes_ref, held, *sems):
    gather = Gather(x_ref, out_ref, *sems[:3], cuts)
    sends, recvs, local = sems[3:]
    z, c, t = spot()
    ns = lax.axis_size("shard")
    width = wq_ref.shape[1]
    held[0, :, :width] = jnp.where(c == 0, wq_ref[...].astype(f32), wv_ref[...].astype(f32)).astype(bf16)
    held[0, :, width : width + SMALL] = small_ref[...]
    held[0, :, width + SMALL :] = jnp.zeros((held.shape[1], SLOT - width - SMALL), bf16)
    held[1, :, :width] = jnp.where(c == 0, wk_ref[...].astype(f32), wo_ref[...].astype(f32).T).astype(bf16)
    held[1, :, width:] = jnp.zeros((held.shape[1], SLOT - width), bf16)
    greet()
    started = []

    def go(k, source, target, **where):
        copy = remote(source, target, sends.at[k], recvs.at[k], **where)
        copy.start()
        started.append(copy)

    def came(k, ref):
        remote(ref, ref, sends.at[k], recvs.at[k], ctx=1 - c).wait_recv()

    for step in range(1, ns):
        go(step, held, ws_ref.at[c, z], shard=lax.rem(z + step, ns))
    go(0, held, ws_ref.at[c, z], ctx=1 - c)
    gather.first()
    go(2 * ns, routes_ref, all_routes_ref.at[c], ctx=1 - c)
    mine = [
        pltpu.make_async_copy(held, ws_ref.at[c, z], local.at[0]),
        pltpu.make_async_copy(routes_ref, all_routes_ref.at[c], local.at[1]),
    ]
    for copy in mine:
        copy.start()
    gather.second()
    for step in range(1, ns):
        back = lax.rem(z + ns - step, ns)
        came(step, ws_ref.at[c, back])
        go(ns + step, ws_ref.at[c, back], ws_ref.at[c, back], ctx=1 - c)
    gather.third()
    gather.last()
    came(0, ws_ref.at[1 - c, z])
    came(2 * ns, all_routes_ref.at[1 - c])
    for step in range(1, ns):
        came(ns + step, ws_ref.at[1 - c, lax.rem(z + ns - step, ns)])
    for copy in started:
        copy.wait_send()
    for copy in mine:
        copy.wait()


def opening(x, wq, wk, wv, wo, small, routes, number):
    cuts = 2
    ns = lax.axis_size("shard")
    depth = wq.shape[0]
    vmem = pl.BlockSpec(memory_space=pltpu.VMEM)
    return pl.pallas_call(
        functools.partial(opening_kernel, cuts),
        in_specs=[vmem] * 7,
        out_specs=anywhere(3),
        out_shape=[
            jax.ShapeDtypeStruct((8,) + x.shape, x.dtype),
            jax.ShapeDtypeStruct((2, ns, 2, depth, SLOT), bf16),
            jax.ShapeDtypeStruct((2,) + routes.shape, routes.dtype),
        ],
        scratch_shapes=[pltpu.VMEM((2, depth, SLOT), bf16)]
        + Gather.scratch(cuts)
        + [
            pltpu.SemaphoreType.DMA((2 * ns + 1,)),
            pltpu.SemaphoreType.DMA((2 * ns + 1,)),
            pltpu.SemaphoreType.DMA((2,)),
        ],
        compiler_params=params(24, collective_id=number, has_side_effects=True),
        cost_estimate=cost(30),
        name="opening",
    )(x, wq, wk, wv, wo, small, routes)


def gather_kernel(cuts, count, *refs):
    xs, comb, outs, combs, sems = refs[:count], refs[count], refs[count + 1 : 2 * count + 1], refs[2 * count + 1], refs[2 * count + 2 :]
    gathers = [Gather(x, out, *sems[3 * i : 3 * i + 3], cuts) for i, (x, out) in enumerate(zip(xs, outs))]
    sends, recvs, local = sems[3 * count :]
    z, c, t = spot()
    own = 4 * c + t
    greet(False)
    for gather in gathers:
        gather.first()
    pairs = []
    for step in range(1, 8):
        other, back = lax.rem(own + step, 8), lax.rem(own + 8 - step, 8)
        where = {"ctx": other // 4, "tp": lax.rem(other, 4)}
        copy = remote(comb, combs.at[own], sends.at[step], recvs.at[step], **where)
        copy.start()
        pairs.append((copy, remote(comb, combs.at[back], sends.at[step], recvs.at[step], **where)))
    mine = pltpu.make_async_copy(comb, combs.at[own], local)
    mine.start()
    for gather in gathers:
        gather.second()
    for gather in gathers:
        gather.third()
    for gather in gathers:
        gather.last()
    for copy, came in pairs:
        came.wait_recv()
        copy.wait_send()
    mine.wait()


def gather_rows(xs, comb, number):
    cuts = 2
    return pl.pallas_call(
        functools.partial(gather_kernel, cuts, len(xs)),
        in_specs=[pl.BlockSpec(memory_space=pltpu.VMEM)] * (len(xs) + 1),
        out_specs=anywhere(len(xs) + 1),
        out_shape=[jax.ShapeDtypeStruct((8,) + x.shape, x.dtype) for x in (*xs, comb)],
        scratch_shapes=Gather.scratch(cuts) * len(xs)
        + [
            pltpu.SemaphoreType.DMA((8,)),
            pltpu.SemaphoreType.DMA((8,)),
            pltpu.SemaphoreType.DMA,
        ],
        compiler_params=params(16, collective_id=number, has_side_effects=True),
        cost_estimate=cost(30 * len(xs)),
        name="gather_rows",
    )(*xs, comb)


def sum_kernel(p_ref, out_ref, *scratch):
    job = Sum(p_ref, *scratch)
    greet(False)
    job.first()
    job.second()
    job.third()
    job.last()
    one, two = job.total()
    out_ref[: job.half] = one.astype(out_ref.dtype)
    out_ref[job.half :] = two.astype(out_ref.dtype)


def sum_rows(p, number):
    _, rows, width = p.shape
    return pl.pallas_call(
        sum_kernel,
        in_specs=anywhere(1),
        out_specs=pl.BlockSpec(memory_space=pltpu.VMEM),
        out_shape=jax.ShapeDtypeStruct((rows, width), f32),
        scratch_shapes=Sum.scratch(rows, width),
        compiler_params=params(40, collective_id=number, has_side_effects=True),
        cost_estimate=cost(35),
        name="sum_rows",
    )(p)


def to_owner_kernel(o_ref, att_ref, send_sem, recv_sem, local_sem):
    z, c, t = spot()
    nt = lax.axis_size("tp")
    own = c * nt + t
    greet(False)
    copies = []
    for i in range(o_ref.shape[0]):
        block = zig(c, i)
        copy = remote(o_ref.at[i], att_ref.at[t], send_sem.at[i], recv_sem.at[t], ctx=block // nt, tp=lax.rem(block, nt))
        local = pltpu.make_async_copy(o_ref.at[i], att_ref.at[t], local_sem)
        copies.append((block == own, copy, local))
    settle(copies)
    mine = lax.rem((own + 1) // 2, 2) == c
    for source in range(nt):

        @pl.when(jnp.logical_or(jnp.logical_not(mine), source != t))
        def _():
            remote(o_ref.at[0], att_ref.at[source], send_sem.at[0], recv_sem.at[source], ctx=c, tp=t).wait_recv()


def settle(copies):
    for here, copy, local in copies:

        @pl.when(jnp.logical_not(here))
        def _():
            copy.start()

        @pl.when(here)
        def _():
            local.start()

    for here, copy, local in copies:

        @pl.when(jnp.logical_not(here))
        def _():
            copy.wait_send()

        @pl.when(here)
        def _():
            local.wait()


def to_heads_kernel(o_ref, got_ref, send_sem, recv_sem, local_sem):
    z, c, t = spot()
    nt = lax.axis_size("tp")
    own = c * nt + t
    greet(False)
    core = lax.rem((own + 1) // 2, 2)
    slot = 2 * (own // 4) + lax.rem(own, 4) // 2
    copies = []
    for target in range(nt):
        here = jnp.logical_and(core == c, target == t)
        copy = remote(o_ref.at[target], got_ref.at[slot], send_sem.at[target], recv_sem.at[slot], ctx=core, tp=target)
        local = pltpu.make_async_copy(o_ref.at[target], got_ref.at[slot], local_sem)
        copies.append((here, copy, local))
    settle(copies)
    for i in range(got_ref.shape[0]):

        @pl.when(zig(c, i) != own)
        def _():
            remote(o_ref.at[0], got_ref.at[i], send_sem.at[0], recv_sem.at[i], ctx=c, tp=t).wait_recv()


def exchange(kernel, o, count, number, name):
    vmem = pl.BlockSpec(memory_space=pltpu.VMEM)
    return pl.pallas_call(
        kernel,
        in_specs=[vmem],
        out_specs=vmem,
        out_shape=jax.ShapeDtypeStruct((count,) + o.shape[1:], o.dtype),
        scratch_shapes=[
            pltpu.SemaphoreType.DMA((o.shape[0],)),
            pltpu.SemaphoreType.DMA((count,)),
            pltpu.SemaphoreType.DMA,
        ],
        compiler_params=params(16, collective_id=number, has_side_effects=True),
        cost_estimate=cost(12),
        name=name,
    )(o)


def closing_kernel(p_ref, gw_ref, small_ref, top_ref, ge0, ge1, ge2, ge3, out_ref, gsum_ref, ssum_ref, tmax_ref, gall_ref,
                   gcore, gline, gmine, sline, splane, tline, mytop, *sems):
    job = Sum(p_ref, *sems[:7])
    sends, recvs, local = sems[7:]
    z, c, t = spot()
    ns = lax.axis_size("shard")
    rows = gw_ref.shape[2]
    own = 4 * c + t
    greet()
    row = lax.broadcasted_iota(jnp.int32, mytop.shape, 0)
    high = jnp.full(mytop.shape, -1e30, f32)
    for h in range(top_ref.shape[0]):
        best = jnp.max(jnp.max(top_ref[h], axis=0), axis=1, keepdims=True)
        high = jnp.where(row == h, best, high)
    mytop[...] = high
    started = []

    def go(k, source, target, **where):
        copy = remote(source, target, sends.at[k], recvs.at[k], **where)
        copy.start()
        started.append(copy)
        return copy

    core = go(0, gw_ref.at[1 - c], gcore, ctx=1 - c)
    small = [go(3 + s, small_ref.at[lax.rem(z + s, ns)], sline.at[s], shard=lax.rem(z + s, ns)) for s in range(1, ns)]
    tops = [go(3 + ns + s, mytop, tline.at[s], shard=lax.rem(z + s, ns)) for s in range(1, ns)]
    own_g = pltpu.make_async_copy(gw_ref.at[c], gmine, local.at[0])
    own_g.start()
    job.first()
    experts = [go(11 + 4 * ns + k, ge, gall_ref.at[k], ctx=1 - c) for k, ge in enumerate((ge0, ge1, ge2, ge3))]
    job.second()
    own_g.wait()
    core.wait_recv()
    gmine[...] = (gmine[...].astype(f32) + gcore[...].astype(f32)).astype(bf16)
    line = [go(3 + 2 * ns + s, gmine.at[lax.rem(z + s, ns)], gline.at[s], shard=lax.rem(z + s, ns)) for s in range(1, ns)]
    for copy in small:
        copy.wait_recv()
    total = small_ref[z]
    for s in range(1, ns):
        total = total + sline[s]
    splane[0] = total
    plane = []
    for s in range(1, 8):
        other = lax.rem(own + s, 8)
        plane.append(go(3 + 3 * ns + s, splane.at[0], splane.at[s], ctx=other // 4, tp=lax.rem(other, 4)))
    for copy in tops:
        copy.wait_recv()
    high = mytop[...]
    for s in range(1, ns):
        high = jnp.maximum(high, tline[s])
    tline[0] = high
    pair = go(2, tline.at[0], tline.at[ns], ctx=1 - c)
    job.third()
    for copy in line:
        copy.wait_recv()
    total = gmine[z].astype(f32)
    for s in range(1, ns):
        total = total + gline[s].astype(f32)
    gsum_ref[c] = total
    final = go(3, gsum_ref.at[c], gsum_ref.at[c], ctx=1 - c)
    for copy in plane:
        copy.wait_recv()
    total = splane[0]
    for s in range(1, 8):
        total = total + splane[s]
    ssum_ref[...] = total
    pair.wait_recv()
    tmax_ref[...] = jnp.maximum(tline[0], tline[ns])
    job.last()
    one, two = job.total()
    out_ref[: job.half] = one
    out_ref[job.half :] = two
    remote(gsum_ref.at[1 - c], gsum_ref.at[1 - c], sends.at[3], recvs.at[3], ctx=1 - c).wait_recv()
    for copy in experts:
        copy.wait_recv()
    for copy in started:
        copy.wait_send()


def closing(p, gw, small, top, experts, number):
    _, rows, width = p.shape
    ns = lax.axis_size("shard")
    vmem = pl.BlockSpec(memory_space=pltpu.VMEM)
    return pl.pallas_call(
        closing_kernel,
        in_specs=anywhere(2) + [vmem, vmem] + anywhere(4),
        out_specs=[vmem, vmem, vmem, vmem] + anywhere(1),
        out_shape=[
            jax.ShapeDtypeStruct((rows, width), f32),
            jax.ShapeDtypeStruct((2,) + gw.shape[2:], f32),
            jax.ShapeDtypeStruct(small.shape[1:], f32),
            jax.ShapeDtypeStruct((8, 128), f32),
            jax.ShapeDtypeStruct((4,) + experts[0].shape, bf16),
        ],
        scratch_shapes=[
            pltpu.VMEM(gw.shape[1:], bf16),
            pltpu.VMEM(gw.shape[1:], bf16),
            pltpu.VMEM(gw.shape[1:], bf16),
            pltpu.VMEM(small.shape, f32),
            pltpu.VMEM((8,) + small.shape[1:], f32),
            pltpu.VMEM((ns + 1, 8, 128), f32),
            pltpu.VMEM((8, 128), f32),
        ]
        + Sum.scratch(rows, width)
        + [
            pltpu.SemaphoreType.DMA((4 * ns + 15,)),
            pltpu.SemaphoreType.DMA((4 * ns + 15,)),
            pltpu.SemaphoreType.DMA((2,)),
        ],
        compiler_params=params(48, collective_id=number, has_side_effects=True),
        cost_estimate=cost(40),
        name="closing",
    )(p, gw, small, top, *experts)


def mixing(n2, wrc, previous, routes):
    z = mm(n2, wrc, NT, lax.Precision.HIGHEST)
    lane = lax.broadcasted_iota(jnp.int32, z.shape, 1)
    logits = z + previous
    hot = [lane == routes[:, r : r + 1] for r in range(2)]
    picked = [jnp.sum(jnp.where(hot[r], logits, 0.0), axis=1, keepdims=True) for r in range(2)]
    most = jnp.maximum(picked[0], picked[1])
    e = [jnp.exp(p - most) for p in picked]
    gates = [v / (e[0] + e[1]) for v in e]
    combine = jnp.where(hot[0], gates[0], 0.0) + jnp.where(hot[1], gates[1], 0.0)

    def column(array, at):
        return jnp.sum(jnp.where(lane == at, array, 0.0), axis=1, keepdims=True)

    alphas = []
    for j in range(2):
        first, second = column(z, EXPERTS + 2 * j), column(z, EXPERTS + 2 * j + 1)
        most = jnp.maximum(first, second)
        a, b = jnp.exp(first - most), jnp.exp(second - most)
        alphas.append((a / (a + b), b / (a + b)))
    weights = [column(combine, FFN_EXPERTS + 1 + j) for j in range(3)]
    return hot, gates, combine, alphas, weights


def forward_kernel(place, x_ref, att_ref, wo_ref, small_ref, prev_ref, routes_ref, res_ref, base_ref, a_ref, comb_ref):
    heads_in = att_ref.shape[0] * att_ref.shape[1]
    att = att_ref[...].reshape(heads_in, att_ref.shape[2])
    wo = wo_ref[...].reshape(heads_in, wo_ref.shape[2])
    res = x_ref[...].astype(f32) + mm(att, wo, TN)
    res_ref[...] = res
    inverse = lax.rsqrt(jnp.mean(res * res, axis=1, keepdims=True) + epsilon)
    n2 = res * inverse * small_ref[19:20]
    a_ref[...] = n2.astype(bf16)
    _, _, combine, alphas, weights = mixing(n2, small_ref[:16], prev_ref[...], routes_ref[...])
    scale = weights[0] + weights[1] * alphas[0][0] + weights[2] * alphas[1][0]
    base_ref[...] = (
        res
        + scale * n2
        + (weights[1] * alphas[0][1]) * small_ref[16:17]
        + (weights[2] * alphas[1][1]) * small_ref[17:18]
    )
    comb_ref[...] = combine.T[:16]


def forward_rows(place, x, att, wo, small, prev, routes):
    rows, width = x.shape
    own = lambda i, p: (p[0], 0)
    return pl.pallas_call(
        forward_kernel,
        grid_spec=pltpu.PrefetchScalarGridSpec(
            num_scalar_prefetch=1,
            grid=(1,),
            in_specs=[
                full(x.shape),
                full(att.shape),
                full(wo.shape),
                full(small.shape),
                pl.BlockSpec((rows, prev.shape[1]), own),
                pl.BlockSpec((rows, 2), own),
            ],
            out_specs=[full((rows, width)), full((rows, width)), full((rows, width)), full((16, rows))],
        ),
        out_shape=[
            jax.ShapeDtypeStruct((rows, width), f32),
            jax.ShapeDtypeStruct((rows, width), f32),
            jax.ShapeDtypeStruct((rows, width), bf16),
            jax.ShapeDtypeStruct((16, rows), f32),
        ],
        compiler_params=params(),
        cost_estimate=cost(8),
        name="forward_rows",
    )(place, x, att, wo, small, prev, routes)


def backward_kernel(place, res_ref, dn_ref, cot_ref, valid_ref, att_ref, wo_ref, par_ref, prev_ref, routes_ref,
                    dres_ref, got_ref, gwo_ref, small_ref):
    width = res_ref.shape[1]
    res = res_ref[...]
    gain = par_ref[19:20]
    inverse = lax.rsqrt(jnp.mean(res * res, axis=1, keepdims=True) + epsilon)
    m = res * inverse
    n2 = m * gain
    hot, gates, _, alphas, weights = mixing(n2, par_ref[:16], prev_ref[...], routes_ref[...])
    g = cot_ref[...].astype(f32) * valid_ref[...]
    inner = jnp.sum(g * n2, axis=1, keepdims=True)
    onto = [jnp.sum(g * par_ref[16 + j : 17 + j], axis=1, keepdims=True) for j in range(2)]
    named = dn_ref[:, width:].astype(f32)
    lane = lax.broadcasted_iota(jnp.int32, hot[0].shape, 1)
    wide = lax.broadcasted_iota(jnp.int32, named.shape, 1)
    local = {
        FFN_EXPERTS + 1: inner,
        FFN_EXPERTS + 2: alphas[0][0] * inner + alphas[0][1] * onto[0],
        FFN_EXPERTS + 3: alphas[1][0] * inner + alphas[1][1] * onto[1],
    }
    routes = routes_ref[...]
    dgates = []
    for r in range(2):
        name = routes[:, r : r + 1]
        there = jnp.where((wide == name) | (wide == name + 16), named, 0.0)
        there = jnp.where(name < FFN_EXPERTS, jnp.sum(there, axis=1, keepdims=True), 0.0)
        for e, value in local.items():
            there = there + jnp.where(name == e, value, 0.0)
        dgates.append(there)
    mean = gates[0] * dgates[0] + gates[1] * dgates[1]
    dz = jnp.where(hot[0], gates[0] * (dgates[0] - mean), 0.0)
    dz = dz + jnp.where(hot[1], gates[1] * (dgates[1] - mean), 0.0)
    for j in range(2):
        da = weights[1 + j] * inner
        db = weights[1 + j] * onto[j]
        centre = alphas[j][0] * da + alphas[j][1] * db
        dz = dz + jnp.where(lane == EXPERTS + 2 * j, alphas[j][0] * (da - centre), 0.0)
        dz = dz + jnp.where(lane == EXPERTS + 2 * j + 1, alphas[j][1] * (db - centre), 0.0)
    scale = weights[0] + weights[1] * alphas[0][0] + weights[2] * alphas[1][0]
    highest = lax.Precision.HIGHEST
    dn2 = dn_ref[:, :width].astype(f32) + scale * g + mm(dz, par_ref[:16], NN, highest)
    small_ref[0:16] = mm(dz, n2, TN, highest)
    small_ref[16:24] = jnp.zeros((8, width), f32)
    small_ref[16:17] = jnp.sum((weights[1] * alphas[0][1]) * g, axis=0, keepdims=True)
    small_ref[17:18] = jnp.sum((weights[2] * alphas[1][1]) * g, axis=0, keepdims=True)
    small_ref[18:19] = jnp.sum(dn2 * m, axis=0, keepdims=True)
    q = dn2 * gain
    dres = g + inverse * (q - m * jnp.mean(q * m, axis=1, keepdims=True))
    dres_ref[...] = dres
    da = dres.astype(bf16)
    wo = wo_ref[...].reshape(-1, width)
    got = mm(wo, da, NT).astype(bf16)
    got_ref[...] = got.reshape(got_ref.shape)
    att = att_ref[...].reshape(got.shape)
    gwo_ref[...] = mm(att, da).astype(bf16).reshape(gwo_ref.shape)


def backward_rows(place, res, dn, cot, valid, att, wo, small, prev, routes):
    rows, width = res.shape
    own = lambda i, p: (p[0], 0)
    return pl.pallas_call(
        backward_kernel,
        grid_spec=pltpu.PrefetchScalarGridSpec(
            num_scalar_prefetch=1,
            grid=(1,),
            in_specs=[
                full(res.shape),
                full(dn.shape),
                full(cot.shape),
                full(valid.shape),
                full(att.shape),
                full(wo.shape),
                full(small.shape),
                pl.BlockSpec((rows, prev.shape[1]), own),
                pl.BlockSpec((rows, 2), own),
            ],
            out_specs=[full((rows, width)), full(att.shape), full(wo.shape), full((24, width))],
        ),
        out_shape=[
            jax.ShapeDtypeStruct((rows, width), f32),
            jax.ShapeDtypeStruct(att.shape, bf16),
            jax.ShapeDtypeStruct(wo.shape, bf16),
            jax.ShapeDtypeStruct((24, width), f32),
        ],
        compiler_params=params(),
        cost_estimate=cost(15),
        name="backward_rows",
    )(place, res, dn, cot, valid, att, wo, small, prev, routes)


def finish_kernel(x_ref, dn_ref, dres_ref, small_ref, base_ref, feed_ref, valid_ref, gw_ref, gs_ref, top_ref, wq_ref, wk_ref, limit_ref, other_ref, *refs):
    local = other_ref.shape[0]
    own, outs = refs[:local], refs[local:]
    gin_ref, out_ref, gate_ref, up_ref, down_ref = outs[:5]
    x = x_ref[...].astype(f32)
    inverse = lax.rsqrt(jnp.mean(x * x, axis=1, keepdims=True) + epsilon)
    m = x * inverse
    q = dn_ref[...] * small_ref[18:19]
    gin_ref[...] = dres_ref[...] + inverse * (q - m * jnp.mean(q * m, axis=1, keepdims=True))
    out_ref[...] = (valid_ref[...] * (base_ref[...] + feed_ref[...])).astype(bf16)
    core = lax.axis_index("ctx")
    for k, target in enumerate((gate_ref, up_ref, down_ref)):
        for j in range(local):
            mine, theirs = own[j][k].astype(f32), other_ref[j, k].astype(f32)
            target[j] = jnp.where(core == 0, mine, theirs)
            target[local + j] = jnp.where(core == 0, theirs, mine)

    @pl.when(pl.program_id(0) == 0)
    def _():
        gq, gk, gv, go, gnorm, gmoe, grouter, gconst, gvec, fac_ref, cq_ref, ck_ref = outs[5:]
        width = wq_ref.shape[1]
        flat = gw_ref[...].reshape(4 * width, gw_ref.shape[2])
        for k, target in enumerate((gq, gk, gv)):
            target[...] = flat[k * width : (k + 1) * width].T
        go[...] = flat[3 * width :]
        sums = gs_ref[...]
        across_rows = sums.T
        grouter[...] = across_rows[:, :EXPERTS]
        gconst[...] = across_rows[:, EXPERTS : EXPERTS + 4]
        gvec[...] = sums[16:18]
        gmoe[...] = sums[18:19]
        gnorm[...] = sums[19:20]
        factors = limit_ref[...] / jnp.maximum(top_ref[...], limit_ref[...])
        fac_ref[...] = factors
        lane = lax.broadcasted_iota(jnp.int32, (1, width), 1)
        root = jnp.zeros((1, width), f32)
        for h in range(width // HEAD_DIM):
            root = jnp.where(lane // HEAD_DIM == h, jnp.sqrt(factors[h : h + 1, :1]), root)
        cq_ref[...] = (wq_ref[...].astype(f32) * root).astype(bf16)
        ck_ref[...] = (wk_ref[...].astype(f32) * root).astype(bf16)


def finish_rows(x, dn, dres, small, base, feed, valid, gw, gs, top, wq, wk, limit, other, own):
    rows, width = x.shape
    local, kinds, depth, hidden = other.shape
    steps = 4 if depth % 64 == 0 else 1
    tile, deep = rows // steps, depth // steps
    by_row = pl.BlockSpec((tile, width), lambda i: (i, 0))
    expert_out = pl.BlockSpec((2 * local, deep, hidden), lambda i: (0, i, 0))
    once = [
        jax.ShapeDtypeStruct(shape, f32)
        for shape in [wq.shape] * 3
        + [(wq.shape[1], depth), (1, depth), (1, depth), (depth, EXPERTS), (depth, 4), (2, depth), (8, 128)]
    ] + [jax.ShapeDtypeStruct(wq.shape, bf16)] * 2
    return pl.pallas_call(
        finish_kernel,
        grid=(steps,),
        in_specs=[
            by_row,
            by_row,
            by_row,
            full(small.shape),
            by_row,
            by_row,
            pl.BlockSpec((tile, 1), lambda i: (i, 0)),
            full(gw.shape),
            full(gs.shape),
            full(top.shape),
            full(wq.shape),
            full(wk.shape),
            full(limit.shape),
            pl.BlockSpec((local, kinds, deep, hidden), lambda i: (0, 0, i, 0)),
        ]
        + [pl.BlockSpec((kinds, deep, hidden), lambda i: (0, i, 0))] * local,
        out_specs=[by_row, by_row, expert_out, expert_out, expert_out] + [full(v.shape) for v in once],
        out_shape=[
            jax.ShapeDtypeStruct((rows, width), f32),
            jax.ShapeDtypeStruct((rows, width), bf16),
        ]
        + [jax.ShapeDtypeStruct((2 * local, depth, hidden), f32)] * 3
        + once,
        compiler_params=params(),
        cost_estimate=cost(8),
        name="finish_rows",
    )(x, dn, dres, small, base, feed, valid, gw, gs, top, wq, wk, limit, other, *own)


def place_kernel(per, rt_ref, rc_ref, row_ref, col_ref):
    total = rt_ref.shape[1]
    one = lax.broadcasted_iota(jnp.int32, (BLOCK, BLOCK), 0)
    two = lax.broadcasted_iota(jnp.int32, (BLOCK, BLOCK), 1)
    before_row = (one < two).astype(bf16)
    before_col = (two < one).astype(bf16)
    row_carry = col_carry = None
    for at in range(0, total, BLOCK):
        if at % per == 0:
            row_carry = jnp.zeros((16, 1), f32)
            col_carry = jnp.zeros((1, 16), f32)
        here = slice(at, at + BLOCK)
        expert = lax.broadcasted_iota(jnp.int32, (16, BLOCK), 0)
        member = (rt_ref[0:1, here] == expert) | (rt_ref[1:2, here] == expert)
        rank = mm(member.astype(bf16), before_row) + row_carry
        row_ref[:, here] = jnp.where(member, rank, -1.0)
        row_carry = row_carry + jnp.sum(member.astype(f32), axis=1, keepdims=True)
        expert = lax.broadcasted_iota(jnp.int32, (BLOCK, 16), 1)
        member = (rc_ref[here, 0:1] == expert) | (rc_ref[here, 1:2] == expert)
        rank = mm(before_col, member.astype(bf16)) + col_carry
        col_ref[here, :] = jnp.where(member, rank, -1.0)
        col_carry = col_carry + jnp.sum(member.astype(f32), axis=0, keepdims=True)


def place_rows(routes, per):
    total = routes.shape[0]
    return pl.pallas_call(
        functools.partial(place_kernel, per),
        out_shape=[
            jax.ShapeDtypeStruct((16, total), f32),
            jax.ShapeDtypeStruct((total, 16), f32),
        ],
        compiler_params=params(),
        cost_estimate=cost(5),
        name="place_rows",
    )(routes.T, routes)


def fetch_kernel(first, row_ref, comb_ref, rows_ref, out_ref, gate_ref):
    expert = first[0] + pl.program_id(1)
    slot = lax.broadcasted_iota(jnp.int32, (CAP, row_ref.shape[1]), 0).astype(f32)
    hot = slot == row_ref[pl.ds(expert, 1), :]
    out_ref[0] = mm(hot.astype(bf16), rows_ref[...]).astype(bf16)
    if gate_ref is not None:
        gate_ref[0] = jnp.sum(jnp.where(hot, comb_ref[pl.ds(expert, 1), :], 0.0), axis=1, keepdims=True)


def fetch_rows(first, row, comb, rows, per, local, gated):
    total, width = rows.shape
    blocks = total // per
    outs = [jax.ShapeDtypeStruct((local, blocks * CAP, width), bf16)]
    specs = [pl.BlockSpec((1, CAP, width), lambda b, j, f: (j, b, 0))]
    ins = [
        pl.BlockSpec((16, per), lambda b, j, f: (0, b)),
        pl.BlockSpec((16, per), lambda b, j, f: (0, b)),
        pl.BlockSpec((per, width), lambda b, j, f: (b, 0)),
    ]
    args = (row, comb, rows)
    if gated:
        outs.append(jax.ShapeDtypeStruct((local, blocks * CAP, 1), f32))
        specs.append(pl.BlockSpec((1, CAP, 1), lambda b, j, f: (j, b, 0)))
        body = fetch_kernel
    else:
        body = lambda f, p, r, o: fetch_kernel(f, p, None, r, o, None)
        del ins[1]
        args = (row, rows)
    return pl.pallas_call(
        body,
        grid_spec=pltpu.PrefetchScalarGridSpec(
            num_scalar_prefetch=1, grid=(blocks, local), in_specs=ins, out_specs=specs
        ),
        out_shape=outs,
        compiler_params=params(),
        cost_estimate=cost(18),
        name="fetch_rows",
    )(first, *args)


def expert_kernel(j, first, x_ref, g_ref, gate_ref, w_ref, feed_ref, back_ref, gw_ref, total):
    i = pl.program_id(0)
    parts, _, _, depth, hidden = w_ref.shape
    width = parts * depth
    wg, wu, wd = [w_ref[:, 0, k].reshape(width, hidden) for k in range(3)]
    x, g, gate = x_ref[0], g_ref[0], gate_ref[0]
    gate_pre = mm(x, wg)
    up = mm(x, wu)
    sigmoid = 1.0 / (1.0 + jnp.exp(-gate_pre))
    activated = gate_pre * sigmoid
    inner = (activated * up).astype(bf16)
    out = mm(inner, wd, NT)
    g32 = g.astype(f32)
    feed_ref[...] = (gate * out).astype(bf16)
    dgate = jnp.sum(g32 * out, axis=1, keepdims=True)
    dout = (gate * g32).astype(bf16)
    dinner = mm(dout, wd)
    dpre = (dinner * up * sigmoid * (1.0 + gate_pre * (1.0 - sigmoid))).astype(bf16)
    dup = (dinner * activated).astype(bf16)
    back_ref[:, :width] = (mm(dpre, wg, NT) + mm(dup, wu, NT)).astype(bf16)
    lane = lax.broadcasted_iota(jnp.int32, (dgate.shape[0], back_ref.shape[1] - width), 1)
    coarse = dgate.astype(bf16).astype(f32)
    at = first[0] + j
    extra = jnp.where(lane == at, coarse, jnp.where(lane == at + 16, dgate - coarse, 0.0))
    back_ref[:, width:] = extra.astype(bf16)

    @pl.when(i == 0)
    def _():
        total[...] = jnp.zeros_like(total)

    total[0] += mm(x, dpre, TN)
    total[1] += mm(x, dup, TN)
    total[2] += mm(dout, inner, TN)

    @pl.when(i == pl.num_programs(0) - 1)
    def _():
        for k in range(3):
            gw_ref[:, k] = total[k].reshape(parts, depth, hidden).astype(bf16)


def expert(j, first, x, g, gate, w):
    slots, width = x.shape[1:]
    parts, _, kinds, depth, hidden = w.shape
    grads = (parts, kinds, depth, hidden)
    pick = lambda i, f: (j, i, 0)
    return pl.pallas_call(
        functools.partial(expert_kernel, j),
        grid_spec=pltpu.PrefetchScalarGridSpec(
            num_scalar_prefetch=1,
            grid=(slots // CAP,),
            in_specs=[
                pl.BlockSpec((1, CAP, width), pick),
                pl.BlockSpec((1, CAP, width), pick),
                pl.BlockSpec((1, CAP, 1), pick),
                pl.BlockSpec((parts, 1, kinds, depth, hidden), lambda i, f: (0, j, 0, 0, 0)),
            ],
            out_specs=[
                pl.BlockSpec((CAP, width), lambda i, f: (i, 0)),
                pl.BlockSpec((CAP, width + EXTRA), lambda i, f: (i, 0)),
                full(grads),
            ],
            scratch_shapes=[pltpu.VMEM((3, width, hidden), f32)],
        ),
        out_shape=[
            jax.ShapeDtypeStruct((slots, width), bf16),
            jax.ShapeDtypeStruct((slots, width + EXTRA), bf16),
            jax.ShapeDtypeStruct(grads, bf16),
        ],
        compiler_params=params(),
        cost_estimate=cost(14),
        name="expert",
    )(first, x, g, gate, w)


def spread_kernel(local, first, col_ref, *refs):
    out_ref = refs[-1]
    lane = lax.broadcasted_iota(jnp.int32, col_ref.shape, 1)
    slot = lax.broadcasted_iota(jnp.int32, (col_ref.shape[0], CAP), 1).astype(f32)
    total = None
    for j in range(local):
        mine = jnp.sum(jnp.where(lane == first[0] + j, col_ref[...], 0.0), axis=1, keepdims=True)
        term = mm((slot == mine).astype(bf16), refs[j][...])
        total = term if total is None else total + term
    out_ref[...] = total.astype(bf16)


def spread_rows(first, col, values, per):
    total = col.shape[0]
    tile = BLOCK
    width = values[0].shape[1]
    return pl.pallas_call(
        functools.partial(spread_kernel, len(values)),
        grid_spec=pltpu.PrefetchScalarGridSpec(
            num_scalar_prefetch=1,
            grid=(total // tile,),
            in_specs=[pl.BlockSpec((tile, 16), lambda i, f: (i, 0))]
            + [pl.BlockSpec((CAP, width), lambda i, f: (i // (per // tile), 0)) for _ in values],
            out_specs=pl.BlockSpec((tile, width), lambda i, f: (i, 0)),
        ),
        out_shape=jax.ShapeDtypeStruct((total, width), bf16),
        compiler_params=params(),
        cost_estimate=cost(20),
        name="spread_rows",
    )(first, col, *values)


def shards(
    hidden_in,
    cotangent,
    lengths,
    routes,
    prev_logits,
    norm_attn,
    w_query,
    w_key,
    w_value,
    w_out,
    norm_moe,
    w_router,
    w_const,
    const_vec,
    w_gate,
    w_up,
    w_down,
    threshold,
):
    plane = ("ctx", "tp")
    core, lane = lax.axis_index("ctx"), lax.axis_index("tp")
    nc, nt, ns = lax.axis_size("ctx"), lax.axis_size("tp"), lax.axis_size("shard")
    own, width = hidden_in.shape
    per = own * nt
    total = per * nc
    depth = w_gate.shape[1]
    heads = w_query.shape[1] // HEAD_DIM
    head_width = heads * HEAD_DIM
    local = FFN_EXPERTS // nc
    count = total // BLOCK // nc
    first_row = core * per + lane * own
    length = lengths[0]
    valid = (first_row + jnp.arange(own, dtype=jnp.int32) < length).astype(f32)[:, None]
    place = lane.astype(jnp.int32)[None]
    first = (core * local).astype(jnp.int32)[None]

    pieces = [
        lax.dynamic_slice_in_dim(w, core * local, local, 0) for w in (w_gate, w_up, w_down)
    ]
    expert_w = lax.all_gather(jnp.stack(pieces, axis=1), "shard", axis=0, tiled=False)
    small = jnp.concatenate(
        [
            w_router,
            w_const,
            const_vec.T,
            norm_attn[:, None],
            norm_moe[:, None],
            jnp.zeros((depth, SMALL - EXPERTS - 8), bf16),
        ],
        axis=1,
    )
    rows_all, attention_w, routes_all = opening(
        hidden_in, w_query, w_key, w_value, w_out, small, routes, 0
    )
    rows_all = rows_all.reshape(total, width)
    routes_all = routes_all.reshape(total, 2)
    prev = jnp.pad(prev_logits, ((0, 0), (0, 4)))
    cosine, sine = rope_tables(total)

    qt, kt, k, v, vt, wt, out_w, small = project(rows_all, attention_w, cosine, sine, heads)
    ot, lse, top, cot_all, out_w = attend(lengths, qt, k, vt, cotangent, out_w, count, 1)
    att = exchange(to_owner_kernel, ot, nt, 2, "to_owner")

    res, base, a2, comb = forward_rows(place, hidden_in, att, out_w, small, prev, routes)

    row_at, col_at = place_rows(routes_all, per)
    a2_all, comb_all = gather_rows((a2,), comb, 3)
    a2_all, cot_all = a2_all.reshape(total, width), cot_all.reshape(total, width)
    (g_slots,) = fetch_rows(first, row_at, None, cot_all, per, local, False)
    comb_all = comb_all.transpose(1, 0, 2).reshape(16, total)
    x_slots, gate_slots = fetch_rows(first, row_at, comb_all, a2_all, per, local, True)
    feeds, backs, grads = [], [], []
    for j in range(local):
        feed, back, grad = expert(j, first, x_slots, g_slots, gate_slots, expert_w)
        feeds.append(feed)
        backs.append(back)
        grads.append(grad)
    back = spread_rows(first, col_at, backs, per).reshape(8, own, width + EXTRA)
    back = sum_rows(back, 4)
    feed = spread_rows(first, col_at, feeds, per).reshape(8, own, width)
    feed = sum_rows(feed, 5)
    grads = [lax.psum_scatter(g, "shard", scatter_dimension=0, tiled=True)[0] for g in grads]

    dres, got, grad_out, gsmall = backward_rows(
        place, res, back, cotangent, valid, att, out_w, small, prev, routes
    )
    got = exchange(to_heads_kernel, got, count, 6, "to_heads")
    dq, dk, dv, grad_out = revisit(qt, k, kt, v, ot, got, lse, grad_out, 7)
    part, grad_w, gsmall = unproject(
        dq, dk, dv, cosine, sine, rows_all, small, wt, grad_out, gsmall, ns
    )
    part, grad_w, gsmall, top, others = closing(part.reshape(8, own, width), grad_w, gsmall, top, grads, 8)
    limit = jnp.broadcast_to(threshold[None], (8, 128))
    (grad_input, output, grad_gate, grad_up, grad_down, grad_q, grad_k, grad_v, grad_out, grad_norm_attn, grad_norm_moe,
     grad_router, grad_const, grad_vec, factors, clipped_query, clipped_key) = finish_rows(
        hidden_in, part, dres, small, base, feed, valid, grad_w, gsmall, top, w_query, w_key, limit, others, grads
    )
    return (
        output,
        grad_input,
        grad_norm_attn[0],
        grad_q,
        grad_k,
        grad_v,
        grad_out,
        grad_norm_moe[0],
        grad_router,
        grad_const,
        grad_vec,
        grad_gate,
        grad_up,
        grad_down,
        factors[:heads, 0],
        clipped_query,
        clipped_key,
    )


def solution(mesh):
    return jax.shard_map(
        shards,
        mesh=mesh,
        in_specs=(
            P(("shard", "ctx", "tp"), None),
            P(("shard", "ctx", "tp"), None),
            P("shard"),
            P(("shard", "ctx"), None),
            P(("shard", "ctx"), None),
            P("shard"),
            P("shard", "tp"),
            P("shard", "tp"),
            P("shard", "tp"),
            P("tp", "shard"),
            P("shard"),
            P("shard", None),
            P("shard", None),
            P(None, "shard"),
            P(None, "shard", "tp"),
            P(None, "shard", "tp"),
            P(None, "shard", "tp"),
            P(),
        ),
        out_specs=(
            P(("shard", "ctx", "tp"), None),
            P(("shard", "ctx", "tp"), None),
            P("shard"),
            P("shard", "tp"),
            P("shard", "tp"),
            P("shard", "tp"),
            P("tp", "shard"),
            P("shard"),
            P("shard", None),
            P("shard", None),
            P(None, "shard"),
            P(None, "shard", "tp"),
            P(None, "shard", "tp"),
            P(None, "shard", "tp"),
            P("tp"),
            P("shard", "tp"),
            P("shard", "tp"),
        ),
        check_vma=False,
    )
```

```python
import functools

import jax
import jax.numpy as jnp
import numpy as np
from jax import lax
from jax.experimental import pallas as pl
from jax.experimental.pallas import tpu as pltpu
from jax.sharding import PartitionSpec as P

HEAD_DIM = 64
EXPERTS = 12
FFN_EXPERTS = 8
CAP = 512
BLOCK = 512
EXTRA = 128
SMALL = 32
SLOT = 256
MESH = pl.DeviceIdType.MESH

epsilon = 1e-06
rope_base = 10000.0
bf16 = jnp.bfloat16
f32 = jnp.float32

NN = (((1,), (0,)), ((), ()))
NT = (((1,), (1,)), ((), ()))
TN = (((0,), (0,)), ((), ()))


def mm(left, right, dims=NN, precision=None):
    return lax.dot_general(
        left, right, dims, preferred_element_type=f32, precision=precision
    )


def params(mib=56, **more):
    return pltpu.CompilerParams(vmem_limit_bytes=mib * 1024 * 1024, **more)


def cost(us):
    return pl.CostEstimate(flops=int(us * 1e9), bytes_accessed=int(us * 3e6), transcendentals=0)


def full(shape):
    return pl.BlockSpec(shape, lambda *_: (0,) * len(shape))


def rope_tables(total):
    half = HEAD_DIM // 2
    freqs = np.float32(rope_base) ** (np.float32(-2.0) * np.arange(half, dtype=np.float32) / np.float32(HEAD_DIM))
    angles = freqs.astype(np.float32)[:, None] * np.arange(total, dtype=np.float32)[None, :]
    angles = angles.astype(np.float64)
    return jnp.asarray(np.cos(angles), f32), jnp.asarray(np.sin(angles), f32)


def zig(core, i):
    return 4 * (i // 2) + (core if i % 2 == 0 else 3 - core)


def anywhere(count):
    return [pl.BlockSpec(memory_space=pl.ANY)] * count


def spot():
    return lax.axis_index("shard"), lax.axis_index("ctx"), lax.axis_index("tp")


def across(t):
    return t + 1 - 2 * lax.rem(t, 2), lax.rem(t + 2, 4), 3 - t


def remote(source, target, sends, recvs, **where):
    return pltpu.make_async_remote_copy(
        src_ref=source,
        dst_ref=target,
        send_sem=sends,
        recv_sem=recvs,
        device_id=where,
        device_id_type=MESH,
    )


def greet(depth=True):
    z, c, t = spot()
    nc, nt, ns = lax.axis_size("ctx"), lax.axis_size("tp"), lax.axis_size("shard")
    barrier = pltpu.get_barrier_semaphore()
    for step in range(1, nc * nt):
        other = lax.rem(c * nt + t + step, nc * nt)
        pl.semaphore_signal(
            barrier,
            inc=1,
            device_id={"ctx": other // nt, "tp": lax.rem(other, nt)},
            device_id_type=MESH,
        )
    if depth:
        for step in range(1, ns):
            pl.semaphore_signal(
                barrier,
                inc=1,
                device_id={"shard": lax.rem(z + step, ns)},
                device_id_type=MESH,
            )
    pl.semaphore_wait(barrier, nc * nt - 1 + (ns - 1 if depth else 0))


class Gather:
    KINDS = 9

    def __init__(self, x, out, sends, recvs, own, cuts, stage=None):
        z, c, t = spot()
        tx, ty, td = across(t)
        rows = x.shape[0] // cuts
        half = rows // 2
        self.cuts = cuts
        self.load = None if stage is None else pltpu.make_async_copy(x, stage, own.at[0])
        self.own = pltpu.make_async_copy(x if stage is None else stage, out.at[4 * c + t], own.at[1])
        sib = {"ctx": 1 - c}
        px, py = {"tp": tx}, {"tp": ty}

        def copies(s):
            whole = pl.ds(s * rows, rows)
            one, two = pl.ds(s * rows, half), pl.ds(s * rows + half, half)

            def at(k, source, target, where):
                return remote(source, target, sends.at[s, k], recvs.at[s, k], **where)

            def keep(k, slot, part, where):
                ref = out.at[4 * c + slot, part]
                return at(k, ref, ref, where)

            mine = [
                at(k, x.at[whole], out.at[4 * c + t, whole], where)
                for k, where in enumerate((px, py, sib))
            ]
            return mine + [
                keep(3, tx, whole, sib),
                keep(4, tx, one, py),
                keep(5, ty, whole, sib),
                keep(6, ty, two, px),
                keep(7, td, one, sib),
                keep(8, td, two, sib),
            ]

        self.copies = [copies(s) for s in range(cuts)]

        def arrivals(s):
            whole = pl.ds(s * rows, rows)
            one, two = pl.ds(s * rows, half), pl.ds(s * rows + half, half)
            where = [(c, tx, whole), (c, ty, whole), (1 - c, t, whole)]
            where += [(1 - c, tx, whole), (c, td, one), (1 - c, ty, whole), (c, td, two)]
            where += [(1 - c, td, one), (1 - c, td, two)]
            return [
                remote(out.at[4 * d + slot, part], out.at[4 * d + slot, part], sends.at[s, k], recvs.at[s, k], **sib)
                for k, (d, slot, part) in enumerate(where)
            ]

        self.arrivals = [arrivals(s) for s in range(cuts)]

    @staticmethod
    def scratch(cuts):
        return [
            pltpu.SemaphoreType.DMA((cuts, Gather.KINDS)),
            pltpu.SemaphoreType.DMA((cuts, Gather.KINDS)),
            pltpu.SemaphoreType.DMA((2,)),
        ]

    def first(self):
        for s in range(self.cuts):
            for k in (0, 1, 2):
                self.copies[s][k].start()
        (self.load or self.own).start()

    def second(self, s):
        if self.load is not None and s == 0:
            self.load.wait()
            self.own.start()
        self.arrivals[s][0].wait_recv()
        self.copies[s][4].start()
        self.copies[s][3].start()
        self.arrivals[s][1].wait_recv()
        self.copies[s][6].start()
        self.copies[s][5].start()

    def third(self, s):
        for k in (4, 6):
            self.arrivals[s][k].wait_recv()
            self.copies[s][7 if k == 4 else 8].start()

    def last(self):
        for s in range(self.cuts):
            for k in (2, 3, 5, 7, 8):
                self.arrivals[s][k].wait_recv()
        for s in range(self.cuts):
            for k in range(self.KINDS):
                self.copies[s][k].wait_send()
        self.own.wait()


class Sum:
    def __init__(self, p, held, came, across_in, across_out, sends, recvs, loads, stage=None):
        z, c, t = spot()
        self.t = t
        tx, ty, td = across(t)
        half = held.shape[1] // 2
        self.half = half
        self.one, self.two = pl.ds(0, half), pl.ds(half, half)
        self.order = (td, tx, ty, t)
        self.held, self.came, self.inn = held, came, across_in
        sib, px, py = {"ctx": 1 - c}, {"tp": tx}, {"tp": ty}
        self.core = []
        for k, o in enumerate(self.order):
            source = p.at[4 * (1 - c) + o] if stage is None else stage.at[k]
            self.core.append(remote(source, came.at[o], sends.at[k], recvs.at[k], **sib))
        self.loads = None
        if stage is None:
            self.loads = [pltpu.make_async_copy(p.at[4 * c + o], held.at[o], loads.at[k]) for k, o in enumerate(self.order)]

        def send(k, source, slot, where):
            return remote(source, across_in.at[slot], sends.at[k], recvs.at[k], **where)

        self.side = {
            "dx": send(4, held.at[td, self.one], 0, px),
            "dy": send(5, held.at[td, self.two], 1, py),
            "x": send(6, held.at[tx, self.one], 2, px),
            "y": send(7, held.at[ty, self.two], 3, py),
            "cy": send(8, across_out.at[0], 4, py),
            "cx": send(9, across_out.at[1], 5, px),
        }
        self.out = across_out
        self.near = (tx, ty, td)

    @staticmethod
    def scratch(rows, width):
        return [
            pltpu.VMEM((4, rows, width), bf16),
            pltpu.VMEM((4, rows, width), bf16),
            pltpu.VMEM((6, rows // 2, width), bf16),
            pltpu.VMEM((2, rows // 2, width), bf16),
            pltpu.SemaphoreType.DMA((10,)),
            pltpu.SemaphoreType.DMA((10,)),
            pltpu.SemaphoreType.DMA((4,)),
        ]

    def first(self):
        for k in range(4):
            self.core[k].start()
            self.loads[k].start()

    def second(self, tile=None):
        for k, o in enumerate(self.order):
            if tile is None:
                self.loads[k].wait()
                mine = self.held[o].astype(f32)
            else:
                mine = tile(o)
            self.core[k].wait_recv()
            self.held[o] = (mine + self.came[o].astype(f32)).astype(bf16)
            if k == 0:
                self.side["dx"].start()
                self.side["dy"].start()
            if k == 1:
                self.side["x"].start()
            if k == 2:
                self.side["y"].start()

    def third(self):
        tx, ty, td = self.near
        self.side["dx"].wait_recv()
        self.out[0] = (self.held[ty, self.one].astype(f32) + self.inn[0].astype(f32)).astype(bf16)
        self.side["cy"].start()
        self.side["dy"].wait_recv()
        self.out[1] = (self.held[tx, self.two].astype(f32) + self.inn[1].astype(f32)).astype(bf16)
        self.side["cx"].start()

    def last(self):
        for k in ("x", "y", "cy", "cx"):
            self.side[k].wait_recv()
        for copy in self.core + list(self.side.values()):
            copy.wait_send()

    def total(self):
        def add(part, a, b):
            return self.held[self.t, part].astype(f32) + self.inn[a].astype(f32) + self.inn[b].astype(f32)

        return add(self.one, 2, 4), add(self.two, 3, 5)


def qkv_kernel(x_ref, w_ref, cos_ref, sin_ref, qt_ref, kt_ref, k_ref, v_ref, vt_ref, wt_ref, wo_ref, small_ref):
    heads = qt_ref.shape[0]
    width = heads * HEAD_DIM
    half = HEAD_DIM // 2

    @pl.when(pl.program_id(0) == 0)
    def _():
        def whole(core, which, here):
            v = w_ref[core, :, which].astype(f32)
            return v.reshape(v.shape[0] * v.shape[1], SLOT)[:, here].T

        mine = slice(0, width)
        wt_ref[:width] = whole(0, 0, mine).astype(bf16)
        wt_ref[width : 2 * width] = whole(0, 1, mine).astype(bf16)
        wt_ref[2 * width :] = whole(1, 0, mine).astype(bf16)
        wo_ref[...] = whole(1, 1, mine).astype(bf16)
        small_ref[...] = whole(0, 0, slice(width, width + SMALL))

    x = x_ref[...].astype(f32)
    inverse = lax.rsqrt(jnp.mean(x * x, axis=1, keepdims=True) + epsilon)
    a = (x * inverse * small_ref[18:19]).astype(bf16)
    y = mm(wt_ref[...], a, NT)
    c, s = cos_ref[...], sin_ref[...]

    def turned(first):
        u, w = y[first : first + half], y[first + half : first + HEAD_DIM]
        return jnp.concatenate([u * c - w * s, w * c + u * s], axis=0)

    for h in range(heads):
        at = h * HEAD_DIM
        qt_ref[h] = (turned(at) * HEAD_DIM**-0.5).astype(bf16)
        key = turned(width + at)
        kt_ref[h] = key.astype(bf16)
        k_ref[h] = key.T.astype(bf16)
        value = y[2 * width + at : 2 * width + at + HEAD_DIM]
        v_ref[h] = value.T.astype(bf16)
        vt_ref[h, :HEAD_DIM] = value.astype(bf16)
        vt_ref[h, HEAD_DIM:] = jnp.ones((16, value.shape[1]), bf16)


def project(rows, w, cosine, sine, heads):
    total, width = rows.shape
    tile = BLOCK
    out = heads * HEAD_DIM
    shapes = [
        jax.ShapeDtypeStruct((heads, HEAD_DIM, total), bf16),
        jax.ShapeDtypeStruct((heads, HEAD_DIM, total), bf16),
        jax.ShapeDtypeStruct((heads, total, HEAD_DIM), bf16),
        jax.ShapeDtypeStruct((heads, total, HEAD_DIM), bf16),
        jax.ShapeDtypeStruct((heads, HEAD_DIM + 16, total), bf16),
        jax.ShapeDtypeStruct((3 * out, width), bf16),
        jax.ShapeDtypeStruct((out, width), bf16),
        jax.ShapeDtypeStruct((SMALL, width), f32),
    ]
    return pl.pallas_call(
        qkv_kernel,
        grid=(total // tile,),
        in_specs=[
            pl.BlockSpec((tile, width), lambda i: (i, 0)),
            full(w.shape),
            pl.BlockSpec((HEAD_DIM // 2, tile), lambda i: (0, i)),
            pl.BlockSpec((HEAD_DIM // 2, tile), lambda i: (0, i)),
        ],
        out_specs=[
            pl.BlockSpec((heads, HEAD_DIM, tile), lambda i: (0, 0, i)),
            pl.BlockSpec((heads, HEAD_DIM, tile), lambda i: (0, 0, i)),
            pl.BlockSpec((heads, tile, HEAD_DIM), lambda i: (0, i, 0)),
            pl.BlockSpec((heads, tile, HEAD_DIM), lambda i: (0, i, 0)),
            pl.BlockSpec((heads, HEAD_DIM + 16, tile), lambda i: (0, 0, i)),
        ]
        + [full(v.shape) for v in shapes[5:]],
        out_shape=shapes,
        compiler_params=params(),
        cost_estimate=cost(13),
        name="project",
    )(rows, w, cosine, sine)


def dealt(core, i):
    return 4 * (i // 2) + jnp.where(lax.rem(i, 2) == 0, core, 3 - core)


def attend_kernel(cuts, length, qt_ref, k_ref, vt_ref, cot_ref, w_ref, ot_ref, lse_ref, top_ref, cots_ref, ws_ref, mask_cot, w_send, w_recv, w_own, *sems):
    z, c, t = spot()
    nt = lax.axis_size("tp")
    h, i = pl.program_id(0), pl.program_id(1)
    count = pl.num_programs(1)
    at_step = h * count + i
    last = pl.num_programs(0) * count - 1
    gather = Gather(mask_cot, cots_ref, *sems, cuts)
    half = w_ref.shape[0] // 2
    mine = pl.ds(c * half, half)
    theirs = pl.ds((1 - c) * half, half)
    away, came = [], []
    for step in range(1, nt):
        there, back = lax.rem(t + step, nt), lax.rem(t + nt - step, nt)
        away.append(remote(w_ref.at[mine], ws_ref.at[t, mine], w_send.at[step], w_recv.at[step], tp=there))
        ref = ws_ref.at[back, mine]
        came.append(remote(ref, ref, w_send.at[nt + step], w_recv.at[step], ctx=1 - c))
        ref = ws_ref.at[back, theirs]
        came.append(remote(ref, ref, w_send.at[nt + step], w_recv.at[nt + step], ctx=1 - c))
    onward = [
        remote(ws_ref.at[lax.rem(t + nt - step, nt), mine], ws_ref.at[lax.rem(t + nt - step, nt), mine],
               w_send.at[nt + step], w_recv.at[nt + step], ctx=1 - c)
        for step in range(1, nt)
    ]
    own_w = pltpu.make_async_copy(w_ref, ws_ref.at[t], w_own)

    @pl.when(at_step == 0)
    def _():
        rows = cot_ref.shape[0]
        position = (c * nt + t) * rows + lax.broadcasted_iota(jnp.int32, cot_ref.shape, 0)
        mask_cot[...] = jnp.where(position < length[0], cot_ref[...].astype(f32), 0.0).astype(bf16)
        greet(False)
        gather.first()
        for copy in away:
            copy.start()
        own_w.start()

    index = dealt(c, i)
    columns = BLOCK
    qt = qt_ref[0, :, pl.ds(pl.multiple_of(index * BLOCK, BLOCK), BLOCK)]

    def step(at, carry, diagonal):
        peak, total = carry
        start = pl.multiple_of(at * BLOCK, BLOCK)
        scores = mm(k_ref[0, pl.ds(start, BLOCK), :], qt)
        if diagonal:
            keys = lax.broadcasted_iota(jnp.int32, scores.shape, 0)
            queries = lax.broadcasted_iota(jnp.int32, scores.shape, 1)
            scores = jnp.where(keys <= queries, scores, -1e30)
        higher = jnp.maximum(peak, jnp.max(scores, axis=0, keepdims=True))
        weights = jnp.exp(scores - higher).astype(bf16)
        total = total * jnp.exp(peak - higher) + mm(vt_ref[0, :, pl.ds(start, BLOCK)], weights)
        return higher, total

    start = (jnp.full((1, columns), -1e30, f32), jnp.zeros((HEAD_DIM + 16, columns), f32))
    carry = lax.fori_loop(0, index, lambda at, c: step(at, c, False), start)
    peak, total = step(index, carry, True)
    mass = total[HEAD_DIM : HEAD_DIM + 1]
    ot_ref[0] = (total[:HEAD_DIM] / mass).astype(bf16)
    lse_ref[0, 0] = peak + jnp.log(mass)
    position = index * BLOCK + lax.broadcasted_iota(jnp.int32, peak.shape, 1)
    top_ref[0, 0] = jnp.where(position < length[0], peak, -1e30)

    @pl.when(at_step == last // 2)
    def _():
        gather.second(0)

    @pl.when(at_step == last - 3)
    def _():
        for s in range(1, cuts):
            gather.second(s)
        for copy, forth in zip(came[0::2], onward):
            copy.wait_recv()
            forth.start()

    @pl.when(at_step == last - 1)
    def _():
        for s in range(cuts):
            gather.third(s)

    @pl.when(at_step == last)
    def _():
        gather.last()
        for copy in came[1::2]:
            copy.wait_recv()
        for copy in away + onward:
            copy.wait_send()
        own_w.wait()


def attend(length, qt, k, vt, cot, w, count, number):
    cuts = 2
    heads, _, total = qt.shape
    nt = lax.axis_size("tp")
    return pl.pallas_call(
        functools.partial(attend_kernel, cuts),
        grid_spec=pltpu.PrefetchScalarGridSpec(
            num_scalar_prefetch=1,
            grid=(heads, count),
            in_specs=[
                pl.BlockSpec((1, HEAD_DIM, total), lambda h, i, n: (h, 0, 0)),
                pl.BlockSpec((1, total, HEAD_DIM), lambda h, i, n: (h, 0, 0)),
                pl.BlockSpec((1, HEAD_DIM + 16, total), lambda h, i, n: (h, 0, 0)),
                full(cot.shape),
                full(w.shape),
            ],
            out_specs=[
                pl.BlockSpec((1, HEAD_DIM, BLOCK), lambda h, i, n: (i, h, 0)),
                pl.BlockSpec((1, 1, 1, BLOCK), lambda h, i, n: (h, i, 0, 0)),
                pl.BlockSpec((1, 1, 1, BLOCK), lambda h, i, n: (h, i, 0, 0)),
            ]
            + anywhere(2),
            scratch_shapes=[
                pltpu.VMEM(cot.shape, bf16),
                pltpu.SemaphoreType.DMA((2 * nt,)),
                pltpu.SemaphoreType.DMA((2 * nt,)),
                pltpu.SemaphoreType.DMA,
            ]
            + Gather.scratch(cuts),
        ),
        out_shape=[
            jax.ShapeDtypeStruct((count, heads * HEAD_DIM, BLOCK), bf16),
            jax.ShapeDtypeStruct((heads, count, 1, BLOCK), f32),
            jax.ShapeDtypeStruct((heads, count, 1, BLOCK), f32),
            jax.ShapeDtypeStruct((8,) + cot.shape, bf16),
            jax.ShapeDtypeStruct((nt,) + w.shape, bf16),
        ],
        compiler_params=params(collective_id=number, has_side_effects=True),
        cost_estimate=cost(35),
        name="attend",
    )(length, qt, k, vt, cot, w)


def revisit_kernel(qt_ref, k_ref, kt_ref, v_ref, ot_ref, got_ref, lse_ref, go_ref, feed_ref, dq_ref, dk_ref, dv_ref, gos_ref, fed_ref, sum_k, sum_v, came_ref, w_send, w_recv, *scratch):
    z, c, t = spot()
    job = Sum(feed_ref, *scratch)
    nt = lax.axis_size("tp")
    h, i = pl.program_id(0), pl.program_id(1)
    count = pl.num_programs(1)
    index = dealt(c, i)
    here = pl.ds(pl.multiple_of(index * BLOCK, BLOCK), BLOCK)
    away = [
        remote(go_ref.at[lax.rem(t + step, nt)], came_ref.at[step], w_send.at[step], w_recv.at[step], tp=lax.rem(t + step, nt))
        for step in range(1, nt)
    ]

    at_step = h * count + i
    end = pl.num_programs(0) * count - 1

    @pl.when(at_step == 0)
    def _():
        greet(False)
        job.first()
        for copy in away:
            copy.start()

    @pl.when(at_step == 3)
    def _():
        job.second()

    @pl.when(at_step == end - 3)
    def _():
        job.third()

    qt, got = qt_ref[0, :, here], got_ref[0]
    lse = lse_ref[0, 0]
    centre = jnp.sum(ot_ref[0].astype(f32) * got.astype(f32), axis=0, keepdims=True)

    @pl.when(i == 0)
    def _():
        sum_k[...] = jnp.zeros_like(sum_k)
        sum_v[...] = jnp.zeros_like(sum_v)
        dq_ref[...] = jnp.zeros_like(dq_ref)

    def step(at, grad, diagonal):
        start = pl.multiple_of(at * BLOCK, BLOCK)
        here = pl.ds(start, BLOCK)
        scores = mm(k_ref[0, here, :], qt)
        probs = jnp.exp(scores - lse)
        if diagonal:
            keys = lax.broadcasted_iota(jnp.int32, scores.shape, 0)
            queries = lax.broadcasted_iota(jnp.int32, scores.shape, 1)
            probs = jnp.where(keys <= queries, probs, 0.0)
        grad_probs = mm(v_ref[0, here, :], got)
        grad_scores = (probs * (grad_probs - centre)).astype(bf16)
        sum_v[here, :] += mm(probs.astype(bf16), got, NT)
        sum_k[here, :] += mm(grad_scores, qt, NT)
        return grad + mm(kt_ref[0, :, here], grad_scores)

    grad = lax.fori_loop(0, index, lambda at, c: step(at, c, False), jnp.zeros(qt.shape, f32))
    dq_ref[0, :, here] = step(index, grad, True) * HEAD_DIM**-0.5

    @pl.when(i == count - 1)
    def _():
        dk_ref[0] = sum_k[...].T
        dv_ref[0] = sum_v[...].T

    @pl.when(at_step == end)
    def _():
        job.last()
        one, two = job.total()
        fed_ref[: job.half] = one
        fed_ref[job.half :] = two
        total = go_ref[t].astype(f32)
        for step, copy in enumerate(away):
            copy.wait_recv()
            total = total + came_ref[step + 1].astype(f32)
            copy.wait_send()
        gos_ref[...] = total.astype(bf16)


def revisit(qt, k, kt, v, ot, got, lse, go, feed, number):
    heads, _, total = qt.shape
    count = ot.shape[0]
    nt = lax.axis_size("tp")
    whole = pl.BlockSpec((1, HEAD_DIM, total), lambda h, i: (h, 0, 0))
    tall = pl.BlockSpec((1, total, HEAD_DIM), lambda h, i: (h, 0, 0))
    some = pl.BlockSpec((1, HEAD_DIM, BLOCK), lambda h, i: (i, h, 0))
    return pl.pallas_call(
        revisit_kernel,
        grid=(heads, count),
        in_specs=[
            whole,
            tall,
            whole,
            tall,
            some,
            some,
            pl.BlockSpec((1, 1, 1, BLOCK), lambda h, i: (h, i, 0, 0)),
            full(go.shape),
        ]
        + anywhere(1),
        out_specs=[whole, whole, whole, full(go.shape[1:]), full(feed.shape[1:])],
        scratch_shapes=[
            pltpu.VMEM((total, HEAD_DIM), f32),
            pltpu.VMEM((total, HEAD_DIM), f32),
            pltpu.VMEM(go.shape, bf16),
            pltpu.SemaphoreType.DMA((nt,)),
            pltpu.SemaphoreType.DMA((nt,)),
        ]
        + Sum.scratch(*feed.shape[1:]),
        out_shape=[jax.ShapeDtypeStruct((heads, HEAD_DIM, total), f32)] * 3
        + [jax.ShapeDtypeStruct(go.shape[1:], bf16), jax.ShapeDtypeStruct(feed.shape[1:], f32)],
        compiler_params=params(collective_id=number, has_side_effects=True),
        cost_estimate=cost(50),
        name="revisit",
    )(qt, k, kt, v, ot, got, lse, go, feed)


def unproject_kernel(dq_ref, dk_ref, dv_ref, cos_ref, sin_ref, x_ref, gain_ref, wt_ref, go_ref, small_ref,
                     part_ref, gw_ref, smalls_ref, total, row):
    heads = dq_ref.shape[0]
    half = HEAD_DIM // 2
    i = pl.program_id(0)
    c, s = cos_ref[...], sin_ref[...]

    def turned(g):
        u, w = g[:half], g[half:]
        return jnp.concatenate([u * c + w * s, w * c - u * s], axis=0)

    @pl.when(i == 0)
    def _():
        total[...] = jnp.zeros_like(total)
        row[...] = jnp.zeros_like(row)

    x = x_ref[...].astype(f32)
    m = x * lax.rsqrt(jnp.mean(x * x, axis=1, keepdims=True) + epsilon)
    a = (m * gain_ref[18:19]).astype(bf16)
    pieces = [turned(dq_ref[h]) for h in range(heads)]
    pieces += [turned(dk_ref[h]) for h in range(heads)]
    pieces += [dv_ref[h] for h in range(heads)]
    grads = jnp.concatenate(pieces, axis=0).astype(bf16)
    part = mm(grads, wt_ref[...], TN)
    part_ref[...] = part.astype(bf16)
    row[...] += jnp.sum(part * m, axis=0, keepdims=True)
    total[...] += mm(grads, a)

    @pl.when(i == pl.num_programs(0) - 1)
    def _():
        _, parts, rows, depth = gw_ref.shape
        mid = rows // 2
        at = lax.broadcasted_iota(jnp.int32, small_ref.shape, 0)
        smalls = small_ref[...] + jnp.where(at == 19, row[...], 0.0)
        for z in range(parts):
            here = slice(z * depth, (z + 1) * depth)
            gw_ref[0, z] = total[:rows, here].astype(bf16)
            gw_ref[1, z, :mid] = total[rows:, here].astype(bf16)
            gw_ref[1, z, mid:] = go_ref[:, here]
            smalls_ref[z] = smalls[:, here]


def unproject(dq, dk, dv, cosine, sine, x, gain, wt, go, small, parts):
    heads, _, rows = dq.shape
    width = x.shape[1]
    out = wt.shape[0]
    depth = width // parts
    piece = pl.BlockSpec((heads, HEAD_DIM, BLOCK), lambda i: (0, 0, i))
    table = pl.BlockSpec((HEAD_DIM // 2, BLOCK), lambda i: (0, i))
    shapes = [
        jax.ShapeDtypeStruct((rows, width), bf16),
        jax.ShapeDtypeStruct((2, parts, 2 * heads * HEAD_DIM, depth), bf16),
        jax.ShapeDtypeStruct((parts,) + small.shape[:1] + (depth,), f32),
    ]
    return pl.pallas_call(
        unproject_kernel,
        grid_spec=pl.GridSpec(
            grid=(rows // BLOCK,),
            in_specs=[
                piece,
                piece,
                piece,
                table,
                table,
                pl.BlockSpec((BLOCK, width), lambda i: (i, 0)),
                full(gain.shape),
                full(wt.shape),
                full(go.shape),
                full(small.shape),
            ],
            out_specs=[pl.BlockSpec((BLOCK, width), lambda i: (i, 0))] + [full(v.shape) for v in shapes[1:]],
            scratch_shapes=[pltpu.VMEM((out, width), f32), pltpu.VMEM((1, width), f32)],
        ),
        out_shape=shapes,
        compiler_params=params(),
        cost_estimate=cost(18),
        name="unproject",
    )(dq, dk, dv, cosine, sine, x, gain, wt, go, small)


def opening_kernel(cuts, x_ref, wq_ref, wk_ref, wv_ref, wo_ref, small_ref, routes_ref, out_ref, ws_ref, all_routes_ref, held, stage, *sems):
    gather = Gather(x_ref, out_ref, *sems[:3], cuts, stage)
    sends, recvs, local = sems[3:]
    z, c, t = spot()
    ns = lax.axis_size("shard")
    width = wq_ref.shape[1]
    held[0, :, :width] = jnp.where(c == 0, wq_ref[...].astype(f32), wv_ref[...].astype(f32)).astype(bf16)
    held[0, :, width : width + SMALL] = small_ref[...]
    held[0, :, width + SMALL :] = jnp.zeros((held.shape[1], SLOT - width - SMALL), bf16)
    held[1, :, :width] = jnp.where(c == 0, wk_ref[...].astype(f32), wo_ref[...].astype(f32).T).astype(bf16)
    held[1, :, width:] = jnp.zeros((held.shape[1], SLOT - width), bf16)
    greet()
    started = []

    def go(k, source, target, **where):
        copy = remote(source, target, sends.at[k], recvs.at[k], **where)
        copy.start()
        started.append(copy)

    def came(k, ref):
        remote(ref, ref, sends.at[k], recvs.at[k], ctx=1 - c).wait_recv()

    for step in range(1, ns):
        go(step, held, ws_ref.at[c, z], shard=lax.rem(z + step, ns))
    go(0, held, ws_ref.at[c, z], ctx=1 - c)
    gather.first()
    go(2 * ns, routes_ref, all_routes_ref.at[c], ctx=1 - c)
    mine = [
        pltpu.make_async_copy(held, ws_ref.at[c, z], local.at[0]),
        pltpu.make_async_copy(routes_ref, all_routes_ref.at[c], local.at[1]),
    ]
    for copy in mine:
        copy.start()
    for s in range(cuts):
        gather.second(s)
    for step in range(1, ns):
        back = lax.rem(z + ns - step, ns)
        came(step, ws_ref.at[c, back])
        go(ns + step, ws_ref.at[c, back], ws_ref.at[c, back], ctx=1 - c)
    for s in range(cuts):
        gather.third(s)
    gather.last()
    came(0, ws_ref.at[1 - c, z])
    came(2 * ns, all_routes_ref.at[1 - c])
    for step in range(1, ns):
        came(ns + step, ws_ref.at[1 - c, lax.rem(z + ns - step, ns)])
    for copy in started:
        copy.wait_send()
    for copy in mine:
        copy.wait()


def opening(x, wq, wk, wv, wo, small, routes, number):
    cuts = 2
    ns = lax.axis_size("shard")
    depth = wq.shape[0]
    vmem = pl.BlockSpec(memory_space=pltpu.VMEM)
    return pl.pallas_call(
        functools.partial(opening_kernel, cuts),
        in_specs=anywhere(1) + [vmem] * 6,
        out_specs=anywhere(3),
        out_shape=[
            jax.ShapeDtypeStruct((8,) + x.shape, x.dtype),
            jax.ShapeDtypeStruct((2, ns, 2, depth, SLOT), bf16),
            jax.ShapeDtypeStruct((2,) + routes.shape, routes.dtype),
        ],
        scratch_shapes=[pltpu.VMEM((2, depth, SLOT), bf16), pltpu.VMEM(x.shape, x.dtype)]
        + Gather.scratch(cuts)
        + [
            pltpu.SemaphoreType.DMA((2 * ns + 1,)),
            pltpu.SemaphoreType.DMA((2 * ns + 1,)),
            pltpu.SemaphoreType.DMA((2,)),
        ],
        compiler_params=params(collective_id=number, has_side_effects=True),
        cost_estimate=cost(30),
        name="opening",
    )(x, wq, wk, wv, wo, small, routes)


def places(routes_ref, row_ref):
    one = lax.broadcasted_iota(jnp.int32, (BLOCK, BLOCK), 0)
    two = lax.broadcasted_iota(jnp.int32, (BLOCK, BLOCK), 1)
    before = (one < two).astype(bf16)
    blocks, _, per = routes_ref.shape
    for b in range(blocks):
        carry = jnp.zeros((16, 1), f32)
        for at in range(0, per, BLOCK):
            here = slice(at, at + BLOCK)
            expert = lax.broadcasted_iota(jnp.int32, (16, BLOCK), 0)
            member = (routes_ref[b, 0:1, here] == expert) | (routes_ref[b, 1:2, here] == expert)
            rank = mm(member.astype(bf16), before) + carry
            row_ref[:, b * per + at : b * per + at + BLOCK] = jnp.where(member, rank, -1.0)
            carry = carry + jnp.sum(member.astype(f32), axis=1, keepdims=True)


def dispatch_kernel(cuts, a_ref, comb_ref, routes_ref, cots_ref, x_out, g_out, gate_ref, row_ref,
                    rows, cots, combs, xs, gs, c_send, c_recv, local, x_sem, g_sem, *sems):
    gather = Gather(a_ref, rows, *sems, cuts)
    z, c, t = spot()
    own = 4 * c + t
    blocks, _, per = routes_ref.shape
    width = rows.shape[2]
    experts = xs.shape[0]
    load = pltpu.make_async_copy(cots_ref, cots, local)
    load.start()
    greet(False)
    gather.first()
    pairs = []
    for step in range(1, 8):
        other, back = lax.rem(own + step, 8), lax.rem(own + 8 - step, 8)
        where = {"ctx": other // 4, "tp": lax.rem(other, 4)}
        copy = remote(comb_ref, combs.at[own], c_send.at[step], c_recv.at[step], **where)
        copy.start()
        pairs.append((copy, remote(comb_ref, combs.at[back], c_send.at[step], c_recv.at[step], **where)))
    combs[own] = comb_ref[...]
    places(routes_ref, row_ref)
    load.wait()

    def fetch(source, target, out, sem, n, gated):
        b, j = n // experts, lax.rem(n, experts)
        here = pl.ds(pl.multiple_of(b * CAP, CAP), CAP)
        named = row_ref[pl.ds(experts * c + j, 1), pl.ds(pl.multiple_of(b * per, per), per)]
        hot = lax.broadcasted_iota(jnp.int32, (CAP, per), 0).astype(f32) == named
        block = source[pl.ds(4 * b, 4)].reshape(per, width)
        target[j, here] = mm(hot.astype(bf16), block).astype(bf16)
        pltpu.make_async_copy(target.at[j, here], out.at[j, here], sem.at[n]).start()
        if gated:
            gate = jnp.zeros((CAP, 1), f32)
            rows_each = per // 4
            for k in range(4):
                part = hot[:, k * rows_each : (k + 1) * rows_each]
                weight = combs[4 * b + k, pl.ds(experts * c + j, 1)]
                gate = gate + jnp.sum(jnp.where(part, weight, 0.0), axis=1, keepdims=True)
            gate_ref[j, here] = gate

    def fetch_g(first, last):
        @pl.loop(first, last)
        def _(n):
            fetch(cots, gs, g_out, g_sem, n, False)

    total = blocks * experts
    fetch_g(0, 1)
    gather.second(0)
    fetch_g(1, 5)
    gather.second(1)
    fetch_g(5, total)
    gather.third(0)
    gather.third(1)
    for copy, came in pairs:
        came.wait_recv()
    gather.last()

    @pl.loop(0, total)
    def _(n):
        fetch(rows, xs, x_out, x_sem, n, True)

    for copy, came in pairs:
        copy.wait_send()

    @pl.loop(0, total)
    def _(n):
        b, j = n // experts, lax.rem(n, experts)
        here = pl.ds(pl.multiple_of(b * CAP, CAP), CAP)
        pltpu.make_async_copy(gs.at[j, here], g_out.at[j, here], g_sem.at[n]).wait()
        pltpu.make_async_copy(xs.at[j, here], x_out.at[j, here], x_sem.at[n]).wait()


def dispatch(a, comb, routes, cots, experts, number):
    cuts = 2
    own, width = a.shape
    blocks, _, per = routes.shape
    slots = jax.ShapeDtypeStruct((experts, blocks * CAP, width), bf16)
    vmem = pl.BlockSpec(memory_space=pltpu.VMEM)
    return pl.pallas_call(
        functools.partial(dispatch_kernel, cuts),
        in_specs=anywhere(1) + [vmem, vmem] + anywhere(1),
        out_specs=anywhere(2) + [vmem, vmem],
        out_shape=[
            slots,
            slots,
            jax.ShapeDtypeStruct((experts, blocks * CAP, 1), f32),
            jax.ShapeDtypeStruct((16, blocks * per), f32),
        ],
        scratch_shapes=[
            pltpu.VMEM((8, own, width), bf16),
            pltpu.VMEM((8, own, width), bf16),
            pltpu.VMEM((8,) + comb.shape, f32),
            pltpu.VMEM(slots.shape, bf16),
            pltpu.VMEM(slots.shape, bf16),
            pltpu.SemaphoreType.DMA((8,)),
            pltpu.SemaphoreType.DMA((8,)),
            pltpu.SemaphoreType.DMA,
            pltpu.SemaphoreType.DMA((blocks * experts,)),
            pltpu.SemaphoreType.DMA((blocks * experts,)),
        ]
        + Gather.scratch(cuts),
        compiler_params=params(collective_id=number, has_side_effects=True),
        cost_estimate=cost(50),
        name="dispatch",
    )(a, comb, routes, cots)


def combine_kernel(experts, row_ref, *refs):
    values_in = refs[: 2 * experts]
    out_ref, feed_out = refs[2 * experts : 2 * experts + 2]
    backs, feeds, stage, staged, b_sem, f_sem, o_sem = refs[2 * experts + 2 : 2 * experts + 9]
    job = Sum(None, *refs[2 * experts + 9 :], stage=stage)
    z, c, t = spot()
    loads = []
    for j in range(experts):
        loads.append(pltpu.make_async_copy(values_in[experts + j], backs.at[j], b_sem.at[j]))
    for j in range(experts):
        loads.append(pltpu.make_async_copy(values_in[j], feeds.at[j], f_sem.at[j]))
    for copy in loads:
        copy.start()
    greet(False)

    def tile(values, owner):
        start = pl.multiple_of(owner * BLOCK, BLOCK)
        place = row_ref[:, pl.ds(start, BLOCK)].T
        lane = lax.broadcasted_iota(jnp.int32, place.shape, 1)
        slot = lax.broadcasted_iota(jnp.int32, (BLOCK, CAP), 1).astype(f32)
        here = pl.ds(pl.multiple_of(owner // 4 * CAP, CAP), CAP)
        total = None
        for j in range(experts):
            mine = jnp.sum(jnp.where(lane == experts * c + j, place, 0.0), axis=1, keepdims=True)
            term = mm((slot == mine).astype(bf16), values[j, here])
            total = term if total is None else total + term
        return total

    for copy in loads[:experts]:
        copy.wait()

    for k, o in enumerate(job.order):
        stage[k] = tile(backs, 4 * (1 - c) + o).astype(bf16)
        job.core[k].start()
    job.second(lambda o: tile(backs, 4 * c + o))
    for copy in loads[experts:]:
        copy.wait()

    def feed(first, last):
        @pl.loop(first, last)
        def _(n):
            staged[n] = tile(feeds, n).astype(bf16)
            pltpu.make_async_copy(staged.at[n], feed_out.at[n], o_sem.at[n]).start()

    feed(0, 4)
    job.third()
    feed(4, 8)
    job.last()
    one, two = job.total()
    out_ref[: job.half] = one
    out_ref[job.half :] = two

    @pl.loop(0, 8)
    def _(n):
        pltpu.make_async_copy(staged.at[n], feed_out.at[n], o_sem.at[n]).wait()


def combine(row, feeds, backs, number):
    experts = len(feeds)
    slots, width = feeds[0].shape
    wide = backs[0].shape[1]
    rows = row.shape[1] // 8
    vmem = pl.BlockSpec(memory_space=pltpu.VMEM)
    return pl.pallas_call(
        functools.partial(combine_kernel, experts),
        in_specs=[vmem] + anywhere(2 * experts),
        out_specs=[vmem] + anywhere(1),
        out_shape=[
            jax.ShapeDtypeStruct((rows, wide), f32),
            jax.ShapeDtypeStruct((8, rows, width), bf16),
        ],
        scratch_shapes=[
            pltpu.VMEM((experts, slots, wide), bf16),
            pltpu.VMEM((experts, slots, width), bf16),
            pltpu.VMEM((4, rows, wide), bf16),
            pltpu.VMEM((8, rows, width), bf16),
            pltpu.SemaphoreType.DMA((experts,)),
            pltpu.SemaphoreType.DMA((experts,)),
            pltpu.SemaphoreType.DMA((8,)),
        ]
        + Sum.scratch(rows, wide),
        compiler_params=params(collective_id=number, has_side_effects=True),
        cost_estimate=cost(45),
        name="combine",
    )(row, *feeds, *backs)


def to_owner_kernel(o_ref, att_ref, send_sem, recv_sem, local_sem):
    z, c, t = spot()
    nt = lax.axis_size("tp")
    own = c * nt + t
    greet(False)
    copies = []
    for i in range(o_ref.shape[0]):
        block = zig(c, i)
        copy = remote(o_ref.at[i], att_ref.at[t], send_sem.at[i], recv_sem.at[t], ctx=block // nt, tp=lax.rem(block, nt))
        local = pltpu.make_async_copy(o_ref.at[i], att_ref.at[t], local_sem)
        copies.append((block == own, copy, local))
    settle(copies)
    mine = lax.rem((own + 1) // 2, 2) == c
    for source in range(nt):

        @pl.when(jnp.logical_or(jnp.logical_not(mine), source != t))
        def _():
            remote(o_ref.at[0], att_ref.at[source], send_sem.at[0], recv_sem.at[source], ctx=c, tp=t).wait_recv()


def settle(copies):
    for here, copy, local in copies:

        @pl.when(jnp.logical_not(here))
        def _():
            copy.start()

        @pl.when(here)
        def _():
            local.start()

    for here, copy, local in copies:

        @pl.when(jnp.logical_not(here))
        def _():
            copy.wait_send()

        @pl.when(here)
        def _():
            local.wait()


def to_heads_kernel(o_ref, got_ref, send_sem, recv_sem, local_sem):
    z, c, t = spot()
    nt = lax.axis_size("tp")
    own = c * nt + t
    greet(False)
    core = lax.rem((own + 1) // 2, 2)
    slot = 2 * (own // 4) + lax.rem(own, 4) // 2
    copies = []
    for target in range(nt):
        here = jnp.logical_and(core == c, target == t)
        copy = remote(o_ref.at[target], got_ref.at[slot], send_sem.at[target], recv_sem.at[slot], ctx=core, tp=target)
        local = pltpu.make_async_copy(o_ref.at[target], got_ref.at[slot], local_sem)
        copies.append((here, copy, local))
    settle(copies)
    for i in range(got_ref.shape[0]):

        @pl.when(zig(c, i) != own)
        def _():
            remote(o_ref.at[0], got_ref.at[i], send_sem.at[0], recv_sem.at[i], ctx=c, tp=t).wait_recv()


def exchange(kernel, o, count, number, name):
    return pl.pallas_call(
        kernel,
        in_specs=anywhere(1),
        out_specs=anywhere(1)[0],
        out_shape=jax.ShapeDtypeStruct((count,) + o.shape[1:], o.dtype),
        scratch_shapes=[
            pltpu.SemaphoreType.DMA((o.shape[0],)),
            pltpu.SemaphoreType.DMA((count,)),
            pltpu.SemaphoreType.DMA,
        ],
        compiler_params=params(collective_id=number, has_side_effects=True),
        cost_estimate=cost(12),
        name=name,
    )(o)


def closing_kernel(p_ref, gw_ref, small_ref, top_ref, ge0, ge1, ge2, ge3, out_ref, gsum_ref, ssum_ref, tmax_ref, gall_ref,
                   gcore, gline, gmine, sline, splane, tline, mytop, *sems):
    job = Sum(p_ref, *sems[:7])
    sends, recvs, local = sems[7:]
    z, c, t = spot()
    ns = lax.axis_size("shard")
    rows = gw_ref.shape[2]
    own = 4 * c + t
    greet()
    row = lax.broadcasted_iota(jnp.int32, mytop.shape, 0)
    high = jnp.full(mytop.shape, -1e30, f32)
    for h in range(top_ref.shape[0]):
        best = jnp.max(jnp.max(top_ref[h], axis=0), axis=1, keepdims=True)
        high = jnp.where(row == h, best, high)
    mytop[...] = high
    started = []

    def go(k, source, target, **where):
        copy = remote(source, target, sends.at[k], recvs.at[k], **where)
        copy.start()
        started.append(copy)
        return copy

    core = go(0, gw_ref.at[1 - c], gcore, ctx=1 - c)
    small = [go(3 + s, small_ref.at[lax.rem(z + s, ns)], sline.at[s], shard=lax.rem(z + s, ns)) for s in range(1, ns)]
    tops = [go(3 + ns + s, mytop, tline.at[s], shard=lax.rem(z + s, ns)) for s in range(1, ns)]
    own_g = pltpu.make_async_copy(gw_ref.at[c], gmine, local.at[0])
    own_g.start()
    job.first()
    experts = [go(11 + 4 * ns + k, ge, gall_ref.at[k], ctx=1 - c) for k, ge in enumerate((ge0, ge1, ge2, ge3))]
    job.second()
    own_g.wait()
    core.wait_recv()
    gmine[...] = (gmine[...].astype(f32) + gcore[...].astype(f32)).astype(bf16)
    line = [go(3 + 2 * ns + s, gmine.at[lax.rem(z + s, ns)], gline.at[s], shard=lax.rem(z + s, ns)) for s in range(1, ns)]
    for copy in small:
        copy.wait_recv()
    total = small_ref[z]
    for s in range(1, ns):
        total = total + sline[s]
    splane[0] = total
    plane = []
    for s in range(1, 8):
        other = lax.rem(own + s, 8)
        plane.append(go(3 + 3 * ns + s, splane.at[0], splane.at[s], ctx=other // 4, tp=lax.rem(other, 4)))
    for copy in tops:
        copy.wait_recv()
    high = mytop[...]
    for s in range(1, ns):
        high = jnp.maximum(high, tline[s])
    tline[0] = high
    pair = go(2, tline.at[0], tline.at[ns], ctx=1 - c)
    job.third()
    for copy in line:
        copy.wait_recv()
    total = gmine[z].astype(f32)
    for s in range(1, ns):
        total = total + gline[s].astype(f32)
    gsum_ref[c] = total
    final = go(3, gsum_ref.at[c], gsum_ref.at[c], ctx=1 - c)
    for copy in plane:
        copy.wait_recv()
    total = splane[0]
    for s in range(1, 8):
        total = total + splane[s]
    ssum_ref[...] = total
    pair.wait_recv()
    tmax_ref[...] = jnp.maximum(tline[0], tline[ns])
    job.last()
    one, two = job.total()
    out_ref[: job.half] = one
    out_ref[job.half :] = two
    remote(gsum_ref.at[1 - c], gsum_ref.at[1 - c], sends.at[3], recvs.at[3], ctx=1 - c).wait_recv()
    for copy in experts:
        copy.wait_recv()
    for copy in started:
        copy.wait_send()


def closing(p, gw, small, top, experts, number):
    _, rows, width = p.shape
    ns = lax.axis_size("shard")
    vmem = pl.BlockSpec(memory_space=pltpu.VMEM)
    return pl.pallas_call(
        closing_kernel,
        in_specs=anywhere(2) + [vmem, vmem] + anywhere(4),
        out_specs=[vmem, vmem, vmem, vmem] + anywhere(1),
        out_shape=[
            jax.ShapeDtypeStruct((rows, width), f32),
            jax.ShapeDtypeStruct((2,) + gw.shape[2:], f32),
            jax.ShapeDtypeStruct(small.shape[1:], f32),
            jax.ShapeDtypeStruct((8, 128), f32),
            jax.ShapeDtypeStruct((4,) + experts[0].shape, bf16),
        ],
        scratch_shapes=[
            pltpu.VMEM(gw.shape[1:], bf16),
            pltpu.VMEM(gw.shape[1:], bf16),
            pltpu.VMEM(gw.shape[1:], bf16),
            pltpu.VMEM(small.shape, f32),
            pltpu.VMEM((8,) + small.shape[1:], f32),
            pltpu.VMEM((ns + 1, 8, 128), f32),
            pltpu.VMEM((8, 128), f32),
        ]
        + Sum.scratch(rows, width)
        + [
            pltpu.SemaphoreType.DMA((4 * ns + 15,)),
            pltpu.SemaphoreType.DMA((4 * ns + 15,)),
            pltpu.SemaphoreType.DMA((2,)),
        ],
        compiler_params=params(collective_id=number, has_side_effects=True),
        cost_estimate=cost(40),
        name="closing",
    )(p, gw, small, top, *experts)


def columns(prev_ref, routes_ref):
    count, rows = prev_ref.shape
    previous = jnp.concatenate([prev_ref[...], jnp.zeros((16 - count, rows), f32)], axis=0).T
    at = lax.broadcasted_iota(jnp.int32, (8, rows), 0)
    routes = routes_ref[...].astype(f32)
    return previous, jnp.where(at == 0, routes[0:1], routes[1:2]).T


def mixing(n2, wrc, previous, routes):
    z = mm(n2, wrc, NT, lax.Precision.HIGHEST)
    lane = lax.broadcasted_iota(jnp.int32, z.shape, 1)
    logits = z + previous
    hot = [lane.astype(f32) == routes[:, r : r + 1] for r in range(2)]
    picked = [jnp.sum(jnp.where(hot[r], logits, 0.0), axis=1, keepdims=True) for r in range(2)]
    most = jnp.maximum(picked[0], picked[1])
    e = [jnp.exp(p - most) for p in picked]
    gates = [v / (e[0] + e[1]) for v in e]
    combine = jnp.where(hot[0], gates[0], 0.0) + jnp.where(hot[1], gates[1], 0.0)

    def column(array, at):
        return jnp.sum(jnp.where(lane == at, array, 0.0), axis=1, keepdims=True)

    alphas = []
    for j in range(2):
        first, second = column(z, EXPERTS + 2 * j), column(z, EXPERTS + 2 * j + 1)
        most = jnp.maximum(first, second)
        a, b = jnp.exp(first - most), jnp.exp(second - most)
        alphas.append((a / (a + b), b / (a + b)))
    weights = [column(combine, FFN_EXPERTS + 1 + j) for j in range(3)]
    return hot, gates, combine, alphas, weights


def forward_kernel(place, x_ref, att_ref, wo_ref, small_ref, prev_ref, routes_ref, res_ref, base_ref, a_ref, comb_ref):
    heads_in = att_ref.shape[0] * att_ref.shape[1]
    att = att_ref[...].reshape(heads_in, att_ref.shape[2])
    wo = wo_ref[...].reshape(heads_in, wo_ref.shape[2])
    res = x_ref[...].astype(f32) + mm(att, wo, TN)
    res_ref[...] = res
    inverse = lax.rsqrt(jnp.mean(res * res, axis=1, keepdims=True) + epsilon)
    n2 = res * inverse * small_ref[19:20]
    a_ref[...] = n2.astype(bf16)
    _, _, combine, alphas, weights = mixing(n2, small_ref[:16], *columns(prev_ref, routes_ref))
    scale = weights[0] + weights[1] * alphas[0][0] + weights[2] * alphas[1][0]
    base_ref[...] = (
        res
        + scale * n2
        + (weights[1] * alphas[0][1]) * small_ref[16:17]
        + (weights[2] * alphas[1][1]) * small_ref[17:18]
    )
    comb_ref[...] = combine.T[:16]


def forward_rows(place, x, att, wo, small, prev, routes):
    rows, width = x.shape
    own = lambda i, p: (0, p[0])
    return pl.pallas_call(
        forward_kernel,
        grid_spec=pltpu.PrefetchScalarGridSpec(
            num_scalar_prefetch=1,
            grid=(1,),
            in_specs=[
                full(x.shape),
                full(att.shape),
                full(wo.shape),
                full(small.shape),
                pl.BlockSpec((prev.shape[0], rows), own),
                pl.BlockSpec((2, rows), own),
            ],
            out_specs=[full((rows, width)), full((rows, width)), full((rows, width)), full((16, rows))],
        ),
        out_shape=[
            jax.ShapeDtypeStruct((rows, width), f32),
            jax.ShapeDtypeStruct((rows, width), f32),
            jax.ShapeDtypeStruct((rows, width), bf16),
            jax.ShapeDtypeStruct((16, rows), f32),
        ],
        compiler_params=params(),
        cost_estimate=cost(8),
        name="forward_rows",
    )(place, x, att, wo, small, prev, routes)


def backward_kernel(place, res_ref, dn_ref, cot_ref, valid_ref, att_ref, wo_ref, par_ref, prev_ref, routes_ref,
                    dres_ref, got_ref, gwo_ref, small_ref):
    width = res_ref.shape[1]
    res = res_ref[...]
    gain = par_ref[19:20]
    inverse = lax.rsqrt(jnp.mean(res * res, axis=1, keepdims=True) + epsilon)
    m = res * inverse
    n2 = m * gain
    previous, routes = columns(prev_ref, routes_ref)
    hot, gates, _, alphas, weights = mixing(n2, par_ref[:16], previous, routes)
    g = cot_ref[...].astype(f32) * valid_ref[...]
    inner = jnp.sum(g * n2, axis=1, keepdims=True)
    onto = [jnp.sum(g * par_ref[16 + j : 17 + j], axis=1, keepdims=True) for j in range(2)]
    named = dn_ref[:, width:].astype(f32)
    lane = lax.broadcasted_iota(jnp.int32, hot[0].shape, 1)
    wide = lax.broadcasted_iota(jnp.int32, named.shape, 1).astype(f32)
    local = {
        FFN_EXPERTS + 1: inner,
        FFN_EXPERTS + 2: alphas[0][0] * inner + alphas[0][1] * onto[0],
        FFN_EXPERTS + 3: alphas[1][0] * inner + alphas[1][1] * onto[1],
    }
    dgates = []
    for r in range(2):
        name = routes[:, r : r + 1]
        there = jnp.where((wide == name) | (wide == name + 16), named, 0.0)
        there = jnp.where(name < FFN_EXPERTS, jnp.sum(there, axis=1, keepdims=True), 0.0)
        for e, value in local.items():
            there = there + jnp.where(name == e, value, 0.0)
        dgates.append(there)
    mean = gates[0] * dgates[0] + gates[1] * dgates[1]
    dz = jnp.where(hot[0], gates[0] * (dgates[0] - mean), 0.0)
    dz = dz + jnp.where(hot[1], gates[1] * (dgates[1] - mean), 0.0)
    for j in range(2):
        da = weights[1 + j] * inner
        db = weights[1 + j] * onto[j]
        centre = alphas[j][0] * da + alphas[j][1] * db
        dz = dz + jnp.where(lane == EXPERTS + 2 * j, alphas[j][0] * (da - centre), 0.0)
        dz = dz + jnp.where(lane == EXPERTS + 2 * j + 1, alphas[j][1] * (db - centre), 0.0)
    scale = weights[0] + weights[1] * alphas[0][0] + weights[2] * alphas[1][0]
    highest = lax.Precision.HIGHEST
    dn2 = dn_ref[:, :width].astype(f32) + scale * g + mm(dz, par_ref[:16], NN, highest)
    small_ref[0:16] = mm(dz, n2, TN, highest)
    small_ref[16:24] = jnp.zeros((8, width), f32)
    small_ref[16:17] = jnp.sum((weights[1] * alphas[0][1]) * g, axis=0, keepdims=True)
    small_ref[17:18] = jnp.sum((weights[2] * alphas[1][1]) * g, axis=0, keepdims=True)
    small_ref[18:19] = jnp.sum(dn2 * m, axis=0, keepdims=True)
    q = dn2 * gain
    dres = g + inverse * (q - m * jnp.mean(q * m, axis=1, keepdims=True))
    dres_ref[...] = dres
    da = dres.astype(bf16)
    wo = wo_ref[...].reshape(-1, width)
    got = mm(wo, da, NT).astype(bf16)
    got_ref[...] = got.reshape(got_ref.shape)
    att = att_ref[...].reshape(got.shape)
    gwo_ref[...] = mm(att, da).astype(bf16).reshape(gwo_ref.shape)


def backward_rows(place, res, dn, cot, valid, att, wo, small, prev, routes):
    rows, width = res.shape
    own = lambda i, p: (0, p[0])
    return pl.pallas_call(
        backward_kernel,
        grid_spec=pltpu.PrefetchScalarGridSpec(
            num_scalar_prefetch=1,
            grid=(1,),
            in_specs=[
                full(res.shape),
                full(dn.shape),
                full(cot.shape),
                full(valid.shape),
                full(att.shape),
                full(wo.shape),
                full(small.shape),
                pl.BlockSpec((prev.shape[0], rows), own),
                pl.BlockSpec((2, rows), own),
            ],
            out_specs=[full((rows, width)), full(att.shape), full(wo.shape), full((24, width))],
        ),
        out_shape=[
            jax.ShapeDtypeStruct((rows, width), f32),
            jax.ShapeDtypeStruct(att.shape, bf16),
            jax.ShapeDtypeStruct(wo.shape, bf16),
            jax.ShapeDtypeStruct((24, width), f32),
        ],
        compiler_params=params(),
        cost_estimate=cost(15),
        name="backward_rows",
    )(place, res, dn, cot, valid, att, wo, small, prev, routes)


def finish_kernel(x_ref, dn_ref, dres_ref, small_ref, base_ref, feed_ref, valid_ref, gw_ref, gs_ref, top_ref, wq_ref, wk_ref, limit_ref, other_ref, *refs):
    local = other_ref.shape[0]
    own, outs = refs[:local], refs[local:]
    gin_ref, out_ref, gate_ref, up_ref, down_ref = outs[:5]
    x = x_ref[...].astype(f32)
    inverse = lax.rsqrt(jnp.mean(x * x, axis=1, keepdims=True) + epsilon)
    m = x * inverse
    q = dn_ref[...] * small_ref[18:19]
    gin_ref[...] = dres_ref[...] + inverse * (q - m * jnp.mean(q * m, axis=1, keepdims=True))
    out_ref[...] = (valid_ref[...] * (base_ref[...] + feed_ref[...])).astype(bf16)
    core = lax.axis_index("ctx")
    for k, target in enumerate((gate_ref, up_ref, down_ref)):
        for j in range(local):
            mine, theirs = own[j][k].astype(f32), other_ref[j, k].astype(f32)
            target[j] = jnp.where(core == 0, mine, theirs)
            target[local + j] = jnp.where(core == 0, theirs, mine)

    @pl.when(pl.program_id(0) == 0)
    def _():
        gq, gk, gv, go, gnorm, gmoe, grouter, gconst, gvec, fac_ref, cq_ref, ck_ref = outs[5:]
        width = wq_ref.shape[1]
        flat = gw_ref[...].reshape(4 * width, gw_ref.shape[2])
        for k, target in enumerate((gq, gk, gv)):
            target[...] = flat[k * width : (k + 1) * width].T
        go[...] = flat[3 * width :]
        sums = gs_ref[...]
        grouter[...] = sums[:EXPERTS]
        gconst[...] = sums[EXPERTS : EXPERTS + 4]
        gvec[...] = sums[16:18]
        gmoe[...] = sums[18:19]
        gnorm[...] = sums[19:20]
        factors = limit_ref[0] / jnp.maximum(top_ref[...], limit_ref[0])
        fac_ref[...] = factors
        lane = lax.broadcasted_iota(jnp.int32, (1, width), 1)
        root = jnp.zeros((1, width), f32)
        for h in range(width // HEAD_DIM):
            root = jnp.where(lane // HEAD_DIM == h, jnp.sqrt(factors[h : h + 1, :1]), root)
        cq_ref[...] = (wq_ref[...].astype(f32) * root).astype(bf16)
        ck_ref[...] = (wk_ref[...].astype(f32) * root).astype(bf16)


def finish_rows(x, dn, dres, small, base, feed, valid, gw, gs, top, wq, wk, limit, other, own):
    rows, width = x.shape
    local, kinds, depth, hidden = other.shape
    steps = 4 if depth % 64 == 0 else 1
    tile, deep = rows // steps, depth // steps
    by_row = pl.BlockSpec((tile, width), lambda i: (i, 0))
    expert_out = pl.BlockSpec((2 * local, deep, hidden), lambda i: (0, i, 0))
    once = [
        jax.ShapeDtypeStruct(shape, f32)
        for shape in [wq.shape] * 3
        + [(wq.shape[1], depth), (1, depth), (1, depth), (EXPERTS, depth), (4, depth), (2, depth), (8, 128)]
    ] + [jax.ShapeDtypeStruct(wq.shape, bf16)] * 2
    return pl.pallas_call(
        finish_kernel,
        grid=(steps,),
        in_specs=[
            by_row,
            by_row,
            by_row,
            full(small.shape),
            by_row,
            by_row,
            pl.BlockSpec((tile, 1), lambda i: (i, 0)),
            full(gw.shape),
            full(gs.shape),
            full(top.shape),
            full(wq.shape),
            full(wk.shape),
            pl.BlockSpec(memory_space=pltpu.SMEM),
            pl.BlockSpec((local, kinds, deep, hidden), lambda i: (0, 0, i, 0)),
        ]
        + [pl.BlockSpec((kinds, deep, hidden), lambda i: (0, i, 0))] * local,
        out_specs=[by_row, by_row, expert_out, expert_out, expert_out] + [full(v.shape) for v in once],
        out_shape=[
            jax.ShapeDtypeStruct((rows, width), f32),
            jax.ShapeDtypeStruct((rows, width), bf16),
        ]
        + [jax.ShapeDtypeStruct((2 * local, depth, hidden), f32)] * 3
        + once,
        compiler_params=params(),
        cost_estimate=cost(8),
        name="finish_rows",
    )(x, dn, dres, small, base, feed, valid, gw, gs, top, wq, wk, limit, other, *own)


def expert_kernel(j, first, x_ref, g_ref, gate_ref, w_ref, feed_ref, back_ref, gw_ref, total):
    i = pl.program_id(0)
    parts, _, _, depth, hidden = w_ref.shape
    width = parts * depth
    wg, wu, wd = [w_ref[:, 0, k].reshape(width, hidden) for k in range(3)]
    x, g, gate = x_ref[0], g_ref[0], gate_ref[0]
    gate_pre = mm(x, wg)
    up = mm(x, wu)
    sigmoid = 1.0 / (1.0 + jnp.exp(-gate_pre))
    activated = gate_pre * sigmoid
    inner = (activated * up).astype(bf16)
    out = mm(inner, wd, NT)
    g32 = g.astype(f32)
    feed_ref[...] = (gate * out).astype(bf16)
    dgate = jnp.sum(g32 * out, axis=1, keepdims=True)
    dout = (gate * g32).astype(bf16)
    dinner = mm(dout, wd)
    dpre = (dinner * up * sigmoid * (1.0 + gate_pre * (1.0 - sigmoid))).astype(bf16)
    dup = (dinner * activated).astype(bf16)
    back_ref[:, :width] = (mm(dpre, wg, NT) + mm(dup, wu, NT)).astype(bf16)
    lane = lax.broadcasted_iota(jnp.int32, (dgate.shape[0], back_ref.shape[1] - width), 1)
    coarse = dgate.astype(bf16).astype(f32)
    at = first[0] + j
    extra = jnp.where(lane == at, coarse, jnp.where(lane == at + 16, dgate - coarse, 0.0))
    back_ref[:, width:] = extra.astype(bf16)

    @pl.when(i == 0)
    def _():
        total[...] = jnp.zeros_like(total)

    total[0] += mm(x, dpre, TN)
    total[1] += mm(x, dup, TN)
    total[2] += mm(dout, inner, TN)

    @pl.when(i == pl.num_programs(0) - 1)
    def _():
        for k in range(3):
            gw_ref[:, k] = total[k].reshape(parts, depth, hidden).astype(bf16)


def expert(j, first, x, g, gate, w):
    slots, width = x.shape[1:]
    parts, _, kinds, depth, hidden = w.shape
    grads = (parts, kinds, depth, hidden)
    pick = lambda i, f: (j, i, 0)
    return pl.pallas_call(
        functools.partial(expert_kernel, j),
        grid_spec=pltpu.PrefetchScalarGridSpec(
            num_scalar_prefetch=1,
            grid=(slots // CAP,),
            in_specs=[
                pl.BlockSpec((1, CAP, width), pick),
                pl.BlockSpec((1, CAP, width), pick),
                pl.BlockSpec((1, CAP, 1), pick),
                pl.BlockSpec((parts, 1, kinds, depth, hidden), lambda i, f: (0, j, 0, 0, 0)),
            ],
            out_specs=[
                pl.BlockSpec((CAP, width), lambda i, f: (i, 0)),
                pl.BlockSpec((CAP, width + EXTRA), lambda i, f: (i, 0)),
                full(grads),
            ],
            scratch_shapes=[pltpu.VMEM((3, width, hidden), f32)],
        ),
        out_shape=[
            jax.ShapeDtypeStruct((slots, width), bf16),
            jax.ShapeDtypeStruct((slots, width + EXTRA), bf16),
            jax.ShapeDtypeStruct(grads, bf16),
        ],
        compiler_params=params(),
        cost_estimate=cost(14),
        name="expert",
    )(first, x, g, gate, w)


def shards(
    hidden_in,
    cotangent,
    lengths,
    routes,
    prev_logits,
    norm_attn,
    w_query,
    w_key,
    w_value,
    w_out,
    norm_moe,
    w_router,
    w_const,
    const_vec,
    w_gate,
    w_up,
    w_down,
    threshold,
):
    plane = ("ctx", "tp")
    core, lane = lax.axis_index("ctx"), lax.axis_index("tp")
    nc, nt, ns = lax.axis_size("ctx"), lax.axis_size("tp"), lax.axis_size("shard")
    own, width = hidden_in.shape
    per = own * nt
    total = per * nc
    depth = w_gate.shape[1]
    heads = w_query.shape[1] // HEAD_DIM
    head_width = heads * HEAD_DIM
    local = FFN_EXPERTS // nc
    count = total // BLOCK // nc
    first_row = core * per + lane * own
    routes, prev = routes.T, prev_logits.T
    length = lengths[0]
    valid = (first_row + jnp.arange(own, dtype=jnp.int32) < length).astype(f32)[:, None]
    place = lane.astype(jnp.int32)[None]
    first = (core * local).astype(jnp.int32)[None]

    pieces = [
        lax.dynamic_slice_in_dim(w, core * local, local, 0) for w in (w_gate, w_up, w_down)
    ]
    expert_w = lax.all_gather(jnp.stack(pieces, axis=1), "shard", axis=0, tiled=False)
    small = jnp.concatenate(
        [
            w_router,
            w_const,
            const_vec.T,
            norm_attn[:, None],
            norm_moe[:, None],
            jnp.zeros((depth, SMALL - EXPERTS - 8), bf16),
        ],
        axis=1,
    )
    rows_all, attention_w, routes_all = opening(
        hidden_in, w_query, w_key, w_value, w_out, small, routes, 0
    )
    rows_all = rows_all.reshape(total, width)
    cosine, sine = rope_tables(total)

    qt, kt, k, v, vt, wt, out_w, small = project(rows_all, attention_w, cosine, sine, heads)
    ot, lse, top, cot_all, out_w = attend(lengths, qt, k, vt, cotangent, out_w, count, 1)
    att = exchange(to_owner_kernel, ot, nt, 2, "to_owner")

    res, base, a2, comb = forward_rows(place, hidden_in, att, out_w, small, prev, routes)

    x_slots, g_slots, gate_slots, row_at = dispatch(a2, comb, routes_all, cot_all, local, 3)
    feeds, backs, grads = [], [], []
    for j in range(local):
        feed, back, grad = expert(j, first, x_slots, g_slots, gate_slots, expert_w)
        feeds.append(feed)
        backs.append(back)
        grads.append(grad)
    back, feed = combine(row_at, feeds, backs, 4)
    grads = [lax.psum_scatter(g, "shard", scatter_dimension=0, tiled=True)[0] for g in grads]

    dres, got, grad_out, gsmall = backward_rows(
        place, res, back, cotangent, valid, att, out_w, small, prev, routes
    )
    got = exchange(to_heads_kernel, got, count, 6, "to_heads")
    dq, dk, dv, grad_out, feed = revisit(qt, k, kt, v, ot, got, lse, grad_out, feed, 7)
    part, grad_w, gsmall = unproject(
        dq, dk, dv, cosine, sine, rows_all, small, wt, grad_out, gsmall, ns
    )
    part, grad_w, gsmall, top, others = closing(part.reshape(8, own, width), grad_w, gsmall, top, grads, 8)
    (grad_input, output, grad_gate, grad_up, grad_down, grad_q, grad_k, grad_v, grad_out, grad_norm_attn, grad_norm_moe,
     grad_router, grad_const, grad_vec, factors, clipped_query, clipped_key) = finish_rows(
        hidden_in, part, dres, small, base, feed, valid, grad_w, gsmall, top, w_query, w_key, threshold, others, grads
    )
    return (
        output,
        grad_input,
        grad_norm_attn[0],
        grad_q,
        grad_k,
        grad_v,
        grad_out,
        grad_norm_moe[0],
        grad_router.T,
        grad_const.T,
        grad_vec,
        grad_gate,
        grad_up,
        grad_down,
        factors[:heads, 0],
        clipped_query,
        clipped_key,
    )


def solution(mesh):
    return jax.shard_map(
        shards,
        mesh=mesh,
        in_specs=(
            P(("shard", "ctx", "tp"), None),
            P(("shard", "ctx", "tp"), None),
            P("shard"),
            P(("shard", "ctx"), None),
            P(("shard", "ctx"), None),
            P("shard"),
            P("shard", "tp"),
            P("shard", "tp"),
            P("shard", "tp"),
            P("tp", "shard"),
            P("shard"),
            P("shard", None),
            P("shard", None),
            P(None, "shard"),
            P(None, "shard", "tp"),
            P(None, "shard", "tp"),
            P(None, "shard", "tp"),
            P(),
        ),
        out_specs=(
            P(("shard", "ctx", "tp"), None),
            P(("shard", "ctx", "tp"), None),
            P("shard"),
            P("shard", "tp"),
            P("shard", "tp"),
            P("shard", "tp"),
            P("tp", "shard"),
            P("shard"),
            P("shard", None),
            P("shard", None),
            P(None, "shard"),
            P(None, "shard", "tp"),
            P(None, "shard", "tp"),
            P(None, "shard", "tp"),
            P("tp"),
            P("shard", "tp"),
            P("shard", "tp"),
        ),
        check_vma=False,
    )
```

```python
import functools

import jax
import jax.numpy as jnp
import numpy as np
from jax import lax
from jax.experimental import pallas as pl
from jax.experimental.pallas import tpu as pltpu
from jax.sharding import PartitionSpec as P

HEAD_DIM = 64
EXPERTS = 12
FFN_EXPERTS = 8
CAP = 512
BLOCK = 512
EXTRA = 128
SMALL = 32
SLOT = 256
MESH = pl.DeviceIdType.MESH

epsilon = 1e-06
rope_base = 10000.0
bf16 = jnp.bfloat16
f32 = jnp.float32

NN = (((1,), (0,)), ((), ()))
NT = (((1,), (1,)), ((), ()))
TN = (((0,), (0,)), ((), ()))


def mm(left, right, dims=NN, precision=None):
    return lax.dot_general(
        left, right, dims, preferred_element_type=f32, precision=precision
    )


def params(mib=56, **more):
    return pltpu.CompilerParams(vmem_limit_bytes=mib * 1024 * 1024, **more)


def cost(us):
    return pl.CostEstimate(flops=int(us * 1e9), bytes_accessed=int(us * 3e6), transcendentals=0)


def full(shape):
    return pl.BlockSpec(shape, lambda *_: (0,) * len(shape))


def rope_tables(total):
    half = HEAD_DIM // 2
    freqs = np.float32(rope_base) ** (np.float32(-2.0) * np.arange(half, dtype=np.float32) / np.float32(HEAD_DIM))
    angles = freqs.astype(np.float32)[:, None] * np.arange(total, dtype=np.float32)[None, :]
    angles = angles.astype(np.float64)
    return jnp.asarray(np.cos(angles), f32), jnp.asarray(np.sin(angles), f32)


def zig(core, i):
    return 4 * (i // 2) + (core if i % 2 == 0 else 3 - core)


def anywhere(count):
    return [pl.BlockSpec(memory_space=pl.ANY)] * count


def spot():
    return lax.axis_index("shard"), lax.axis_index("ctx"), lax.axis_index("tp")


def across(t):
    return t + 1 - 2 * lax.rem(t, 2), lax.rem(t + 2, 4), 3 - t


def remote(source, target, sends, recvs, **where):
    return pltpu.make_async_remote_copy(
        src_ref=source,
        dst_ref=target,
        send_sem=sends,
        recv_sem=recvs,
        device_id=where,
        device_id_type=MESH,
    )


def greet(depth=True):
    z, c, t = spot()
    nc, nt, ns = lax.axis_size("ctx"), lax.axis_size("tp"), lax.axis_size("shard")
    barrier = pltpu.get_barrier_semaphore()
    for step in range(1, nc * nt):
        other = lax.rem(c * nt + t + step, nc * nt)
        pl.semaphore_signal(
            barrier,
            inc=1,
            device_id={"ctx": other // nt, "tp": lax.rem(other, nt)},
            device_id_type=MESH,
        )
    if depth:
        for step in range(1, ns):
            pl.semaphore_signal(
                barrier,
                inc=1,
                device_id={"shard": lax.rem(z + step, ns)},
                device_id_type=MESH,
            )
    pl.semaphore_wait(barrier, nc * nt - 1 + (ns - 1 if depth else 0))


class Gather:
    KINDS = 9

    def __init__(self, x, out, sends, recvs, own, cuts, stage=None):
        z, c, t = spot()
        tx, ty, td = across(t)
        rows = x.shape[0] // cuts
        half = rows // 2
        self.cuts = cuts
        self.load = None if stage is None else pltpu.make_async_copy(x, stage, own.at[0])
        self.own = pltpu.make_async_copy(x if stage is None else stage, out.at[4 * c + t], own.at[1])
        sib = {"ctx": 1 - c}
        px, py = {"tp": tx}, {"tp": ty}

        def copies(s):
            whole = pl.ds(s * rows, rows)
            one, two = pl.ds(s * rows, half), pl.ds(s * rows + half, half)

            def at(k, source, target, where):
                return remote(source, target, sends.at[s, k], recvs.at[s, k], **where)

            def keep(k, slot, part, where):
                ref = out.at[4 * c + slot, part]
                return at(k, ref, ref, where)

            mine = [
                at(k, x.at[whole], out.at[4 * c + t, whole], where)
                for k, where in enumerate((px, py, sib))
            ]
            return mine + [
                keep(3, tx, whole, sib),
                keep(4, tx, one, py),
                keep(5, ty, whole, sib),
                keep(6, ty, two, px),
                keep(7, td, one, sib),
                keep(8, td, two, sib),
            ]

        self.copies = [copies(s) for s in range(cuts)]

        def arrivals(s):
            whole = pl.ds(s * rows, rows)
            one, two = pl.ds(s * rows, half), pl.ds(s * rows + half, half)
            where = [(c, tx, whole), (c, ty, whole), (1 - c, t, whole)]
            where += [(1 - c, tx, whole), (c, td, one), (1 - c, ty, whole), (c, td, two)]
            where += [(1 - c, td, one), (1 - c, td, two)]
            return [
                remote(out.at[4 * d + slot, part], out.at[4 * d + slot, part], sends.at[s, k], recvs.at[s, k], **sib)
                for k, (d, slot, part) in enumerate(where)
            ]

        self.arrivals = [arrivals(s) for s in range(cuts)]

    @staticmethod
    def scratch(cuts):
        return [
            pltpu.SemaphoreType.DMA((cuts, Gather.KINDS)),
            pltpu.SemaphoreType.DMA((cuts, Gather.KINDS)),
            pltpu.SemaphoreType.DMA((2,)),
        ]

    def first(self):
        for s in range(self.cuts):
            for k in (0, 1, 2):
                self.copies[s][k].start()
        (self.load or self.own).start()

    def second(self, s):
        if self.load is not None and s == 0:
            self.load.wait()
            self.own.start()
        self.arrivals[s][0].wait_recv()
        self.copies[s][4].start()
        self.copies[s][3].start()
        self.arrivals[s][1].wait_recv()
        self.copies[s][6].start()
        self.copies[s][5].start()

    def third(self, s):
        for k in (4, 6):
            self.arrivals[s][k].wait_recv()
            self.copies[s][7 if k == 4 else 8].start()

    def last(self):
        for s in range(self.cuts):
            for k in (2, 3, 5, 7, 8):
                self.arrivals[s][k].wait_recv()
        for s in range(self.cuts):
            for k in range(self.KINDS):
                self.copies[s][k].wait_send()
        self.own.wait()


class Sum:
    def __init__(self, p, held, came, across_in, across_out, sends, recvs, loads, stage=None):
        z, c, t = spot()
        self.t = t
        tx, ty, td = across(t)
        half = held.shape[1] // 2
        self.half = half
        self.one, self.two = pl.ds(0, half), pl.ds(half, half)
        self.order = (td, tx, ty, t)
        self.held, self.came, self.inn = held, came, across_in
        sib, px, py = {"ctx": 1 - c}, {"tp": tx}, {"tp": ty}
        self.core = []
        for k, o in enumerate(self.order):
            source = p.at[4 * (1 - c) + o] if stage is None else stage.at[k]
            self.core.append(remote(source, came.at[o], sends.at[k], recvs.at[k], **sib))
        self.loads = None
        if stage is None:
            self.loads = [pltpu.make_async_copy(p.at[4 * c + o], held.at[o], loads.at[k]) for k, o in enumerate(self.order)]

        def send(k, source, slot, where):
            return remote(source, across_in.at[slot], sends.at[k], recvs.at[k], **where)

        self.side = {
            "dx": send(4, held.at[td, self.one], 0, px),
            "dy": send(5, held.at[td, self.two], 1, py),
            "x": send(6, held.at[tx, self.one], 2, px),
            "y": send(7, held.at[ty, self.two], 3, py),
            "cy": send(8, across_out.at[0], 4, py),
            "cx": send(9, across_out.at[1], 5, px),
        }
        self.out = across_out
        self.near = (tx, ty, td)

    @staticmethod
    def scratch(rows, width):
        return [
            pltpu.VMEM((4, rows, width), bf16),
            pltpu.VMEM((4, rows, width), bf16),
            pltpu.VMEM((6, rows // 2, width), bf16),
            pltpu.VMEM((2, rows // 2, width), bf16),
            pltpu.SemaphoreType.DMA((10,)),
            pltpu.SemaphoreType.DMA((10,)),
            pltpu.SemaphoreType.DMA((4,)),
        ]

    def first(self):
        for k in range(4):
            self.core[k].start()
            self.loads[k].start()

    def second(self, tile=None):
        for k, o in enumerate(self.order):
            if tile is None:
                self.loads[k].wait()
                mine = self.held[o]
            else:
                mine = tile(o)
            self.core[k].wait_recv()
            self.held[o] = (mine + self.came[o].astype(mine.dtype)).astype(bf16)
            if k == 0:
                self.side["dx"].start()
                self.side["dy"].start()
            if k == 1:
                self.side["x"].start()
            if k == 2:
                self.side["y"].start()

    def third(self):
        tx, ty, td = self.near
        self.side["dx"].wait_recv()
        self.out[0] = self.held[ty, self.one] + self.inn[0]
        self.side["cy"].start()
        self.side["dy"].wait_recv()
        self.out[1] = self.held[tx, self.two] + self.inn[1]
        self.side["cx"].start()

    def last(self):
        for k in ("x", "y", "cy", "cx"):
            self.side[k].wait_recv()
        for copy in self.core + list(self.side.values()):
            copy.wait_send()

    def total(self):
        def add(part, a, b):
            return self.held[self.t, part].astype(f32) + self.inn[a].astype(f32) + self.inn[b].astype(f32)

        return add(self.one, 2, 4), add(self.two, 3, 5)


def qkv_kernel(x_ref, w_ref, cos_ref, sin_ref, qt_ref, kt_ref, k_ref, v_ref, vt_ref, wt_ref, wo_ref, small_ref):
    heads = qt_ref.shape[0]
    width = heads * HEAD_DIM
    half = HEAD_DIM // 2

    @pl.when(pl.program_id(0) == 0)
    def _():
        def whole(core, which, here):
            v = w_ref[core, :, which].astype(f32)
            return v.reshape(v.shape[0] * v.shape[1], SLOT)[:, here].T

        mine = slice(0, width)
        wt_ref[:width] = whole(0, 0, mine).astype(bf16)
        wt_ref[width : 2 * width] = whole(0, 1, mine).astype(bf16)
        wt_ref[2 * width :] = whole(1, 0, mine).astype(bf16)
        wo_ref[...] = whole(1, 1, mine).astype(bf16)
        small_ref[...] = whole(0, 0, slice(width, width + SMALL))

    x = x_ref[...].astype(f32)
    inverse = lax.rsqrt(jnp.mean(x * x, axis=1, keepdims=True) + epsilon)
    a = (x * inverse * small_ref[18:19]).astype(bf16)
    y = mm(wt_ref[...], a, NT)
    c, s = cos_ref[...], sin_ref[...]

    def turned(first):
        u, w = y[first : first + half], y[first + half : first + HEAD_DIM]
        return jnp.concatenate([u * c - w * s, w * c + u * s], axis=0)

    for h in range(heads):
        at = h * HEAD_DIM
        qt_ref[h] = (turned(at) * HEAD_DIM**-0.5).astype(bf16)
        key = turned(width + at)
        kt_ref[h] = key.astype(bf16)
        k_ref[h] = key.T.astype(bf16)
        value = y[2 * width + at : 2 * width + at + HEAD_DIM]
        v_ref[h] = value.T.astype(bf16)
        vt_ref[h, :HEAD_DIM] = value.astype(bf16)
        vt_ref[h, HEAD_DIM:] = jnp.ones((16, value.shape[1]), bf16)


def project(rows, w, cosine, sine, heads):
    total, width = rows.shape
    tile = BLOCK
    out = heads * HEAD_DIM
    shapes = [
        jax.ShapeDtypeStruct((heads, HEAD_DIM, total), bf16),
        jax.ShapeDtypeStruct((heads, HEAD_DIM, total), bf16),
        jax.ShapeDtypeStruct((heads, total, HEAD_DIM), bf16),
        jax.ShapeDtypeStruct((heads, total, HEAD_DIM), bf16),
        jax.ShapeDtypeStruct((heads, HEAD_DIM + 16, total), bf16),
        jax.ShapeDtypeStruct((3 * out, width), bf16),
        jax.ShapeDtypeStruct((out, width), bf16),
        jax.ShapeDtypeStruct((SMALL, width), f32),
    ]
    return pl.pallas_call(
        qkv_kernel,
        grid=(total // tile,),
        in_specs=[
            pl.BlockSpec((tile, width), lambda i: (i, 0)),
            full(w.shape),
            pl.BlockSpec((HEAD_DIM // 2, tile), lambda i: (0, i)),
            pl.BlockSpec((HEAD_DIM // 2, tile), lambda i: (0, i)),
        ],
        out_specs=[
            pl.BlockSpec((heads, HEAD_DIM, tile), lambda i: (0, 0, i)),
            pl.BlockSpec((heads, HEAD_DIM, tile), lambda i: (0, 0, i)),
            pl.BlockSpec((heads, tile, HEAD_DIM), lambda i: (0, i, 0)),
            pl.BlockSpec((heads, tile, HEAD_DIM), lambda i: (0, i, 0)),
            pl.BlockSpec((heads, HEAD_DIM + 16, tile), lambda i: (0, 0, i)),
        ]
        + [full(v.shape) for v in shapes[5:]],
        out_shape=shapes,
        compiler_params=params(),
        cost_estimate=cost(13),
        name="project",
    )(rows, w, cosine, sine)


def dealt(core, i):
    return 4 * (i // 2) + jnp.where(lax.rem(i, 2) == 0, core, 3 - core)


def attend_kernel(cuts, length, qt_ref, k_ref, vt_ref, cot_ref, w_ref, ot_ref, lse_ref, top_ref, cots_ref, ws_ref, mask_cot, w_send, w_recv, w_own, *sems):
    z, c, t = spot()
    nt = lax.axis_size("tp")
    h, i = pl.program_id(0), pl.program_id(1)
    count = pl.num_programs(1)
    at_step = h * count + i
    last = pl.num_programs(0) * count - 1
    gather = Gather(mask_cot, cots_ref, *sems, cuts)
    half = w_ref.shape[0] // 2
    mine = pl.ds(c * half, half)
    theirs = pl.ds((1 - c) * half, half)
    away, came = [], []
    for step in range(1, nt):
        there, back = lax.rem(t + step, nt), lax.rem(t + nt - step, nt)
        away.append(remote(w_ref.at[mine], ws_ref.at[t, mine], w_send.at[step], w_recv.at[step], tp=there))
        ref = ws_ref.at[back, mine]
        came.append(remote(ref, ref, w_send.at[nt + step], w_recv.at[step], ctx=1 - c))
        ref = ws_ref.at[back, theirs]
        came.append(remote(ref, ref, w_send.at[nt + step], w_recv.at[nt + step], ctx=1 - c))
    onward = [
        remote(ws_ref.at[lax.rem(t + nt - step, nt), mine], ws_ref.at[lax.rem(t + nt - step, nt), mine],
               w_send.at[nt + step], w_recv.at[nt + step], ctx=1 - c)
        for step in range(1, nt)
    ]
    own_w = pltpu.make_async_copy(w_ref, ws_ref.at[t], w_own)

    @pl.when(at_step == 0)
    def _():
        rows = cot_ref.shape[0]
        position = (c * nt + t) * rows + lax.broadcasted_iota(jnp.int32, cot_ref.shape, 0)
        mask_cot[...] = jnp.where(position < length[0], cot_ref[...].astype(f32), 0.0).astype(bf16)
        greet(False)
        gather.first()
        for copy in away:
            copy.start()
        own_w.start()

    index = dealt(c, i)
    columns = BLOCK
    qt = qt_ref[0, :, pl.ds(pl.multiple_of(index * BLOCK, BLOCK), BLOCK)]

    def step(at, carry, diagonal):
        peak, total = carry
        start = pl.multiple_of(at * BLOCK, BLOCK)
        scores = mm(k_ref[0, pl.ds(start, BLOCK), :], qt)
        if diagonal:
            keys = lax.broadcasted_iota(jnp.int32, scores.shape, 0)
            queries = lax.broadcasted_iota(jnp.int32, scores.shape, 1)
            scores = jnp.where(keys <= queries, scores, -1e30)
        higher = jnp.maximum(peak, jnp.max(scores, axis=0, keepdims=True))
        weights = jnp.exp(scores - higher).astype(bf16)
        total = total * jnp.exp(peak - higher) + mm(vt_ref[0, :, pl.ds(start, BLOCK)], weights)
        return higher, total

    start = (jnp.full((1, columns), -1e30, f32), jnp.zeros((HEAD_DIM + 16, columns), f32))
    carry = lax.fori_loop(0, index, lambda at, c: step(at, c, False), start)
    peak, total = step(index, carry, True)
    mass = total[HEAD_DIM : HEAD_DIM + 1]
    ot_ref[0] = (total[:HEAD_DIM] / mass).astype(bf16)
    lse_ref[0, 0] = peak + jnp.log(mass)
    position = index * BLOCK + lax.broadcasted_iota(jnp.int32, peak.shape, 1)
    top_ref[0, 0] = jnp.where(position < length[0], peak, -1e30)

    @pl.when(at_step == last - 3)
    def _():
        for s in range(cuts):
            gather.second(s)
        for copy, forth in zip(came[0::2], onward):
            copy.wait_recv()
            forth.start()

    @pl.when(at_step == last)
    def _():
        for s in range(cuts):
            gather.third(s)
        gather.last()
        for copy in came[1::2]:
            copy.wait_recv()
        for copy in away + onward:
            copy.wait_send()
        own_w.wait()


def attend(length, qt, k, vt, cot, w, count, number):
    cuts = 1
    heads, _, total = qt.shape
    nt = lax.axis_size("tp")
    return pl.pallas_call(
        functools.partial(attend_kernel, cuts),
        grid_spec=pltpu.PrefetchScalarGridSpec(
            num_scalar_prefetch=1,
            grid=(heads, count),
            in_specs=[
                pl.BlockSpec((1, HEAD_DIM, total), lambda h, i, n: (h, 0, 0)),
                pl.BlockSpec((1, total, HEAD_DIM), lambda h, i, n: (h, 0, 0)),
                pl.BlockSpec((1, HEAD_DIM + 16, total), lambda h, i, n: (h, 0, 0)),
                full(cot.shape),
                full(w.shape),
            ],
            out_specs=[
                pl.BlockSpec((1, HEAD_DIM, BLOCK), lambda h, i, n: (i, h, 0)),
                pl.BlockSpec((1, 1, 1, BLOCK), lambda h, i, n: (h, i, 0, 0)),
                pl.BlockSpec((1, 1, 1, BLOCK), lambda h, i, n: (h, i, 0, 0)),
            ]
            + anywhere(2),
            scratch_shapes=[
                pltpu.VMEM(cot.shape, bf16),
                pltpu.SemaphoreType.DMA((2 * nt,)),
                pltpu.SemaphoreType.DMA((2 * nt,)),
                pltpu.SemaphoreType.DMA,
            ]
            + Gather.scratch(cuts),
        ),
        out_shape=[
            jax.ShapeDtypeStruct((count, heads * HEAD_DIM, BLOCK), bf16),
            jax.ShapeDtypeStruct((heads, count, 1, BLOCK), f32),
            jax.ShapeDtypeStruct((heads, count, 1, BLOCK), f32),
            jax.ShapeDtypeStruct((8,) + cot.shape, bf16),
            jax.ShapeDtypeStruct((nt,) + w.shape, bf16),
        ],
        compiler_params=params(collective_id=number, has_side_effects=True),
        cost_estimate=cost(35),
        name="attend",
    )(length, qt, k, vt, cot, w)


def revisit_kernel(qt_ref, k_ref, kt_ref, v_ref, ot_ref, got_ref, lse_ref, go_ref, feed_ref, dq_ref, dk_ref, dv_ref, gos_ref, fed_ref, sum_k, sum_v, came_ref, w_send, w_recv, *scratch):
    z, c, t = spot()
    job = Sum(feed_ref, *scratch)
    nt = lax.axis_size("tp")
    h, i = pl.program_id(0), pl.program_id(1)
    count = pl.num_programs(1)
    index = dealt(c, i)
    here = pl.ds(pl.multiple_of(index * BLOCK, BLOCK), BLOCK)
    away = [
        remote(go_ref.at[lax.rem(t + step, nt)], came_ref.at[step], w_send.at[step], w_recv.at[step], tp=lax.rem(t + step, nt))
        for step in range(1, nt)
    ]

    at_step = h * count + i
    end = pl.num_programs(0) * count - 1

    @pl.when(at_step == 0)
    def _():
        greet(False)
        job.first()
        for copy in away:
            copy.start()

    @pl.when(at_step == 3)
    def _():
        job.second()

    @pl.when(at_step == end - 3)
    def _():
        job.third()

    qt, got = qt_ref[0, :, here], got_ref[0]
    lse = lse_ref[0, 0]
    centre = jnp.sum(ot_ref[0].astype(f32) * got.astype(f32), axis=0, keepdims=True)

    @pl.when(i == 0)
    def _():
        sum_k[...] = jnp.zeros_like(sum_k)
        sum_v[...] = jnp.zeros_like(sum_v)
        dq_ref[...] = jnp.zeros_like(dq_ref)

    def step(at, grad, diagonal):
        start = pl.multiple_of(at * BLOCK, BLOCK)
        here = pl.ds(start, BLOCK)
        scores = mm(k_ref[0, here, :], qt)
        probs = jnp.exp(scores - lse)
        if diagonal:
            keys = lax.broadcasted_iota(jnp.int32, scores.shape, 0)
            queries = lax.broadcasted_iota(jnp.int32, scores.shape, 1)
            probs = jnp.where(keys <= queries, probs, 0.0)
        grad_probs = mm(v_ref[0, here, :], got)
        grad_scores = (probs * (grad_probs - centre)).astype(bf16)
        sum_v[:, here] += mm(got, probs.astype(bf16), NT)
        sum_k[:, here] += mm(qt, grad_scores, NT)
        return grad + mm(kt_ref[0, :, here], grad_scores)

    grad = lax.fori_loop(0, index, lambda at, c: step(at, c, False), jnp.zeros(qt.shape, f32))
    dq_ref[0, :, here] = step(index, grad, True) * HEAD_DIM**-0.5

    @pl.when(i == count - 1)
    def _():
        dk_ref[0] = sum_k[...]
        dv_ref[0] = sum_v[...]

    @pl.when(at_step == end)
    def _():
        job.last()
        one, two = job.total()
        fed_ref[: job.half] = one
        fed_ref[job.half :] = two
        total = go_ref[t].astype(f32)
        for step, copy in enumerate(away):
            copy.wait_recv()
            total = total + came_ref[step + 1].astype(f32)
            copy.wait_send()
        gos_ref[...] = total.astype(bf16)


def revisit(qt, k, kt, v, ot, got, lse, go, feed, number):
    heads, _, total = qt.shape
    count = ot.shape[0]
    nt = lax.axis_size("tp")
    whole = pl.BlockSpec((1, HEAD_DIM, total), lambda h, i: (h, 0, 0))
    tall = pl.BlockSpec((1, total, HEAD_DIM), lambda h, i: (h, 0, 0))
    some = pl.BlockSpec((1, HEAD_DIM, BLOCK), lambda h, i: (i, h, 0))
    return pl.pallas_call(
        revisit_kernel,
        grid=(heads, count),
        in_specs=[
            whole,
            tall,
            whole,
            tall,
            some,
            some,
            pl.BlockSpec((1, 1, 1, BLOCK), lambda h, i: (h, i, 0, 0)),
            full(go.shape),
        ]
        + anywhere(1),
        out_specs=[whole, whole, whole, full(go.shape[1:]), full(feed.shape[1:])],
        scratch_shapes=[
            pltpu.VMEM((HEAD_DIM, total), f32),
            pltpu.VMEM((HEAD_DIM, total), f32),
            pltpu.VMEM(go.shape, bf16),
            pltpu.SemaphoreType.DMA((nt,)),
            pltpu.SemaphoreType.DMA((nt,)),
        ]
        + Sum.scratch(*feed.shape[1:]),
        out_shape=[jax.ShapeDtypeStruct((heads, HEAD_DIM, total), f32)] * 3
        + [jax.ShapeDtypeStruct(go.shape[1:], bf16), jax.ShapeDtypeStruct(feed.shape[1:], f32)],
        compiler_params=params(collective_id=number, has_side_effects=True),
        cost_estimate=cost(50),
        name="revisit",
    )(qt, k, kt, v, ot, got, lse, go, feed)


def opening_kernel(cuts, x_ref, wq_ref, wk_ref, wv_ref, wo_ref, small_ref, routes_ref, out_ref, ws_ref, all_routes_ref, held, stage, *sems):
    gather = Gather(x_ref, out_ref, *sems[:3], cuts, stage)
    sends, recvs, local = sems[3:]
    z, c, t = spot()
    ns = lax.axis_size("shard")
    width = wq_ref.shape[1]
    held[0, :, :width] = jnp.where(c == 0, wq_ref[...].astype(f32), wv_ref[...].astype(f32)).astype(bf16)
    held[0, :, width : width + SMALL] = small_ref[...]
    held[0, :, width + SMALL :] = jnp.zeros((held.shape[1], SLOT - width - SMALL), bf16)
    held[1, :, :width] = jnp.where(c == 0, wk_ref[...].astype(f32), wo_ref[...].astype(f32).T).astype(bf16)
    held[1, :, width:] = jnp.zeros((held.shape[1], SLOT - width), bf16)
    greet()
    started = []

    def go(k, source, target, **where):
        copy = remote(source, target, sends.at[k], recvs.at[k], **where)
        copy.start()
        started.append(copy)

    def came(k, ref):
        remote(ref, ref, sends.at[k], recvs.at[k], ctx=1 - c).wait_recv()

    for step in range(1, ns):
        go(step, held, ws_ref.at[c, z], shard=lax.rem(z + step, ns))
    go(0, held, ws_ref.at[c, z], ctx=1 - c)
    gather.first()
    go(2 * ns, routes_ref, all_routes_ref.at[c], ctx=1 - c)
    mine = [
        pltpu.make_async_copy(held, ws_ref.at[c, z], local.at[0]),
        pltpu.make_async_copy(routes_ref, all_routes_ref.at[c], local.at[1]),
    ]
    for copy in mine:
        copy.start()
    for s in range(cuts):
        gather.second(s)
    for step in range(1, ns):
        back = lax.rem(z + ns - step, ns)
        came(step, ws_ref.at[c, back])
        go(ns + step, ws_ref.at[c, back], ws_ref.at[c, back], ctx=1 - c)
    for s in range(cuts):
        gather.third(s)
    gather.last()
    came(0, ws_ref.at[1 - c, z])
    came(2 * ns, all_routes_ref.at[1 - c])
    for step in range(1, ns):
        came(ns + step, ws_ref.at[1 - c, lax.rem(z + ns - step, ns)])
    for copy in started:
        copy.wait_send()
    for copy in mine:
        copy.wait()


def opening(x, wq, wk, wv, wo, small, routes, number):
    cuts = 2
    ns = lax.axis_size("shard")
    depth = wq.shape[0]
    vmem = pl.BlockSpec(memory_space=pltpu.VMEM)
    return pl.pallas_call(
        functools.partial(opening_kernel, cuts),
        in_specs=anywhere(1) + [vmem] * 6,
        out_specs=anywhere(3),
        out_shape=[
            jax.ShapeDtypeStruct((8,) + x.shape, x.dtype),
            jax.ShapeDtypeStruct((2, ns, 2, depth, SLOT), bf16),
            jax.ShapeDtypeStruct((2,) + routes.shape, routes.dtype),
        ],
        scratch_shapes=[pltpu.VMEM((2, depth, SLOT), bf16), pltpu.VMEM(x.shape, x.dtype)]
        + Gather.scratch(cuts)
        + [
            pltpu.SemaphoreType.DMA((2 * ns + 1,)),
            pltpu.SemaphoreType.DMA((2 * ns + 1,)),
            pltpu.SemaphoreType.DMA((2,)),
        ],
        compiler_params=params(collective_id=number, has_side_effects=True),
        cost_estimate=cost(30),
        name="opening",
    )(x, wq, wk, wv, wo, small, routes)


def places(routes_ref, row_ref):
    one = lax.broadcasted_iota(jnp.int32, (BLOCK, BLOCK), 0)
    two = lax.broadcasted_iota(jnp.int32, (BLOCK, BLOCK), 1)
    before = (one < two).astype(bf16)
    blocks, _, per = routes_ref.shape
    for b in range(blocks):
        carry = jnp.zeros((16, 1), f32)
        for at in range(0, per, BLOCK):
            here = slice(at, at + BLOCK)
            expert = lax.broadcasted_iota(jnp.int32, (16, BLOCK), 0)
            member = (routes_ref[b, 0:1, here] == expert) | (routes_ref[b, 1:2, here] == expert)
            rank = mm(member.astype(bf16), before) + carry
            row_ref[:, b * per + at : b * per + at + BLOCK] = jnp.where(member, rank, -1.0)
            carry = carry + jnp.sum(member.astype(f32), axis=1, keepdims=True)


def route_kernel(cuts, o_ref, x_ref, wo_ref, small_ref, prev_ref, routes_ref, cots_ref,
                 att, res_out, base_out, x_out, g_out, gate_ref, row_ref,
                 x_in, wo_in, res, base, a, comb, rows, cots, combs, xs, gs,
                 o_send, o_recv, c_send, c_recv, local, out_sem, x_sem, g_sem, *sems):
    gather = Gather(a, rows, *sems, cuts)
    z, c, t = spot()
    nt = lax.axis_size("tp")
    own = 4 * c + t
    blocks, _, per = routes_ref.shape
    width = rows.shape[2]
    experts = xs.shape[0]
    here = pl.ds(pl.multiple_of(t * BLOCK, BLOCK), BLOCK)
    loads = [
        pltpu.make_async_copy(cots_ref, cots, local.at[0]),
        pltpu.make_async_copy(x_ref, x_in, local.at[1]),
        pltpu.make_async_copy(wo_ref, wo_in, local.at[2]),
    ]
    for copy in loads:
        copy.start()
    greet(False)

    copies = []
    for i in range(o_ref.shape[0]):
        block = zig(c, i)
        copy = remote(o_ref.at[i], att.at[t], o_send.at[i], o_recv.at[t], ctx=block // nt, tp=lax.rem(block, nt))
        copies.append((block == own, copy, pltpu.make_async_copy(o_ref.at[i], att.at[t], local.at[3])))
    for mine, copy, inside in copies:

        @pl.when(jnp.logical_not(mine))
        def _():
            copy.start()

        @pl.when(mine)
        def _():
            inside.start()

    def fetch(source, target, out, sem, n, gated):
        b, j = n // experts, lax.rem(n, experts)
        here = pl.ds(pl.multiple_of(b * CAP, CAP), CAP)
        named = row_ref[pl.ds(experts * c + j, 1), pl.ds(pl.multiple_of(b * per, per), per)]
        hot = lax.broadcasted_iota(jnp.int32, (CAP, per), 0).astype(f32) == named
        block = source[pl.ds(4 * b, 4)].reshape(per, width)
        target[j, here] = mm(hot.astype(bf16), block).astype(bf16)
        pltpu.make_async_copy(target.at[j, here], out.at[j, here], sem.at[n]).start()
        if gated:
            gate = jnp.zeros((CAP, 1), f32)
            rows_each = per // 4
            for k in range(4):
                part = hot[:, k * rows_each : (k + 1) * rows_each]
                weight = combs[4 * b + k, pl.ds(experts * c + j, 1)]
                gate = gate + jnp.sum(jnp.where(part, weight, 0.0), axis=1, keepdims=True)
            gate_ref[j, here] = gate

    def fetch_g(first, last):
        @pl.loop(first, last)
        def _(n):
            fetch(cots, gs, g_out, g_sem, n, False)

    places(routes_ref, row_ref)
    for copy in loads:
        copy.wait()
    fetch_g(0, 2)
    for mine, copy, inside in copies:

        @pl.when(jnp.logical_not(mine))
        def _():
            copy.wait_send()

        @pl.when(mine)
        def _():
            inside.wait()

    mine = lax.rem((own + 1) // 2, 2) == c
    for source in range(nt):

        @pl.when(jnp.logical_or(jnp.logical_not(mine), source != t))
        def _():
            remote(o_ref.at[0], att.at[source], o_send.at[0], o_recv.at[source], ctx=c, tp=t).wait_recv()

    attended = att[...].reshape(-1, BLOCK)
    r = x_in[...].astype(f32) + mm(attended, wo_in[...].reshape(-1, width), TN)
    inverse = lax.rsqrt(jnp.mean(r * r, axis=1, keepdims=True) + epsilon)
    n2 = r * inverse * small_ref[19:20]
    a[...] = n2.astype(bf16)
    gather.first()
    res[...] = r
    _, _, combined, alphas, weights = mixing(n2, small_ref[:16], *columns(prev_ref[:, here], routes_ref[c, :, here]))
    comb[...] = combined.T[:16]
    pairs = []
    for step in range(1, 8):
        other, back = lax.rem(own + step, 8), lax.rem(own + 8 - step, 8)
        where = {"ctx": other // 4, "tp": lax.rem(other, 4)}
        copy = remote(comb, combs.at[own], c_send.at[step], c_recv.at[step], **where)
        copy.start()
        pairs.append((copy, remote(comb, combs.at[back], c_send.at[step], c_recv.at[step], **where)))
    combs[own] = comb[...]
    scale = weights[0] + weights[1] * alphas[0][0] + weights[2] * alphas[1][0]
    base[...] = (
        r
        + scale * n2
        + (weights[1] * alphas[0][1]) * small_ref[16:17]
        + (weights[2] * alphas[1][1]) * small_ref[17:18]
    )
    outs = [
        pltpu.make_async_copy(res, res_out, out_sem.at[0]),
        pltpu.make_async_copy(base, base_out, out_sem.at[1]),
    ]
    for copy in outs:
        copy.start()

    total = blocks * experts
    fetch_g(2, 4)
    gather.second(0)
    fetch_g(4, total)
    gather.second(1)
    gather.third(0)
    gather.third(1)
    for copy, came in pairs:
        came.wait_recv()
    gather.last()

    @pl.loop(0, total)
    def _(n):
        fetch(rows, xs, x_out, x_sem, n, True)

    for copy, came in pairs:
        copy.wait_send()
    for copy in outs:
        copy.wait()

    @pl.loop(0, total)
    def _(n):
        b, j = n // experts, lax.rem(n, experts)
        here = pl.ds(pl.multiple_of(b * CAP, CAP), CAP)
        pltpu.make_async_copy(gs.at[j, here], g_out.at[j, here], g_sem.at[n]).wait()
        pltpu.make_async_copy(xs.at[j, here], x_out.at[j, here], x_sem.at[n]).wait()


def route(o, x, wo, small, prev, routes, cots, experts, number):
    cuts = 2
    own, width = x.shape
    nt = lax.axis_size("tp")
    blocks, _, per = routes.shape
    slots = jax.ShapeDtypeStruct((experts, blocks * CAP, width), bf16)
    vmem = pl.BlockSpec(memory_space=pltpu.VMEM)
    return pl.pallas_call(
        functools.partial(route_kernel, cuts),
        in_specs=anywhere(3) + [vmem, vmem, vmem] + anywhere(1),
        out_specs=[vmem] + anywhere(4) + [vmem, vmem],
        out_shape=[
            jax.ShapeDtypeStruct((nt,) + o.shape[1:], bf16),
            jax.ShapeDtypeStruct((own, width), f32),
            jax.ShapeDtypeStruct((own, width), f32),
            slots,
            slots,
            jax.ShapeDtypeStruct((experts, blocks * CAP, 1), f32),
            jax.ShapeDtypeStruct((16, blocks * per), f32),
        ],
        scratch_shapes=[
            pltpu.VMEM((own, width), bf16),
            pltpu.VMEM(wo.shape, bf16),
            pltpu.VMEM((own, width), f32),
            pltpu.VMEM((own, width), f32),
            pltpu.VMEM((own, width), bf16),
            pltpu.VMEM((16, own), f32),
            pltpu.VMEM((8, own, width), bf16),
            pltpu.VMEM((8, own, width), bf16),
            pltpu.VMEM((8, 16, own), f32),
            pltpu.VMEM(slots.shape, bf16),
            pltpu.VMEM(slots.shape, bf16),
            pltpu.SemaphoreType.DMA((o.shape[0],)),
            pltpu.SemaphoreType.DMA((nt,)),
            pltpu.SemaphoreType.DMA((8,)),
            pltpu.SemaphoreType.DMA((8,)),
            pltpu.SemaphoreType.DMA((4,)),
            pltpu.SemaphoreType.DMA((2,)),
            pltpu.SemaphoreType.DMA((blocks * experts,)),
            pltpu.SemaphoreType.DMA((blocks * experts,)),
        ]
        + Gather.scratch(cuts),
        compiler_params=params(collective_id=number, has_side_effects=True),
        cost_estimate=cost(65),
        name="route",
    )(o, x, wo, small, prev, routes, cots)


def combine_kernel(experts, row_ref, *refs):
    groups = 2
    each = experts // groups
    values_in = refs[: 2 * groups]
    out_ref, feed_out = refs[2 * groups : 2 * groups + 2]
    backs, feeds, stage, staged, b_sem, f_sem, o_sem = refs[2 * groups + 2 : 2 * groups + 9]
    job = Sum(None, *refs[2 * groups + 9 :], stage=stage)
    z, c, t = spot()
    loads = []
    for j in range(groups):
        loads.append(pltpu.make_async_copy(values_in[groups + j], backs.at[pl.ds(j * each, each)], b_sem.at[j]))
    for j in range(groups):
        loads.append(pltpu.make_async_copy(values_in[j], feeds.at[pl.ds(j * each, each)], f_sem.at[j]))
    for copy in loads:
        copy.start()
    greet(False)

    def tile(values, owner):
        start = pl.multiple_of(owner * BLOCK, BLOCK)
        place = row_ref[:, pl.ds(start, BLOCK)].T
        lane = lax.broadcasted_iota(jnp.int32, place.shape, 1)
        slot = lax.broadcasted_iota(jnp.int32, (BLOCK, CAP), 1).astype(f32)
        here = pl.ds(pl.multiple_of(owner // 4 * CAP, CAP), CAP)
        total = None
        for j in range(experts):
            mine = jnp.sum(jnp.where(lane == experts * c + j, place, 0.0), axis=1, keepdims=True)
            term = mm((slot == mine).astype(bf16), values[j, here])
            total = term if total is None else total + term
        return total

    for copy in loads[:groups]:
        copy.wait()

    for k, o in enumerate(job.order):
        stage[k] = tile(backs, 4 * (1 - c) + o).astype(bf16)
        job.core[k].start()
    job.second(lambda o: tile(backs, 4 * c + o))
    for copy in loads[groups:]:
        copy.wait()

    def feed(first, last):
        @pl.loop(first, last)
        def _(n):
            staged[n] = tile(feeds, n).astype(bf16)
            pltpu.make_async_copy(staged.at[n], feed_out.at[n], o_sem.at[n]).start()

    feed(0, 4)
    job.third()
    feed(4, 8)
    job.last()
    one, two = job.total()
    out_ref[: job.half] = one
    out_ref[job.half :] = two

    @pl.loop(0, 8)
    def _(n):
        pltpu.make_async_copy(staged.at[n], feed_out.at[n], o_sem.at[n]).wait()


def combine(row, feeds, backs, number):
    experts = sum(f.shape[0] for f in feeds)
    _, slots, width = feeds[0].shape
    wide = backs[0].shape[2]
    rows = row.shape[1] // 8
    vmem = pl.BlockSpec(memory_space=pltpu.VMEM)
    return pl.pallas_call(
        functools.partial(combine_kernel, experts),
        in_specs=[vmem] + anywhere(len(feeds) + len(backs)),
        out_specs=[vmem] + anywhere(1),
        out_shape=[
            jax.ShapeDtypeStruct((rows, wide), f32),
            jax.ShapeDtypeStruct((8, rows, width), bf16),
        ],
        scratch_shapes=[
            pltpu.VMEM((experts, slots, wide), bf16),
            pltpu.VMEM((experts, slots, width), bf16),
            pltpu.VMEM((4, rows, wide), bf16),
            pltpu.VMEM((8, rows, width), bf16),
            pltpu.SemaphoreType.DMA((len(feeds),)),
            pltpu.SemaphoreType.DMA((len(feeds),)),
            pltpu.SemaphoreType.DMA((8,)),
        ]
        + Sum.scratch(rows, wide),
        compiler_params=params(collective_id=number, has_side_effects=True),
        cost_estimate=cost(45),
        name="combine",
    )(row, *feeds, *backs)


def closing_kernel(dq_ref, dk_ref, dv_ref, x_ref, cos_ref, sin_ref, wt_ref, par_ref, go_ref, small_ref, top_ref, ge_ref,
                   out_ref, gsum_ref, ssum_ref, tmax_ref, gall_ref,
                   dqs, dks, dvs, xs, total, row, gother, gcore, gline, gmine, smine, sline, splane, tline, mytop, stage, l_sem, *sems):
    job = Sum(None, *sems[:7], stage=stage)
    sends, recvs = sems[7:]
    z, c, t = spot()
    ns = lax.axis_size("shard")
    heads = dqs.shape[0]
    half = HEAD_DIM // 2
    own = 4 * c + t
    order = [4 * (1 - c) + o for o in job.order] + [4 * c + o for o in job.order]

    def lanes(o):
        return pl.ds(pl.multiple_of(o * BLOCK, BLOCK), BLOCK)

    loads = []
    for n, o in enumerate(order):
        here = lanes(o)
        loads.append(
            [
                pltpu.make_async_copy(dq_ref.at[:, :, here], dqs.at[:, :, here], l_sem.at[n, 0]),
                pltpu.make_async_copy(dk_ref.at[:, :, here], dks.at[:, :, here], l_sem.at[n, 1]),
                pltpu.make_async_copy(dv_ref.at[:, :, here], dvs.at[:, :, here], l_sem.at[n, 2]),
                pltpu.make_async_copy(x_ref.at[here], xs.at[here], l_sem.at[n, 3]),
            ]
        )
        for copy in loads[-1]:
            copy.start()
    greet()
    started = []

    def go(k, source, target, **where):
        copy = remote(source, target, sends.at[k], recvs.at[k], **where)
        copy.start()
        started.append(copy)
        return copy

    line_row = lax.broadcasted_iota(jnp.int32, mytop.shape, 0)
    high = jnp.full(mytop.shape, -1e30, f32)
    for h in range(top_ref.shape[0]):
        best = jnp.max(jnp.max(top_ref[h], axis=0), axis=1, keepdims=True)
        high = jnp.where(line_row == h, best, high)
    mytop[...] = high
    tops = [go(3 + ns + s, mytop, tline.at[s], shard=lax.rem(z + s, ns)) for s in range(1, ns)]
    experts = go(1, ge_ref, gall_ref, ctx=1 - c)
    total[...] = jnp.zeros_like(total)
    row[...] = jnp.zeros_like(row)

    def tile(o):
        here = lanes(o)
        cosine, sine = cos_ref[:, here], sin_ref[:, here]

        def turned(g):
            u, w = g[:half], g[half:]
            return jnp.concatenate([u * cosine + w * sine, w * cosine - u * sine], axis=0)

        x = xs[here].astype(f32)
        m = x * lax.rsqrt(jnp.mean(x * x, axis=1, keepdims=True) + epsilon)
        a = (m * par_ref[18:19]).astype(bf16)
        pieces = [turned(dqs[h, :, here]) for h in range(heads)]
        pieces += [turned(dks[h, :, here]) for h in range(heads)]
        pieces += [dvs[h, :, here] for h in range(heads)]
        grads = jnp.concatenate(pieces, axis=0).astype(bf16)
        part = mm(grads, wt_ref[...], TN)
        row[...] += jnp.sum(part * m, axis=0, keepdims=True)
        total[...] += mm(grads, a)
        return part

    for k in range(4):
        for copy in loads[k]:
            copy.wait()
        stage[k] = tile(order[k]).astype(bf16)
        job.core[k].start()

    def mine(o):
        return tile(4 * c + o)

    for k in range(4, 8):
        for copy in loads[k]:
            copy.wait()
    job.second(mine)

    cut_rows, depth = gmine.shape[1:]
    mid = cut_rows // 2
    at = lax.broadcasted_iota(jnp.int32, small_ref.shape, 0)
    smalls = small_ref[...] + jnp.where(at == 19, row[...], 0.0)
    for s in range(ns):
        here = slice(s * depth, (s + 1) * depth)
        one = total[:cut_rows, here].astype(bf16)
        two = jnp.concatenate([total[cut_rows:, here].astype(bf16), go_ref[:, here]], axis=0)
        gmine[s] = jnp.where(c == 0, one.astype(f32), two.astype(f32)).astype(bf16)
        gother[s] = jnp.where(c == 0, two.astype(f32), one.astype(f32)).astype(bf16)
        smine[s] = smalls[:, here]
    core = go(0, gother, gcore, ctx=1 - c)
    small = [go(3 + s, smine.at[lax.rem(z + s, ns)], sline.at[s], shard=lax.rem(z + s, ns)) for s in range(1, ns)]
    core.wait_recv()
    gmine[...] = gmine[...] + gcore[...]
    line = [go(3 + 2 * ns + s, gmine.at[lax.rem(z + s, ns)], gline.at[s], shard=lax.rem(z + s, ns)) for s in range(1, ns)]
    job.third()
    for copy in small:
        copy.wait_recv()
    value = smine[z]
    for s in range(1, ns):
        value = value + sline[s]
    splane[0] = value
    plane = []
    for s in range(1, 8):
        other = lax.rem(own + s, 8)
        plane.append(go(3 + 3 * ns + s, splane.at[0], splane.at[s], ctx=other // 4, tp=lax.rem(other, 4)))
    for copy in tops:
        copy.wait_recv()
    high = mytop[...]
    for s in range(1, ns):
        high = jnp.maximum(high, tline[s])
    tline[0] = high
    pair = go(2, tline.at[0], tline.at[ns], ctx=1 - c)
    for copy in line:
        copy.wait_recv()
    value = gmine[z].astype(f32)
    for s in range(1, ns):
        value = value + gline[s].astype(f32)
    gsum_ref[c] = value
    go(3, gsum_ref.at[c], gsum_ref.at[c], ctx=1 - c)
    for copy in plane:
        copy.wait_recv()
    value = splane[0]
    for s in range(1, 8):
        value = value + splane[s]
    ssum_ref[...] = value
    pair.wait_recv()
    tmax_ref[...] = jnp.maximum(tline[0], tline[ns])
    job.last()
    one, two = job.total()
    out_ref[: job.half] = one
    out_ref[job.half :] = two
    remote(gsum_ref.at[1 - c], gsum_ref.at[1 - c], sends.at[3], recvs.at[3], ctx=1 - c).wait_recv()
    experts.wait_recv()
    for copy in started:
        copy.wait_send()


def closing(dq, dk, dv, x, cosine, sine, wt, par, go, small, top, ge, number):
    heads, _, total = dq.shape
    width = x.shape[1]
    rows = total // 8
    ns = lax.axis_size("shard")
    depth = width // ns
    cut_rows = 2 * heads * HEAD_DIM
    pieces = (ns, cut_rows, depth)
    smalls = (ns,) + small.shape[:1] + (depth,)
    vmem = pl.BlockSpec(memory_space=pltpu.VMEM)
    return pl.pallas_call(
        closing_kernel,
        in_specs=anywhere(4) + [vmem] * 7 + anywhere(1),
        out_specs=[vmem, vmem, vmem, vmem] + anywhere(1),
        out_shape=[
            jax.ShapeDtypeStruct((rows, width), f32),
            jax.ShapeDtypeStruct((2, cut_rows, depth), f32),
            jax.ShapeDtypeStruct(smalls[1:], f32),
            jax.ShapeDtypeStruct((8, 128), f32),
            jax.ShapeDtypeStruct(ge.shape, bf16),
        ],
        scratch_shapes=[
            pltpu.VMEM(dq.shape, f32),
            pltpu.VMEM(dq.shape, f32),
            pltpu.VMEM(dq.shape, f32),
            pltpu.VMEM(x.shape, bf16),
            pltpu.VMEM(wt.shape, f32),
            pltpu.VMEM((1, width), f32),
            pltpu.VMEM(pieces, bf16),
            pltpu.VMEM(pieces, bf16),
            pltpu.VMEM(pieces, bf16),
            pltpu.VMEM(pieces, bf16),
            pltpu.VMEM(smalls, f32),
            pltpu.VMEM(smalls, f32),
            pltpu.VMEM((8,) + smalls[1:], f32),
            pltpu.VMEM((ns + 1, 8, 128), f32),
            pltpu.VMEM((8, 128), f32),
            pltpu.VMEM((4, rows, width), bf16),
            pltpu.SemaphoreType.DMA((8, 4)),
        ]
        + Sum.scratch(rows, width)
        + [
            pltpu.SemaphoreType.DMA((3 * ns + 11,)),
            pltpu.SemaphoreType.DMA((3 * ns + 11,)),
        ],
        compiler_params=params(collective_id=number, has_side_effects=True),
        cost_estimate=cost(45),
        name="closing",
    )(dq, dk, dv, x, cosine, sine, wt, par, go, small, top, ge)


def swap_kernel(ge_ref, other_ref, send, recv):
    z, c, t = spot()
    greet_core()
    copy = remote(ge_ref, other_ref, send, recv, ctx=1 - c)
    copy.start()
    copy.wait()


def greet_core():
    z, c, t = spot()
    barrier = pltpu.get_barrier_semaphore()
    pl.semaphore_signal(barrier, inc=1, device_id={"ctx": 1 - c}, device_id_type=MESH)
    pl.semaphore_wait(barrier, 1)


def swap(ge, number):
    return pl.pallas_call(
        swap_kernel,
        in_specs=anywhere(1),
        out_specs=anywhere(1)[0],
        out_shape=jax.ShapeDtypeStruct(ge.shape, ge.dtype),
        scratch_shapes=[pltpu.SemaphoreType.DMA, pltpu.SemaphoreType.DMA],
        compiler_params=params(collective_id=number, has_side_effects=True),
        cost_estimate=cost(5),
        name="swap",
    )(ge)


def columns(previous, routes):
    count, rows = previous.shape
    previous = jnp.concatenate([previous, jnp.zeros((16 - count, rows), f32)], axis=0).T
    at = lax.broadcasted_iota(jnp.int32, (8, rows), 0)
    routes = routes.astype(f32)
    return previous, jnp.where(at == 0, routes[0:1], routes[1:2]).T


def mixing(n2, wrc, previous, routes):
    z = mm(n2, wrc, NT, lax.Precision.HIGHEST)
    lane = lax.broadcasted_iota(jnp.int32, z.shape, 1)
    logits = z + previous
    hot = [lane.astype(f32) == routes[:, r : r + 1] for r in range(2)]
    picked = [jnp.sum(jnp.where(hot[r], logits, 0.0), axis=1, keepdims=True) for r in range(2)]
    most = jnp.maximum(picked[0], picked[1])
    e = [jnp.exp(p - most) for p in picked]
    gates = [v / (e[0] + e[1]) for v in e]
    combine = jnp.where(hot[0], gates[0], 0.0) + jnp.where(hot[1], gates[1], 0.0)

    def column(array, at):
        return jnp.sum(jnp.where(lane == at, array, 0.0), axis=1, keepdims=True)

    alphas = []
    for j in range(2):
        first, second = column(z, EXPERTS + 2 * j), column(z, EXPERTS + 2 * j + 1)
        most = jnp.maximum(first, second)
        a, b = jnp.exp(first - most), jnp.exp(second - most)
        alphas.append((a / (a + b), b / (a + b)))
    weights = [column(combine, FFN_EXPERTS + 1 + j) for j in range(3)]
    return hot, gates, combine, alphas, weights


def turn_kernel(length, res_ref, dn_ref, cot_ref, att_ref, wo_ref, par_ref, prev_ref, routes_ref,
                dres_ref, heads_ref, gwo_ref, small_ref, got_ref, send_sem, recv_sem, local_sem):
    z, c, t = spot()
    nt = lax.axis_size("tp")
    own = c * nt + t
    rows, width = res_ref.shape
    greet(False)
    here = pl.ds(pl.multiple_of(t * rows, rows), rows)
    res = res_ref[...]
    gain = par_ref[19:20]
    inverse = lax.rsqrt(jnp.mean(res * res, axis=1, keepdims=True) + epsilon)
    m = res * inverse
    n2 = m * gain
    previous, routes = columns(prev_ref[:, here], routes_ref[c, :, here])
    hot, gates, _, alphas, weights = mixing(n2, par_ref[:16], previous, routes)
    position = own * rows + lax.broadcasted_iota(jnp.int32, cot_ref.shape, 0)
    g = jnp.where(position < length[0], cot_ref[...].astype(f32), 0.0)
    inner = jnp.sum(g * n2, axis=1, keepdims=True)
    onto = [jnp.sum(g * par_ref[16 + j : 17 + j], axis=1, keepdims=True) for j in range(2)]
    named = dn_ref[:, width:].astype(f32)
    lane = lax.broadcasted_iota(jnp.int32, hot[0].shape, 1)
    wide = lax.broadcasted_iota(jnp.int32, named.shape, 1).astype(f32)
    local = {
        FFN_EXPERTS + 1: inner,
        FFN_EXPERTS + 2: alphas[0][0] * inner + alphas[0][1] * onto[0],
        FFN_EXPERTS + 3: alphas[1][0] * inner + alphas[1][1] * onto[1],
    }
    dgates = []
    for r in range(2):
        name = routes[:, r : r + 1]
        there = jnp.where((wide == name) | (wide == name + 16), named, 0.0)
        there = jnp.where(name < FFN_EXPERTS, jnp.sum(there, axis=1, keepdims=True), 0.0)
        for e, value in local.items():
            there = there + jnp.where(name == e, value, 0.0)
        dgates.append(there)
    mean = gates[0] * dgates[0] + gates[1] * dgates[1]
    dz = jnp.where(hot[0], gates[0] * (dgates[0] - mean), 0.0)
    dz = dz + jnp.where(hot[1], gates[1] * (dgates[1] - mean), 0.0)
    for j in range(2):
        da = weights[1 + j] * inner
        db = weights[1 + j] * onto[j]
        centre = alphas[j][0] * da + alphas[j][1] * db
        dz = dz + jnp.where(lane == EXPERTS + 2 * j, alphas[j][0] * (da - centre), 0.0)
        dz = dz + jnp.where(lane == EXPERTS + 2 * j + 1, alphas[j][1] * (db - centre), 0.0)
    scale = weights[0] + weights[1] * alphas[0][0] + weights[2] * alphas[1][0]
    highest = lax.Precision.HIGHEST
    dn2 = dn_ref[:, :width].astype(f32) + scale * g + mm(dz, par_ref[:16], NN, highest)
    q = dn2 * gain
    dres = g + inverse * (q - m * jnp.mean(q * m, axis=1, keepdims=True))
    dres_ref[...] = dres
    da = dres.astype(bf16)
    wo = wo_ref[...].reshape(-1, width)
    got_ref[...] = mm(wo, da, NT).astype(bf16).reshape(got_ref.shape)

    core = lax.rem((own + 1) // 2, 2)
    slot = 2 * (own // 4) + lax.rem(own, 4) // 2
    copies = []
    for target in range(nt):
        inside = jnp.logical_and(core == c, target == t)
        copy = remote(got_ref.at[target], heads_ref.at[slot], send_sem.at[target], recv_sem.at[slot], ctx=core, tp=target)
        copies.append((inside, copy, pltpu.make_async_copy(got_ref.at[target], heads_ref.at[slot], local_sem)))
    for inside, copy, kept in copies:

        @pl.when(jnp.logical_not(inside))
        def _():
            copy.start()

        @pl.when(inside)
        def _():
            kept.start()

    small_ref[0:16] = mm(dz, n2, TN, highest)
    small_ref[16:24] = jnp.zeros((8, width), f32)
    small_ref[16:17] = jnp.sum((weights[1] * alphas[0][1]) * g, axis=0, keepdims=True)
    small_ref[17:18] = jnp.sum((weights[2] * alphas[1][1]) * g, axis=0, keepdims=True)
    small_ref[18:19] = jnp.sum(dn2 * m, axis=0, keepdims=True)
    att = att_ref[...].reshape(-1, rows)
    gwo_ref[...] = mm(att, da).astype(bf16).reshape(gwo_ref.shape)
    for inside, copy, kept in copies:

        @pl.when(jnp.logical_not(inside))
        def _():
            copy.wait_send()

        @pl.when(inside)
        def _():
            kept.wait()

    for i in range(heads_ref.shape[0]):

        @pl.when(zig(c, i) != own)
        def _():
            remote(got_ref.at[0], heads_ref.at[i], send_sem.at[0], recv_sem.at[i], ctx=c, tp=t).wait_recv()


def turn(length, res, dn, cot, att, wo, small, prev, routes, count, number):
    rows, width = res.shape
    nt = lax.axis_size("tp")
    args = (res, dn, cot, att, wo, small, prev, routes)
    return pl.pallas_call(
        turn_kernel,
        grid_spec=pltpu.PrefetchScalarGridSpec(
            num_scalar_prefetch=1,
            grid=(1,),
            in_specs=[full(v.shape) for v in args],
            out_specs=[full((rows, width))] + anywhere(1) + [full(wo.shape), full((24, width))],
            scratch_shapes=[
                pltpu.VMEM(att.shape, bf16),
                pltpu.SemaphoreType.DMA((nt,)),
                pltpu.SemaphoreType.DMA((count,)),
                pltpu.SemaphoreType.DMA,
            ],
        ),
        out_shape=[
            jax.ShapeDtypeStruct((rows, width), f32),
            jax.ShapeDtypeStruct((count,) + att.shape[1:], bf16),
            jax.ShapeDtypeStruct(wo.shape, bf16),
            jax.ShapeDtypeStruct((24, width), f32),
        ],
        compiler_params=params(collective_id=number, has_side_effects=True),
        cost_estimate=cost(18),
        name="turn",
    )(length, *args)


def finish_kernel(x_ref, dn_ref, dres_ref, small_ref, base_ref, feed_ref, gw_ref, gs_ref, top_ref, wq_ref, wk_ref, limit_ref, length_ref, own_a, own_b, other_a, other_b, *outs):
    each = own_a.shape[0]
    local = 2 * each
    gin_ref, out_ref, gate_ref, up_ref, down_ref = outs[:5]
    x = x_ref[...].astype(f32)
    inverse = lax.rsqrt(jnp.mean(x * x, axis=1, keepdims=True) + epsilon)
    m = x * inverse
    q = dn_ref[...] * small_ref[18:19]
    gin_ref[...] = dres_ref[...] + inverse * (q - m * jnp.mean(q * m, axis=1, keepdims=True))
    core = lax.axis_index("ctx")
    rows = x.shape[0]
    first = (core * lax.axis_size("tp") + lax.axis_index("tp")) * pl.num_programs(0) + pl.program_id(0)
    position = first * rows + lax.broadcasted_iota(jnp.int32, x.shape, 0)
    out_ref[...] = jnp.where(position < length_ref[0], base_ref[...] + feed_ref[...], 0.0).astype(bf16)
    for k, target in enumerate((gate_ref, up_ref, down_ref)):
        for j in range(local):
            own, other = ((own_a, other_a), (own_b, other_b))[j // each]
            mine, theirs = own[j % each, k].astype(f32), other[j % each, k].astype(f32)
            target[j] = jnp.where(core == 0, mine, theirs)
            target[local + j] = jnp.where(core == 0, theirs, mine)

    @pl.when(pl.program_id(0) == 0)
    def _():
        gq, gk, gv, go, gnorm, gmoe, grouter, gconst, gvec, fac_ref, cq_ref, ck_ref = outs[5:]
        width = wq_ref.shape[1]
        flat = gw_ref[...].reshape(4 * width, gw_ref.shape[2])
        for k, target in enumerate((gq, gk, gv)):
            target[...] = flat[k * width : (k + 1) * width].T
        go[...] = flat[3 * width :]
        sums = gs_ref[...]
        grouter[...] = sums[:EXPERTS]
        gconst[...] = sums[EXPERTS : EXPERTS + 4]
        gvec[...] = sums[16:18]
        gmoe[...] = sums[18:19]
        gnorm[...] = sums[19:20]
        factors = limit_ref[0] / jnp.maximum(top_ref[...], limit_ref[0])
        fac_ref[...] = factors
        lane = lax.broadcasted_iota(jnp.int32, (1, width), 1)
        root = jnp.zeros((1, width), f32)
        for h in range(width // HEAD_DIM):
            root = jnp.where(lane // HEAD_DIM == h, jnp.sqrt(factors[h : h + 1, :1]), root)
        cq_ref[...] = (wq_ref[...].astype(f32) * root).astype(bf16)
        ck_ref[...] = (wk_ref[...].astype(f32) * root).astype(bf16)


def finish_rows(x, dn, dres, small, base, feed, gw, gs, top, wq, wk, limit, length, own, other):
    rows, width = x.shape
    each, kinds, depth, hidden = own[0].shape
    local = 2 * each
    steps = 4 if depth % 64 == 0 else 1
    tile, deep = rows // steps, depth // steps
    by_row = pl.BlockSpec((tile, width), lambda i: (i, 0))
    expert_out = pl.BlockSpec((2 * local, deep, hidden), lambda i: (0, i, 0))
    once = [
        jax.ShapeDtypeStruct(shape, f32)
        for shape in [wq.shape] * 3
        + [(wq.shape[1], depth), (1, depth), (1, depth), (EXPERTS, depth), (4, depth), (2, depth), (8, 128)]
    ] + [jax.ShapeDtypeStruct(wq.shape, bf16)] * 2
    return pl.pallas_call(
        finish_kernel,
        grid=(steps,),
        in_specs=[
            by_row,
            by_row,
            by_row,
            full(small.shape),
            by_row,
            by_row,
            full(gw.shape),
            full(gs.shape),
            full(top.shape),
            full(wq.shape),
            full(wk.shape),
            pl.BlockSpec(memory_space=pltpu.SMEM),
            pl.BlockSpec(memory_space=pltpu.SMEM),
        ]
        + [pl.BlockSpec((each, kinds, deep, hidden), lambda i: (0, 0, i, 0))] * 4,
        out_specs=[by_row, by_row, expert_out, expert_out, expert_out] + [full(v.shape) for v in once],
        out_shape=[
            jax.ShapeDtypeStruct((rows, width), f32),
            jax.ShapeDtypeStruct((rows, width), bf16),
        ]
        + [jax.ShapeDtypeStruct((2 * local, depth, hidden), f32)] * 3
        + once,
        compiler_params=params(),
        cost_estimate=cost(8),
        name="finish_rows",
    )(x, dn, dres, small, base, feed, gw, gs, top, wq, wk, limit, length, *own, *other)


def expert_kernel(start, first, x_ref, g_ref, gate_ref, w_ref, feed_ref, back_ref, gw_ref):
    parts, _, _, depth, hidden = w_ref.shape
    width = parts * depth
    wg, wu, wd = [w_ref[:, 0, k].reshape(width, hidden) for k in range(3)]
    x, g, gate = x_ref[0], g_ref[0], gate_ref[0]
    gate_pre = mm(x, wg)
    up = mm(x, wu)
    sigmoid = 1.0 / (1.0 + jnp.exp(-gate_pre))
    activated = gate_pre * sigmoid
    inner = (activated * up).astype(bf16)
    g32 = g.astype(f32)
    dout = (gate * g32).astype(bf16)
    dinner = mm(dout, wd)
    out = mm(inner, wd, NT)
    feed_ref[0] = (gate * out).astype(bf16)
    dgate = jnp.sum(g32 * out, axis=1, keepdims=True)
    dpre = (dinner * up * sigmoid * (1.0 + gate_pre * (1.0 - sigmoid))).astype(bf16)
    dup = (dinner * activated).astype(bf16)
    back_ref[0, :, :width] = (mm(dpre, wg, NT) + mm(dup, wu, NT)).astype(bf16)
    lane = lax.broadcasted_iota(jnp.int32, (dgate.shape[0], back_ref.shape[2] - width), 1)
    coarse = dgate.astype(bf16).astype(f32)
    at = first[0] + start + pl.program_id(0)
    extra = jnp.where(lane == at, coarse, jnp.where(lane == at + 16, dgate - coarse, 0.0))
    back_ref[0, :, width:] = extra.astype(bf16)
    for k, (left, right) in enumerate(((x, dpre), (x, dup), (dout, inner))):
        gw_ref[:, 0, k] = mm(left, right, TN).reshape(parts, depth, hidden).astype(bf16)


def expert(start, first, x, g, gate, w):
    slots, width = x.shape[1:]
    parts, some, kinds, depth, hidden = w.shape
    pick = lambda i, f: (start + i, 0, 0)
    return pl.pallas_call(
        functools.partial(expert_kernel, start),
        grid_spec=pltpu.PrefetchScalarGridSpec(
            num_scalar_prefetch=1,
            grid=(some,),
            in_specs=[
                pl.BlockSpec((1, slots, width), pick),
                pl.BlockSpec((1, slots, width), pick),
                pl.BlockSpec((1, slots, 1), pick),
                pl.BlockSpec((parts, 1, kinds, depth, hidden), lambda i, f: (0, i, 0, 0, 0)),
            ],
            out_specs=[
                pl.BlockSpec((1, slots, width), lambda i, f: (i, 0, 0)),
                pl.BlockSpec((1, slots, width + EXTRA), lambda i, f: (i, 0, 0)),
                pl.BlockSpec((parts, 1, kinds, depth, hidden), lambda i, f: (0, i, 0, 0, 0)),
            ],
        ),
        out_shape=[
            jax.ShapeDtypeStruct((some, slots, width), bf16),
            jax.ShapeDtypeStruct((some, slots, width + EXTRA), bf16),
            jax.ShapeDtypeStruct(w.shape, bf16),
        ],
        compiler_params=params(),
        cost_estimate=cost(12 * some),
        name="expert",
    )(first, x, g, gate, w)


def shards(
    hidden_in,
    cotangent,
    lengths,
    routes,
    prev_logits,
    norm_attn,
    w_query,
    w_key,
    w_value,
    w_out,
    norm_moe,
    w_router,
    w_const,
    const_vec,
    w_gate,
    w_up,
    w_down,
    threshold,
):
    plane = ("ctx", "tp")
    core = lax.axis_index("ctx")
    nc, nt, ns = lax.axis_size("ctx"), lax.axis_size("tp"), lax.axis_size("shard")
    own, width = hidden_in.shape
    per = own * nt
    total = per * nc
    depth = w_gate.shape[1]
    heads = w_query.shape[1] // HEAD_DIM
    head_width = heads * HEAD_DIM
    local = FFN_EXPERTS // nc
    count = total // BLOCK // nc
    routes, prev = routes.T, prev_logits.T
    first = (core * local).astype(jnp.int32)[None]

    expert_w = []
    for start in range(0, local, 2):
        pieces = [
            lax.dynamic_slice_in_dim(w, core * local + start, 2, 0) for w in (w_gate, w_up, w_down)
        ]
        expert_w.append(lax.all_gather(jnp.stack(pieces, axis=1), "shard", axis=0, tiled=False))
    small = jnp.concatenate(
        [
            w_router,
            w_const,
            const_vec.T,
            norm_attn[:, None],
            norm_moe[:, None],
            jnp.zeros((depth, SMALL - EXPERTS - 8), bf16),
        ],
        axis=1,
    )
    rows_all, attention_w, routes_all = opening(
        hidden_in, w_query, w_key, w_value, w_out, small, routes, 0
    )
    rows_all = rows_all.reshape(total, width)
    cosine, sine = rope_tables(total)

    qt, kt, k, v, vt, wt, out_w, small = project(rows_all, attention_w, cosine, sine, heads)
    ot, lse, top, cot_all, out_w = attend(lengths, qt, k, vt, cotangent, out_w, count, 1)
    att, res, base, x_slots, g_slots, gate_slots, row_at = route(
        ot, hidden_in, out_w, small, prev, routes_all, cot_all, local, 2
    )

    feeds, backs, grads = [], [], []
    for j, w in enumerate(expert_w):
        feed, back, grad = expert(2 * j, first, x_slots, g_slots, gate_slots, w)
        feeds.append(feed)
        backs.append(back)
        grads.append(lax.psum_scatter(grad, "shard", scatter_dimension=0, tiled=True)[0])
    back, feed = combine(row_at, feeds, backs, 3)

    dres, got, grad_out, gsmall = turn(
        lengths, res, back, cotangent, att, out_w, small, prev, routes_all, count, 4
    )
    dq, dk, dv, grad_out, feed = revisit(qt, k, kt, v, ot, got, lse, grad_out, feed, 5)
    part, grad_w, gsmall, top, other = closing(
        dq, dk, dv, rows_all, cosine, sine, wt, small, grad_out, gsmall, top, grads[1], 6
    )
    others = (swap(grads[0], 7), other)
    (grad_input, output, grad_gate, grad_up, grad_down, grad_q, grad_k, grad_v, grad_out, grad_norm_attn, grad_norm_moe,
     grad_router, grad_const, grad_vec, factors, clipped_query, clipped_key) = finish_rows(
        hidden_in, part, dres, small, base, feed, grad_w, gsmall, top, w_query, w_key, threshold, lengths, grads, others
    )
    return (
        output,
        grad_input,
        grad_norm_attn[0],
        grad_q,
        grad_k,
        grad_v,
        grad_out,
        grad_norm_moe[0],
        grad_router.T,
        grad_const.T,
        grad_vec,
        grad_gate,
        grad_up,
        grad_down,
        factors[:heads, 0],
        clipped_query,
        clipped_key,
    )


def solution(mesh):
    return jax.shard_map(
        shards,
        mesh=mesh,
        in_specs=(
            P(("shard", "ctx", "tp"), None),
            P(("shard", "ctx", "tp"), None),
            P("shard"),
            P(("shard", "ctx"), None),
            P(("shard", "ctx"), None),
            P("shard"),
            P("shard", "tp"),
            P("shard", "tp"),
            P("shard", "tp"),
            P("tp", "shard"),
            P("shard"),
            P("shard", None),
            P("shard", None),
            P(None, "shard"),
            P(None, "shard", "tp"),
            P(None, "shard", "tp"),
            P(None, "shard", "tp"),
            P(),
        ),
        out_specs=(
            P(("shard", "ctx", "tp"), None),
            P(("shard", "ctx", "tp"), None),
            P("shard"),
            P("shard", "tp"),
            P("shard", "tp"),
            P("shard", "tp"),
            P("tp", "shard"),
            P("shard"),
            P("shard", None),
            P("shard", None),
            P(None, "shard"),
            P(None, "shard", "tp"),
            P(None, "shard", "tp"),
            P(None, "shard", "tp"),
            P("tp"),
            P("shard", "tp"),
            P("shard", "tp"),
        ),
        check_vma=False,
    )
```

```python
import functools

import jax
import jax.numpy as jnp
import numpy as np
from jax import lax
from jax.experimental import pallas as pl
from jax.experimental.pallas import tpu as pltpu
from jax.sharding import PartitionSpec as P

HEAD_DIM = 64
EXPERTS = 12
FFN_EXPERTS = 8
CAP = 512
BLOCK = 512
EXTRA = 128
SMALL = 32
MESH = pl.DeviceIdType.MESH

epsilon = 1e-06
rope_base = 10000.0
bf16 = jnp.bfloat16
f32 = jnp.float32

NN = (((1,), (0,)), ((), ()))
NT = (((1,), (1,)), ((), ()))
TN = (((0,), (0,)), ((), ()))


def mm(left, right, dims=NN, precision=None):
    return lax.dot_general(
        left, right, dims, preferred_element_type=f32, precision=precision
    )


def params(mib=56, **more):
    return pltpu.CompilerParams(vmem_limit_bytes=mib * 1024 * 1024, **more)


def cost(us):
    return pl.CostEstimate(flops=int(us * 1e9), bytes_accessed=int(us * 3e6), transcendentals=0)


def full(shape):
    return pl.BlockSpec(shape, lambda *_: (0,) * len(shape))


def rope_tables(total):
    half = HEAD_DIM // 2
    freqs = np.float32(rope_base) ** (np.float32(-2.0) * np.arange(half, dtype=np.float32) / np.float32(HEAD_DIM))
    angles = freqs.astype(np.float32)[:, None] * np.arange(total, dtype=np.float32)[None, :]
    angles = angles.astype(np.float64)
    return jnp.asarray(np.cos(angles), f32), jnp.asarray(np.sin(angles), f32)


def zig(core, i):
    return 4 * (i // 2) + (core if i % 2 == 0 else 3 - core)


def anywhere(count):
    return [pl.BlockSpec(memory_space=pl.ANY)] * count


def spot():
    return lax.axis_index("shard"), lax.axis_index("ctx"), lax.axis_index("tp")


def across(t):
    return t + 1 - 2 * lax.rem(t, 2), lax.rem(t + 2, 4), 3 - t


def remote(source, target, sends, recvs, **where):
    return pltpu.make_async_remote_copy(
        src_ref=source,
        dst_ref=target,
        send_sem=sends,
        recv_sem=recvs,
        device_id=where,
        device_id_type=MESH,
    )


def greet(depth=True):
    z, c, t = spot()
    nc, nt, ns = lax.axis_size("ctx"), lax.axis_size("tp"), lax.axis_size("shard")
    barrier = pltpu.get_barrier_semaphore()
    for step in range(1, nc * nt):
        other = lax.rem(c * nt + t + step, nc * nt)
        pl.semaphore_signal(
            barrier,
            inc=1,
            device_id={"ctx": other // nt, "tp": lax.rem(other, nt)},
            device_id_type=MESH,
        )
    if depth:
        for step in range(1, ns):
            pl.semaphore_signal(
                barrier,
                inc=1,
                device_id={"shard": lax.rem(z + step, ns)},
                device_id_type=MESH,
            )
    pl.semaphore_wait(barrier, nc * nt - 1 + (ns - 1 if depth else 0))


class Gather:
    KINDS = 9

    def __init__(self, x, out, sends, recvs, own, cuts, stage=None, relative=False):
        z, c, t = spot()
        tx, ty, td = across(t)
        rows = x.shape[0] // cuts
        half = rows // 2
        self.cuts = cuts
        sib = {"ctx": 1 - c}
        px, py = {"tp": tx}, {"tp": ty}
        near = (t, tx, ty, td)
        if relative:
            here, there = list(range(8)), list(range(8))
            mine = (1, 2, 4)
            passed = ((1, 5), (1, 3), (2, 6), (2, 3), (3, 7), (3, 7))
        else:
            here = [4 * c + n for n in near] + [4 * (1 - c) + n for n in near]
            there = here[:4]
            mine = (here[0],) * 3
            passed = tuple((here[n], here[n]) for n in (1, 1, 2, 2, 3, 3))
        self.load = None if stage is None else pltpu.make_async_copy(x, stage, own.at[0])
        self.own = pltpu.make_async_copy(x if stage is None else stage, out.at[here[0]], own.at[1])

        def parts(s):
            whole = pl.ds(s * rows, rows)
            one, two = pl.ds(s * rows, half), pl.ds(s * rows + half, half)
            return whole, one, two

        def copies(s):
            whole, one, two = parts(s)
            made = [
                remote(x.at[whole], out.at[slot, whole], sends.at[s, k], recvs.at[s, k], **where)
                for k, (slot, where) in enumerate(zip(mine, (px, py, sib)))
            ]
            ways = ((whole, sib), (one, py), (whole, sib), (two, px), (one, sib), (two, sib))
            for k, ((source, target), (part, where)) in enumerate(zip(passed, ways)):
                made.append(
                    remote(out.at[source, part], out.at[target, part], sends.at[s, k + 3], recvs.at[s, k + 3], **where)
                )
            return made

        self.copies = [copies(s) for s in range(cuts)]

        def arrivals(s):
            whole, one, two = parts(s)
            where = [(1, whole), (2, whole), (4, whole), (5, whole), (3, one), (6, whole), (3, two), (7, one), (7, two)]
            return [
                remote(out.at[here[n], part], out.at[here[n], part], sends.at[s, k], recvs.at[s, k], **sib)
                for k, (n, part) in enumerate(where)
            ]

        self.arrivals = [arrivals(s) for s in range(cuts)]

    @staticmethod
    def scratch(cuts):
        return [
            pltpu.SemaphoreType.DMA((cuts, Gather.KINDS)),
            pltpu.SemaphoreType.DMA((cuts, Gather.KINDS)),
            pltpu.SemaphoreType.DMA((2,)),
        ]

    def first(self):
        for s in range(self.cuts):
            for k in (0, 1, 2):
                self.copies[s][k].start()
        (self.load or self.own).start()

    def second(self, s):
        if self.load is not None and s == 0:
            self.load.wait()
            self.own.start()
        self.arrivals[s][0].wait_recv()
        self.copies[s][4].start()
        self.copies[s][3].start()
        self.arrivals[s][1].wait_recv()
        self.copies[s][6].start()
        self.copies[s][5].start()

    def third(self, s):
        for k in (4, 6):
            self.arrivals[s][k].wait_recv()
            self.copies[s][7 if k == 4 else 8].start()

    def beside(self):
        for s in range(self.cuts):
            for k in (2, 3, 5):
                self.arrivals[s][k].wait_recv()

    def last(self, rest=False):
        for s in range(self.cuts):
            for k in (7, 8) if rest else (2, 3, 5, 7, 8):
                self.arrivals[s][k].wait_recv()
        for s in range(self.cuts):
            for k in range(self.KINDS):
                self.copies[s][k].wait_send()
        if not rest:
            self.own.wait()


class Sum:
    def __init__(self, p, held, came, across_in, across_out, sends, recvs, loads, stage=None):
        z, c, t = spot()
        self.t = t
        tx, ty, td = across(t)
        half = held.shape[1] // 2
        self.half = half
        self.one, self.two = pl.ds(0, half), pl.ds(half, half)
        self.order = (td, tx, ty, t)
        self.held, self.came, self.inn = held, came, across_in
        sib, px, py = {"ctx": 1 - c}, {"tp": tx}, {"tp": ty}
        self.core = []
        for k, o in enumerate(self.order):
            source = p.at[4 * (1 - c) + o] if stage is None else stage.at[k]
            self.core.append(remote(source, came.at[o], sends.at[k], recvs.at[k], **sib))
        self.loads = None
        if stage is None:
            self.loads = [pltpu.make_async_copy(p.at[4 * c + o], held.at[o], loads.at[k]) for k, o in enumerate(self.order)]

        def send(k, source, slot, where):
            return remote(source, across_in.at[slot], sends.at[k], recvs.at[k], **where)

        self.side = {
            "dx": send(4, held.at[td, self.one], 0, px),
            "dy": send(5, held.at[td, self.two], 1, py),
            "x": send(6, held.at[tx, self.one], 2, px),
            "y": send(7, held.at[ty, self.two], 3, py),
            "cy": send(8, across_out.at[0], 4, py),
            "cx": send(9, across_out.at[1], 5, px),
        }
        self.out = across_out
        self.near = (tx, ty, td)

    @staticmethod
    def scratch(rows, width):
        return [
            pltpu.VMEM((4, rows, width), bf16),
            pltpu.VMEM((4, rows, width), bf16),
            pltpu.VMEM((6, rows // 2, width), bf16),
            pltpu.VMEM((2, rows // 2, width), bf16),
            pltpu.SemaphoreType.DMA((10,)),
            pltpu.SemaphoreType.DMA((10,)),
            pltpu.SemaphoreType.DMA((4,)),
        ]

    def first(self):
        for k in range(4):
            self.core[k].start()
            self.loads[k].start()

    def add(self, k, mine):
        o = self.order[k]
        self.core[k].wait_recv()
        self.held[o] = (mine + self.came[o].astype(mine.dtype)).astype(bf16)
        for name in (("dx", "dy"), ("x",), ("y",), ())[k]:
            self.side[name].start()

    def second(self):
        for k, o in enumerate(self.order):
            self.loads[k].wait()
            self.add(k, self.held[o])

    def third(self):
        tx, ty, td = self.near
        self.side["dx"].wait_recv()
        self.out[0] = self.held[ty, self.one] + self.inn[0]
        self.side["cy"].start()
        self.side["dy"].wait_recv()
        self.out[1] = self.held[tx, self.two] + self.inn[1]
        self.side["cx"].start()

    def last(self):
        for k in ("x", "y", "cy", "cx"):
            self.side[k].wait_recv()
        for copy in self.core + list(self.side.values()):
            copy.wait_send()

    def total(self):
        def add(part, a, b):
            return self.held[self.t, part].astype(f32) + self.inn[a].astype(f32) + self.inn[b].astype(f32)

        return add(self.one, 2, 4), add(self.two, 3, 5)


def qkv_kernel(x_ref, w_ref, s_ref, cos_ref, sin_ref, qt_ref, kt_ref, k_ref, v_ref, vt_ref, wt_ref, small_ref, wo_ref, wo, send, recv, local):
    heads = qt_ref.shape[0]
    width = heads * HEAD_DIM
    half = HEAD_DIM // 2
    z, c, t = spot()
    nt = lax.axis_size("tp")
    mid = width // 2
    mine, theirs = pl.ds(c * mid, mid), pl.ds((1 - c) * mid, mid)
    away, came, onward, there = [], [], [], []
    for step in range(1, nt):
        back = lax.rem(t + nt - step, nt)
        away.append(remote(wo.at[mine], wo_ref.at[t, mine], send.at[step], recv.at[step], tp=lax.rem(t + step, nt)))
        ref = wo_ref.at[back, mine]
        came.append(remote(ref, ref, send.at[nt + step], recv.at[step], ctx=1 - c))
        onward.append(remote(ref, ref, send.at[nt + step], recv.at[nt + step], ctx=1 - c))
        ref = wo_ref.at[back, theirs]
        there.append(remote(ref, ref, send.at[nt + step], recv.at[nt + step], ctx=1 - c))
    own = pltpu.make_async_copy(wo, wo_ref.at[t], local)
    i = pl.program_id(0)

    @pl.when(i == 0)
    def _():
        def flat(v):
            return v.astype(f32).reshape(v.shape[0] * v.shape[1], v.shape[2])

        def whole(core, which):
            rest = flat(w_ref[core, :, 2])[:, which * (width - 128) : (which + 1) * (width - 128)]
            return jnp.concatenate([flat(w_ref[core, :, which]), rest], axis=1).T.astype(bf16)

        wo[...] = whole(1, 1)
        greet(False)
        for copy in away:
            copy.start()
        own.start()
        wt_ref[:width] = whole(0, 0)
        wt_ref[width : 2 * width] = whole(0, 1)
        wt_ref[2 * width :] = whole(1, 0)
        small_ref[...] = jnp.concatenate([s_ref[n].astype(f32) for n in range(s_ref.shape[0])], axis=1)

    x = x_ref[...].astype(f32)
    inverse = lax.rsqrt(jnp.mean(x * x, axis=1, keepdims=True) + epsilon)
    a = (x * inverse * small_ref[18:19]).astype(bf16)
    y = mm(wt_ref[...], a, NT)
    cosine, sine = cos_ref[...], sin_ref[...]

    def turned(first):
        u, w = y[first : first + half], y[first + half : first + HEAD_DIM]
        return jnp.concatenate([u * cosine - w * sine, w * cosine + u * sine], axis=0)

    for h in range(heads):
        at = h * HEAD_DIM
        qt_ref[h] = (turned(at) * HEAD_DIM**-0.5).astype(bf16)
        key = turned(width + at)
        kt_ref[h] = key.astype(bf16)
        k_ref[h] = key.T.astype(bf16)
        value = y[2 * width + at : 2 * width + at + HEAD_DIM]
        v_ref[h] = value.T.astype(bf16)
        vt_ref[h, :HEAD_DIM] = value.astype(bf16)
        vt_ref[h, HEAD_DIM:] = jnp.ones((16, value.shape[1]), bf16)

    @pl.when(i == pl.num_programs(0) - 2)
    def _():
        for copy, forth in zip(came, onward):
            copy.wait_recv()
            forth.start()

    @pl.when(i == pl.num_programs(0) - 1)
    def _():
        for copy in there:
            copy.wait_recv()
        for copy in away + onward:
            copy.wait_send()
        own.wait()


def project(rows, w, small, cosine, sine, heads, number):
    total, width = rows.shape
    tile = BLOCK
    out = heads * HEAD_DIM
    nt = lax.axis_size("tp")
    shapes = [
        jax.ShapeDtypeStruct((heads, HEAD_DIM, total), bf16),
        jax.ShapeDtypeStruct((heads, HEAD_DIM, total), bf16),
        jax.ShapeDtypeStruct((heads, total, HEAD_DIM), bf16),
        jax.ShapeDtypeStruct((heads, total, HEAD_DIM), bf16),
        jax.ShapeDtypeStruct((heads, HEAD_DIM + 16, total), bf16),
        jax.ShapeDtypeStruct((3 * out, width), bf16),
        jax.ShapeDtypeStruct((SMALL, width), f32),
        jax.ShapeDtypeStruct((nt, out, width), bf16),
    ]
    return pl.pallas_call(
        qkv_kernel,
        grid=(total // tile,),
        in_specs=[
            pl.BlockSpec((tile, width), lambda i: (i, 0)),
            full(w.shape),
            full(small.shape),
            pl.BlockSpec((HEAD_DIM // 2, tile), lambda i: (0, i)),
            pl.BlockSpec((HEAD_DIM // 2, tile), lambda i: (0, i)),
        ],
        out_specs=[
            pl.BlockSpec((heads, HEAD_DIM, tile), lambda i: (0, 0, i)),
            pl.BlockSpec((heads, HEAD_DIM, tile), lambda i: (0, 0, i)),
            pl.BlockSpec((heads, tile, HEAD_DIM), lambda i: (0, i, 0)),
            pl.BlockSpec((heads, tile, HEAD_DIM), lambda i: (0, i, 0)),
            pl.BlockSpec((heads, HEAD_DIM + 16, tile), lambda i: (0, 0, i)),
        ]
        + [full(v.shape) for v in shapes[5:7]]
        + anywhere(1),
        scratch_shapes=[
            pltpu.VMEM((out, width), bf16),
            pltpu.SemaphoreType.DMA((2 * nt,)),
            pltpu.SemaphoreType.DMA((2 * nt,)),
            pltpu.SemaphoreType.DMA,
        ],
        out_shape=shapes,
        compiler_params=params(collective_id=number, has_side_effects=True),
        cost_estimate=cost(14),
        name="project",
    )(rows, w, small, cosine, sine)


def dealt(core, i):
    return 4 * (i // 2) + jnp.where(lax.rem(i, 2) == 0, core, 3 - core)


def attend_kernel(cuts, length, qt_ref, k_ref, vt_ref, cot_ref, ot_ref, lse_ref, top_ref, cots_ref, mask_cot, *sems):
    z, c, t = spot()
    nt = lax.axis_size("tp")
    h, i = pl.program_id(0), pl.program_id(1)
    count = pl.num_programs(1)
    at_step = h * count + i
    last = pl.num_programs(0) * count - 1
    gather = Gather(mask_cot, cots_ref, *sems, cuts)

    @pl.when(at_step == 0)
    def _():
        rows = cot_ref.shape[0]
        position = (c * nt + t) * rows + lax.broadcasted_iota(jnp.int32, cot_ref.shape, 0)
        mask_cot[...] = jnp.where(position < length[0], cot_ref[...].astype(f32), 0.0).astype(bf16)
        greet(False)
        gather.first()

    index = dealt(c, i)
    columns = BLOCK
    qt = qt_ref[0, :, pl.ds(pl.multiple_of(index * BLOCK, BLOCK), BLOCK)]

    def step(at, carry, diagonal):
        peak, total = carry
        start = pl.multiple_of(at * BLOCK, BLOCK)
        scores = mm(k_ref[0, pl.ds(start, BLOCK), :], qt)
        if diagonal:
            keys = lax.broadcasted_iota(jnp.int32, scores.shape, 0)
            queries = lax.broadcasted_iota(jnp.int32, scores.shape, 1)
            scores = jnp.where(keys <= queries, scores, -1e30)
        higher = jnp.maximum(peak, jnp.max(scores, axis=0, keepdims=True))
        weights = jnp.exp(scores - higher).astype(bf16)
        total = total * jnp.exp(peak - higher) + mm(vt_ref[0, :, pl.ds(start, BLOCK)], weights)
        return higher, total

    start = (jnp.full((1, columns), -1e30, f32), jnp.zeros((HEAD_DIM + 16, columns), f32))
    carry = lax.fori_loop(0, index, lambda at, c: step(at, c, False), start)
    peak, total = step(index, carry, True)
    mass = total[HEAD_DIM : HEAD_DIM + 1]
    ot_ref[0] = (total[:HEAD_DIM] / mass).astype(bf16)
    lse_ref[0, 0] = peak + jnp.log(mass)
    position = index * BLOCK + lax.broadcasted_iota(jnp.int32, peak.shape, 1)
    top_ref[0, 0] = jnp.where(position < length[0], peak, -1e30)

    @pl.when(at_step == last - 3)
    def _():
        for s in range(cuts):
            gather.second(s)

    @pl.when(at_step == last)
    def _():
        for s in range(cuts):
            gather.third(s)
        gather.last()


def attend(length, qt, k, vt, cot, count, number):
    cuts = 1
    heads, _, total = qt.shape
    return pl.pallas_call(
        functools.partial(attend_kernel, cuts),
        grid_spec=pltpu.PrefetchScalarGridSpec(
            num_scalar_prefetch=1,
            grid=(heads, count),
            in_specs=[
                pl.BlockSpec((1, HEAD_DIM, total), lambda h, i, n: (h, 0, 0)),
                pl.BlockSpec((1, total, HEAD_DIM), lambda h, i, n: (h, 0, 0)),
                pl.BlockSpec((1, HEAD_DIM + 16, total), lambda h, i, n: (h, 0, 0)),
                full(cot.shape),
            ],
            out_specs=[
                pl.BlockSpec((1, HEAD_DIM, BLOCK), lambda h, i, n: (i, h, 0)),
                pl.BlockSpec((1, 1, 1, BLOCK), lambda h, i, n: (h, i, 0, 0)),
                pl.BlockSpec((1, 1, 1, BLOCK), lambda h, i, n: (h, i, 0, 0)),
            ]
            + anywhere(1),
            scratch_shapes=[
                pltpu.VMEM(cot.shape, bf16),
            ]
            + Gather.scratch(cuts),
        ),
        out_shape=[
            jax.ShapeDtypeStruct((count, heads * HEAD_DIM, BLOCK), bf16),
            jax.ShapeDtypeStruct((heads, count, 1, BLOCK), f32),
            jax.ShapeDtypeStruct((heads, count, 1, BLOCK), f32),
            jax.ShapeDtypeStruct((8,) + cot.shape, bf16),
        ],
        compiler_params=params(collective_id=number, has_side_effects=True),
        cost_estimate=cost(35),
        name="attend",
    )(length, qt, k, vt, cot)


def revisit_kernel(qt_ref, k_ref, kt_ref, v_ref, ot_ref, got_ref, lse_ref, go_ref, feed_ref, dq_ref, dk_ref, dv_ref, gos_ref, fed_ref, sum_k, sum_v, came_ref, w_send, w_recv, *scratch):
    z, c, t = spot()
    job = Sum(feed_ref, *scratch)
    nt = lax.axis_size("tp")
    h, i = pl.program_id(0), pl.program_id(1)
    count = pl.num_programs(1)
    index = dealt(c, i)
    here = pl.ds(pl.multiple_of(index * BLOCK, BLOCK), BLOCK)
    away = [
        remote(go_ref.at[lax.rem(t + step, nt)], came_ref.at[step], w_send.at[step], w_recv.at[step], tp=lax.rem(t + step, nt))
        for step in range(1, nt)
    ]

    at_step = h * count + i
    end = pl.num_programs(0) * count - 1

    @pl.when(at_step == 0)
    def _():
        greet(False)
        job.first()
        for copy in away:
            copy.start()

    @pl.when(at_step == 3)
    def _():
        job.second()

    @pl.when(at_step == end - 3)
    def _():
        job.third()

    qt, got = qt_ref[0, :, here], got_ref[0]
    lse = lse_ref[0, 0]
    centre = jnp.sum(ot_ref[0].astype(f32) * got.astype(f32), axis=0, keepdims=True)

    @pl.when(i == 0)
    def _():
        sum_k[...] = jnp.zeros_like(sum_k)
        sum_v[...] = jnp.zeros_like(sum_v)
        dq_ref[...] = jnp.zeros_like(dq_ref)

    def step(at, grad, diagonal):
        start = pl.multiple_of(at * BLOCK, BLOCK)
        here = pl.ds(start, BLOCK)
        scores = mm(k_ref[0, here, :], qt)
        probs = jnp.exp(scores - lse)
        if diagonal:
            keys = lax.broadcasted_iota(jnp.int32, scores.shape, 0)
            queries = lax.broadcasted_iota(jnp.int32, scores.shape, 1)
            probs = jnp.where(keys <= queries, probs, 0.0)
        grad_probs = mm(v_ref[0, here, :], got)
        grad_scores = (probs * (grad_probs - centre)).astype(bf16)
        sum_v[:, here] += mm(got, probs.astype(bf16), NT)
        sum_k[:, here] += mm(qt, grad_scores, NT)
        return grad + mm(kt_ref[0, :, here], grad_scores)

    grad = lax.fori_loop(0, index, lambda at, c: step(at, c, False), jnp.zeros(qt.shape, f32))
    dq_ref[0, :, here] = step(index, grad, True) * HEAD_DIM**-0.5

    @pl.when(i == count - 1)
    def _():
        dk_ref[0] = sum_k[...]
        dv_ref[0] = sum_v[...]

    @pl.when(at_step == end)
    def _():
        job.last()
        one, two = job.total()
        fed_ref[: job.half] = one
        fed_ref[job.half :] = two
        total = go_ref[t].astype(f32)
        for step, copy in enumerate(away):
            copy.wait_recv()
            total = total + came_ref[step + 1].astype(f32)
            copy.wait_send()
        gos_ref[...] = total.astype(bf16)


def revisit(qt, k, kt, v, ot, got, lse, go, feed, number):
    heads, _, total = qt.shape
    count = ot.shape[0]
    nt = lax.axis_size("tp")
    whole = pl.BlockSpec((1, HEAD_DIM, total), lambda h, i: (h, 0, 0))
    tall = pl.BlockSpec((1, total, HEAD_DIM), lambda h, i: (h, 0, 0))
    some = pl.BlockSpec((1, HEAD_DIM, BLOCK), lambda h, i: (i, h, 0))
    return pl.pallas_call(
        revisit_kernel,
        grid=(heads, count),
        in_specs=[
            whole,
            tall,
            whole,
            tall,
            some,
            some,
            pl.BlockSpec((1, 1, 1, BLOCK), lambda h, i: (h, i, 0, 0)),
            full(go.shape),
        ]
        + anywhere(1),
        out_specs=[whole, whole, whole, full(go.shape[1:]), full(feed.shape[1:])],
        scratch_shapes=[
            pltpu.VMEM((HEAD_DIM, total), f32),
            pltpu.VMEM((HEAD_DIM, total), f32),
            pltpu.VMEM(go.shape, bf16),
            pltpu.SemaphoreType.DMA((nt,)),
            pltpu.SemaphoreType.DMA((nt,)),
        ]
        + Sum.scratch(*feed.shape[1:]),
        out_shape=[jax.ShapeDtypeStruct((heads, HEAD_DIM, total), f32)] * 3
        + [jax.ShapeDtypeStruct(go.shape[1:], bf16), jax.ShapeDtypeStruct(feed.shape[1:], f32)],
        compiler_params=params(collective_id=number, has_side_effects=True),
        cost_estimate=cost(50),
        name="revisit",
    )(qt, k, kt, v, ot, got, lse, go, feed)


def opening_kernel(cuts, x_ref, wq_ref, wk_ref, wv_ref, wo_ref, wr_ref, wc_ref, vec_ref, na_ref, nm_ref, routes_ref, out_ref, ws_ref, smalls_ref, all_routes_ref, held, stage, small_ref, *sems):
    gather = Gather(x_ref, out_ref, *sems[:3], cuts, stage)
    sends, recvs, local = sems[3:]
    z, c, t = spot()
    ns = lax.axis_size("shard")
    one = jnp.where(c == 0, wq_ref[...].astype(f32), wv_ref[...].astype(f32))
    two = jnp.where(c == 0, wk_ref[...].astype(f32), wo_ref[...].astype(f32).T)
    held[0] = one[:, :128].astype(bf16)
    held[1] = two[:, :128].astype(bf16)
    parts = [v[...].astype(f32) for v in (wr_ref, wc_ref, vec_ref, na_ref, nm_ref)]
    used = sum(v.shape[0] for v in parts)
    parts.append(jnp.zeros((SMALL - used, parts[0].shape[1]), f32))
    small_ref[...] = jnp.concatenate(parts, axis=0).astype(bf16)
    held[2] = jnp.concatenate([one[:, 128:], two[:, 128:]], axis=1).astype(bf16)
    greet()
    started = []

    def go(k, source, target, **where):
        copy = remote(source, target, sends.at[k], recvs.at[k], **where)
        copy.start()
        started.append(copy)

    def came(k, ref):
        remote(ref, ref, sends.at[k], recvs.at[k], ctx=1 - c).wait_recv()

    for step in range(1, ns):
        go(step, held, ws_ref.at[c, z], shard=lax.rem(z + step, ns))
    gather.first()
    for step in range(1, ns):
        go(2 * ns + step, small_ref, smalls_ref.at[z], shard=lax.rem(z + step, ns))
    go(0, held, ws_ref.at[c, z], ctx=1 - c)
    go(ns, routes_ref, all_routes_ref.at[c], ctx=1 - c)
    mine = [
        pltpu.make_async_copy(held, ws_ref.at[c, z], local.at[0]),
        pltpu.make_async_copy(small_ref, smalls_ref.at[z], local.at[1]),
        pltpu.make_async_copy(routes_ref, all_routes_ref.at[c], local.at[2]),
    ]
    for copy in mine:
        copy.start()
    for s in range(cuts):
        gather.second(s)
    for s in range(cuts):
        gather.third(s)
    for step in range(1, ns):
        back = lax.rem(z + ns - step, ns)
        came(step, ws_ref.at[c, back])
        go(ns + step, ws_ref.at[c, back], ws_ref.at[c, back], ctx=1 - c)
    gather.last()
    came(0, ws_ref.at[1 - c, z])
    came(ns, all_routes_ref.at[1 - c])
    for step in range(1, ns):
        back = lax.rem(z + ns - step, ns)
        came(2 * ns + step, smalls_ref.at[back])
        came(ns + step, ws_ref.at[1 - c, back])
    for copy in started:
        copy.wait_send()
    for copy in mine:
        copy.wait()


def opening(x, weights, small, routes, number):
    cuts = 2
    ns = lax.axis_size("shard")
    depth = weights[0].shape[0]
    held = (3, depth, 128)
    vmem = pl.BlockSpec(memory_space=pltpu.VMEM)
    return pl.pallas_call(
        functools.partial(opening_kernel, cuts),
        in_specs=anywhere(1) + [vmem] * (len(weights) + len(small) + 1),
        out_specs=anywhere(4),
        out_shape=[
            jax.ShapeDtypeStruct((8,) + x.shape, x.dtype),
            jax.ShapeDtypeStruct((2, ns) + held, bf16),
            jax.ShapeDtypeStruct((ns, SMALL, depth), bf16),
            jax.ShapeDtypeStruct((2,) + routes.shape, routes.dtype),
        ],
        scratch_shapes=[pltpu.VMEM(held, bf16), pltpu.VMEM(x.shape, x.dtype), pltpu.VMEM((SMALL, depth), bf16)]
        + Gather.scratch(cuts)
        + [
            pltpu.SemaphoreType.DMA((3 * ns,)),
            pltpu.SemaphoreType.DMA((3 * ns,)),
            pltpu.SemaphoreType.DMA((3,)),
        ],
        compiler_params=params(collective_id=number, has_side_effects=True),
        cost_estimate=cost(30),
        name="opening",
    )(x, *weights, *small, routes)


def places(routes_ref, row_ref):
    one = lax.broadcasted_iota(jnp.int32, (BLOCK, BLOCK), 0)
    two = lax.broadcasted_iota(jnp.int32, (BLOCK, BLOCK), 1)
    before = (one < two).astype(bf16)
    blocks, _, per = routes_ref.shape
    for b in range(blocks):
        carry = jnp.zeros((16, 1), f32)
        for at in range(0, per, BLOCK):
            here = slice(at, at + BLOCK)
            expert = lax.broadcasted_iota(jnp.int32, (16, BLOCK), 0)
            member = (routes_ref[b, 0:1, here] == expert) | (routes_ref[b, 1:2, here] == expert)
            rank = mm(member.astype(bf16), before) + carry
            row_ref[:, b * per + at : b * per + at + BLOCK] = jnp.where(member, rank, -1.0)
            carry = carry + jnp.sum(member.astype(f32), axis=1, keepdims=True)


def route_kernel(cuts, o_ref, x_ref, wo_ref, small_ref, prev_ref, routes_ref, cots_ref,
                 att, res_out, base_out, x_out, g_out, gate_ref, row_ref,
                 x_in, wo_in, res, base, a, comb, rows, cots, combs, xs, gs,
                 o_send, o_recv, c_send, c_recv, local, out_sem, x_sem, g_sem, *sems):
    gather = Gather(a, rows, *sems, cuts, relative=True)
    z, c, t = spot()
    nt = lax.axis_size("tp")
    own = 4 * c + t
    near = (t,) + across(t)
    blocks, _, per = routes_ref.shape
    width = rows.shape[2]
    experts = xs.shape[0]
    here = pl.ds(pl.multiple_of(t * BLOCK, BLOCK), BLOCK)
    loads = [
        pltpu.make_async_copy(cots_ref, cots, local.at[0]),
        pltpu.make_async_copy(x_ref, x_in, local.at[1]),
        pltpu.make_async_copy(wo_ref, wo_in, local.at[2]),
    ]
    for copy in loads:
        copy.start()
    greet(False)

    copies = []
    for i in range(o_ref.shape[0]):
        block = zig(c, i)
        copy = remote(o_ref.at[i], att.at[t], o_send.at[i], o_recv.at[t], ctx=block // nt, tp=lax.rem(block, nt))
        copies.append((block == own, copy, pltpu.make_async_copy(o_ref.at[i], att.at[t], local.at[3])))
    for mine, copy, inside in copies:

        @pl.when(jnp.logical_not(mine))
        def _():
            copy.start()

        @pl.when(mine)
        def _():
            inside.start()

    each = per // nt

    def names(b, j, order):
        start = pl.multiple_of(b * per, per)
        mine = row_ref[pl.ds(experts * c + j, 1), pl.ds(start, per)] if order is None else jnp.concatenate(
            [row_ref[pl.ds(experts * c + j, 1), pl.ds(pl.multiple_of(start + o * each, each), each)] for o in order], axis=1
        )
        return lax.broadcasted_iota(jnp.int32, (CAP, mine.shape[1]), 0).astype(f32) == mine

    def fetch(n):
        b, j = n // experts, lax.rem(n, experts)
        here = pl.ds(pl.multiple_of(b * CAP, CAP), CAP)
        hot = names(b, j, None)
        gs[j, here] = mm(hot.astype(bf16), cots[pl.ds(4 * b, 4)].reshape(per, width)).astype(bf16)
        pltpu.make_async_copy(gs.at[j, here], g_out.at[j, here], g_sem.at[n]).start()

    def fetch_x(beside, j, which):
        b = 1 - c if beside else c
        here = pl.ds(pl.multiple_of(b * CAP, CAP), CAP)
        order = [near[k] for k in which]
        hot = names(b, j, order)
        first = 4 * beside + which[0]
        got = mm(hot.astype(bf16), rows[first : first + len(which)].reshape(len(which) * each, width)).astype(bf16)
        gate = jnp.zeros((CAP, 1), f32)
        for k, o in enumerate(order):
            weight = combs[4 * b + o, pl.ds(experts * c + j, 1)]
            gate = gate + jnp.sum(jnp.where(hot[:, k * each : (k + 1) * each], weight, 0.0), axis=1, keepdims=True)
        if which[0] == 0:
            xs[j, here] = got
            gate_ref[j, here] = gate
        else:
            xs[j, here] = xs[j, here] + got
            gate_ref[j, here] = gate_ref[j, here] + gate
            n = b * experts + j
            pltpu.make_async_copy(xs.at[j, here], x_out.at[j, here], x_sem.at[n]).start()

    def all_x(beside, which):
        @pl.loop(0, experts)
        def _(j):
            fetch_x(beside, j, which)

    def fetch_g(first, last):
        @pl.loop(first, last)
        def _(n):
            fetch(n)

    places(routes_ref, row_ref)
    for copy in loads:
        copy.wait()
    fetch_g(0, 2)
    for mine, copy, inside in copies:

        @pl.when(jnp.logical_not(mine))
        def _():
            copy.wait_send()

        @pl.when(mine)
        def _():
            inside.wait()

    mine = lax.rem((own + 1) // 2, 2) == c
    for source in range(nt):

        @pl.when(jnp.logical_or(jnp.logical_not(mine), source != t))
        def _():
            remote(o_ref.at[0], att.at[source], o_send.at[0], o_recv.at[source], ctx=c, tp=t).wait_recv()

    attended = att[...].reshape(-1, BLOCK)
    r = x_in[...].astype(f32) + mm(attended, wo_in[...].reshape(-1, width), TN)
    inverse = lax.rsqrt(jnp.mean(r * r, axis=1, keepdims=True) + epsilon)
    n2 = r * inverse * small_ref[19:20]
    a[...] = n2.astype(bf16)
    gather.first()
    res[...] = r
    _, _, combined, alphas, weights = mixing(n2, small_ref[:16], *columns(prev_ref[:, here], routes_ref[c, :, here]))
    comb[...] = combined.T[:16]
    pairs = []
    for step in range(1, 8):
        other, back = lax.rem(own + step, 8), lax.rem(own + 8 - step, 8)
        where = {"ctx": other // 4, "tp": lax.rem(other, 4)}
        copy = remote(comb, combs.at[own], c_send.at[step], c_recv.at[step], **where)
        copy.start()
        pairs.append((copy, remote(comb, combs.at[back], c_send.at[step], c_recv.at[step], **where)))
    combs[own] = comb[...]
    scale = weights[0] + weights[1] * alphas[0][0] + weights[2] * alphas[1][0]
    base[...] = (
        r
        + scale * n2
        + (weights[1] * alphas[0][1]) * small_ref[16:17]
        + (weights[2] * alphas[1][1]) * small_ref[17:18]
    )
    outs = [
        pltpu.make_async_copy(res, res_out, out_sem.at[0]),
        pltpu.make_async_copy(base, base_out, out_sem.at[1]),
    ]
    for copy in outs:
        copy.start()

    total = blocks * experts
    fetch_g(2, 4)
    gather.second(0)
    fetch_g(4, total)
    gather.second(1)
    gather.own.wait()
    for copy, came in pairs:
        came.wait_recv()
    all_x(0, (0, 1, 2))
    gather.third(0)
    gather.third(1)
    gather.beside()
    all_x(1, (0, 1, 2))
    all_x(0, (3,))
    gather.last(True)
    all_x(1, (3,))

    for copy, came in pairs:
        copy.wait_send()
    for copy in outs:
        copy.wait()

    @pl.loop(0, total)
    def _(n):
        b, j = n // experts, lax.rem(n, experts)
        here = pl.ds(pl.multiple_of(b * CAP, CAP), CAP)
        pltpu.make_async_copy(gs.at[j, here], g_out.at[j, here], g_sem.at[n]).wait()
        pltpu.make_async_copy(xs.at[j, here], x_out.at[j, here], x_sem.at[n]).wait()


def route(o, x, wo, small, prev, routes, cots, experts, number):
    cuts = 2
    own, width = x.shape
    nt = lax.axis_size("tp")
    blocks, _, per = routes.shape
    slots = jax.ShapeDtypeStruct((experts, blocks * CAP, width), bf16)
    vmem = pl.BlockSpec(memory_space=pltpu.VMEM)
    return pl.pallas_call(
        functools.partial(route_kernel, cuts),
        in_specs=anywhere(3) + [vmem, vmem, vmem] + anywhere(1),
        out_specs=[vmem] + anywhere(4) + [vmem, vmem],
        out_shape=[
            jax.ShapeDtypeStruct((nt,) + o.shape[1:], bf16),
            jax.ShapeDtypeStruct((own, width), f32),
            jax.ShapeDtypeStruct((own, width), f32),
            slots,
            slots,
            jax.ShapeDtypeStruct((experts, blocks * CAP, 1), f32),
            jax.ShapeDtypeStruct((16, blocks * per), f32),
        ],
        scratch_shapes=[
            pltpu.VMEM((own, width), bf16),
            pltpu.VMEM(wo.shape, bf16),
            pltpu.VMEM((own, width), f32),
            pltpu.VMEM((own, width), f32),
            pltpu.VMEM((own, width), bf16),
            pltpu.VMEM((16, own), f32),
            pltpu.VMEM((8, own, width), bf16),
            pltpu.VMEM((8, own, width), bf16),
            pltpu.VMEM((8, 16, own), f32),
            pltpu.VMEM(slots.shape, bf16),
            pltpu.VMEM(slots.shape, bf16),
            pltpu.SemaphoreType.DMA((o.shape[0],)),
            pltpu.SemaphoreType.DMA((nt,)),
            pltpu.SemaphoreType.DMA((8,)),
            pltpu.SemaphoreType.DMA((8,)),
            pltpu.SemaphoreType.DMA((4,)),
            pltpu.SemaphoreType.DMA((2,)),
            pltpu.SemaphoreType.DMA((blocks * experts,)),
            pltpu.SemaphoreType.DMA((blocks * experts,)),
        ]
        + Gather.scratch(cuts),
        compiler_params=params(collective_id=number, has_side_effects=True),
        cost_estimate=cost(65),
        name="route",
    )(o, x, wo, small, prev, routes, cots)


def spot_rows(place, c, experts, first, some, values, at):
    lane = lax.broadcasted_iota(jnp.int32, place.shape, 1)
    slot = lax.broadcasted_iota(jnp.int32, (place.shape[0], CAP), 1).astype(f32)
    total = None
    for j in range(some):
        mine = jnp.sum(jnp.where(lane == experts * c + first + j, place, 0.0), axis=1, keepdims=True)
        term = mm((slot == mine).astype(bf16), values[j, at])
        total = term if total is None else total + term
    return total


def spread_kernel(experts, row_ref, feed_ref, out_ref):
    c = lax.axis_index("ctx")
    out_ref[0] = spot_rows(row_ref[...].T, c, experts, 0, feed_ref.shape[0], feed_ref, slice(None)).astype(bf16)


def spread(row, feed, experts):
    some, slots, width = feed.shape
    rows = row.shape[1] // 8
    return pl.pallas_call(
        functools.partial(spread_kernel, experts),
        grid=(8,),
        in_specs=[
            pl.BlockSpec((16, rows), lambda i: (0, i)),
            pl.BlockSpec((some, CAP, width), lambda i: (0, i // 4, 0)),
        ],
        out_specs=pl.BlockSpec((1, rows, width), lambda i: (i, 0, 0)),
        out_shape=jax.ShapeDtypeStruct((8, rows, width), bf16),
        compiler_params=params(),
        cost_estimate=cost(10),
        name="spread",
    )(row, feed)


def combine_kernel(experts, row_ref, *refs):
    values_in, part_ref, feed_ref = refs[:2], refs[2], refs[3]
    out_ref, feed_out, gates_ref = refs[4:7]
    backs, feeds, stage, staged, gsend, gcame, b_sem, f_sem, p_sem, o_sem, g_send, g_recv = refs[7:19]
    job = Sum(None, *refs[19:], stage=stage)
    each, some = backs.shape[0] // 2, feeds.shape[0]
    z, c, t = spot()
    own = 4 * c + t
    width = stage.shape[2]
    loads = [pltpu.make_async_copy(v, backs.at[pl.ds(j * each, each)], b_sem.at[j]) for j, v in enumerate(values_in)]
    more = [pltpu.make_async_copy(feed_ref, feeds, f_sem)]
    more += [pltpu.make_async_copy(part_ref.at[o], staged.at[o], p_sem.at[o]) for o in range(8)]
    for copy in loads + more:
        copy.start()
    greet(False)

    def tile(values, owner):
        start = pl.multiple_of(owner * BLOCK, BLOCK)
        place = row_ref[:, pl.ds(start, BLOCK)].T
        here = pl.ds(pl.multiple_of(owner // 4 * CAP, CAP), CAP)
        count = values.shape[0]
        return spot_rows(place, c, experts, experts - count, count, values, here)

    def back(owner):
        got = tile(backs, owner)
        named = got[:, width:].T
        gsend[owner] = named[:FFN_EXPERTS] + named[16 : 16 + FFN_EXPERTS]
        return got[:, :width]

    for copy in loads:
        copy.wait()
    for k, o in enumerate(job.order):
        stage[k] = back(4 * (1 - c) + o).astype(bf16)
        job.core[k].start()
        job.add(k, back(4 * c + o))
    pairs = []
    for step in range(1, 8):
        other = lax.rem(own + step, 8)
        copy = remote(gsend.at[other], gcame.at[step], g_send.at[step], g_recv.at[step], ctx=other // 4, tp=lax.rem(other, 4))
        copy.start()
        pairs.append(copy)
    for copy in more:
        copy.wait()

    def feed(first, last):
        @pl.loop(first, last)
        def _(n):
            staged[n] = (tile(feeds, n) + staged[n].astype(f32)).astype(bf16)
            pltpu.make_async_copy(staged.at[n], feed_out.at[n], o_sem.at[n]).start()

    feed(0, 4)
    job.third()
    feed(4, 8)
    gates = gsend[own]
    for step, copy in enumerate(pairs):
        copy.wait_recv()
        gates = gates + gcame[step + 1]
        copy.wait_send()
    gates_ref[...] = gates
    job.last()
    one, two = job.total()
    out_ref[: job.half] = one
    out_ref[job.half :] = two

    @pl.loop(0, 8)
    def _(n):
        pltpu.make_async_copy(staged.at[n], feed_out.at[n], o_sem.at[n]).wait()


def combine(row, backs, part, feed, number):
    experts = sum(b.shape[0] for b in backs)
    _, slots, width = feed.shape
    wide = backs[0].shape[2]
    rows = row.shape[1] // 8
    vmem = pl.BlockSpec(memory_space=pltpu.VMEM)
    return pl.pallas_call(
        functools.partial(combine_kernel, experts),
        in_specs=[vmem] + anywhere(4),
        out_specs=[vmem] + anywhere(1) + [vmem],
        out_shape=[
            jax.ShapeDtypeStruct((rows, width), f32),
            jax.ShapeDtypeStruct((8, rows, width), bf16),
            jax.ShapeDtypeStruct((FFN_EXPERTS, rows), f32),
        ],
        scratch_shapes=[
            pltpu.VMEM((experts, slots, wide), bf16),
            pltpu.VMEM(feed.shape, bf16),
            pltpu.VMEM((4, rows, width), bf16),
            pltpu.VMEM((8, rows, width), bf16),
            pltpu.VMEM((8, FFN_EXPERTS, rows), f32),
            pltpu.VMEM((8, FFN_EXPERTS, rows), f32),
            pltpu.SemaphoreType.DMA((2,)),
            pltpu.SemaphoreType.DMA,
            pltpu.SemaphoreType.DMA((8,)),
            pltpu.SemaphoreType.DMA((8,)),
            pltpu.SemaphoreType.DMA((8,)),
            pltpu.SemaphoreType.DMA((8,)),
        ]
        + Sum.scratch(rows, width),
        compiler_params=params(collective_id=number, has_side_effects=True),
        cost_estimate=cost(45),
        name="combine",
    )(row, *backs, part, feed)


def closing_kernel(dq_ref, dk_ref, dv_ref, x_ref, cos_ref, sin_ref, wt_ref, par_ref, go_ref, small_ref, top_ref, ge_ref,
                   out_ref, gsum_ref, ssum_ref, tmax_ref, gall_ref,
                   dqs, dks, dvs, xs, total, row, gother, gcore, gline, gmine, smine, sline, splane, tline, mytop, stage, l_sem, *sems):
    job = Sum(None, *sems[:7], stage=stage)
    sends, recvs = sems[7:]
    z, c, t = spot()
    ns = lax.axis_size("shard")
    heads = dqs.shape[0]
    half = HEAD_DIM // 2
    own = 4 * c + t
    order = [4 * (1 - c) + o for o in job.order] + [4 * c + o for o in job.order]

    def lanes(o):
        return pl.ds(pl.multiple_of(o * BLOCK, BLOCK), BLOCK)

    loads = []
    for n, o in enumerate(order):
        here = lanes(o)
        loads.append(
            [
                pltpu.make_async_copy(dq_ref.at[:, :, here], dqs.at[:, :, here], l_sem.at[n, 0]),
                pltpu.make_async_copy(dk_ref.at[:, :, here], dks.at[:, :, here], l_sem.at[n, 1]),
                pltpu.make_async_copy(dv_ref.at[:, :, here], dvs.at[:, :, here], l_sem.at[n, 2]),
                pltpu.make_async_copy(x_ref.at[here], xs.at[here], l_sem.at[n, 3]),
            ]
        )
    for k in range(4):
        for copy in loads[k] + loads[4 + k]:
            copy.start()
    greet()
    started = []

    def go(k, source, target, **where):
        copy = remote(source, target, sends.at[k], recvs.at[k], **where)
        copy.start()
        started.append(copy)
        return copy

    line_row = lax.broadcasted_iota(jnp.int32, mytop.shape, 0)
    high = jnp.full(mytop.shape, -1e30, f32)
    for h in range(top_ref.shape[0]):
        best = jnp.max(jnp.max(top_ref[h], axis=0), axis=1, keepdims=True)
        high = jnp.where(line_row == h, best, high)
    mytop[...] = high
    tops = [go(3 + ns + s, mytop, tline.at[s], shard=lax.rem(z + s, ns)) for s in range(1, ns)]
    experts = go(1, ge_ref, gall_ref, ctx=1 - c)
    total[...] = jnp.zeros_like(total)
    row[...] = jnp.zeros_like(row)

    def tile(o):
        here = lanes(o)
        cosine, sine = cos_ref[:, here], sin_ref[:, here]

        def turned(g):
            u, w = g[:half], g[half:]
            return jnp.concatenate([u * cosine + w * sine, w * cosine - u * sine], axis=0)

        x = xs[here].astype(f32)
        m = x * lax.rsqrt(jnp.mean(x * x, axis=1, keepdims=True) + epsilon)
        a = (m * par_ref[18:19]).astype(bf16)
        pieces = [turned(dqs[h, :, here]) for h in range(heads)]
        pieces += [turned(dks[h, :, here]) for h in range(heads)]
        pieces += [dvs[h, :, here] for h in range(heads)]
        grads = jnp.concatenate(pieces, axis=0).astype(bf16)
        part = mm(grads, wt_ref[...], TN)
        row[...] += jnp.sum(part * m, axis=0, keepdims=True)
        total[...] += mm(grads, a)
        return part

    for k in range(4):
        for copy in loads[k] + loads[4 + k]:
            copy.wait()
        stage[k] = tile(order[k]).astype(bf16)
        job.core[k].start()
        job.add(k, tile(order[4 + k]))

    cut_rows, depth = gmine.shape[1:]
    mid = cut_rows // 2
    at = lax.broadcasted_iota(jnp.int32, small_ref.shape, 0)
    smalls = small_ref[...] + jnp.where(at == 19, row[...], 0.0)
    for s in range(ns):
        here = slice(s * depth, (s + 1) * depth)
        one = total[:cut_rows, here].astype(bf16)
        two = jnp.concatenate([total[cut_rows:, here].astype(bf16), go_ref[:, here]], axis=0)
        gmine[s] = jnp.where(c == 0, one.astype(f32), two.astype(f32)).astype(bf16)
        gother[s] = jnp.where(c == 0, two.astype(f32), one.astype(f32)).astype(bf16)
        smine[s] = smalls[:, here]
    core = go(0, gother, gcore, ctx=1 - c)
    small = [go(3 + s, smine.at[lax.rem(z + s, ns)], sline.at[s], shard=lax.rem(z + s, ns)) for s in range(1, ns)]
    core.wait_recv()
    gmine[...] = gmine[...] + gcore[...]
    line = [go(3 + 2 * ns + s, gmine.at[lax.rem(z + s, ns)], gline.at[s], shard=lax.rem(z + s, ns)) for s in range(1, ns)]
    job.third()
    for copy in small:
        copy.wait_recv()
    value = smine[z]
    for s in range(1, ns):
        value = value + sline[s]
    splane[0] = value
    plane = []
    for s in range(1, 8):
        other = lax.rem(own + s, 8)
        plane.append(go(3 + 3 * ns + s, splane.at[0], splane.at[s], ctx=other // 4, tp=lax.rem(other, 4)))
    for copy in tops:
        copy.wait_recv()
    high = mytop[...]
    for s in range(1, ns):
        high = jnp.maximum(high, tline[s])
    tline[0] = high
    pair = go(2, tline.at[0], tline.at[ns], ctx=1 - c)
    for copy in line:
        copy.wait_recv()
    value = gmine[z].astype(f32)
    for s in range(1, ns):
        value = value + gline[s].astype(f32)
    gsum_ref[c] = value
    go(3, gsum_ref.at[c], gsum_ref.at[c], ctx=1 - c)
    for copy in plane:
        copy.wait_recv()
    value = splane[0]
    for s in range(1, 8):
        value = value + splane[s]
    ssum_ref[...] = value
    pair.wait_recv()
    tmax_ref[...] = jnp.maximum(tline[0], tline[ns])
    job.last()
    one, two = job.total()
    out_ref[: job.half] = one
    out_ref[job.half :] = two
    remote(gsum_ref.at[1 - c], gsum_ref.at[1 - c], sends.at[3], recvs.at[3], ctx=1 - c).wait_recv()
    experts.wait_recv()
    for copy in started:
        copy.wait_send()


def closing(dq, dk, dv, x, cosine, sine, wt, par, go, small, top, ge, number):
    heads, _, total = dq.shape
    width = x.shape[1]
    rows = total // 8
    ns = lax.axis_size("shard")
    depth = width // ns
    cut_rows = 2 * heads * HEAD_DIM
    pieces = (ns, cut_rows, depth)
    smalls = (ns,) + small.shape[:1] + (depth,)
    vmem = pl.BlockSpec(memory_space=pltpu.VMEM)
    return pl.pallas_call(
        closing_kernel,
        in_specs=anywhere(4) + [vmem] * 7 + anywhere(1),
        out_specs=[vmem, vmem, vmem, vmem] + anywhere(1),
        out_shape=[
            jax.ShapeDtypeStruct((rows, width), f32),
            jax.ShapeDtypeStruct((2, cut_rows, depth), f32),
            jax.ShapeDtypeStruct(smalls[1:], f32),
            jax.ShapeDtypeStruct((8, 128), f32),
            jax.ShapeDtypeStruct(ge.shape, bf16),
        ],
        scratch_shapes=[
            pltpu.VMEM(dq.shape, f32),
            pltpu.VMEM(dq.shape, f32),
            pltpu.VMEM(dq.shape, f32),
            pltpu.VMEM(x.shape, bf16),
            pltpu.VMEM(wt.shape, f32),
            pltpu.VMEM((1, width), f32),
            pltpu.VMEM(pieces, bf16),
            pltpu.VMEM(pieces, bf16),
            pltpu.VMEM(pieces, bf16),
            pltpu.VMEM(pieces, bf16),
            pltpu.VMEM(smalls, f32),
            pltpu.VMEM(smalls, f32),
            pltpu.VMEM((8,) + smalls[1:], f32),
            pltpu.VMEM((ns + 1, 8, 128), f32),
            pltpu.VMEM((8, 128), f32),
            pltpu.VMEM((4, rows, width), bf16),
            pltpu.SemaphoreType.DMA((8, 4)),
        ]
        + Sum.scratch(rows, width)
        + [
            pltpu.SemaphoreType.DMA((3 * ns + 11,)),
            pltpu.SemaphoreType.DMA((3 * ns + 11,)),
        ],
        compiler_params=params(collective_id=number, has_side_effects=True),
        cost_estimate=cost(45),
        name="closing",
    )(dq, dk, dv, x, cosine, sine, wt, par, go, small, top, ge)


def swap_kernel(ge_ref, other_ref, send, recv):
    z, c, t = spot()
    greet_core()
    copy = remote(ge_ref, other_ref, send, recv, ctx=1 - c)
    copy.start()
    copy.wait()


def greet_core():
    z, c, t = spot()
    barrier = pltpu.get_barrier_semaphore()
    pl.semaphore_signal(barrier, inc=1, device_id={"ctx": 1 - c}, device_id_type=MESH)
    pl.semaphore_wait(barrier, 1)


def swap(ge, number):
    return pl.pallas_call(
        swap_kernel,
        in_specs=anywhere(1),
        out_specs=anywhere(1)[0],
        out_shape=jax.ShapeDtypeStruct(ge.shape, ge.dtype),
        scratch_shapes=[pltpu.SemaphoreType.DMA, pltpu.SemaphoreType.DMA],
        compiler_params=params(collective_id=number, has_side_effects=True),
        cost_estimate=cost(5),
        name="swap",
    )(ge)


def columns(previous, routes):
    count, rows = previous.shape
    previous = jnp.concatenate([previous, jnp.zeros((16 - count, rows), f32)], axis=0).T
    at = lax.broadcasted_iota(jnp.int32, (8, rows), 0)
    routes = routes.astype(f32)
    return previous, jnp.where(at == 0, routes[0:1], routes[1:2]).T


def mixing(n2, wrc, previous, routes):
    z = mm(n2, wrc, NT, lax.Precision.HIGHEST)
    lane = lax.broadcasted_iota(jnp.int32, z.shape, 1)
    logits = z + previous
    hot = [lane.astype(f32) == routes[:, r : r + 1] for r in range(2)]
    picked = [jnp.sum(jnp.where(hot[r], logits, 0.0), axis=1, keepdims=True) for r in range(2)]
    most = jnp.maximum(picked[0], picked[1])
    e = [jnp.exp(p - most) for p in picked]
    gates = [v / (e[0] + e[1]) for v in e]
    combine = jnp.where(hot[0], gates[0], 0.0) + jnp.where(hot[1], gates[1], 0.0)

    def column(array, at):
        return jnp.sum(jnp.where(lane == at, array, 0.0), axis=1, keepdims=True)

    alphas = []
    for j in range(2):
        first, second = column(z, EXPERTS + 2 * j), column(z, EXPERTS + 2 * j + 1)
        most = jnp.maximum(first, second)
        a, b = jnp.exp(first - most), jnp.exp(second - most)
        alphas.append((a / (a + b), b / (a + b)))
    weights = [column(combine, FFN_EXPERTS + 1 + j) for j in range(3)]
    return hot, gates, combine, alphas, weights


def turn_kernel(length, res_ref, dn_ref, named_ref, cot_ref, att_ref, wo_ref, par_ref, prev_ref, routes_ref,
                dres_ref, heads_ref, gwo_ref, small_ref, got_ref, send_sem, recv_sem, local_sem):
    z, c, t = spot()
    nt = lax.axis_size("tp")
    own = c * nt + t
    rows, width = res_ref.shape
    greet(False)
    here = pl.ds(pl.multiple_of(t * rows, rows), rows)
    res = res_ref[...]
    gain = par_ref[19:20]
    inverse = lax.rsqrt(jnp.mean(res * res, axis=1, keepdims=True) + epsilon)
    m = res * inverse
    n2 = m * gain
    previous, routes = columns(prev_ref[:, here], routes_ref[c, :, here])
    hot, gates, _, alphas, weights = mixing(n2, par_ref[:16], previous, routes)
    position = own * rows + lax.broadcasted_iota(jnp.int32, cot_ref.shape, 0)
    g = jnp.where(position < length[0], cot_ref[...].astype(f32), 0.0)
    inner = jnp.sum(g * n2, axis=1, keepdims=True)
    onto = [jnp.sum(g * par_ref[16 + j : 17 + j], axis=1, keepdims=True) for j in range(2)]
    named = named_ref[...].T
    lane = lax.broadcasted_iota(jnp.int32, hot[0].shape, 1)
    wide = lax.broadcasted_iota(jnp.int32, named.shape, 1).astype(f32)
    local = {
        FFN_EXPERTS + 1: inner,
        FFN_EXPERTS + 2: alphas[0][0] * inner + alphas[0][1] * onto[0],
        FFN_EXPERTS + 3: alphas[1][0] * inner + alphas[1][1] * onto[1],
    }
    dgates = []
    for r in range(2):
        name = routes[:, r : r + 1]
        there = jnp.where(wide == name, named, 0.0)
        there = jnp.where(name < FFN_EXPERTS, jnp.sum(there, axis=1, keepdims=True), 0.0)
        for e, value in local.items():
            there = there + jnp.where(name == e, value, 0.0)
        dgates.append(there)
    mean = gates[0] * dgates[0] + gates[1] * dgates[1]
    dz = jnp.where(hot[0], gates[0] * (dgates[0] - mean), 0.0)
    dz = dz + jnp.where(hot[1], gates[1] * (dgates[1] - mean), 0.0)
    for j in range(2):
        da = weights[1 + j] * inner
        db = weights[1 + j] * onto[j]
        centre = alphas[j][0] * da + alphas[j][1] * db
        dz = dz + jnp.where(lane == EXPERTS + 2 * j, alphas[j][0] * (da - centre), 0.0)
        dz = dz + jnp.where(lane == EXPERTS + 2 * j + 1, alphas[j][1] * (db - centre), 0.0)
    scale = weights[0] + weights[1] * alphas[0][0] + weights[2] * alphas[1][0]
    highest = lax.Precision.HIGHEST
    dn2 = dn_ref[...] + scale * g + mm(dz, par_ref[:16], NN, highest)
    q = dn2 * gain
    dres = g + inverse * (q - m * jnp.mean(q * m, axis=1, keepdims=True))
    dres_ref[...] = dres
    da = dres.astype(bf16)
    wo = wo_ref[...].reshape(-1, width)
    got_ref[...] = mm(wo, da, NT).astype(bf16).reshape(got_ref.shape)

    core = lax.rem((own + 1) // 2, 2)
    slot = 2 * (own // 4) + lax.rem(own, 4) // 2
    copies = []
    for target in range(nt):
        inside = jnp.logical_and(core == c, target == t)
        copy = remote(got_ref.at[target], heads_ref.at[slot], send_sem.at[target], recv_sem.at[slot], ctx=core, tp=target)
        copies.append((inside, copy, pltpu.make_async_copy(got_ref.at[target], heads_ref.at[slot], local_sem)))
    for inside, copy, kept in copies:

        @pl.when(jnp.logical_not(inside))
        def _():
            copy.start()

        @pl.when(inside)
        def _():
            kept.start()

    small_ref[0:16] = mm(dz, n2, TN, highest)
    small_ref[16:24] = jnp.zeros((8, width), f32)
    small_ref[16:17] = jnp.sum((weights[1] * alphas[0][1]) * g, axis=0, keepdims=True)
    small_ref[17:18] = jnp.sum((weights[2] * alphas[1][1]) * g, axis=0, keepdims=True)
    small_ref[18:19] = jnp.sum(dn2 * m, axis=0, keepdims=True)
    att = att_ref[...].reshape(-1, rows)
    gwo_ref[...] = mm(att, da).astype(bf16).reshape(gwo_ref.shape)
    for inside, copy, kept in copies:

        @pl.when(jnp.logical_not(inside))
        def _():
            copy.wait_send()

        @pl.when(inside)
        def _():
            kept.wait()

    for i in range(heads_ref.shape[0]):

        @pl.when(zig(c, i) != own)
        def _():
            remote(got_ref.at[0], heads_ref.at[i], send_sem.at[0], recv_sem.at[i], ctx=c, tp=t).wait_recv()


def turn(length, res, dn, named, cot, att, wo, small, prev, routes, count, number):
    rows, width = res.shape
    nt = lax.axis_size("tp")
    args = (res, dn, named, cot, att, wo, small, prev, routes)
    return pl.pallas_call(
        turn_kernel,
        grid_spec=pltpu.PrefetchScalarGridSpec(
            num_scalar_prefetch=1,
            grid=(1,),
            in_specs=[full(v.shape) for v in args],
            out_specs=[full((rows, width))] + anywhere(1) + [full(wo.shape), full((24, width))],
            scratch_shapes=[
                pltpu.VMEM(att.shape, bf16),
                pltpu.SemaphoreType.DMA((nt,)),
                pltpu.SemaphoreType.DMA((count,)),
                pltpu.SemaphoreType.DMA,
            ],
        ),
        out_shape=[
            jax.ShapeDtypeStruct((rows, width), f32),
            jax.ShapeDtypeStruct((count,) + att.shape[1:], bf16),
            jax.ShapeDtypeStruct(wo.shape, bf16),
            jax.ShapeDtypeStruct((24, width), f32),
        ],
        compiler_params=params(collective_id=number, has_side_effects=True),
        cost_estimate=cost(18),
        name="turn",
    )(length, *args)


def finish_kernel(x_ref, dn_ref, dres_ref, small_ref, base_ref, feed_ref, gw_ref, gs_ref, top_ref, wq_ref, wk_ref, limit_ref, length_ref, own_a, own_b, other_a, other_b, *outs):
    each = own_a.shape[0]
    local = 2 * each
    gin_ref, out_ref, gate_ref, up_ref, down_ref = outs[:5]
    x = x_ref[...].astype(f32)
    inverse = lax.rsqrt(jnp.mean(x * x, axis=1, keepdims=True) + epsilon)
    m = x * inverse
    q = dn_ref[...] * small_ref[18:19]
    gin_ref[...] = dres_ref[...] + inverse * (q - m * jnp.mean(q * m, axis=1, keepdims=True))
    core = lax.axis_index("ctx")
    rows = x.shape[0]
    first = (core * lax.axis_size("tp") + lax.axis_index("tp")) * pl.num_programs(0) + pl.program_id(0)
    position = first * rows + lax.broadcasted_iota(jnp.int32, x.shape, 0)
    out_ref[...] = jnp.where(position < length_ref[0], base_ref[...] + feed_ref[...], 0.0).astype(bf16)
    for k, target in enumerate((gate_ref, up_ref, down_ref)):
        for j in range(local):
            own, other = ((own_a, other_a), (own_b, other_b))[j // each]
            mine, theirs = own[j % each, k].astype(f32), other[j % each, k].astype(f32)
            target[j] = jnp.where(core == 0, mine, theirs)
            target[local + j] = jnp.where(core == 0, theirs, mine)

    @pl.when(pl.program_id(0) == 0)
    def _():
        gq, gk, gv, go, gnorm, gmoe, grouter, gconst, gvec, fac_ref, cq_ref, ck_ref = outs[5:]
        width = wq_ref.shape[1]
        flat = gw_ref[...].reshape(4 * width, gw_ref.shape[2])
        for k, target in enumerate((gq, gk, gv)):
            target[...] = flat[k * width : (k + 1) * width].T
        go[...] = flat[3 * width :]
        sums = gs_ref[...]
        grouter[...] = sums[:EXPERTS]
        gconst[...] = sums[EXPERTS : EXPERTS + 4]
        gvec[...] = sums[16:18]
        gmoe[...] = sums[18:19]
        gnorm[...] = sums[19:20]
        factors = limit_ref[0] / jnp.maximum(top_ref[...], limit_ref[0])
        for h in range(fac_ref.shape[0]):
            fac_ref[h] = factors[h, 0]
        lane = lax.broadcasted_iota(jnp.int32, (1, width), 1)
        root = jnp.zeros((1, width), f32)
        for h in range(width // HEAD_DIM):
            root = jnp.where(lane // HEAD_DIM == h, jnp.sqrt(factors[h : h + 1, :1]), root)
        cq_ref[...] = (wq_ref[...].astype(f32) * root).astype(bf16)
        ck_ref[...] = (wk_ref[...].astype(f32) * root).astype(bf16)


def finish_rows(x, dn, dres, small, base, feed, gw, gs, top, wq, wk, limit, length, own, other):
    rows, width = x.shape
    each, kinds, depth, hidden = own[0].shape
    local = 2 * each
    steps = 4 if depth % 64 == 0 else 1
    tile, deep = rows // steps, depth // steps
    by_row = pl.BlockSpec((tile, width), lambda i: (i, 0))
    expert_out = pl.BlockSpec((2 * local, deep, hidden), lambda i: (0, i, 0))
    once = [
        jax.ShapeDtypeStruct(shape, f32)
        for shape in [wq.shape] * 3
        + [(wq.shape[1], depth), (1, depth), (1, depth), (EXPERTS, depth), (4, depth), (2, depth), (wq.shape[1] // HEAD_DIM,)]
    ] + [jax.ShapeDtypeStruct(wq.shape, bf16)] * 2
    return pl.pallas_call(
        finish_kernel,
        grid=(steps,),
        in_specs=[
            by_row,
            by_row,
            by_row,
            full(small.shape),
            by_row,
            by_row,
            full(gw.shape),
            full(gs.shape),
            full(top.shape),
            full(wq.shape),
            full(wk.shape),
            pl.BlockSpec(memory_space=pltpu.SMEM),
            pl.BlockSpec(memory_space=pltpu.SMEM),
        ]
        + [pl.BlockSpec((each, kinds, deep, hidden), lambda i: (0, 0, i, 0))] * 4,
        out_specs=[by_row, by_row, expert_out, expert_out, expert_out] + [full(v.shape) if v.ndim > 1 else pl.BlockSpec(memory_space=pltpu.SMEM) for v in once],
        out_shape=[
            jax.ShapeDtypeStruct((rows, width), f32),
            jax.ShapeDtypeStruct((rows, width), bf16),
        ]
        + [jax.ShapeDtypeStruct((2 * local, depth, hidden), f32)] * 3
        + once,
        compiler_params=params(),
        cost_estimate=cost(8),
        name="finish_rows",
    )(x, dn, dres, small, base, feed, gw, gs, top, wq, wk, limit, length, *own, *other)


def expert_kernel(start, first, x_ref, g_ref, gate_ref, w_ref, feed_ref, back_ref, gw_ref):
    parts, _, _, depth, hidden = w_ref.shape
    width = parts * depth
    wg, wu, wd = [w_ref[:, 0, k].reshape(width, hidden) for k in range(3)]
    x, g, gate = x_ref[0], g_ref[0], gate_ref[0]
    gate_pre = mm(x, wg)
    up = mm(x, wu)
    sigmoid = 1.0 / (1.0 + jnp.exp(-gate_pre))
    activated = gate_pre * sigmoid
    inner = (activated * up).astype(bf16)
    g32 = g.astype(f32)
    dout = (gate * g32).astype(bf16)
    dinner = mm(dout, wd)
    out = mm(inner, wd, NT)
    feed_ref[0] = (gate * out).astype(bf16)
    dgate = jnp.sum(g32 * out, axis=1, keepdims=True)
    dpre = (dinner * up * sigmoid * (1.0 + gate_pre * (1.0 - sigmoid))).astype(bf16)
    dup = (dinner * activated).astype(bf16)
    back_ref[0, :, :width] = (mm(dpre, wg, NT) + mm(dup, wu, NT)).astype(bf16)
    lane = lax.broadcasted_iota(jnp.int32, (dgate.shape[0], back_ref.shape[2] - width), 1)
    coarse = dgate.astype(bf16).astype(f32)
    at = first[0] + start + pl.program_id(0)
    extra = jnp.where(lane == at, coarse, jnp.where(lane == at + 16, dgate - coarse, 0.0))
    back_ref[0, :, width:] = extra.astype(bf16)
    for k, (left, right) in enumerate(((x, dpre), (x, dup), (dout, inner))):
        gw_ref[:, 0, k] = mm(left, right, TN).reshape(parts, depth, hidden).astype(bf16)


def expert(start, first, x, g, gate, w):
    slots, width = x.shape[1:]
    parts, some, kinds, depth, hidden = w.shape
    pick = lambda i, f: (start + i, 0, 0)
    return pl.pallas_call(
        functools.partial(expert_kernel, start),
        grid_spec=pltpu.PrefetchScalarGridSpec(
            num_scalar_prefetch=1,
            grid=(some,),
            in_specs=[
                pl.BlockSpec((1, slots, width), pick),
                pl.BlockSpec((1, slots, width), pick),
                pl.BlockSpec((1, slots, 1), pick),
                pl.BlockSpec((parts, 1, kinds, depth, hidden), lambda i, f: (0, i, 0, 0, 0)),
            ],
            out_specs=[
                pl.BlockSpec((1, slots, width), lambda i, f: (i, 0, 0)),
                pl.BlockSpec((1, slots, width + EXTRA), lambda i, f: (i, 0, 0)),
                pl.BlockSpec((parts, 1, kinds, depth, hidden), lambda i, f: (0, i, 0, 0, 0)),
            ],
        ),
        out_shape=[
            jax.ShapeDtypeStruct((some, slots, width), bf16),
            jax.ShapeDtypeStruct((some, slots, width + EXTRA), bf16),
            jax.ShapeDtypeStruct(w.shape, bf16),
        ],
        compiler_params=params(),
        cost_estimate=cost(12 * some),
        name="expert",
    )(first, x, g, gate, w)


def shards(
    hidden_in,
    cotangent,
    lengths,
    routes,
    prev_logits,
    norm_attn,
    w_query,
    w_key,
    w_value,
    w_out,
    norm_moe,
    w_router,
    w_const,
    const_vec,
    w_gate,
    w_up,
    w_down,
    threshold,
):
    plane = ("ctx", "tp")
    core = lax.axis_index("ctx")
    nc, nt, ns = lax.axis_size("ctx"), lax.axis_size("tp"), lax.axis_size("shard")
    own, width = hidden_in.shape
    per = own * nt
    total = per * nc
    depth = w_gate.shape[1]
    heads = w_query.shape[1] // HEAD_DIM
    head_width = heads * HEAD_DIM
    local = FFN_EXPERTS // nc
    count = total // BLOCK // nc
    routes, prev = routes.T, prev_logits.T
    first = (core * local).astype(jnp.int32)[None]

    expert_w = []
    for start in range(0, local, 2):
        pieces = [
            lax.dynamic_slice_in_dim(w, core * local + start, 2, 0) for w in (w_gate, w_up, w_down)
        ]
        expert_w.append(lax.all_gather(jnp.stack(pieces, axis=1), "shard", axis=0, tiled=False))
    rows_all, attention_w, small, routes_all = opening(
        hidden_in,
        (w_query, w_key, w_value, w_out),
        (w_router.T, w_const.T, const_vec, norm_attn[None], norm_moe[None]),
        routes,
        0,
    )
    rows_all = rows_all.reshape(total, width)
    cosine, sine = rope_tables(total)

    qt, kt, k, v, vt, wt, small, out_w = project(rows_all, attention_w, small, cosine, sine, heads, 8)
    ot, lse, top, cot_all = attend(lengths, qt, k, vt, cotangent, count, 1)
    att, res, base, x_slots, g_slots, gate_slots, row_at = route(
        ot, hidden_in, out_w, small, prev, routes_all, cot_all, local, 2
    )

    feeds, backs, grads = [], [], []
    for j, w in enumerate(expert_w):
        if grads:
            part = spread(row_at, feeds[0], local)
            x_slots, part = lax.optimization_barrier((x_slots, part))
        feed, back, raw = expert(2 * j, first, x_slots, g_slots, gate_slots, w)
        feeds.append(feed)
        backs.append(back)
        grads.append(lax.psum_scatter(raw, "shard", scatter_dimension=0, tiled=True)[0])
    back, feed, named = combine(row_at, backs, part, feeds[1], 3)

    dres, got, grad_out, gsmall = turn(
        lengths, res, back, named, cotangent, att, out_w, small, prev, routes_all, count, 4
    )
    dq, dk, dv, grad_out, feed = revisit(qt, k, kt, v, ot, got, lse, grad_out, feed, 5)
    part, grad_w, gsmall, top, other = closing(
        dq, dk, dv, rows_all, cosine, sine, wt, small, grad_out, gsmall, top, grads[0], 6
    )
    late, top = lax.optimization_barrier((grads[1], top))
    others = (other, swap(late, 7))
    (grad_input, output, grad_gate, grad_up, grad_down, grad_q, grad_k, grad_v, grad_out, grad_norm_attn, grad_norm_moe,
     grad_router, grad_const, grad_vec, factors, clipped_query, clipped_key) = finish_rows(
        hidden_in, part, dres, small, base, feed, grad_w, gsmall, top, w_query, w_key, threshold, lengths, grads, others
    )
    return (
        output,
        grad_input,
        grad_norm_attn[0],
        grad_q,
        grad_k,
        grad_v,
        grad_out,
        grad_norm_moe[0],
        grad_router.T,
        grad_const.T,
        grad_vec,
        grad_gate,
        grad_up,
        grad_down,
        factors,
        clipped_query,
        clipped_key,
    )


def solution(mesh):
    return jax.shard_map(
        shards,
        mesh=mesh,
        in_specs=(
            P(("shard", "ctx", "tp"), None),
            P(("shard", "ctx", "tp"), None),
            P("shard"),
            P(("shard", "ctx"), None),
            P(("shard", "ctx"), None),
            P("shard"),
            P("shard", "tp"),
            P("shard", "tp"),
            P("shard", "tp"),
            P("tp", "shard"),
            P("shard"),
            P("shard", None),
            P("shard", None),
            P(None, "shard"),
            P(None, "shard", "tp"),
            P(None, "shard", "tp"),
            P(None, "shard", "tp"),
            P(),
        ),
        out_specs=(
            P(("shard", "ctx", "tp"), None),
            P(("shard", "ctx", "tp"), None),
            P("shard"),
            P("shard", "tp"),
            P("shard", "tp"),
            P("shard", "tp"),
            P("tp", "shard"),
            P("shard"),
            P("shard", None),
            P("shard", None),
            P(None, "shard"),
            P(None, "shard", "tp"),
            P(None, "shard", "tp"),
            P(None, "shard", "tp"),
            P("tp"),
            P("shard", "tp"),
            P("shard", "tp"),
        ),
        check_vma=False,
    )
```

```python
import functools

import jax
import jax.numpy as jnp
import numpy as np
from jax import lax
from jax.experimental import pallas as pl
from jax.experimental.pallas import tpu as pltpu
from jax.sharding import PartitionSpec as P

HEAD_DIM = 64
EXPERTS = 12
FFN_EXPERTS = 8
CAP = 512
BLOCK = 512
EXTRA = 128
SMALL = 32
MESH = pl.DeviceIdType.MESH

epsilon = 1e-06
rope_base = 10000.0
bf16 = jnp.bfloat16
f32 = jnp.float32

NN = (((1,), (0,)), ((), ()))
NT = (((1,), (1,)), ((), ()))
TN = (((0,), (0,)), ((), ()))


def mm(left, right, dims=NN, precision=None):
    return lax.dot_general(
        left, right, dims, preferred_element_type=f32, precision=precision
    )


def params(mib=56, **more):
    return pltpu.CompilerParams(vmem_limit_bytes=mib * 1024 * 1024, **more)


def cost(us):
    return pl.CostEstimate(flops=int(us * 1e9), bytes_accessed=int(us * 3e6), transcendentals=0)


def full(shape):
    return pl.BlockSpec(shape, lambda *_: (0,) * len(shape))


def rope_tables(total):
    half = HEAD_DIM // 2
    freqs = np.float32(rope_base) ** (np.float32(-2.0) * np.arange(half, dtype=np.float32) / np.float32(HEAD_DIM))
    angles = freqs.astype(np.float32)[:, None] * np.arange(total, dtype=np.float32)[None, :]
    angles = angles.astype(np.float64)
    return jnp.asarray(np.cos(angles), f32), jnp.asarray(np.sin(angles), f32)


def zig(core, i):
    return 4 * (i // 2) + (core if i % 2 == 0 else 3 - core)


def anywhere(count):
    return [pl.BlockSpec(memory_space=pl.ANY)] * count


def spot():
    return lax.axis_index("shard"), lax.axis_index("ctx"), lax.axis_index("tp")


def across(t):
    return t + 1 - 2 * lax.rem(t, 2), lax.rem(t + 2, 4), 3 - t


def remote(source, target, sends, recvs, **where):
    return pltpu.make_async_remote_copy(
        src_ref=source,
        dst_ref=target,
        send_sem=sends,
        recv_sem=recvs,
        device_id=where,
        device_id_type=MESH,
    )


def greet(depth=True):
    z, c, t = spot()
    nc, nt, ns = lax.axis_size("ctx"), lax.axis_size("tp"), lax.axis_size("shard")
    barrier = pltpu.get_barrier_semaphore()
    for step in range(1, nc * nt):
        other = lax.rem(c * nt + t + step, nc * nt)
        pl.semaphore_signal(
            barrier,
            inc=1,
            device_id={"ctx": other // nt, "tp": lax.rem(other, nt)},
            device_id_type=MESH,
        )
    if depth:
        for step in range(1, ns):
            pl.semaphore_signal(
                barrier,
                inc=1,
                device_id={"shard": lax.rem(z + step, ns)},
                device_id_type=MESH,
            )
    pl.semaphore_wait(barrier, nc * nt - 1 + (ns - 1 if depth else 0))


class Gather:
    KINDS = 9

    def __init__(self, x, out, sends, recvs, own, cuts, stage=None, relative=False):
        z, c, t = spot()
        tx, ty, td = across(t)
        rows = x.shape[0] // cuts
        half = rows // 2
        self.cuts = cuts
        sib = {"ctx": 1 - c}
        px, py = {"tp": tx}, {"tp": ty}
        near = (t, tx, ty, td)
        if relative:
            here, there = list(range(8)), list(range(8))
            mine = (1, 2, 4)
            passed = ((1, 5), (1, 3), (2, 6), (2, 3), (3, 7), (3, 7))
        else:
            here = [4 * c + n for n in near] + [4 * (1 - c) + n for n in near]
            there = here[:4]
            mine = (here[0],) * 3
            passed = tuple((here[n], here[n]) for n in (1, 1, 2, 2, 3, 3))
        self.load = None if stage is None else pltpu.make_async_copy(x, stage, own.at[0])
        self.own = pltpu.make_async_copy(x if stage is None else stage, out.at[here[0]], own.at[1])

        def parts(s):
            whole = pl.ds(s * rows, rows)
            one, two = pl.ds(s * rows, half), pl.ds(s * rows + half, half)
            return whole, one, two

        def copies(s):
            whole, one, two = parts(s)
            made = [
                remote(x.at[whole], out.at[slot, whole], sends.at[s, k], recvs.at[s, k], **where)
                for k, (slot, where) in enumerate(zip(mine, (px, py, sib)))
            ]
            ways = ((whole, sib), (one, py), (whole, sib), (two, px), (one, sib), (two, sib))
            for k, ((source, target), (part, where)) in enumerate(zip(passed, ways)):
                made.append(
                    remote(out.at[source, part], out.at[target, part], sends.at[s, k + 3], recvs.at[s, k + 3], **where)
                )
            return made

        self.copies = [copies(s) for s in range(cuts)]

        def arrivals(s):
            whole, one, two = parts(s)
            where = [(1, whole), (2, whole), (4, whole), (5, whole), (3, one), (6, whole), (3, two), (7, one), (7, two)]
            return [
                remote(out.at[here[n], part], out.at[here[n], part], sends.at[s, k], recvs.at[s, k], **sib)
                for k, (n, part) in enumerate(where)
            ]

        self.arrivals = [arrivals(s) for s in range(cuts)]

    @staticmethod
    def scratch(cuts):
        return [
            pltpu.SemaphoreType.DMA((cuts, Gather.KINDS)),
            pltpu.SemaphoreType.DMA((cuts, Gather.KINDS)),
            pltpu.SemaphoreType.DMA((2,)),
        ]

    def first(self):
        for s in range(self.cuts):
            for k in (0, 1, 2):
                self.copies[s][k].start()
        (self.load or self.own).start()

    def second(self, s):
        if self.load is not None and s == 0:
            self.load.wait()
            self.own.start()
        self.arrivals[s][0].wait_recv()
        self.copies[s][4].start()
        self.copies[s][3].start()
        self.arrivals[s][1].wait_recv()
        self.copies[s][6].start()
        self.copies[s][5].start()

    def third(self, s):
        for k in (4, 6):
            self.arrivals[s][k].wait_recv()
            self.copies[s][7 if k == 4 else 8].start()

    def beside(self):
        for s in range(self.cuts):
            for k in (2, 3, 5):
                self.arrivals[s][k].wait_recv()

    def last(self, rest=False):
        for s in range(self.cuts):
            for k in (7, 8) if rest else (2, 3, 5, 7, 8):
                self.arrivals[s][k].wait_recv()
        for s in range(self.cuts):
            for k in range(self.KINDS):
                self.copies[s][k].wait_send()
        if not rest:
            self.own.wait()


class Sum:
    def __init__(self, p, held, came, across_in, across_out, sends, recvs, loads, stage=None):
        z, c, t = spot()
        self.t = t
        tx, ty, td = across(t)
        half = held.shape[1] // 2
        self.half = half
        self.one, self.two = pl.ds(0, half), pl.ds(half, half)
        self.order = (td, tx, ty, t)
        self.held, self.came, self.inn = held, came, across_in
        sib, px, py = {"ctx": 1 - c}, {"tp": tx}, {"tp": ty}
        self.core = []
        for k, o in enumerate(self.order):
            source = p.at[4 * (1 - c) + o] if stage is None else stage.at[k]
            self.core.append(remote(source, came.at[o], sends.at[k], recvs.at[k], **sib))
        self.loads = None
        if stage is None:
            self.loads = [pltpu.make_async_copy(p.at[4 * c + o], held.at[o], loads.at[k]) for k, o in enumerate(self.order)]

        def send(k, source, slot, where):
            return remote(source, across_in.at[slot], sends.at[k], recvs.at[k], **where)

        self.side = {
            "dx": send(4, held.at[td, self.one], 0, px),
            "dy": send(5, held.at[td, self.two], 1, py),
            "x": send(6, held.at[tx, self.one], 2, px),
            "y": send(7, held.at[ty, self.two], 3, py),
            "cy": send(8, across_out.at[0], 4, py),
            "cx": send(9, across_out.at[1], 5, px),
        }
        self.out = across_out
        self.near = (tx, ty, td)

    @staticmethod
    def scratch(rows, width):
        return [
            pltpu.VMEM((4, rows, width), bf16),
            pltpu.VMEM((4, rows, width), bf16),
            pltpu.VMEM((6, rows // 2, width), bf16),
            pltpu.VMEM((2, rows // 2, width), bf16),
            pltpu.SemaphoreType.DMA((10,)),
            pltpu.SemaphoreType.DMA((10,)),
            pltpu.SemaphoreType.DMA((4,)),
        ]

    def first(self):
        for k in range(4):
            self.core[k].start()
            self.loads[k].start()

    def add(self, k, mine):
        o = self.order[k]
        self.core[k].wait_recv()
        self.held[o] = (mine + self.came[o].astype(mine.dtype)).astype(bf16)
        for name in (("dx", "dy"), ("x",), ("y",), ())[k]:
            self.side[name].start()

    def second(self):
        for k, o in enumerate(self.order):
            self.loads[k].wait()
            self.add(k, self.held[o])

    def third(self):
        tx, ty, td = self.near
        self.side["dx"].wait_recv()
        self.out[0] = self.held[ty, self.one] + self.inn[0]
        self.side["cy"].start()
        self.side["dy"].wait_recv()
        self.out[1] = self.held[tx, self.two] + self.inn[1]
        self.side["cx"].start()

    def last(self):
        for k in ("x", "y", "cy", "cx"):
            self.side[k].wait_recv()
        for copy in self.core + list(self.side.values()):
            copy.wait_send()

    def total(self):
        def add(part, a, b):
            return self.held[self.t, part].astype(f32) + self.inn[a].astype(f32) + self.inn[b].astype(f32)

        return add(self.one, 2, 4), add(self.two, 3, 5)


def qkv_kernel(x_ref, w_ref, s_ref, cos_ref, sin_ref, qt_ref, kt_ref, k_ref, v_ref, vt_ref, wt_ref, small_ref, wo_ref, wo, send, recv, local):
    heads = qt_ref.shape[0]
    width = heads * HEAD_DIM
    half = HEAD_DIM // 2
    z, c, t = spot()
    nt = lax.axis_size("tp")
    mid = width // 2
    mine, theirs = pl.ds(c * mid, mid), pl.ds((1 - c) * mid, mid)
    away, came, onward, there = [], [], [], []
    for step in range(1, nt):
        back = lax.rem(t + nt - step, nt)
        away.append(remote(wo.at[mine], wo_ref.at[t, mine], send.at[step], recv.at[step], tp=lax.rem(t + step, nt)))
        ref = wo_ref.at[back, mine]
        came.append(remote(ref, ref, send.at[nt + step], recv.at[step], ctx=1 - c))
        onward.append(remote(ref, ref, send.at[nt + step], recv.at[nt + step], ctx=1 - c))
        ref = wo_ref.at[back, theirs]
        there.append(remote(ref, ref, send.at[nt + step], recv.at[nt + step], ctx=1 - c))
    own = pltpu.make_async_copy(wo, wo_ref.at[t], local)
    i = pl.program_id(0)

    @pl.when(i == 0)
    def _():
        def flat(v):
            return v.astype(f32).reshape(v.shape[0] * v.shape[1], v.shape[2])

        def whole(core, which):
            rest = flat(w_ref[core, :, 2])[:, which * (width - 128) : (which + 1) * (width - 128)]
            return jnp.concatenate([flat(w_ref[core, :, which]), rest], axis=1).T.astype(bf16)

        wo[...] = whole(1, 1)
        greet(False)
        for copy in away:
            copy.start()
        own.start()
        wt_ref[:width] = whole(0, 0)
        wt_ref[width : 2 * width] = whole(0, 1)
        wt_ref[2 * width :] = whole(1, 0)
        small_ref[...] = jnp.concatenate([s_ref[n].astype(f32) for n in range(s_ref.shape[0])], axis=1)

    x = x_ref[...].astype(f32)
    inverse = lax.rsqrt(jnp.mean(x * x, axis=1, keepdims=True) + epsilon)
    a = (x * inverse * small_ref[18:19]).astype(bf16)
    y = mm(wt_ref[...], a, NT)
    cosine, sine = cos_ref[...], sin_ref[...]

    def turned(first):
        u, w = y[first : first + half], y[first + half : first + HEAD_DIM]
        return jnp.concatenate([u * cosine - w * sine, w * cosine + u * sine], axis=0)

    for h in range(heads):
        at = h * HEAD_DIM
        qt_ref[h] = (turned(at) * HEAD_DIM**-0.5).astype(bf16)
        key = turned(width + at)
        kt_ref[h] = key.astype(bf16)
        k_ref[h] = key.T.astype(bf16)
        value = y[2 * width + at : 2 * width + at + HEAD_DIM]
        v_ref[h] = value.T.astype(bf16)
        vt_ref[h, :HEAD_DIM] = value.astype(bf16)
        vt_ref[h, HEAD_DIM:] = jnp.ones((16, value.shape[1]), bf16)

    @pl.when(i == pl.num_programs(0) - 2)
    def _():
        for copy, forth in zip(came, onward):
            copy.wait_recv()
            forth.start()

    @pl.when(i == pl.num_programs(0) - 1)
    def _():
        for copy in there:
            copy.wait_recv()
        for copy in away + onward:
            copy.wait_send()
        own.wait()


def project(rows, w, small, cosine, sine, heads, number):
    total, width = rows.shape
    tile = BLOCK
    out = heads * HEAD_DIM
    nt = lax.axis_size("tp")
    shapes = [
        jax.ShapeDtypeStruct((heads, HEAD_DIM, total), bf16),
        jax.ShapeDtypeStruct((heads, HEAD_DIM, total), bf16),
        jax.ShapeDtypeStruct((heads, total, HEAD_DIM), bf16),
        jax.ShapeDtypeStruct((heads, total, HEAD_DIM), bf16),
        jax.ShapeDtypeStruct((heads, HEAD_DIM + 16, total), bf16),
        jax.ShapeDtypeStruct((3 * out, width), bf16),
        jax.ShapeDtypeStruct((SMALL, width), f32),
        jax.ShapeDtypeStruct((nt, out, width), bf16),
    ]
    return pl.pallas_call(
        qkv_kernel,
        grid=(total // tile,),
        in_specs=[
            pl.BlockSpec((tile, width), lambda i: (i, 0)),
            full(w.shape),
            full(small.shape),
            pl.BlockSpec((HEAD_DIM // 2, tile), lambda i: (0, i)),
            pl.BlockSpec((HEAD_DIM // 2, tile), lambda i: (0, i)),
        ],
        out_specs=[
            pl.BlockSpec((heads, HEAD_DIM, tile), lambda i: (0, 0, i)),
            pl.BlockSpec((heads, HEAD_DIM, tile), lambda i: (0, 0, i)),
            pl.BlockSpec((heads, tile, HEAD_DIM), lambda i: (0, i, 0)),
            pl.BlockSpec((heads, tile, HEAD_DIM), lambda i: (0, i, 0)),
            pl.BlockSpec((heads, HEAD_DIM + 16, tile), lambda i: (0, 0, i)),
        ]
        + [full(v.shape) for v in shapes[5:7]]
        + anywhere(1),
        scratch_shapes=[
            pltpu.VMEM((out, width), bf16),
            pltpu.SemaphoreType.DMA((2 * nt,)),
            pltpu.SemaphoreType.DMA((2 * nt,)),
            pltpu.SemaphoreType.DMA,
        ],
        out_shape=shapes,
        compiler_params=params(collective_id=number, has_side_effects=True),
        cost_estimate=cost(14),
        name="project",
    )(rows, w, small, cosine, sine)


def dealt(core, i):
    return 4 * (i // 2) + jnp.where(lax.rem(i, 2) == 0, core, 3 - core)


def attend_kernel(cuts, length, qt_ref, k_ref, vt_ref, cot_ref, ot_ref, lse_ref, top_ref, cots_ref, mask_cot, *sems):
    z, c, t = spot()
    nt = lax.axis_size("tp")
    h, i = pl.program_id(0), pl.program_id(1)
    count = pl.num_programs(1)
    at_step = h * count + i
    last = pl.num_programs(0) * count - 1
    gather = Gather(mask_cot, cots_ref, *sems, cuts)

    @pl.when(at_step == 0)
    def _():
        rows = cot_ref.shape[0]
        position = (c * nt + t) * rows + lax.broadcasted_iota(jnp.int32, cot_ref.shape, 0)
        mask_cot[...] = jnp.where(position < length[0], cot_ref[...].astype(f32), 0.0).astype(bf16)
        greet(False)
        gather.first()

    index = dealt(c, i)
    columns = BLOCK
    qt = qt_ref[0, :, pl.ds(pl.multiple_of(index * BLOCK, BLOCK), BLOCK)]

    def step(at, carry, diagonal):
        peak, total = carry
        start = pl.multiple_of(at * BLOCK, BLOCK)
        scores = mm(k_ref[0, pl.ds(start, BLOCK), :], qt)
        if diagonal:
            keys = lax.broadcasted_iota(jnp.int32, scores.shape, 0)
            queries = lax.broadcasted_iota(jnp.int32, scores.shape, 1)
            scores = jnp.where(keys <= queries, scores, -1e30)
        higher = jnp.maximum(peak, jnp.max(scores, axis=0, keepdims=True))
        weights = jnp.exp(scores - higher).astype(bf16)
        total = total * jnp.exp(peak - higher) + mm(vt_ref[0, :, pl.ds(start, BLOCK)], weights)
        return higher, total

    start = (jnp.full((1, columns), -1e30, f32), jnp.zeros((HEAD_DIM + 16, columns), f32))
    carry = lax.fori_loop(0, index, lambda at, c: step(at, c, False), start)
    peak, total = step(index, carry, True)
    mass = total[HEAD_DIM : HEAD_DIM + 1]
    ot_ref[0] = (total[:HEAD_DIM] / mass).astype(bf16)
    lse_ref[0, 0] = peak + jnp.log(mass)
    position = index * BLOCK + lax.broadcasted_iota(jnp.int32, peak.shape, 1)
    top_ref[0, 0] = jnp.where(position < length[0], peak, -1e30)

    @pl.when(at_step == last - 3)
    def _():
        for s in range(cuts):
            gather.second(s)

    @pl.when(at_step == last)
    def _():
        for s in range(cuts):
            gather.third(s)
        gather.last()


def attend(length, qt, k, vt, cot, count, number):
    cuts = 1
    heads, _, total = qt.shape
    return pl.pallas_call(
        functools.partial(attend_kernel, cuts),
        grid_spec=pltpu.PrefetchScalarGridSpec(
            num_scalar_prefetch=1,
            grid=(heads, count),
            in_specs=[
                pl.BlockSpec((1, HEAD_DIM, total), lambda h, i, n: (h, 0, 0)),
                pl.BlockSpec((1, total, HEAD_DIM), lambda h, i, n: (h, 0, 0)),
                pl.BlockSpec((1, HEAD_DIM + 16, total), lambda h, i, n: (h, 0, 0)),
                full(cot.shape),
            ],
            out_specs=[
                pl.BlockSpec((1, HEAD_DIM, BLOCK), lambda h, i, n: (i, h, 0)),
                pl.BlockSpec((1, 1, 1, BLOCK), lambda h, i, n: (h, i, 0, 0)),
                pl.BlockSpec((1, 1, 1, BLOCK), lambda h, i, n: (h, i, 0, 0)),
            ]
            + anywhere(1),
            scratch_shapes=[
                pltpu.VMEM(cot.shape, bf16),
            ]
            + Gather.scratch(cuts),
        ),
        out_shape=[
            jax.ShapeDtypeStruct((count, heads * HEAD_DIM, BLOCK), bf16),
            jax.ShapeDtypeStruct((heads, count, 1, BLOCK), f32),
            jax.ShapeDtypeStruct((heads, count, 1, BLOCK), f32),
            jax.ShapeDtypeStruct((8,) + cot.shape, bf16),
        ],
        compiler_params=params(collective_id=number, has_side_effects=True),
        cost_estimate=cost(35),
        name="attend",
    )(length, qt, k, vt, cot)


def revisit_kernel(qt_ref, k_ref, kt_ref, v_ref, ot_ref, got_ref, lse_ref, go_ref, feed_ref, dq_ref, dk_ref, dv_ref, gos_ref, fed_ref, sum_k, sum_v, came_ref, w_send, w_recv, *scratch):
    z, c, t = spot()
    job = Sum(feed_ref, *scratch)
    nt = lax.axis_size("tp")
    h, i = pl.program_id(0), pl.program_id(1)
    count = pl.num_programs(1)
    index = dealt(c, i)
    here = pl.ds(pl.multiple_of(index * BLOCK, BLOCK), BLOCK)
    away = [
        remote(go_ref.at[lax.rem(t + step, nt)], came_ref.at[step], w_send.at[step], w_recv.at[step], tp=lax.rem(t + step, nt))
        for step in range(1, nt)
    ]

    at_step = h * count + i
    end = pl.num_programs(0) * count - 1

    @pl.when(at_step == 0)
    def _():
        greet(False)
        job.first()
        for copy in away:
            copy.start()

    @pl.when(at_step == 3)
    def _():
        job.second()

    @pl.when(at_step == end - 3)
    def _():
        job.third()

    qt, got = qt_ref[0, :, here], got_ref[0]
    lse = lse_ref[0, 0]
    centre = jnp.sum(ot_ref[0].astype(f32) * got.astype(f32), axis=0, keepdims=True)

    @pl.when(i == 0)
    def _():
        sum_k[...] = jnp.zeros_like(sum_k)
        sum_v[...] = jnp.zeros_like(sum_v)
        dq_ref[...] = jnp.zeros_like(dq_ref)

    def step(at, grad, diagonal):
        start = pl.multiple_of(at * BLOCK, BLOCK)
        here = pl.ds(start, BLOCK)
        scores = mm(k_ref[0, here, :], qt)
        probs = jnp.exp(scores - lse)
        if diagonal:
            keys = lax.broadcasted_iota(jnp.int32, scores.shape, 0)
            queries = lax.broadcasted_iota(jnp.int32, scores.shape, 1)
            probs = jnp.where(keys <= queries, probs, 0.0)
        grad_probs = mm(v_ref[0, here, :], got)
        grad_scores = (probs * (grad_probs - centre)).astype(bf16)
        sum_v[:, here] += mm(got, probs.astype(bf16), NT)
        sum_k[:, here] += mm(qt, grad_scores, NT)
        return grad + mm(kt_ref[0, :, here], grad_scores)

    grad = lax.fori_loop(0, index, lambda at, c: step(at, c, False), jnp.zeros(qt.shape, f32))
    dq_ref[0, :, here] = step(index, grad, True) * HEAD_DIM**-0.5

    @pl.when(i == count - 1)
    def _():
        dk_ref[0] = sum_k[...]
        dv_ref[0] = sum_v[...]

    @pl.when(at_step == end)
    def _():
        job.last()
        one, two = job.total()
        fed_ref[: job.half] = one
        fed_ref[job.half :] = two
        total = go_ref[t].astype(f32)
        for step, copy in enumerate(away):
            copy.wait_recv()
            total = total + came_ref[step + 1].astype(f32)
            copy.wait_send()
        gos_ref[...] = total.astype(bf16)


def revisit(qt, k, kt, v, ot, got, lse, go, feed, number):
    heads, _, total = qt.shape
    count = ot.shape[0]
    nt = lax.axis_size("tp")
    whole = pl.BlockSpec((1, HEAD_DIM, total), lambda h, i: (h, 0, 0))
    tall = pl.BlockSpec((1, total, HEAD_DIM), lambda h, i: (h, 0, 0))
    some = pl.BlockSpec((1, HEAD_DIM, BLOCK), lambda h, i: (i, h, 0))
    return pl.pallas_call(
        revisit_kernel,
        grid=(heads, count),
        in_specs=[
            whole,
            tall,
            whole,
            tall,
            some,
            some,
            pl.BlockSpec((1, 1, 1, BLOCK), lambda h, i: (h, i, 0, 0)),
            full(go.shape),
        ]
        + anywhere(1),
        out_specs=[whole, whole, whole, full(go.shape[1:]), full(feed.shape[1:])],
        scratch_shapes=[
            pltpu.VMEM((HEAD_DIM, total), f32),
            pltpu.VMEM((HEAD_DIM, total), f32),
            pltpu.VMEM(go.shape, bf16),
            pltpu.SemaphoreType.DMA((nt,)),
            pltpu.SemaphoreType.DMA((nt,)),
        ]
        + Sum.scratch(*feed.shape[1:]),
        out_shape=[jax.ShapeDtypeStruct((heads, HEAD_DIM, total), f32)] * 3
        + [jax.ShapeDtypeStruct(go.shape[1:], bf16), jax.ShapeDtypeStruct(feed.shape[1:], f32)],
        compiler_params=params(collective_id=number, has_side_effects=True),
        cost_estimate=cost(50),
        name="revisit",
    )(qt, k, kt, v, ot, got, lse, go, feed)


def opening_kernel(cuts, x_ref, wq_ref, wk_ref, wv_ref, wo_ref, wr_ref, wc_ref, vec_ref, na_ref, nm_ref, routes_ref, out_ref, ws_ref, smalls_ref, all_routes_ref, held, stage, small_ref, *sems):
    gather = Gather(x_ref, out_ref, *sems[:3], cuts, stage)
    sends, recvs, local = sems[3:]
    z, c, t = spot()
    ns = lax.axis_size("shard")
    one = jnp.where(c == 0, wq_ref[...].astype(f32), wv_ref[...].astype(f32))
    two = jnp.where(c == 0, wk_ref[...].astype(f32), wo_ref[...].astype(f32).T)
    held[0] = one[:, :128].astype(bf16)
    held[1] = two[:, :128].astype(bf16)
    parts = [v[...].astype(f32) for v in (wr_ref, wc_ref, vec_ref, na_ref, nm_ref)]
    used = sum(v.shape[0] for v in parts)
    parts.append(jnp.zeros((SMALL - used, parts[0].shape[1]), f32))
    small_ref[...] = jnp.concatenate(parts, axis=0).astype(bf16)
    held[2] = jnp.concatenate([one[:, 128:], two[:, 128:]], axis=1).astype(bf16)
    greet()
    started = []

    def go(k, source, target, **where):
        copy = remote(source, target, sends.at[k], recvs.at[k], **where)
        copy.start()
        started.append(copy)

    def came(k, ref):
        remote(ref, ref, sends.at[k], recvs.at[k], ctx=1 - c).wait_recv()

    for step in range(1, ns):
        go(step, held, ws_ref.at[c, z], shard=lax.rem(z + step, ns))
    gather.first()
    for step in range(1, ns):
        go(2 * ns + step, small_ref, smalls_ref.at[z], shard=lax.rem(z + step, ns))
    go(0, held, ws_ref.at[c, z], ctx=1 - c)
    go(ns, routes_ref, all_routes_ref.at[c], ctx=1 - c)
    mine = [
        pltpu.make_async_copy(held, ws_ref.at[c, z], local.at[0]),
        pltpu.make_async_copy(small_ref, smalls_ref.at[z], local.at[1]),
        pltpu.make_async_copy(routes_ref, all_routes_ref.at[c], local.at[2]),
    ]
    for copy in mine:
        copy.start()
    for s in range(cuts):
        gather.second(s)
    for s in range(cuts):
        gather.third(s)
    for step in range(1, ns):
        back = lax.rem(z + ns - step, ns)
        came(step, ws_ref.at[c, back])
        go(ns + step, ws_ref.at[c, back], ws_ref.at[c, back], ctx=1 - c)
    gather.last()
    came(0, ws_ref.at[1 - c, z])
    came(ns, all_routes_ref.at[1 - c])
    for step in range(1, ns):
        back = lax.rem(z + ns - step, ns)
        came(2 * ns + step, smalls_ref.at[back])
        came(ns + step, ws_ref.at[1 - c, back])
    for copy in started:
        copy.wait_send()
    for copy in mine:
        copy.wait()


def opening(x, weights, small, routes, number):
    cuts = 2
    ns = lax.axis_size("shard")
    depth = weights[0].shape[0]
    held = (3, depth, 128)
    vmem = pl.BlockSpec(memory_space=pltpu.VMEM)
    return pl.pallas_call(
        functools.partial(opening_kernel, cuts),
        in_specs=anywhere(1) + [vmem] * (len(weights) + len(small) + 1),
        out_specs=anywhere(4),
        out_shape=[
            jax.ShapeDtypeStruct((8,) + x.shape, x.dtype),
            jax.ShapeDtypeStruct((2, ns) + held, bf16),
            jax.ShapeDtypeStruct((ns, SMALL, depth), bf16),
            jax.ShapeDtypeStruct((2,) + routes.shape, routes.dtype),
        ],
        scratch_shapes=[pltpu.VMEM(held, bf16), pltpu.VMEM(x.shape, x.dtype), pltpu.VMEM((SMALL, depth), bf16)]
        + Gather.scratch(cuts)
        + [
            pltpu.SemaphoreType.DMA((3 * ns,)),
            pltpu.SemaphoreType.DMA((3 * ns,)),
            pltpu.SemaphoreType.DMA((3,)),
        ],
        compiler_params=params(collective_id=number, has_side_effects=True),
        cost_estimate=cost(30),
        name="opening",
    )(x, *weights, *small, routes)


def places(routes_ref, row_ref):
    one = lax.broadcasted_iota(jnp.int32, (BLOCK, BLOCK), 0)
    two = lax.broadcasted_iota(jnp.int32, (BLOCK, BLOCK), 1)
    before = (one < two).astype(bf16)
    blocks, _, per = routes_ref.shape
    for b in range(blocks):
        carry = jnp.zeros((16, 1), f32)
        for at in range(0, per, BLOCK):
            here = slice(at, at + BLOCK)
            expert = lax.broadcasted_iota(jnp.int32, (16, BLOCK), 0)
            member = (routes_ref[b, 0:1, here] == expert) | (routes_ref[b, 1:2, here] == expert)
            rank = mm(member.astype(bf16), before) + carry
            row_ref[:, b * per + at : b * per + at + BLOCK] = jnp.where(member, rank, -1.0)
            carry = carry + jnp.sum(member.astype(f32), axis=1, keepdims=True)


def route_kernel(cuts, o_ref, x_ref, wo_ref, small_ref, prev_ref, routes_ref, cots_ref,
                 att, res_out, base_out, x_out, g_out, gate_ref, row_ref,
                 x_in, wo_in, res, base, a, comb, rows, cots, combs, xs, gs,
                 o_send, o_recv, c_send, c_recv, local, out_sem, x_sem, g_sem, *sems):
    gather = Gather(a, rows, *sems, cuts, relative=True)
    z, c, t = spot()
    nt = lax.axis_size("tp")
    own = 4 * c + t
    near = (t,) + across(t)
    blocks, _, per = routes_ref.shape
    width = rows.shape[2]
    experts = xs.shape[0]
    here = pl.ds(pl.multiple_of(t * BLOCK, BLOCK), BLOCK)
    loads = [
        pltpu.make_async_copy(cots_ref, cots, local.at[0]),
        pltpu.make_async_copy(x_ref, x_in, local.at[1]),
        pltpu.make_async_copy(wo_ref, wo_in, local.at[2]),
    ]
    for copy in loads:
        copy.start()
    greet(False)

    copies = []
    for i in range(o_ref.shape[0]):
        block = zig(c, i)
        copy = remote(o_ref.at[i], att.at[t], o_send.at[i], o_recv.at[t], ctx=block // nt, tp=lax.rem(block, nt))
        copies.append((block == own, copy, pltpu.make_async_copy(o_ref.at[i], att.at[t], local.at[3])))
    for mine, copy, inside in copies:

        @pl.when(jnp.logical_not(mine))
        def _():
            copy.start()

        @pl.when(mine)
        def _():
            inside.start()

    each = per // nt

    def names(b, j, order):
        start = pl.multiple_of(b * per, per)
        mine = row_ref[pl.ds(experts * c + j, 1), pl.ds(start, per)] if order is None else jnp.concatenate(
            [row_ref[pl.ds(experts * c + j, 1), pl.ds(pl.multiple_of(start + o * each, each), each)] for o in order], axis=1
        )
        return lax.broadcasted_iota(jnp.int32, (CAP, mine.shape[1]), 0).astype(f32) == mine

    def fetch(n):
        b, j = n // experts, lax.rem(n, experts)
        here = pl.ds(pl.multiple_of(b * CAP, CAP), CAP)
        hot = names(b, j, None)
        gs[j, here] = mm(hot.astype(bf16), cots[pl.ds(4 * b, 4)].reshape(per, width)).astype(bf16)
        pltpu.make_async_copy(gs.at[j, here], g_out.at[j, here], g_sem.at[n]).start()

    def fetch_x(beside, j, which):
        b = 1 - c if beside else c
        here = pl.ds(pl.multiple_of(b * CAP, CAP), CAP)
        order = [near[k] for k in which]
        hot = names(b, j, order)
        first = 4 * beside + which[0]
        got = mm(hot.astype(bf16), rows[first : first + len(which)].reshape(len(which) * each, width)).astype(bf16)
        gate = jnp.zeros((CAP, 1), f32)
        for k, o in enumerate(order):
            weight = combs[4 * b + o, pl.ds(experts * c + j, 1)]
            gate = gate + jnp.sum(jnp.where(hot[:, k * each : (k + 1) * each], weight, 0.0), axis=1, keepdims=True)
        if which[0] == 0:
            xs[j, here] = got
            gate_ref[j, here] = gate
        else:
            xs[j, here] = xs[j, here] + got
            gate_ref[j, here] = gate_ref[j, here] + gate
            n = b * experts + j
            pltpu.make_async_copy(xs.at[j, here], x_out.at[j, here], x_sem.at[n]).start()

    def all_x(beside, which):
        @pl.loop(0, experts)
        def _(j):
            fetch_x(beside, j, which)

    def fetch_g(first, last):
        @pl.loop(first, last)
        def _(n):
            fetch(n)

    places(routes_ref, row_ref)
    for copy in loads:
        copy.wait()
    fetch_g(0, 2)
    for mine, copy, inside in copies:

        @pl.when(jnp.logical_not(mine))
        def _():
            copy.wait_send()

        @pl.when(mine)
        def _():
            inside.wait()

    mine = lax.rem((own + 1) // 2, 2) == c
    for source in range(nt):

        @pl.when(jnp.logical_or(jnp.logical_not(mine), source != t))
        def _():
            remote(o_ref.at[0], att.at[source], o_send.at[0], o_recv.at[source], ctx=c, tp=t).wait_recv()

    attended = att[...].reshape(-1, BLOCK)
    r = x_in[...].astype(f32) + mm(attended, wo_in[...].reshape(-1, width), TN)
    inverse = lax.rsqrt(jnp.mean(r * r, axis=1, keepdims=True) + epsilon)
    n2 = r * inverse * small_ref[19:20]
    a[...] = n2.astype(bf16)
    gather.first()
    res[...] = r
    _, _, combined, alphas, weights = mixing(n2, small_ref[:16], *laid(prev_ref[:, here], routes_ref[c, :, here]))
    comb[...] = combined
    pairs = []
    for step in range(1, 8):
        other, back = lax.rem(own + step, 8), lax.rem(own + 8 - step, 8)
        where = {"ctx": other // 4, "tp": lax.rem(other, 4)}
        copy = remote(comb, combs.at[own], c_send.at[step], c_recv.at[step], **where)
        copy.start()
        pairs.append((copy, remote(comb, combs.at[back], c_send.at[step], c_recv.at[step], **where)))
    combs[own] = comb[...]
    scale, one, two = scales(alphas, weights)
    base[...] = r + scale * n2 + one * small_ref[16:17] + two * small_ref[17:18]
    outs = [
        pltpu.make_async_copy(res, res_out, out_sem.at[0]),
        pltpu.make_async_copy(base, base_out, out_sem.at[1]),
    ]
    for copy in outs:
        copy.start()

    total = blocks * experts
    fetch_g(2, 4)
    gather.second(0)
    fetch_g(4, total)
    gather.second(1)
    gather.own.wait()
    for copy, came in pairs:
        came.wait_recv()
    all_x(0, (0, 1, 2))
    gather.third(0)
    gather.third(1)
    gather.beside()
    all_x(1, (0, 1, 2))
    all_x(0, (3,))
    gather.last(True)
    all_x(1, (3,))

    for copy, came in pairs:
        copy.wait_send()
    for copy in outs:
        copy.wait()

    @pl.loop(0, total)
    def _(n):
        b, j = n // experts, lax.rem(n, experts)
        here = pl.ds(pl.multiple_of(b * CAP, CAP), CAP)
        pltpu.make_async_copy(gs.at[j, here], g_out.at[j, here], g_sem.at[n]).wait()
        pltpu.make_async_copy(xs.at[j, here], x_out.at[j, here], x_sem.at[n]).wait()


def route(o, x, wo, small, prev, routes, cots, experts, number):
    cuts = 2
    own, width = x.shape
    nt = lax.axis_size("tp")
    blocks, _, per = routes.shape
    slots = jax.ShapeDtypeStruct((experts, blocks * CAP, width), bf16)
    vmem = pl.BlockSpec(memory_space=pltpu.VMEM)
    return pl.pallas_call(
        functools.partial(route_kernel, cuts),
        in_specs=anywhere(3) + [vmem, vmem, vmem] + anywhere(1),
        out_specs=[vmem] + anywhere(4) + [vmem, vmem],
        out_shape=[
            jax.ShapeDtypeStruct((nt,) + o.shape[1:], bf16),
            jax.ShapeDtypeStruct((own, width), f32),
            jax.ShapeDtypeStruct((own, width), f32),
            slots,
            slots,
            jax.ShapeDtypeStruct((experts, blocks * CAP, 1), f32),
            jax.ShapeDtypeStruct((16, blocks * per), f32),
        ],
        scratch_shapes=[
            pltpu.VMEM((own, width), bf16),
            pltpu.VMEM(wo.shape, bf16),
            pltpu.VMEM((own, width), f32),
            pltpu.VMEM((own, width), f32),
            pltpu.VMEM((own, width), bf16),
            pltpu.VMEM((16, own), f32),
            pltpu.VMEM((8, own, width), bf16),
            pltpu.VMEM((8, own, width), bf16),
            pltpu.VMEM((8, 16, own), f32),
            pltpu.VMEM(slots.shape, bf16),
            pltpu.VMEM(slots.shape, bf16),
            pltpu.SemaphoreType.DMA((o.shape[0],)),
            pltpu.SemaphoreType.DMA((nt,)),
            pltpu.SemaphoreType.DMA((8,)),
            pltpu.SemaphoreType.DMA((8,)),
            pltpu.SemaphoreType.DMA((4,)),
            pltpu.SemaphoreType.DMA((2,)),
            pltpu.SemaphoreType.DMA((blocks * experts,)),
            pltpu.SemaphoreType.DMA((blocks * experts,)),
        ]
        + Gather.scratch(cuts),
        compiler_params=params(collective_id=number, has_side_effects=True),
        cost_estimate=cost(65),
        name="route",
    )(o, x, wo, small, prev, routes, cots)


def spot_rows(place, c, experts, first, some, values, at):
    lane = lax.broadcasted_iota(jnp.int32, place.shape, 1)
    slot = lax.broadcasted_iota(jnp.int32, (place.shape[0], CAP), 1).astype(f32)
    total = None
    for j in range(some):
        mine = jnp.sum(jnp.where(lane == experts * c + first + j, place, 0.0), axis=1, keepdims=True)
        term = mm((slot == mine).astype(bf16), values[j, at])
        total = term if total is None else total + term
    return total


def spread_kernel(experts, row_ref, feed_ref, out_ref):
    c = lax.axis_index("ctx")
    out_ref[0] = spot_rows(row_ref[...].T, c, experts, 0, feed_ref.shape[0], feed_ref, slice(None)).astype(bf16)


def spread(row, feed, experts):
    some, slots, width = feed.shape
    rows = row.shape[1] // 8
    return pl.pallas_call(
        functools.partial(spread_kernel, experts),
        grid=(8,),
        in_specs=[
            pl.BlockSpec((16, rows), lambda i: (0, i)),
            pl.BlockSpec((some, CAP, width), lambda i: (0, i // 4, 0)),
        ],
        out_specs=pl.BlockSpec((1, rows, width), lambda i: (i, 0, 0)),
        out_shape=jax.ShapeDtypeStruct((8, rows, width), bf16),
        compiler_params=params(),
        cost_estimate=cost(10),
        name="spread",
    )(row, feed)


def combine_kernel(experts, row_ref, *refs):
    values_in, part_ref, feed_ref = refs[:2], refs[2], refs[3]
    out_ref, feed_out, gates_ref = refs[4:7]
    backs, feeds, stage, staged, gsend, gcame, b_sem, f_sem, p_sem, o_sem, g_send, g_recv = refs[7:19]
    job = Sum(None, *refs[19:], stage=stage)
    each, some = backs.shape[0] // 2, feeds.shape[0]
    z, c, t = spot()
    own = 4 * c + t
    width = stage.shape[2]
    loads = [pltpu.make_async_copy(v, backs.at[pl.ds(j * each, each)], b_sem.at[j]) for j, v in enumerate(values_in)]
    more = [pltpu.make_async_copy(feed_ref, feeds, f_sem)]
    more += [pltpu.make_async_copy(part_ref.at[o], staged.at[o], p_sem.at[o]) for o in range(8)]
    for copy in loads + more:
        copy.start()
    greet(False)

    def tile(values, owner):
        start = pl.multiple_of(owner * BLOCK, BLOCK)
        place = row_ref[:, pl.ds(start, BLOCK)].T
        here = pl.ds(pl.multiple_of(owner // 4 * CAP, CAP), CAP)
        count = values.shape[0]
        return spot_rows(place, c, experts, experts - count, count, values, here)

    def back(owner):
        got = tile(backs, owner)
        named = got[:, width:].T
        gsend[owner] = named[:FFN_EXPERTS] + named[16 : 16 + FFN_EXPERTS]
        return got[:, :width]

    for copy in loads:
        copy.wait()
    for k, o in enumerate(job.order):
        stage[k] = back(4 * (1 - c) + o).astype(bf16)
        job.core[k].start()
        job.add(k, back(4 * c + o))
    job.third()
    pairs = []
    for step in range(1, 8):
        other = lax.rem(own + step, 8)
        copy = remote(gsend.at[other], gcame.at[step], g_send.at[step], g_recv.at[step], ctx=other // 4, tp=lax.rem(other, 4))
        copy.start()
        pairs.append(copy)
    for copy in more:
        copy.wait()

    def feed(first, last):
        @pl.loop(first, last)
        def _(n):
            staged[n] = (tile(feeds, n) + staged[n].astype(f32)).astype(bf16)
            pltpu.make_async_copy(staged.at[n], feed_out.at[n], o_sem.at[n]).start()

    feed(0, 8)
    gates = gsend[own]
    for step, copy in enumerate(pairs):
        copy.wait_recv()
        gates = gates + gcame[step + 1]
        copy.wait_send()
    gates_ref[...] = gates
    job.last()
    one, two = job.total()
    out_ref[: job.half] = one
    out_ref[job.half :] = two

    @pl.loop(0, 8)
    def _(n):
        pltpu.make_async_copy(staged.at[n], feed_out.at[n], o_sem.at[n]).wait()


def combine(row, backs, part, feed, number):
    experts = sum(b.shape[0] for b in backs)
    _, slots, width = feed.shape
    wide = backs[0].shape[2]
    rows = row.shape[1] // 8
    vmem = pl.BlockSpec(memory_space=pltpu.VMEM)
    return pl.pallas_call(
        functools.partial(combine_kernel, experts),
        in_specs=[vmem] + anywhere(4),
        out_specs=[vmem] + anywhere(1) + [vmem],
        out_shape=[
            jax.ShapeDtypeStruct((rows, width), f32),
            jax.ShapeDtypeStruct((8, rows, width), bf16),
            jax.ShapeDtypeStruct((FFN_EXPERTS, rows), f32),
        ],
        scratch_shapes=[
            pltpu.VMEM((experts, slots, wide), bf16),
            pltpu.VMEM(feed.shape, bf16),
            pltpu.VMEM((4, rows, width), bf16),
            pltpu.VMEM((8, rows, width), bf16),
            pltpu.VMEM((8, FFN_EXPERTS, rows), f32),
            pltpu.VMEM((8, FFN_EXPERTS, rows), f32),
            pltpu.SemaphoreType.DMA((2,)),
            pltpu.SemaphoreType.DMA,
            pltpu.SemaphoreType.DMA((8,)),
            pltpu.SemaphoreType.DMA((8,)),
            pltpu.SemaphoreType.DMA((8,)),
            pltpu.SemaphoreType.DMA((8,)),
        ]
        + Sum.scratch(rows, width),
        compiler_params=params(collective_id=number, has_side_effects=True),
        cost_estimate=cost(45),
        name="combine",
    )(row, *backs, part, feed)


def closing_kernel(dq_ref, dk_ref, dv_ref, x_ref, cos_ref, sin_ref, wt_ref, par_ref, go_ref, small_ref, top_ref, ge_ref,
                   out_ref, gsum_ref, ssum_ref, tmax_ref, gall_ref,
                   dqs, dks, dvs, xs, total, row, gother, gcore, gline, gmine, smine, sline, splane, tline, mytop, stage, l_sem, *sems):
    job = Sum(None, *sems[:7], stage=stage)
    sends, recvs = sems[7:]
    z, c, t = spot()
    ns = lax.axis_size("shard")
    heads = dqs.shape[0]
    half = HEAD_DIM // 2
    own = 4 * c + t
    order = [4 * (1 - c) + o for o in job.order] + [4 * c + o for o in job.order]

    def lanes(o):
        return pl.ds(pl.multiple_of(o * BLOCK, BLOCK), BLOCK)

    loads = []
    for n, o in enumerate(order):
        here = lanes(o)
        loads.append(
            [
                pltpu.make_async_copy(dq_ref.at[:, :, here], dqs.at[:, :, here], l_sem.at[n, 0]),
                pltpu.make_async_copy(dk_ref.at[:, :, here], dks.at[:, :, here], l_sem.at[n, 1]),
                pltpu.make_async_copy(dv_ref.at[:, :, here], dvs.at[:, :, here], l_sem.at[n, 2]),
                pltpu.make_async_copy(x_ref.at[here], xs.at[here], l_sem.at[n, 3]),
            ]
        )
    for k in range(4):
        for copy in loads[k] + loads[4 + k]:
            copy.start()
    greet()
    started = []

    def go(k, source, target, **where):
        copy = remote(source, target, sends.at[k], recvs.at[k], **where)
        copy.start()
        started.append(copy)
        return copy

    line_row = lax.broadcasted_iota(jnp.int32, mytop.shape, 0)
    high = jnp.full(mytop.shape, -1e30, f32)
    for h in range(top_ref.shape[0]):
        best = jnp.max(jnp.max(top_ref[h], axis=0), axis=1, keepdims=True)
        high = jnp.where(line_row == h, best, high)
    mytop[...] = high
    tops = [go(3 + ns + s, mytop, tline.at[s], shard=lax.rem(z + s, ns)) for s in range(1, ns)]
    experts = go(1, ge_ref, gall_ref, ctx=1 - c)
    total[...] = jnp.zeros_like(total)
    row[...] = jnp.zeros_like(row)

    def tile(o):
        here = lanes(o)
        cosine, sine = cos_ref[:, here], sin_ref[:, here]

        def turned(g):
            u, w = g[:half], g[half:]
            return jnp.concatenate([u * cosine + w * sine, w * cosine - u * sine], axis=0)

        x = xs[here].astype(f32)
        m = x * lax.rsqrt(jnp.mean(x * x, axis=1, keepdims=True) + epsilon)
        a = (m * par_ref[18:19]).astype(bf16)
        pieces = [turned(dqs[h, :, here]) for h in range(heads)]
        pieces += [turned(dks[h, :, here]) for h in range(heads)]
        pieces += [dvs[h, :, here] for h in range(heads)]
        grads = jnp.concatenate(pieces, axis=0).astype(bf16)
        part = mm(grads, wt_ref[...], TN)
        row[...] += jnp.sum(part * m, axis=0, keepdims=True)
        total[...] += mm(grads, a)
        return part

    for k in range(4):
        for copy in loads[k] + loads[4 + k]:
            copy.wait()
        stage[k] = tile(order[k]).astype(bf16)
        job.core[k].start()
        job.add(k, tile(order[4 + k]))

    cut_rows, depth = gsum_ref.shape[1:]
    at = lax.broadcasted_iota(jnp.int32, small_ref.shape, 0)
    smalls = small_ref[...] + jnp.where(at == 19, row[...], 0.0)
    for s in range(ns):
        here = slice(s * depth, (s + 1) * depth)
        one = total[:cut_rows, here].astype(bf16)
        two = jnp.concatenate([total[cut_rows:, here].astype(bf16), go_ref[:, here]], axis=0)
        gmine[s] = packed(jnp.where(c == 0, one.astype(f32), two.astype(f32))).astype(bf16)
        gother[s] = packed(jnp.where(c == 0, two.astype(f32), one.astype(f32))).astype(bf16)
        smine[s] = smalls[:, here]
    core = go(0, gother, gcore, ctx=1 - c)
    small = [go(3 + s, smine.at[lax.rem(z + s, ns)], sline.at[s], shard=lax.rem(z + s, ns)) for s in range(1, ns)]
    core.wait_recv()
    gmine[...] = gmine[...] + gcore[...]
    line = [go(3 + 2 * ns + s, gmine.at[lax.rem(z + s, ns)], gline.at[s], shard=lax.rem(z + s, ns)) for s in range(1, ns)]
    job.third()
    for copy in small:
        copy.wait_recv()
    value = smine[z]
    for s in range(1, ns):
        value = value + sline[s]
    splane[0] = value
    plane = []
    for s in range(1, 8):
        other = lax.rem(own + s, 8)
        plane.append(go(3 + 3 * ns + s, splane.at[0], splane.at[s], ctx=other // 4, tp=lax.rem(other, 4)))
    for copy in tops:
        copy.wait_recv()
    high = mytop[...]
    for s in range(1, ns):
        high = jnp.maximum(high, tline[s])
    tline[0] = high
    pair = go(2, tline.at[0], tline.at[ns], ctx=1 - c)
    for copy in line:
        copy.wait_recv()
    value = gmine[z].astype(f32)
    for s in range(1, ns):
        value = value + gline[s].astype(f32)
    gsum_ref[c] = unpacked(value, depth)
    go(3, gsum_ref.at[c], gsum_ref.at[c], ctx=1 - c)
    for copy in plane:
        copy.wait_recv()
    value = splane[0]
    for s in range(1, 8):
        value = value + splane[s]
    ssum_ref[...] = value
    pair.wait_recv()
    tmax_ref[...] = jnp.maximum(tline[0], tline[ns])
    job.last()
    one, two = job.total()
    out_ref[: job.half] = one
    out_ref[job.half :] = two
    remote(gsum_ref.at[1 - c], gsum_ref.at[1 - c], sends.at[3], recvs.at[3], ctx=1 - c).wait_recv()
    experts.wait_recv()
    for copy in started:
        copy.wait_send()


def closing(dq, dk, dv, x, cosine, sine, wt, par, go, small, top, ge, number):
    heads, _, total = dq.shape
    width = x.shape[1]
    rows = total // 8
    ns = lax.axis_size("shard")
    depth = width // ns
    cut_rows = 2 * heads * HEAD_DIM
    pieces = (ns, cut_rows * 3 // 2, 128) if depth == 192 else (ns, cut_rows, depth)
    smalls = (ns,) + small.shape[:1] + (depth,)
    vmem = pl.BlockSpec(memory_space=pltpu.VMEM)
    return pl.pallas_call(
        closing_kernel,
        in_specs=anywhere(4) + [vmem] * 7 + anywhere(1),
        out_specs=[vmem, vmem, vmem, vmem] + anywhere(1),
        out_shape=[
            jax.ShapeDtypeStruct((rows, width), f32),
            jax.ShapeDtypeStruct((2, cut_rows, depth), f32),
            jax.ShapeDtypeStruct(smalls[1:], f32),
            jax.ShapeDtypeStruct((8, 128), f32),
            jax.ShapeDtypeStruct(ge.shape, bf16),
        ],
        scratch_shapes=[
            pltpu.VMEM(dq.shape, f32),
            pltpu.VMEM(dq.shape, f32),
            pltpu.VMEM(dq.shape, f32),
            pltpu.VMEM(x.shape, bf16),
            pltpu.VMEM(wt.shape, f32),
            pltpu.VMEM((1, width), f32),
            pltpu.VMEM(pieces, bf16),
            pltpu.VMEM(pieces, bf16),
            pltpu.VMEM(pieces, bf16),
            pltpu.VMEM(pieces, bf16),
            pltpu.VMEM(smalls, f32),
            pltpu.VMEM(smalls, f32),
            pltpu.VMEM((8,) + smalls[1:], f32),
            pltpu.VMEM((ns + 1, 8, 128), f32),
            pltpu.VMEM((8, 128), f32),
            pltpu.VMEM((4, rows, width), bf16),
            pltpu.SemaphoreType.DMA((8, 4)),
        ]
        + Sum.scratch(rows, width)
        + [
            pltpu.SemaphoreType.DMA((3 * ns + 11,)),
            pltpu.SemaphoreType.DMA((3 * ns + 11,)),
        ],
        compiler_params=params(collective_id=number, has_side_effects=True),
        cost_estimate=cost(45),
        name="closing",
    )(dq, dk, dv, x, cosine, sine, wt, par, go, small, top, ge)


def packed(v):
    rows, lanes = v.shape
    if lanes != 192:
        return v
    rest = jnp.concatenate([v[: rows // 2, 128:], v[rows // 2 :, 128:]], axis=1)
    return jnp.concatenate([v[:, :128], rest], axis=0)


def unpacked(v, lanes):
    if lanes != 192:
        return v
    rows = v.shape[0] // 3 * 2
    rest = jnp.concatenate([v[rows:, :64], v[rows:, 64:]], axis=0)
    return jnp.concatenate([v[:rows], rest], axis=1)


def swap_kernel(ge_ref, other_ref, send, recv):
    z, c, t = spot()
    greet_core()
    copy = remote(ge_ref, other_ref, send, recv, ctx=1 - c)
    copy.start()
    copy.wait()


def greet_core():
    z, c, t = spot()
    barrier = pltpu.get_barrier_semaphore()
    pl.semaphore_signal(barrier, inc=1, device_id={"ctx": 1 - c}, device_id_type=MESH)
    pl.semaphore_wait(barrier, 1)


def swap(ge, number):
    return pl.pallas_call(
        swap_kernel,
        in_specs=anywhere(1),
        out_specs=anywhere(1)[0],
        out_shape=jax.ShapeDtypeStruct(ge.shape, ge.dtype),
        scratch_shapes=[pltpu.SemaphoreType.DMA, pltpu.SemaphoreType.DMA],
        compiler_params=params(collective_id=number, has_side_effects=True),
        cost_estimate=cost(5),
        name="swap",
    )(ge)


def laid(previous, routes):
    count, rows = previous.shape
    return jnp.concatenate([previous, jnp.zeros((16 - count, rows), f32)], axis=0), routes.astype(f32)


def mixing(n2, wrc, previous, routes):
    z = mm(wrc, n2, NT, lax.Precision.HIGHEST)
    expert = lax.broadcasted_iota(jnp.int32, z.shape, 0).astype(f32)
    logits = z + previous
    hot = [expert == routes[r : r + 1] for r in range(2)]
    picked = [jnp.sum(jnp.where(hot[r], logits, 0.0), axis=0, keepdims=True) for r in range(2)]
    most = jnp.maximum(picked[0], picked[1])
    e = [jnp.exp(p - most) for p in picked]
    gates = [v / (e[0] + e[1]) for v in e]
    combine = jnp.where(hot[0], gates[0], 0.0) + jnp.where(hot[1], gates[1], 0.0)
    alphas = []
    for j in range(2):
        first, second = z[EXPERTS + 2 * j : EXPERTS + 2 * j + 1], z[EXPERTS + 2 * j + 1 : EXPERTS + 2 * j + 2]
        most = jnp.maximum(first, second)
        a, b = jnp.exp(first - most), jnp.exp(second - most)
        alphas.append((a / (a + b), b / (a + b)))
    weights = [combine[FFN_EXPERTS + 1 + j : FFN_EXPERTS + 2 + j] for j in range(3)]
    return hot, gates, combine, alphas, weights


def scales(alphas, weights):
    scale = weights[0] + weights[1] * alphas[0][0] + weights[2] * alphas[1][0]
    at = lax.broadcasted_iota(jnp.int32, (8, scale.shape[1]), 0)
    value = jnp.where(at == 0, scale, jnp.where(at == 1, weights[1] * alphas[0][1], weights[2] * alphas[1][1])).T
    return value[:, 0:1], value[:, 1:2], value[:, 2:3]


def turn_kernel(length, res_ref, dn_ref, named_ref, cot_ref, att_ref, wo_ref, par_ref, prev_ref, routes_ref,
                dres_ref, heads_ref, gwo_ref, small_ref, got_ref, send_sem, recv_sem, local_sem):
    z, c, t = spot()
    nt = lax.axis_size("tp")
    own = c * nt + t
    rows, width = res_ref.shape
    greet(False)
    here = pl.ds(pl.multiple_of(t * rows, rows), rows)
    res = res_ref[...]
    gain = par_ref[19:20]
    inverse = lax.rsqrt(jnp.mean(res * res, axis=1, keepdims=True) + epsilon)
    m = res * inverse
    n2 = m * gain
    previous, routes = laid(prev_ref[:, here], routes_ref[c, :, here])
    hot, gates, _, alphas, weights = mixing(n2, par_ref[:16], previous, routes)
    position = own * rows + lax.broadcasted_iota(jnp.int32, cot_ref.shape, 0)
    g = jnp.where(position < length[0], cot_ref[...].astype(f32), 0.0)
    inner = jnp.broadcast_to(jnp.sum(g * n2, axis=1, keepdims=True), (rows, 8)).T[0:1]
    onto = mm(par_ref[16:18].astype(bf16), g.astype(bf16), NT)
    onto = [onto[j : j + 1] for j in range(2)]
    named = named_ref[...]
    expert = lax.broadcasted_iota(jnp.int32, hot[0].shape, 0)
    local = {
        FFN_EXPERTS + 1: inner,
        FFN_EXPERTS + 2: alphas[0][0] * inner + alphas[0][1] * onto[0],
        FFN_EXPERTS + 3: alphas[1][0] * inner + alphas[1][1] * onto[1],
    }
    dgates = []
    for r in range(2):
        there = jnp.sum(jnp.where(hot[r][:FFN_EXPERTS], named, 0.0), axis=0, keepdims=True)
        for e, value in local.items():
            there = there + jnp.where(hot[r][e : e + 1], value, 0.0)
        dgates.append(there)
    mean = gates[0] * dgates[0] + gates[1] * dgates[1]
    dz = jnp.where(hot[0], gates[0] * (dgates[0] - mean), 0.0)
    dz = dz + jnp.where(hot[1], gates[1] * (dgates[1] - mean), 0.0)
    for j in range(2):
        da = weights[1 + j] * inner
        db = weights[1 + j] * onto[j]
        centre = alphas[j][0] * da + alphas[j][1] * db
        dz = dz + jnp.where(expert == EXPERTS + 2 * j, alphas[j][0] * (da - centre), 0.0)
        dz = dz + jnp.where(expert == EXPERTS + 2 * j + 1, alphas[j][1] * (db - centre), 0.0)
    scale, first_vec, second_vec = scales(alphas, weights)
    highest = lax.Precision.HIGHEST
    dn2 = dn_ref[...] + scale * g + mm(dz, par_ref[:16], TN, highest)
    q = dn2 * gain
    dres = g + inverse * (q - m * jnp.mean(q * m, axis=1, keepdims=True))
    dres_ref[...] = dres
    da = dres.astype(bf16)
    wo = wo_ref[...].reshape(-1, width)
    got_ref[...] = mm(wo, da, NT).astype(bf16).reshape(got_ref.shape)

    core = lax.rem((own + 1) // 2, 2)
    slot = 2 * (own // 4) + lax.rem(own, 4) // 2
    copies = []
    for target in range(nt):
        inside = jnp.logical_and(core == c, target == t)
        copy = remote(got_ref.at[target], heads_ref.at[slot], send_sem.at[target], recv_sem.at[slot], ctx=core, tp=target)
        copies.append((inside, copy, pltpu.make_async_copy(got_ref.at[target], heads_ref.at[slot], local_sem)))
    for inside, copy, kept in copies:

        @pl.when(jnp.logical_not(inside))
        def _():
            copy.start()

        @pl.when(inside)
        def _():
            kept.start()

    small_ref[0:16] = mm(dz, n2, NN, highest)
    small_ref[16:24] = jnp.zeros((8, width), f32)
    small_ref[16:17] = jnp.sum(first_vec * g, axis=0, keepdims=True)
    small_ref[17:18] = jnp.sum(second_vec * g, axis=0, keepdims=True)
    small_ref[18:19] = jnp.sum(dn2 * m, axis=0, keepdims=True)
    att = att_ref[...].reshape(-1, rows)
    gwo_ref[...] = mm(att, da).astype(bf16).reshape(gwo_ref.shape)
    for inside, copy, kept in copies:

        @pl.when(jnp.logical_not(inside))
        def _():
            copy.wait_send()

        @pl.when(inside)
        def _():
            kept.wait()

    for i in range(heads_ref.shape[0]):

        @pl.when(zig(c, i) != own)
        def _():
            remote(got_ref.at[0], heads_ref.at[i], send_sem.at[0], recv_sem.at[i], ctx=c, tp=t).wait_recv()


def turn(length, res, dn, named, cot, att, wo, small, prev, routes, count, number):
    rows, width = res.shape
    nt = lax.axis_size("tp")
    args = (res, dn, named, cot, att, wo, small, prev, routes)
    return pl.pallas_call(
        turn_kernel,
        grid_spec=pltpu.PrefetchScalarGridSpec(
            num_scalar_prefetch=1,
            grid=(1,),
            in_specs=[full(v.shape) for v in args],
            out_specs=[full((rows, width))] + anywhere(1) + [full(wo.shape), full((24, width))],
            scratch_shapes=[
                pltpu.VMEM(att.shape, bf16),
                pltpu.SemaphoreType.DMA((nt,)),
                pltpu.SemaphoreType.DMA((count,)),
                pltpu.SemaphoreType.DMA,
            ],
        ),
        out_shape=[
            jax.ShapeDtypeStruct((rows, width), f32),
            jax.ShapeDtypeStruct((count,) + att.shape[1:], bf16),
            jax.ShapeDtypeStruct(wo.shape, bf16),
            jax.ShapeDtypeStruct((24, width), f32),
        ],
        compiler_params=params(collective_id=number, has_side_effects=True),
        cost_estimate=cost(18),
        name="turn",
    )(length, *args)


def finish_kernel(x_ref, dn_ref, dres_ref, small_ref, base_ref, feed_ref, gw_ref, gs_ref, top_ref, wq_ref, wk_ref, limit_ref, length_ref, own_a, own_b, other_a, other_b, *outs):
    each = own_a.shape[0]
    local = 2 * each
    gin_ref, out_ref, gate_ref, up_ref, down_ref = outs[:5]
    x = x_ref[...].astype(f32)
    inverse = lax.rsqrt(jnp.mean(x * x, axis=1, keepdims=True) + epsilon)
    m = x * inverse
    q = dn_ref[...] * small_ref[18:19]
    gin_ref[...] = dres_ref[...] + inverse * (q - m * jnp.mean(q * m, axis=1, keepdims=True))
    core = lax.axis_index("ctx")
    rows = x.shape[0]
    first = (core * lax.axis_size("tp") + lax.axis_index("tp")) * pl.num_programs(0) + pl.program_id(0)
    position = first * rows + lax.broadcasted_iota(jnp.int32, x.shape, 0)
    out_ref[...] = jnp.where(position < length_ref[0], base_ref[...] + feed_ref[...], 0.0).astype(bf16)
    for k, target in enumerate((gate_ref, up_ref, down_ref)):
        for j in range(local):
            own, other = ((own_a, other_a), (own_b, other_b))[j // each]
            mine, theirs = own[j % each, k].astype(f32), other[j % each, k].astype(f32)
            target[j] = jnp.where(core == 0, mine, theirs)
            target[local + j] = jnp.where(core == 0, theirs, mine)

    @pl.when(pl.program_id(0) == 0)
    def _():
        gq, gk, gv, go, gnorm, gmoe, grouter, gconst, gvec, fac_ref, cq_ref, ck_ref = outs[5:]
        width = wq_ref.shape[1]
        flat = gw_ref[...].reshape(4 * width, gw_ref.shape[2])
        for k, target in enumerate((gq, gk, gv)):
            target[...] = flat[k * width : (k + 1) * width].T
        go[...] = flat[3 * width :]
        sums = gs_ref[...]
        grouter[...] = sums[:EXPERTS]
        gconst[...] = sums[EXPERTS : EXPERTS + 4]
        gvec[...] = sums[16:18]
        gmoe[...] = sums[18:19]
        gnorm[...] = sums[19:20]
        factors = limit_ref[0] / jnp.maximum(top_ref[...], limit_ref[0])
        for h in range(fac_ref.shape[0]):
            fac_ref[h] = factors[h, 0]
        lane = lax.broadcasted_iota(jnp.int32, (1, width), 1)
        root = jnp.zeros((1, width), f32)
        for h in range(width // HEAD_DIM):
            root = jnp.where(lane // HEAD_DIM == h, jnp.sqrt(factors[h : h + 1, :1]), root)
        cq_ref[...] = (wq_ref[...].astype(f32) * root).astype(bf16)
        ck_ref[...] = (wk_ref[...].astype(f32) * root).astype(bf16)


def finish_rows(x, dn, dres, small, base, feed, gw, gs, top, wq, wk, limit, length, own, other):
    rows, width = x.shape
    each, kinds, depth, hidden = own[0].shape
    local = 2 * each
    steps = 4 if depth % 64 == 0 else 1
    tile, deep = rows // steps, depth // steps
    by_row = pl.BlockSpec((tile, width), lambda i: (i, 0))
    expert_out = pl.BlockSpec((2 * local, deep, hidden), lambda i: (0, i, 0))
    once = [
        jax.ShapeDtypeStruct(shape, f32)
        for shape in [wq.shape] * 3
        + [(wq.shape[1], depth), (1, depth), (1, depth), (EXPERTS, depth), (4, depth), (2, depth), (wq.shape[1] // HEAD_DIM,)]
    ] + [jax.ShapeDtypeStruct(wq.shape, bf16)] * 2
    return pl.pallas_call(
        finish_kernel,
        grid=(steps,),
        in_specs=[
            by_row,
            by_row,
            by_row,
            full(small.shape),
            by_row,
            by_row,
            full(gw.shape),
            full(gs.shape),
            full(top.shape),
            full(wq.shape),
            full(wk.shape),
            pl.BlockSpec(memory_space=pltpu.SMEM),
            pl.BlockSpec(memory_space=pltpu.SMEM),
        ]
        + [pl.BlockSpec((each, kinds, deep, hidden), lambda i: (0, 0, i, 0))] * 4,
        out_specs=[by_row, by_row, expert_out, expert_out, expert_out] + [full(v.shape) if v.ndim > 1 else pl.BlockSpec(memory_space=pltpu.SMEM) for v in once],
        out_shape=[
            jax.ShapeDtypeStruct((rows, width), f32),
            jax.ShapeDtypeStruct((rows, width), bf16),
        ]
        + [jax.ShapeDtypeStruct((2 * local, depth, hidden), f32)] * 3
        + once,
        compiler_params=params(),
        cost_estimate=cost(8),
        name="finish_rows",
    )(x, dn, dres, small, base, feed, gw, gs, top, wq, wk, limit, length, *own, *other)


def expert_kernel(start, first, x_ref, g_ref, gate_ref, w_ref, feed_ref, back_ref, gw_ref):
    parts, _, _, depth, hidden = w_ref.shape
    width = parts * depth
    wg, wu, wd = [w_ref[:, 0, k].reshape(width, hidden) for k in range(3)]
    x, g, gate = x_ref[0], g_ref[0], gate_ref[0]
    gate_pre = mm(x, wg)
    up = mm(x, wu)
    sigmoid = 1.0 / (1.0 + jnp.exp(-gate_pre))
    activated = gate_pre * sigmoid
    inner = (activated * up).astype(bf16)
    g32 = g.astype(f32)
    dout = (gate * g32).astype(bf16)
    dinner = mm(dout, wd)
    out = mm(inner, wd, NT)
    feed_ref[0] = (gate * out).astype(bf16)
    dgate = jnp.sum(g32 * out, axis=1, keepdims=True)
    dpre = (dinner * up * sigmoid * (1.0 + gate_pre * (1.0 - sigmoid))).astype(bf16)
    dup = (dinner * activated).astype(bf16)
    back_ref[0, :, :width] = (mm(dpre, wg, NT) + mm(dup, wu, NT)).astype(bf16)
    lane = lax.broadcasted_iota(jnp.int32, (dgate.shape[0], back_ref.shape[2] - width), 1)
    coarse = dgate.astype(bf16).astype(f32)
    at = first[0] + start + pl.program_id(0)
    extra = jnp.where(lane == at, coarse, jnp.where(lane == at + 16, dgate - coarse, 0.0))
    back_ref[0, :, width:] = extra.astype(bf16)
    for k, (left, right) in enumerate(((x, dpre), (x, dup), (dout, inner))):
        gw_ref[:, 0, k] = mm(left, right, TN).reshape(parts, depth, hidden).astype(bf16)


def expert(start, first, x, g, gate, w):
    slots, width = x.shape[1:]
    parts, some, kinds, depth, hidden = w.shape
    pick = lambda i, f: (start + i, 0, 0)
    return pl.pallas_call(
        functools.partial(expert_kernel, start),
        grid_spec=pltpu.PrefetchScalarGridSpec(
            num_scalar_prefetch=1,
            grid=(some,),
            in_specs=[
                pl.BlockSpec((1, slots, width), pick),
                pl.BlockSpec((1, slots, width), pick),
                pl.BlockSpec((1, slots, 1), pick),
                pl.BlockSpec((parts, 1, kinds, depth, hidden), lambda i, f: (0, i, 0, 0, 0)),
            ],
            out_specs=[
                pl.BlockSpec((1, slots, width), lambda i, f: (i, 0, 0)),
                pl.BlockSpec((1, slots, width + EXTRA), lambda i, f: (i, 0, 0)),
                pl.BlockSpec((parts, 1, kinds, depth, hidden), lambda i, f: (0, i, 0, 0, 0)),
            ],
        ),
        out_shape=[
            jax.ShapeDtypeStruct((some, slots, width), bf16),
            jax.ShapeDtypeStruct((some, slots, width + EXTRA), bf16),
            jax.ShapeDtypeStruct(w.shape, bf16),
        ],
        compiler_params=params(),
        cost_estimate=cost(12 * some),
        name="expert",
    )(first, x, g, gate, w)


def shards(
    hidden_in,
    cotangent,
    lengths,
    routes,
    prev_logits,
    norm_attn,
    w_query,
    w_key,
    w_value,
    w_out,
    norm_moe,
    w_router,
    w_const,
    const_vec,
    w_gate,
    w_up,
    w_down,
    threshold,
):
    plane = ("ctx", "tp")
    core = lax.axis_index("ctx")
    nc, nt, ns = lax.axis_size("ctx"), lax.axis_size("tp"), lax.axis_size("shard")
    own, width = hidden_in.shape
    per = own * nt
    total = per * nc
    depth = w_gate.shape[1]
    heads = w_query.shape[1] // HEAD_DIM
    head_width = heads * HEAD_DIM
    local = FFN_EXPERTS // nc
    count = total // BLOCK // nc
    routes, prev = routes.T, prev_logits.T
    first = (core * local).astype(jnp.int32)[None]

    expert_w = []
    for start in range(0, local, 2):
        pieces = [
            lax.dynamic_slice_in_dim(w, core * local + start, 2, 0) for w in (w_gate, w_up, w_down)
        ]
        expert_w.append(lax.all_gather(jnp.stack(pieces, axis=1), "shard", axis=0, tiled=False))
    rows_all, attention_w, small, routes_all = opening(
        hidden_in,
        (w_query, w_key, w_value, w_out),
        (w_router.T, w_const.T, const_vec, norm_attn[None], norm_moe[None]),
        routes,
        0,
    )
    rows_all = rows_all.reshape(total, width)
    cosine, sine = rope_tables(total)

    qt, kt, k, v, vt, wt, small, out_w = project(rows_all, attention_w, small, cosine, sine, heads, 8)
    ot, lse, top, cot_all = attend(lengths, qt, k, vt, cotangent, count, 1)
    att, res, base, x_slots, g_slots, gate_slots, row_at = route(
        ot, hidden_in, out_w, small, prev, routes_all, cot_all, local, 2
    )

    feeds, backs, grads = [], [], []
    for j, w in enumerate(expert_w):
        if grads:
            part = spread(row_at, feeds[0], local)
            x_slots, part = lax.optimization_barrier((x_slots, part))
        feed, back, raw = expert(2 * j, first, x_slots, g_slots, gate_slots, w)
        feeds.append(feed)
        backs.append(back)
        grads.append(lax.psum_scatter(raw, "shard", scatter_dimension=0, tiled=True)[0])
    back, feed, named = combine(row_at, backs, part, feeds[1], 3)

    dres, got, grad_out, gsmall = turn(
        lengths, res, back, named, cotangent, att, out_w, small, prev, routes_all, count, 4
    )
    dq, dk, dv, grad_out, feed = revisit(qt, k, kt, v, ot, got, lse, grad_out, feed, 5)
    part, grad_w, gsmall, top, other = closing(
        dq, dk, dv, rows_all, cosine, sine, wt, small, grad_out, gsmall, top, grads[0], 6
    )
    late, top = lax.optimization_barrier((grads[1], top))
    others = (other, swap(late, 7))
    (grad_input, output, grad_gate, grad_up, grad_down, grad_q, grad_k, grad_v, grad_out, grad_norm_attn, grad_norm_moe,
     grad_router, grad_const, grad_vec, factors, clipped_query, clipped_key) = finish_rows(
        hidden_in, part, dres, small, base, feed, grad_w, gsmall, top, w_query, w_key, threshold, lengths, grads, others
    )
    return (
        output,
        grad_input,
        grad_norm_attn[0],
        grad_q,
        grad_k,
        grad_v,
        grad_out,
        grad_norm_moe[0],
        grad_router.T,
        grad_const.T,
        grad_vec,
        grad_gate,
        grad_up,
        grad_down,
        factors,
        clipped_query,
        clipped_key,
    )


def solution(mesh):
    return jax.shard_map(
        shards,
        mesh=mesh,
        in_specs=(
            P(("shard", "ctx", "tp"), None),
            P(("shard", "ctx", "tp"), None),
            P("shard"),
            P(("shard", "ctx"), None),
            P(("shard", "ctx"), None),
            P("shard"),
            P("shard", "tp"),
            P("shard", "tp"),
            P("shard", "tp"),
            P("tp", "shard"),
            P("shard"),
            P("shard", None),
            P("shard", None),
            P(None, "shard"),
            P(None, "shard", "tp"),
            P(None, "shard", "tp"),
            P(None, "shard", "tp"),
            P(),
        ),
        out_specs=(
            P(("shard", "ctx", "tp"), None),
            P(("shard", "ctx", "tp"), None),
            P("shard"),
            P("shard", "tp"),
            P("shard", "tp"),
            P("shard", "tp"),
            P("tp", "shard"),
            P("shard"),
            P("shard", None),
            P("shard", None),
            P(None, "shard"),
            P(None, "shard", "tp"),
            P(None, "shard", "tp"),
            P(None, "shard", "tp"),
            P("tp"),
            P("shard", "tp"),
            P("shard", "tp"),
        ),
        check_vma=False,
    )
```

```python
import functools

import jax
import jax.numpy as jnp
import numpy as np
from jax import lax
from jax.experimental import pallas as pl
from jax.experimental.pallas import tpu as pltpu
from jax.sharding import PartitionSpec as P

HEAD_DIM = 64
EXPERTS = 12
FFN_EXPERTS = 8
CAP = 512
BLOCK = 512
EXTRA = 128
SMALL = 32
MESH = pl.DeviceIdType.MESH

epsilon = 1e-06
rope_base = 10000.0
bf16 = jnp.bfloat16
f32 = jnp.float32

NN = (((1,), (0,)), ((), ()))
NT = (((1,), (1,)), ((), ()))
TN = (((0,), (0,)), ((), ()))


def mm(left, right, dims=NN, precision=None):
    return lax.dot_general(
        left, right, dims, preferred_element_type=f32, precision=precision
    )


def params(mib=56, **more):
    return pltpu.CompilerParams(vmem_limit_bytes=mib * 1024 * 1024, **more)


def cost(us):
    return pl.CostEstimate(flops=int(us * 1e9), bytes_accessed=int(us * 3e6), transcendentals=0)


def full(shape):
    return pl.BlockSpec(shape, lambda *_: (0,) * len(shape))


def rope_tables(total):
    half = HEAD_DIM // 2
    freqs = np.float32(rope_base) ** (np.float32(-2.0) * np.arange(half, dtype=np.float32) / np.float32(HEAD_DIM))
    angles = freqs.astype(np.float32)[:, None] * np.arange(total, dtype=np.float32)[None, :]
    angles = angles.astype(np.float64)
    return jnp.asarray(np.cos(angles), f32), jnp.asarray(np.sin(angles), f32)


def zig(core, i):
    return 4 * (i // 2) + (core if i % 2 == 0 else 3 - core)


def anywhere(count):
    return [pl.BlockSpec(memory_space=pl.ANY)] * count


def spot():
    return lax.axis_index("shard"), lax.axis_index("ctx"), lax.axis_index("tp")


def across(t):
    return t + 1 - 2 * lax.rem(t, 2), lax.rem(t + 2, 4), 3 - t


def remote(source, target, sends, recvs, **where):
    return pltpu.make_async_remote_copy(
        src_ref=source,
        dst_ref=target,
        send_sem=sends,
        recv_sem=recvs,
        device_id=where,
        device_id_type=MESH,
    )


def greet(depth=True):
    z, c, t = spot()
    nc, nt, ns = lax.axis_size("ctx"), lax.axis_size("tp"), lax.axis_size("shard")
    barrier = pltpu.get_barrier_semaphore()
    for step in range(1, nc * nt):
        other = lax.rem(c * nt + t + step, nc * nt)
        pl.semaphore_signal(
            barrier,
            inc=1,
            device_id={"ctx": other // nt, "tp": lax.rem(other, nt)},
            device_id_type=MESH,
        )
    if depth:
        for step in range(1, ns):
            pl.semaphore_signal(
                barrier,
                inc=1,
                device_id={"shard": lax.rem(z + step, ns)},
                device_id_type=MESH,
            )
    pl.semaphore_wait(barrier, nc * nt - 1 + (ns - 1 if depth else 0))


class Gather:
    KINDS = 9

    def __init__(self, x, out, sends, recvs, own, cuts, stage=None, relative=False):
        z, c, t = spot()
        tx, ty, td = across(t)
        rows = x.shape[0] // cuts
        half = rows // 2
        self.cuts = cuts
        sib = {"ctx": 1 - c}
        px, py = {"tp": tx}, {"tp": ty}
        near = (t, tx, ty, td)
        if relative:
            here, there = list(range(8)), list(range(8))
            mine = (1, 2, 4)
            passed = ((1, 5), (1, 3), (2, 6), (2, 3), (3, 7), (3, 7))
        else:
            here = [4 * c + n for n in near] + [4 * (1 - c) + n for n in near]
            there = here[:4]
            mine = (here[0],) * 3
            passed = tuple((here[n], here[n]) for n in (1, 1, 2, 2, 3, 3))
        self.load = None if stage is None else pltpu.make_async_copy(x, stage, own.at[0])
        self.own = pltpu.make_async_copy(x if stage is None else stage, out.at[here[0]], own.at[1])

        def parts(s):
            whole = pl.ds(s * rows, rows)
            one, two = pl.ds(s * rows, half), pl.ds(s * rows + half, half)
            return whole, one, two

        def copies(s):
            whole, one, two = parts(s)
            made = [
                remote(x.at[whole], out.at[slot, whole], sends.at[s, k], recvs.at[s, k], **where)
                for k, (slot, where) in enumerate(zip(mine, (px, py, sib)))
            ]
            ways = ((whole, sib), (one, py), (whole, sib), (two, px), (one, sib), (two, sib))
            for k, ((source, target), (part, where)) in enumerate(zip(passed, ways)):
                made.append(
                    remote(out.at[source, part], out.at[target, part], sends.at[s, k + 3], recvs.at[s, k + 3], **where)
                )
            return made

        self.copies = [copies(s) for s in range(cuts)]

        def arrivals(s):
            whole, one, two = parts(s)
            where = [(1, whole), (2, whole), (4, whole), (5, whole), (3, one), (6, whole), (3, two), (7, one), (7, two)]
            return [
                remote(out.at[here[n], part], out.at[here[n], part], sends.at[s, k], recvs.at[s, k], **sib)
                for k, (n, part) in enumerate(where)
            ]

        self.arrivals = [arrivals(s) for s in range(cuts)]

    @staticmethod
    def scratch(cuts):
        return [
            pltpu.SemaphoreType.DMA((cuts, Gather.KINDS)),
            pltpu.SemaphoreType.DMA((cuts, Gather.KINDS)),
            pltpu.SemaphoreType.DMA((2,)),
        ]

    def first(self):
        for s in range(self.cuts):
            for k in (0, 1, 2):
                self.copies[s][k].start()
        (self.load or self.own).start()

    def second(self, s):
        if self.load is not None and s == 0:
            self.load.wait()
            self.own.start()
        self.arrivals[s][0].wait_recv()
        self.copies[s][4].start()
        self.copies[s][3].start()
        self.arrivals[s][1].wait_recv()
        self.copies[s][6].start()
        self.copies[s][5].start()

    def third(self, s):
        for k in (4, 6):
            self.arrivals[s][k].wait_recv()
            self.copies[s][7 if k == 4 else 8].start()

    def beside(self):
        for s in range(self.cuts):
            for k in (2, 3, 5):
                self.arrivals[s][k].wait_recv()

    def last(self, rest=False):
        for s in range(self.cuts):
            for k in (7, 8) if rest else (2, 3, 5, 7, 8):
                self.arrivals[s][k].wait_recv()
        for s in range(self.cuts):
            for k in range(self.KINDS):
                self.copies[s][k].wait_send()
        if not rest:
            self.own.wait()


class Sum:
    def __init__(self, p, held, came, across_in, across_out, sends, recvs, loads, stage=None):
        z, c, t = spot()
        self.t = t
        tx, ty, td = across(t)
        half = held.shape[1] // 2
        self.half = half
        self.one, self.two = pl.ds(0, half), pl.ds(half, half)
        self.order = (td, tx, ty, t)
        self.held, self.came, self.inn = held, came, across_in
        sib, px, py = {"ctx": 1 - c}, {"tp": tx}, {"tp": ty}
        self.core = []
        for k, o in enumerate(self.order):
            source = p.at[4 * (1 - c) + o] if stage is None else stage.at[k]
            self.core.append(remote(source, came.at[o], sends.at[k], recvs.at[k], **sib))
        self.loads = None
        if stage is None:
            self.loads = [pltpu.make_async_copy(p.at[4 * c + o], held.at[o], loads.at[k]) for k, o in enumerate(self.order)]

        def send(k, source, slot, where):
            return remote(source, across_in.at[slot], sends.at[k], recvs.at[k], **where)

        self.side = {
            "dx": send(4, held.at[td, self.one], 0, px),
            "dy": send(5, held.at[td, self.two], 1, py),
            "x": send(6, held.at[tx, self.one], 2, px),
            "y": send(7, held.at[ty, self.two], 3, py),
            "cy": send(8, across_out.at[0], 4, py),
            "cx": send(9, across_out.at[1], 5, px),
        }
        self.out = across_out
        self.near = (tx, ty, td)

    @staticmethod
    def scratch(rows, width):
        return [
            pltpu.VMEM((4, rows, width), bf16),
            pltpu.VMEM((4, rows, width), bf16),
            pltpu.VMEM((6, rows // 2, width), bf16),
            pltpu.VMEM((2, rows // 2, width), bf16),
            pltpu.SemaphoreType.DMA((10,)),
            pltpu.SemaphoreType.DMA((10,)),
            pltpu.SemaphoreType.DMA((4,)),
        ]

    def first(self):
        for k in range(4):
            self.core[k].start()
            self.loads[k].start()

    def add(self, k, mine):
        o = self.order[k]
        self.core[k].wait_recv()
        self.held[o] = (mine + self.came[o].astype(mine.dtype)).astype(bf16)
        for name in (("dx", "dy"), ("x",), ("y",), ())[k]:
            self.side[name].start()

    def second(self):
        for k, o in enumerate(self.order):
            self.loads[k].wait()
            self.add(k, self.held[o])

    def third(self):
        tx, ty, td = self.near
        self.side["dx"].wait_recv()
        self.out[0] = self.held[ty, self.one] + self.inn[0]
        self.side["cy"].start()
        self.side["dy"].wait_recv()
        self.out[1] = self.held[tx, self.two] + self.inn[1]
        self.side["cx"].start()

    def last(self):
        for k in ("x", "y", "cy", "cx"):
            self.side[k].wait_recv()
        for copy in self.core + list(self.side.values()):
            copy.wait_send()

    def total(self):
        def add(part, a, b):
            return self.held[self.t, part].astype(f32) + self.inn[a].astype(f32) + self.inn[b].astype(f32)

        return add(self.one, 2, 4), add(self.two, 3, 5)


def qkv_kernel(x_ref, w_ref, s_ref, cos_ref, sin_ref, qt_ref, kt_ref, k_ref, v_ref, vt_ref, wt_ref, small_ref, wo_ref, wo, send, recv, local):
    heads = qt_ref.shape[0]
    width = heads * HEAD_DIM
    half = HEAD_DIM // 2
    z, c, t = spot()
    nt = lax.axis_size("tp")
    mid = width // 2
    mine, theirs = pl.ds(c * mid, mid), pl.ds((1 - c) * mid, mid)
    away, came, onward, there = [], [], [], []
    for step in range(1, nt):
        back = lax.rem(t + nt - step, nt)
        away.append(remote(wo.at[mine], wo_ref.at[t, mine], send.at[step], recv.at[step], tp=lax.rem(t + step, nt)))
        ref = wo_ref.at[back, mine]
        came.append(remote(ref, ref, send.at[nt + step], recv.at[step], ctx=1 - c))
        onward.append(remote(ref, ref, send.at[nt + step], recv.at[nt + step], ctx=1 - c))
        ref = wo_ref.at[back, theirs]
        there.append(remote(ref, ref, send.at[nt + step], recv.at[nt + step], ctx=1 - c))
    own = pltpu.make_async_copy(wo, wo_ref.at[t], local)
    i = pl.program_id(0)

    @pl.when(i == 0)
    def _():
        def flat(v):
            return v.astype(f32).reshape(v.shape[0] * v.shape[1], v.shape[2])

        def whole(core, which):
            rest = flat(w_ref[core, :, 2])[:, which * (width - 128) : (which + 1) * (width - 128)]
            return jnp.concatenate([flat(w_ref[core, :, which]), rest], axis=1).T.astype(bf16)

        wo[...] = whole(1, 1)
        greet(False)
        for copy in away:
            copy.start()
        own.start()
        wt_ref[:width] = whole(0, 0)
        wt_ref[width : 2 * width] = whole(0, 1)
        wt_ref[2 * width :] = whole(1, 0)
        small_ref[...] = jnp.concatenate([s_ref[n].astype(f32) for n in range(s_ref.shape[0])], axis=1)

    x = x_ref[...].astype(f32)
    inverse = lax.rsqrt(jnp.mean(x * x, axis=1, keepdims=True) + epsilon)
    a = (x * inverse * small_ref[18:19]).astype(bf16)
    y = mm(wt_ref[...], a, NT)
    cosine, sine = cos_ref[...], sin_ref[...]

    def turned(first):
        u, w = y[first : first + half], y[first + half : first + HEAD_DIM]
        return jnp.concatenate([u * cosine - w * sine, w * cosine + u * sine], axis=0)

    for h in range(heads):
        at = h * HEAD_DIM
        qt_ref[h] = (turned(at) * HEAD_DIM**-0.5).astype(bf16)
        key = turned(width + at)
        kt_ref[h] = key.astype(bf16)
        k_ref[h] = key.T.astype(bf16)
        value = y[2 * width + at : 2 * width + at + HEAD_DIM]
        v_ref[h] = value.T.astype(bf16)
        vt_ref[h, :HEAD_DIM] = value.astype(bf16)
        vt_ref[h, HEAD_DIM:] = jnp.ones((16, value.shape[1]), bf16)

    @pl.when(i == pl.num_programs(0) - 2)
    def _():
        for copy, forth in zip(came, onward):
            copy.wait_recv()
            forth.start()

    @pl.when(i == pl.num_programs(0) - 1)
    def _():
        for copy in there:
            copy.wait_recv()
        for copy in away + onward:
            copy.wait_send()
        own.wait()


def project(rows, w, small, cosine, sine, heads, number):
    total, width = rows.shape
    tile = BLOCK
    out = heads * HEAD_DIM
    nt = lax.axis_size("tp")
    shapes = [
        jax.ShapeDtypeStruct((heads, HEAD_DIM, total), bf16),
        jax.ShapeDtypeStruct((heads, HEAD_DIM, total), bf16),
        jax.ShapeDtypeStruct((heads, total, HEAD_DIM), bf16),
        jax.ShapeDtypeStruct((heads, total, HEAD_DIM), bf16),
        jax.ShapeDtypeStruct((heads, HEAD_DIM + 16, total), bf16),
        jax.ShapeDtypeStruct((3 * out, width), bf16),
        jax.ShapeDtypeStruct((SMALL, width), f32),
        jax.ShapeDtypeStruct((nt, out, width), bf16),
    ]
    return pl.pallas_call(
        qkv_kernel,
        grid=(total // tile,),
        in_specs=[
            pl.BlockSpec((tile, width), lambda i: (i, 0)),
            full(w.shape),
            full(small.shape),
            pl.BlockSpec((HEAD_DIM // 2, tile), lambda i: (0, i)),
            pl.BlockSpec((HEAD_DIM // 2, tile), lambda i: (0, i)),
        ],
        out_specs=[
            pl.BlockSpec((heads, HEAD_DIM, tile), lambda i: (0, 0, i)),
            pl.BlockSpec((heads, HEAD_DIM, tile), lambda i: (0, 0, i)),
            pl.BlockSpec((heads, tile, HEAD_DIM), lambda i: (0, i, 0)),
            pl.BlockSpec((heads, tile, HEAD_DIM), lambda i: (0, i, 0)),
            pl.BlockSpec((heads, HEAD_DIM + 16, tile), lambda i: (0, 0, i)),
        ]
        + [full(v.shape) for v in shapes[5:7]]
        + anywhere(1),
        scratch_shapes=[
            pltpu.VMEM((out, width), bf16),
            pltpu.SemaphoreType.DMA((2 * nt,)),
            pltpu.SemaphoreType.DMA((2 * nt,)),
            pltpu.SemaphoreType.DMA,
        ],
        out_shape=shapes,
        compiler_params=params(collective_id=number, has_side_effects=True),
        cost_estimate=cost(14),
        name="project",
    )(rows, w, small, cosine, sine)


def dealt(core, i):
    return 4 * (i // 2) + jnp.where(lax.rem(i, 2) == 0, core, 3 - core)


def attend_kernel(cuts, length, qt_ref, k_ref, vt_ref, cot_ref, ot_ref, lse_ref, top_ref, cots_ref, mask_cot, *sems):
    z, c, t = spot()
    nt = lax.axis_size("tp")
    h, i = pl.program_id(0), pl.program_id(1)
    count = pl.num_programs(1)
    at_step = h * count + i
    last = pl.num_programs(0) * count - 1
    gather = Gather(mask_cot, cots_ref, *sems, cuts)

    @pl.when(at_step == 0)
    def _():
        rows = cot_ref.shape[0]
        position = (c * nt + t) * rows + lax.broadcasted_iota(jnp.int32, cot_ref.shape, 0)
        mask_cot[...] = jnp.where(position < length[0], cot_ref[...].astype(f32), 0.0).astype(bf16)
        greet(False)
        gather.first()

    index = dealt(c, i)
    columns = BLOCK
    qt = qt_ref[0, :, pl.ds(pl.multiple_of(index * BLOCK, BLOCK), BLOCK)]

    def step(at, carry, diagonal):
        peak, total = carry
        start = pl.multiple_of(at * BLOCK, BLOCK)
        scores = mm(k_ref[0, pl.ds(start, BLOCK), :], qt)
        if diagonal:
            keys = lax.broadcasted_iota(jnp.int32, scores.shape, 0)
            queries = lax.broadcasted_iota(jnp.int32, scores.shape, 1)
            scores = jnp.where(keys <= queries, scores, -1e30)
        higher = jnp.maximum(peak, jnp.max(scores, axis=0, keepdims=True))
        weights = jnp.exp(scores - higher).astype(bf16)
        total = total * jnp.exp(peak - higher) + mm(vt_ref[0, :, pl.ds(start, BLOCK)], weights)
        return higher, total

    start = (jnp.full((1, columns), -1e30, f32), jnp.zeros((HEAD_DIM + 16, columns), f32))
    carry = lax.fori_loop(0, index, lambda at, c: step(at, c, False), start)
    peak, total = step(index, carry, True)
    mass = total[HEAD_DIM : HEAD_DIM + 1]
    ot_ref[0] = (total[:HEAD_DIM] / mass).astype(bf16)
    lse_ref[0, 0] = peak + jnp.log(mass)
    position = index * BLOCK + lax.broadcasted_iota(jnp.int32, peak.shape, 1)
    top_ref[0, 0] = jnp.where(position < length[0], peak, -1e30)

    @pl.when(at_step == last - 3)
    def _():
        for s in range(cuts):
            gather.second(s)

    @pl.when(at_step == last)
    def _():
        for s in range(cuts):
            gather.third(s)
        gather.last()


def attend(length, qt, k, vt, cot, count, number):
    cuts = 1
    heads, _, total = qt.shape
    return pl.pallas_call(
        functools.partial(attend_kernel, cuts),
        grid_spec=pltpu.PrefetchScalarGridSpec(
            num_scalar_prefetch=1,
            grid=(heads, count),
            in_specs=[
                pl.BlockSpec((1, HEAD_DIM, total), lambda h, i, n: (h, 0, 0)),
                pl.BlockSpec((1, total, HEAD_DIM), lambda h, i, n: (h, 0, 0)),
                pl.BlockSpec((1, HEAD_DIM + 16, total), lambda h, i, n: (h, 0, 0)),
                full(cot.shape),
            ],
            out_specs=[
                pl.BlockSpec((1, HEAD_DIM, BLOCK), lambda h, i, n: (i, h, 0)),
                pl.BlockSpec((1, 1, 1, BLOCK), lambda h, i, n: (h, i, 0, 0)),
                pl.BlockSpec((1, 1, 1, BLOCK), lambda h, i, n: (h, i, 0, 0)),
            ]
            + anywhere(1),
            scratch_shapes=[
                pltpu.VMEM(cot.shape, bf16),
            ]
            + Gather.scratch(cuts),
        ),
        out_shape=[
            jax.ShapeDtypeStruct((count, heads * HEAD_DIM, BLOCK), bf16),
            jax.ShapeDtypeStruct((heads, count, 1, BLOCK), f32),
            jax.ShapeDtypeStruct((heads, count, 1, BLOCK), f32),
            jax.ShapeDtypeStruct((8,) + cot.shape, bf16),
        ],
        compiler_params=params(collective_id=number, has_side_effects=True),
        cost_estimate=cost(35),
        name="attend",
    )(length, qt, k, vt, cot)


def revisit_kernel(qt_ref, k_ref, kt_ref, v_ref, ot_ref, got_ref, lse_ref, go_ref, feed_ref, dq_ref, dk_ref, dv_ref, gos_ref, fed_ref, sum_k, sum_v, came_ref, w_send, w_recv, *scratch):
    z, c, t = spot()
    job = Sum(feed_ref, *scratch)
    nt = lax.axis_size("tp")
    h, i = pl.program_id(0), pl.program_id(1)
    count = pl.num_programs(1)
    index = dealt(c, i)
    here = pl.ds(pl.multiple_of(index * BLOCK, BLOCK), BLOCK)
    away = [
        remote(go_ref.at[lax.rem(t + step, nt)], came_ref.at[step], w_send.at[step], w_recv.at[step], tp=lax.rem(t + step, nt))
        for step in range(1, nt)
    ]

    at_step = h * count + i
    end = pl.num_programs(0) * count - 1

    @pl.when(at_step == 0)
    def _():
        greet(False)
        job.first()
        for copy in away:
            copy.start()

    @pl.when(at_step == 3)
    def _():
        job.second()

    @pl.when(at_step == end - 3)
    def _():
        job.third()

    qt, got = qt_ref[0, :, here], got_ref[0]
    lse = lse_ref[0, 0]
    centre = jnp.sum(ot_ref[0].astype(f32) * got.astype(f32), axis=0, keepdims=True)

    @pl.when(i == 0)
    def _():
        sum_k[...] = jnp.zeros_like(sum_k)
        sum_v[...] = jnp.zeros_like(sum_v)
        dq_ref[...] = jnp.zeros_like(dq_ref)

    def step(at, grad, diagonal):
        start = pl.multiple_of(at * BLOCK, BLOCK)
        here = pl.ds(start, BLOCK)
        scores = mm(k_ref[0, here, :], qt)
        probs = jnp.exp(scores - lse)
        if diagonal:
            keys = lax.broadcasted_iota(jnp.int32, scores.shape, 0)
            queries = lax.broadcasted_iota(jnp.int32, scores.shape, 1)
            probs = jnp.where(keys <= queries, probs, 0.0)
        grad_probs = mm(v_ref[0, here, :], got)
        grad_scores = (probs * (grad_probs - centre)).astype(bf16)
        sum_v[:, here] += mm(got, probs.astype(bf16), NT)
        sum_k[:, here] += mm(qt, grad_scores, NT)
        return grad + mm(kt_ref[0, :, here], grad_scores)

    grad = lax.fori_loop(0, index, lambda at, c: step(at, c, False), jnp.zeros(qt.shape, f32))
    dq_ref[0, :, here] = step(index, grad, True) * HEAD_DIM**-0.5

    @pl.when(i == count - 1)
    def _():
        dk_ref[0] = sum_k[...]
        dv_ref[0] = sum_v[...]

    @pl.when(at_step == end)
    def _():
        job.last()
        one, two = job.total()
        fed_ref[: job.half] = one
        fed_ref[job.half :] = two
        total = go_ref[t].astype(f32)
        for step, copy in enumerate(away):
            copy.wait_recv()
            total = total + came_ref[step + 1].astype(f32)
            copy.wait_send()
        gos_ref[...] = total.astype(bf16)


def revisit(qt, k, kt, v, ot, got, lse, go, feed, number):
    heads, _, total = qt.shape
    count = ot.shape[0]
    nt = lax.axis_size("tp")
    whole = pl.BlockSpec((1, HEAD_DIM, total), lambda h, i: (h, 0, 0))
    tall = pl.BlockSpec((1, total, HEAD_DIM), lambda h, i: (h, 0, 0))
    some = pl.BlockSpec((1, HEAD_DIM, BLOCK), lambda h, i: (i, h, 0))
    return pl.pallas_call(
        revisit_kernel,
        grid=(heads, count),
        in_specs=[
            whole,
            tall,
            whole,
            tall,
            some,
            some,
            pl.BlockSpec((1, 1, 1, BLOCK), lambda h, i: (h, i, 0, 0)),
            full(go.shape),
        ]
        + anywhere(1),
        out_specs=[whole, whole, whole, full(go.shape[1:]), full(feed.shape[1:])],
        scratch_shapes=[
            pltpu.VMEM((HEAD_DIM, total), f32),
            pltpu.VMEM((HEAD_DIM, total), f32),
            pltpu.VMEM(go.shape, bf16),
            pltpu.SemaphoreType.DMA((nt,)),
            pltpu.SemaphoreType.DMA((nt,)),
        ]
        + Sum.scratch(*feed.shape[1:]),
        out_shape=[jax.ShapeDtypeStruct((heads, HEAD_DIM, total), f32)] * 3
        + [jax.ShapeDtypeStruct(go.shape[1:], bf16), jax.ShapeDtypeStruct(feed.shape[1:], f32)],
        compiler_params=params(collective_id=number, has_side_effects=True),
        cost_estimate=cost(50),
        name="revisit",
    )(qt, k, kt, v, ot, got, lse, go, feed)


def opening_kernel(cuts, x_ref, wq_ref, wk_ref, wv_ref, wo_ref, wr_ref, wc_ref, vec_ref, na_ref, nm_ref, routes_ref, out_ref, ws_ref, smalls_ref, all_routes_ref, held, stage, small_ref, *sems):
    gather = Gather(x_ref, out_ref, *sems[:3], cuts, stage)
    sends, recvs, local = sems[3:]
    z, c, t = spot()
    ns = lax.axis_size("shard")
    one = jnp.where(c == 0, wq_ref[...].astype(f32), wv_ref[...].astype(f32))
    two = jnp.where(c == 0, wk_ref[...].astype(f32), wo_ref[...].astype(f32).T)
    held[0] = one[:, :128].astype(bf16)
    held[1] = two[:, :128].astype(bf16)
    parts = [v[...].astype(f32) for v in (wr_ref, wc_ref, vec_ref, na_ref, nm_ref)]
    used = sum(v.shape[0] for v in parts)
    parts.append(jnp.zeros((SMALL - used, parts[0].shape[1]), f32))
    small_ref[...] = jnp.concatenate(parts, axis=0).astype(bf16)
    held[2] = jnp.concatenate([one[:, 128:], two[:, 128:]], axis=1).astype(bf16)
    greet()
    started = []

    def go(k, source, target, **where):
        copy = remote(source, target, sends.at[k], recvs.at[k], **where)
        copy.start()
        started.append(copy)

    def came(k, ref):
        remote(ref, ref, sends.at[k], recvs.at[k], ctx=1 - c).wait_recv()

    for step in range(1, ns):
        go(step, held, ws_ref.at[c, z], shard=lax.rem(z + step, ns))
    gather.first()
    for step in range(1, ns):
        go(2 * ns + step, small_ref, smalls_ref.at[z], shard=lax.rem(z + step, ns))
    go(0, held, ws_ref.at[c, z], ctx=1 - c)
    go(ns, routes_ref, all_routes_ref.at[c], ctx=1 - c)
    mine = [
        pltpu.make_async_copy(held, ws_ref.at[c, z], local.at[0]),
        pltpu.make_async_copy(small_ref, smalls_ref.at[z], local.at[1]),
        pltpu.make_async_copy(routes_ref, all_routes_ref.at[c], local.at[2]),
    ]
    for copy in mine:
        copy.start()
    for s in range(cuts):
        gather.second(s)
    for s in range(cuts):
        gather.third(s)
    for step in range(1, ns):
        back = lax.rem(z + ns - step, ns)
        came(step, ws_ref.at[c, back])
        go(ns + step, ws_ref.at[c, back], ws_ref.at[c, back], ctx=1 - c)
    gather.last()
    came(0, ws_ref.at[1 - c, z])
    came(ns, all_routes_ref.at[1 - c])
    for step in range(1, ns):
        back = lax.rem(z + ns - step, ns)
        came(2 * ns + step, smalls_ref.at[back])
        came(ns + step, ws_ref.at[1 - c, back])
    for copy in started:
        copy.wait_send()
    for copy in mine:
        copy.wait()


def opening(x, weights, small, routes, number):
    cuts = 2
    ns = lax.axis_size("shard")
    depth = weights[0].shape[0]
    held = (3, depth, 128)
    vmem = pl.BlockSpec(memory_space=pltpu.VMEM)
    return pl.pallas_call(
        functools.partial(opening_kernel, cuts),
        in_specs=anywhere(1) + [vmem] * (len(weights) + len(small) + 1),
        out_specs=anywhere(4),
        out_shape=[
            jax.ShapeDtypeStruct((8,) + x.shape, x.dtype),
            jax.ShapeDtypeStruct((2, ns) + held, bf16),
            jax.ShapeDtypeStruct((ns, SMALL, depth), bf16),
            jax.ShapeDtypeStruct((2,) + routes.shape, routes.dtype),
        ],
        scratch_shapes=[pltpu.VMEM(held, bf16), pltpu.VMEM(x.shape, x.dtype), pltpu.VMEM((SMALL, depth), bf16)]
        + Gather.scratch(cuts)
        + [
            pltpu.SemaphoreType.DMA((3 * ns,)),
            pltpu.SemaphoreType.DMA((3 * ns,)),
            pltpu.SemaphoreType.DMA((3,)),
        ],
        compiler_params=params(collective_id=number, has_side_effects=True),
        cost_estimate=cost(30),
        name="opening",
    )(x, *weights, *small, routes)


def places(routes_ref, row_ref):
    one = lax.broadcasted_iota(jnp.int32, (BLOCK, BLOCK), 0)
    two = lax.broadcasted_iota(jnp.int32, (BLOCK, BLOCK), 1)
    before = (one < two).astype(bf16)
    blocks, _, per = routes_ref.shape
    for b in range(blocks):
        carry = jnp.zeros((16, 1), f32)
        for at in range(0, per, BLOCK):
            here = slice(at, at + BLOCK)
            expert = lax.broadcasted_iota(jnp.int32, (16, BLOCK), 0)
            member = (routes_ref[b, 0:1, here] == expert) | (routes_ref[b, 1:2, here] == expert)
            rank = mm(member.astype(bf16), before) + carry
            row_ref[:, b * per + at : b * per + at + BLOCK] = jnp.where(member, rank, -1.0)
            carry = carry + jnp.sum(member.astype(f32), axis=1, keepdims=True)


def route_kernel(cuts, o_ref, x_ref, wo_ref, small_ref, prev_ref, routes_ref, cots_ref,
                 att, res_out, base_out, x_out, g_out, gate_ref, row_ref,
                 x_in, wo_in, res, base, a, comb, rows, cots, combs, xs, gs,
                 o_send, o_recv, c_send, c_recv, local, out_sem, x_sem, g_sem, *sems):
    gather = Gather(a, rows, *sems, cuts, relative=True)
    z, c, t = spot()
    nt = lax.axis_size("tp")
    own = 4 * c + t
    near = (t,) + across(t)
    blocks, _, per = routes_ref.shape
    width = rows.shape[2]
    experts = xs.shape[0]
    here = pl.ds(pl.multiple_of(t * BLOCK, BLOCK), BLOCK)
    loads = [
        pltpu.make_async_copy(cots_ref, cots, local.at[0]),
        pltpu.make_async_copy(x_ref, x_in, local.at[1]),
        pltpu.make_async_copy(wo_ref, wo_in, local.at[2]),
    ]
    for copy in loads:
        copy.start()
    greet(False)

    copies = []
    for i in range(o_ref.shape[0]):
        block = zig(c, i)
        copy = remote(o_ref.at[i], att.at[t], o_send.at[i], o_recv.at[t], ctx=block // nt, tp=lax.rem(block, nt))
        copies.append((block == own, copy, pltpu.make_async_copy(o_ref.at[i], att.at[t], local.at[3])))
    for mine, copy, inside in copies:

        @pl.when(jnp.logical_not(mine))
        def _():
            copy.start()

        @pl.when(mine)
        def _():
            inside.start()

    each = per // nt

    def names(b, j, order):
        start = pl.multiple_of(b * per, per)
        mine = row_ref[pl.ds(experts * c + j, 1), pl.ds(start, per)] if order is None else jnp.concatenate(
            [row_ref[pl.ds(experts * c + j, 1), pl.ds(pl.multiple_of(start + o * each, each), each)] for o in order], axis=1
        )
        return lax.broadcasted_iota(jnp.int32, (CAP, mine.shape[1]), 0).astype(f32) == mine

    def fetch(n):
        b, j = n // experts, lax.rem(n, experts)
        here = pl.ds(pl.multiple_of(b * CAP, CAP), CAP)
        hot = names(b, j, None)
        gs[j, here] = mm(hot.astype(bf16), cots[pl.ds(4 * b, 4)].reshape(per, width)).astype(bf16)
        pltpu.make_async_copy(gs.at[j, here], g_out.at[j, here], g_sem.at[n]).start()

    def fetch_x(beside, j, which):
        b = 1 - c if beside else c
        here = pl.ds(pl.multiple_of(b * CAP, CAP), CAP)
        order = [near[k] for k in which]
        hot = names(b, j, order)
        first = 4 * beside + which[0]
        got = mm(hot.astype(bf16), rows[first : first + len(which)].reshape(len(which) * each, width)).astype(bf16)
        gate = jnp.zeros((CAP, 1), f32)
        for k, o in enumerate(order):
            weight = combs[4 * b + o, pl.ds(experts * c + j, 1)]
            gate = gate + jnp.sum(jnp.where(hot[:, k * each : (k + 1) * each], weight, 0.0), axis=1, keepdims=True)
        if which[0] == 0:
            xs[j, here] = got
            gate_ref[j, here] = gate
        else:
            xs[j, here] = xs[j, here] + got
            gate_ref[j, here] = gate_ref[j, here] + gate
            n = b * experts + j
            pltpu.make_async_copy(xs.at[j, here], x_out.at[j, here], x_sem.at[n]).start()

    def all_x(beside, which):
        @pl.loop(0, experts)
        def _(j):
            fetch_x(beside, j, which)

    def fetch_g(first, last):
        @pl.loop(first, last)
        def _(n):
            fetch(n)

    places(routes_ref, row_ref)
    for copy in loads:
        copy.wait()
    fetch_g(0, 2)
    for mine, copy, inside in copies:

        @pl.when(jnp.logical_not(mine))
        def _():
            copy.wait_send()

        @pl.when(mine)
        def _():
            inside.wait()

    mine = lax.rem((own + 1) // 2, 2) == c
    for source in range(nt):

        @pl.when(jnp.logical_or(jnp.logical_not(mine), source != t))
        def _():
            remote(o_ref.at[0], att.at[source], o_send.at[0], o_recv.at[source], ctx=c, tp=t).wait_recv()

    attended = att[...].reshape(-1, BLOCK)
    r = x_in[...].astype(f32) + mm(attended, wo_in[...].reshape(-1, width), TN)
    inverse = lax.rsqrt(jnp.mean(r * r, axis=1, keepdims=True) + epsilon)
    n2 = r * inverse * small_ref[19:20]
    a[...] = n2.astype(bf16)
    gather.first()
    res[...] = r
    _, _, combined, alphas, weights = mixing(n2, small_ref[:16], *laid(prev_ref[:, here], routes_ref[c, :, here]))
    comb[...] = combined
    pairs = []
    for step in range(1, 8):
        other, back = lax.rem(own + step, 8), lax.rem(own + 8 - step, 8)
        where = {"ctx": other // 4, "tp": lax.rem(other, 4)}
        copy = remote(comb, combs.at[own], c_send.at[step], c_recv.at[step], **where)
        copy.start()
        pairs.append((copy, remote(comb, combs.at[back], c_send.at[step], c_recv.at[step], **where)))
    combs[own] = comb[...]
    scale, one, two = scales(alphas, weights)
    base[...] = r + scale * n2 + one * small_ref[16:17] + two * small_ref[17:18]
    outs = [
        pltpu.make_async_copy(res, res_out, out_sem.at[0]),
        pltpu.make_async_copy(base, base_out, out_sem.at[1]),
    ]
    for copy in outs:
        copy.start()

    total = blocks * experts
    fetch_g(2, 4)
    gather.second(0)
    fetch_g(4, total)
    gather.second(1)
    gather.own.wait()
    for copy, came in pairs:
        came.wait_recv()
    all_x(0, (0, 1, 2))
    gather.third(0)
    gather.third(1)
    gather.beside()
    all_x(1, (0, 1, 2))
    all_x(0, (3,))
    gather.last(True)
    all_x(1, (3,))

    for copy, came in pairs:
        copy.wait_send()
    for copy in outs:
        copy.wait()

    @pl.loop(0, total)
    def _(n):
        b, j = n // experts, lax.rem(n, experts)
        here = pl.ds(pl.multiple_of(b * CAP, CAP), CAP)
        pltpu.make_async_copy(gs.at[j, here], g_out.at[j, here], g_sem.at[n]).wait()
        pltpu.make_async_copy(xs.at[j, here], x_out.at[j, here], x_sem.at[n]).wait()


def route(o, x, wo, small, prev, routes, cots, experts, number):
    cuts = 2
    own, width = x.shape
    nt = lax.axis_size("tp")
    blocks, _, per = routes.shape
    slots = jax.ShapeDtypeStruct((experts, blocks * CAP, width), bf16)
    vmem = pl.BlockSpec(memory_space=pltpu.VMEM)
    return pl.pallas_call(
        functools.partial(route_kernel, cuts),
        in_specs=anywhere(3) + [vmem, vmem, vmem] + anywhere(1),
        out_specs=[vmem] + anywhere(4) + [vmem, vmem],
        out_shape=[
            jax.ShapeDtypeStruct((nt,) + o.shape[1:], bf16),
            jax.ShapeDtypeStruct((own, width), f32),
            jax.ShapeDtypeStruct((own, width), f32),
            slots,
            slots,
            jax.ShapeDtypeStruct((experts, blocks * CAP, 1), f32),
            jax.ShapeDtypeStruct((16, blocks * per), f32),
        ],
        scratch_shapes=[
            pltpu.VMEM((own, width), bf16),
            pltpu.VMEM(wo.shape, bf16),
            pltpu.VMEM((own, width), f32),
            pltpu.VMEM((own, width), f32),
            pltpu.VMEM((own, width), bf16),
            pltpu.VMEM((16, own), f32),
            pltpu.VMEM((8, own, width), bf16),
            pltpu.VMEM((8, own, width), bf16),
            pltpu.VMEM((8, 16, own), f32),
            pltpu.VMEM(slots.shape, bf16),
            pltpu.VMEM(slots.shape, bf16),
            pltpu.SemaphoreType.DMA((o.shape[0],)),
            pltpu.SemaphoreType.DMA((nt,)),
            pltpu.SemaphoreType.DMA((8,)),
            pltpu.SemaphoreType.DMA((8,)),
            pltpu.SemaphoreType.DMA((4,)),
            pltpu.SemaphoreType.DMA((2,)),
            pltpu.SemaphoreType.DMA((blocks * experts,)),
            pltpu.SemaphoreType.DMA((blocks * experts,)),
        ]
        + Gather.scratch(cuts),
        compiler_params=params(collective_id=number, has_side_effects=True),
        cost_estimate=cost(65),
        name="route",
    )(o, x, wo, small, prev, routes, cots)


def spot_rows(place, c, experts, first, some, values, at):
    lane = lax.broadcasted_iota(jnp.int32, place.shape, 1)
    slot = lax.broadcasted_iota(jnp.int32, (place.shape[0], CAP), 1).astype(f32)
    total = None
    for j in range(some):
        mine = jnp.sum(jnp.where(lane == experts * c + first + j, place, 0.0), axis=1, keepdims=True)
        term = mm((slot == mine).astype(bf16), values[j, at])
        total = term if total is None else total + term
    return total


def spread_kernel(experts, row_ref, feed_ref, out_ref):
    c = lax.axis_index("ctx")
    out_ref[0] = spot_rows(row_ref[...].T, c, experts, 0, feed_ref.shape[0], feed_ref, slice(None)).astype(bf16)


def spread(row, feed, experts):
    some, slots, width = feed.shape
    rows = row.shape[1] // 8
    return pl.pallas_call(
        functools.partial(spread_kernel, experts),
        grid=(8,),
        in_specs=[
            pl.BlockSpec((16, rows), lambda i: (0, i)),
            pl.BlockSpec((some, CAP, width), lambda i: (0, i // 4, 0)),
        ],
        out_specs=pl.BlockSpec((1, rows, width), lambda i: (i, 0, 0)),
        out_shape=jax.ShapeDtypeStruct((8, rows, width), bf16),
        compiler_params=params(),
        cost_estimate=cost(10),
        name="spread",
    )(row, feed)


def combine_kernel(experts, row_ref, *refs):
    values_in, part_ref, feed_ref = refs[:2], refs[2], refs[3]
    out_ref, feed_out, gates_ref = refs[4:7]
    backs, feeds, stage, staged, gsend, gcame, b_sem, f_sem, p_sem, o_sem, g_send, g_recv = refs[7:19]
    job = Sum(None, *refs[19:], stage=stage)
    each, some = backs.shape[0] // 2, feeds.shape[0]
    z, c, t = spot()
    own = 4 * c + t
    width = stage.shape[2]
    loads = [pltpu.make_async_copy(v, backs.at[pl.ds(j * each, each)], b_sem.at[j]) for j, v in enumerate(values_in)]
    more = [pltpu.make_async_copy(feed_ref, feeds, f_sem)]
    more += [pltpu.make_async_copy(part_ref.at[o], staged.at[o], p_sem.at[o]) for o in range(8)]
    for copy in loads + more:
        copy.start()
    greet(False)

    def tile(values, owner):
        start = pl.multiple_of(owner * BLOCK, BLOCK)
        place = row_ref[:, pl.ds(start, BLOCK)].T
        here = pl.ds(pl.multiple_of(owner // 4 * CAP, CAP), CAP)
        count = values.shape[0]
        return spot_rows(place, c, experts, experts - count, count, values, here)

    def back(owner):
        got = tile(backs, owner)
        named = got[:, width:].T
        gsend[owner] = named[:FFN_EXPERTS] + named[16 : 16 + FFN_EXPERTS]
        return got[:, :width]

    for copy in loads:
        copy.wait()
    for k, o in enumerate(job.order):
        stage[k] = back(4 * (1 - c) + o).astype(bf16)
        job.core[k].start()
        job.add(k, back(4 * c + o))
    job.third()
    pairs = []
    for step in range(1, 8):
        other = lax.rem(own + step, 8)
        copy = remote(gsend.at[other], gcame.at[step], g_send.at[step], g_recv.at[step], ctx=other // 4, tp=lax.rem(other, 4))
        copy.start()
        pairs.append(copy)
    for copy in more:
        copy.wait()

    def feed(first, last):
        @pl.loop(first, last)
        def _(n):
            staged[n] = (tile(feeds, n) + staged[n].astype(f32)).astype(bf16)
            pltpu.make_async_copy(staged.at[n], feed_out.at[n], o_sem.at[n]).start()

    feed(0, 8)
    gates = gsend[own]
    for step, copy in enumerate(pairs):
        copy.wait_recv()
        gates = gates + gcame[step + 1]
        copy.wait_send()
    gates_ref[...] = gates
    job.last()
    one, two = job.total()
    out_ref[: job.half] = one
    out_ref[job.half :] = two

    @pl.loop(0, 8)
    def _(n):
        pltpu.make_async_copy(staged.at[n], feed_out.at[n], o_sem.at[n]).wait()


def combine(row, backs, part, feed, number):
    experts = sum(b.shape[0] for b in backs)
    _, slots, width = feed.shape
    wide = backs[0].shape[2]
    rows = row.shape[1] // 8
    vmem = pl.BlockSpec(memory_space=pltpu.VMEM)
    return pl.pallas_call(
        functools.partial(combine_kernel, experts),
        in_specs=[vmem] + anywhere(4),
        out_specs=[vmem] + anywhere(1) + [vmem],
        out_shape=[
            jax.ShapeDtypeStruct((rows, width), f32),
            jax.ShapeDtypeStruct((8, rows, width), bf16),
            jax.ShapeDtypeStruct((FFN_EXPERTS, rows), f32),
        ],
        scratch_shapes=[
            pltpu.VMEM((experts, slots, wide), bf16),
            pltpu.VMEM(feed.shape, bf16),
            pltpu.VMEM((4, rows, width), bf16),
            pltpu.VMEM((8, rows, width), bf16),
            pltpu.VMEM((8, FFN_EXPERTS, rows), f32),
            pltpu.VMEM((8, FFN_EXPERTS, rows), f32),
            pltpu.SemaphoreType.DMA((2,)),
            pltpu.SemaphoreType.DMA,
            pltpu.SemaphoreType.DMA((8,)),
            pltpu.SemaphoreType.DMA((8,)),
            pltpu.SemaphoreType.DMA((8,)),
            pltpu.SemaphoreType.DMA((8,)),
        ]
        + Sum.scratch(rows, width),
        compiler_params=params(collective_id=number, has_side_effects=True),
        cost_estimate=cost(45),
        name="combine",
    )(row, *backs, part, feed)


def closing_kernel(dq_ref, dk_ref, dv_ref, x_ref, cos_ref, sin_ref, wt_ref, par_ref, go_ref, small_ref, top_ref,
                   out_ref, gsum_ref, ssum_ref, tmax_ref,
                   dqs, dks, dvs, xs, total, row, gother, gcore, gline, gmine, smine, sline, splane, tline, mytop, stage, l_sem, *sems):
    job = Sum(None, *sems[:7], stage=stage)
    sends, recvs = sems[7:]
    z, c, t = spot()
    ns = lax.axis_size("shard")
    heads = dqs.shape[0]
    half = HEAD_DIM // 2
    own = 4 * c + t
    order = [4 * (1 - c) + o for o in job.order] + [4 * c + o for o in job.order]

    def lanes(o):
        return pl.ds(pl.multiple_of(o * BLOCK, BLOCK), BLOCK)

    loads = []
    for n, o in enumerate(order):
        here = lanes(o)
        loads.append(
            [
                pltpu.make_async_copy(dq_ref.at[:, :, here], dqs.at[:, :, here], l_sem.at[n, 0]),
                pltpu.make_async_copy(dk_ref.at[:, :, here], dks.at[:, :, here], l_sem.at[n, 1]),
                pltpu.make_async_copy(dv_ref.at[:, :, here], dvs.at[:, :, here], l_sem.at[n, 2]),
                pltpu.make_async_copy(x_ref.at[here], xs.at[here], l_sem.at[n, 3]),
            ]
        )
    for k in range(4):
        for copy in loads[k] + loads[4 + k]:
            copy.start()
    greet()
    started = []

    def go(k, source, target, **where):
        copy = remote(source, target, sends.at[k], recvs.at[k], **where)
        copy.start()
        started.append(copy)
        return copy

    line_row = lax.broadcasted_iota(jnp.int32, mytop.shape, 0)
    high = jnp.full(mytop.shape, -1e30, f32)
    for h in range(top_ref.shape[0]):
        best = jnp.max(jnp.max(top_ref[h], axis=0), axis=1, keepdims=True)
        high = jnp.where(line_row == h, best, high)
    mytop[...] = high
    tops = [go(3 + ns + s, mytop, tline.at[s], shard=lax.rem(z + s, ns)) for s in range(1, ns)]
    total[...] = jnp.zeros_like(total)
    row[...] = jnp.zeros_like(row)

    def tile(o):
        here = lanes(o)
        cosine, sine = cos_ref[:, here], sin_ref[:, here]

        def turned(g):
            u, w = g[:half], g[half:]
            return jnp.concatenate([u * cosine + w * sine, w * cosine - u * sine], axis=0)

        x = xs[here].astype(f32)
        m = x * lax.rsqrt(jnp.mean(x * x, axis=1, keepdims=True) + epsilon)
        a = (m * par_ref[18:19]).astype(bf16)
        pieces = [turned(dqs[h, :, here]) for h in range(heads)]
        pieces += [turned(dks[h, :, here]) for h in range(heads)]
        pieces += [dvs[h, :, here] for h in range(heads)]
        grads = jnp.concatenate(pieces, axis=0).astype(bf16)
        part = mm(grads, wt_ref[...], TN)
        row[...] += jnp.sum(part * m, axis=0, keepdims=True)
        total[...] += mm(grads, a)
        return part

    for k in range(4):
        for copy in loads[k] + loads[4 + k]:
            copy.wait()
        stage[k] = tile(order[k]).astype(bf16)
        job.core[k].start()
        job.add(k, tile(order[4 + k]))

    cut_rows, depth = gsum_ref.shape[1:]
    at = lax.broadcasted_iota(jnp.int32, small_ref.shape, 0)
    smalls = small_ref[...] + jnp.where(at == 19, row[...], 0.0)
    for s in range(ns):
        here = slice(s * depth, (s + 1) * depth)
        one = total[:cut_rows, here].astype(bf16)
        two = jnp.concatenate([total[cut_rows:, here].astype(bf16), go_ref[:, here]], axis=0)
        gmine[s] = packed(jnp.where(c == 0, one.astype(f32), two.astype(f32))).astype(bf16)
        gother[s] = packed(jnp.where(c == 0, two.astype(f32), one.astype(f32))).astype(bf16)
        smine[s] = smalls[:, here]
    core = go(0, gother, gcore, ctx=1 - c)
    small = [go(3 + s, smine.at[lax.rem(z + s, ns)], sline.at[s], shard=lax.rem(z + s, ns)) for s in range(1, ns)]
    core.wait_recv()
    gmine[...] = gmine[...] + gcore[...]
    line = [go(3 + 2 * ns + s, gmine.at[lax.rem(z + s, ns)], gline.at[s], shard=lax.rem(z + s, ns)) for s in range(1, ns)]
    job.third()
    for copy in small:
        copy.wait_recv()
    value = smine[z]
    for s in range(1, ns):
        value = value + sline[s]
    splane[0] = value
    plane = []
    for s in range(1, 8):
        other = lax.rem(own + s, 8)
        plane.append(go(3 + 3 * ns + s, splane.at[0], splane.at[s], ctx=other // 4, tp=lax.rem(other, 4)))
    for copy in tops:
        copy.wait_recv()
    high = mytop[...]
    for s in range(1, ns):
        high = jnp.maximum(high, tline[s])
    tline[0] = high
    pair = go(2, tline.at[0], tline.at[ns], ctx=1 - c)
    for copy in line:
        copy.wait_recv()
    value = gmine[z].astype(f32)
    for s in range(1, ns):
        value = value + gline[s].astype(f32)
    gsum_ref[c] = unpacked(value, depth)
    go(3, gsum_ref.at[c], gsum_ref.at[c], ctx=1 - c)
    for copy in plane:
        copy.wait_recv()
    value = splane[0]
    for s in range(1, 8):
        value = value + splane[s]
    ssum_ref[...] = value
    pair.wait_recv()
    tmax_ref[...] = jnp.maximum(tline[0], tline[ns])
    job.last()
    one, two = job.total()
    out_ref[: job.half] = one
    out_ref[job.half :] = two
    remote(gsum_ref.at[1 - c], gsum_ref.at[1 - c], sends.at[3], recvs.at[3], ctx=1 - c).wait_recv()
    for copy in started:
        copy.wait_send()


def closing(dq, dk, dv, x, cosine, sine, wt, par, go, small, top, number):
    heads, _, total = dq.shape
    width = x.shape[1]
    rows = total // 8
    ns = lax.axis_size("shard")
    depth = width // ns
    cut_rows = 2 * heads * HEAD_DIM
    pieces = (ns, cut_rows * 3 // 2, 128) if depth == 192 else (ns, cut_rows, depth)
    smalls = (ns,) + small.shape[:1] + (depth,)
    vmem = pl.BlockSpec(memory_space=pltpu.VMEM)
    return pl.pallas_call(
        closing_kernel,
        in_specs=anywhere(4) + [vmem] * 7,
        out_specs=[vmem] * 4,
        out_shape=[
            jax.ShapeDtypeStruct((rows, width), f32),
            jax.ShapeDtypeStruct((2, cut_rows, depth), f32),
            jax.ShapeDtypeStruct(smalls[1:], f32),
            jax.ShapeDtypeStruct((8, 128), f32),
        ],
        scratch_shapes=[
            pltpu.VMEM(dq.shape, f32),
            pltpu.VMEM(dq.shape, f32),
            pltpu.VMEM(dq.shape, f32),
            pltpu.VMEM(x.shape, bf16),
            pltpu.VMEM(wt.shape, f32),
            pltpu.VMEM((1, width), f32),
            pltpu.VMEM(pieces, bf16),
            pltpu.VMEM(pieces, bf16),
            pltpu.VMEM(pieces, bf16),
            pltpu.VMEM(pieces, bf16),
            pltpu.VMEM(smalls, f32),
            pltpu.VMEM(smalls, f32),
            pltpu.VMEM((8,) + smalls[1:], f32),
            pltpu.VMEM((ns + 1, 8, 128), f32),
            pltpu.VMEM((8, 128), f32),
            pltpu.VMEM((4, rows, width), bf16),
            pltpu.SemaphoreType.DMA((8, 4)),
        ]
        + Sum.scratch(rows, width)
        + [
            pltpu.SemaphoreType.DMA((3 * ns + 11,)),
            pltpu.SemaphoreType.DMA((3 * ns + 11,)),
        ],
        compiler_params=params(collective_id=number, has_side_effects=True),
        cost_estimate=cost(45),
        name="closing",
    )(dq, dk, dv, x, cosine, sine, wt, par, go, small, top)


def packed(v):
    rows, lanes = v.shape
    if lanes != 192:
        return v
    rest = jnp.concatenate([v[: rows // 2, 128:], v[rows // 2 :, 128:]], axis=1)
    return jnp.concatenate([v[:, :128], rest], axis=0)


def unpacked(v, lanes):
    if lanes != 192:
        return v
    rows = v.shape[0] // 3 * 2
    rest = jnp.concatenate([v[rows:, :64], v[rows:, 64:]], axis=0)
    return jnp.concatenate([v[:rows], rest], axis=1)


def swap_kernel(ge_ref, other_ref, send, recv):
    z, c, t = spot()
    greet_core()
    copy = remote(ge_ref, other_ref, send, recv, ctx=1 - c)
    copy.start()
    copy.wait()


def greet_core():
    z, c, t = spot()
    barrier = pltpu.get_barrier_semaphore()
    pl.semaphore_signal(barrier, inc=1, device_id={"ctx": 1 - c}, device_id_type=MESH)
    pl.semaphore_wait(barrier, 1)


def swap(ge, number):
    return pl.pallas_call(
        swap_kernel,
        in_specs=anywhere(1),
        out_specs=anywhere(1)[0],
        out_shape=jax.ShapeDtypeStruct(ge.shape, ge.dtype),
        scratch_shapes=[pltpu.SemaphoreType.DMA, pltpu.SemaphoreType.DMA],
        compiler_params=params(collective_id=number, has_side_effects=True),
        cost_estimate=cost(5),
        name="swap",
    )(ge)


def laid(previous, routes):
    count, rows = previous.shape
    return jnp.concatenate([previous, jnp.zeros((16 - count, rows), f32)], axis=0), routes.astype(f32)


def thirds(v):
    a = v.astype(bf16)
    rest = v - a.astype(f32)
    b = rest.astype(bf16)
    return a, b, (rest - b.astype(f32)).astype(bf16)


def mixing(n2, wrc, previous, routes):
    z = sum(mm(wrc.astype(bf16), part, NT) for part in thirds(n2))
    expert = lax.broadcasted_iota(jnp.int32, z.shape, 0).astype(f32)
    logits = z + previous
    hot = [expert == routes[r : r + 1] for r in range(2)]
    picked = [jnp.sum(jnp.where(hot[r], logits, 0.0), axis=0, keepdims=True) for r in range(2)]
    most = jnp.maximum(picked[0], picked[1])
    e = [jnp.exp(p - most) for p in picked]
    gates = [v / (e[0] + e[1]) for v in e]
    combine = jnp.where(hot[0], gates[0], 0.0) + jnp.where(hot[1], gates[1], 0.0)
    alphas = []
    for j in range(2):
        first, second = z[EXPERTS + 2 * j : EXPERTS + 2 * j + 1], z[EXPERTS + 2 * j + 1 : EXPERTS + 2 * j + 2]
        most = jnp.maximum(first, second)
        a, b = jnp.exp(first - most), jnp.exp(second - most)
        alphas.append((a / (a + b), b / (a + b)))
    weights = [combine[FFN_EXPERTS + 1 + j : FFN_EXPERTS + 2 + j] for j in range(3)]
    return hot, gates, combine, alphas, weights


def scales(alphas, weights):
    scale = weights[0] + weights[1] * alphas[0][0] + weights[2] * alphas[1][0]
    at = lax.broadcasted_iota(jnp.int32, (8, scale.shape[1]), 0)
    value = jnp.where(at == 0, scale, jnp.where(at == 1, weights[1] * alphas[0][1], weights[2] * alphas[1][1])).T
    return value[:, 0:1], value[:, 1:2], value[:, 2:3]


def turn_kernel(length, res_ref, dn_ref, named_ref, cot_ref, att_ref, wo_ref, par_ref, prev_ref, routes_ref,
                dres_ref, heads_ref, gwo_ref, small_ref, got_ref, send_sem, recv_sem, local_sem):
    z, c, t = spot()
    nt = lax.axis_size("tp")
    own = c * nt + t
    rows, width = res_ref.shape
    greet(False)
    here = pl.ds(pl.multiple_of(t * rows, rows), rows)
    res = res_ref[...]
    gain = par_ref[19:20]
    inverse = lax.rsqrt(jnp.mean(res * res, axis=1, keepdims=True) + epsilon)
    m = res * inverse
    n2 = m * gain
    previous, routes = laid(prev_ref[:, here], routes_ref[c, :, here])
    hot, gates, _, alphas, weights = mixing(n2, par_ref[:16], previous, routes)
    position = own * rows + lax.broadcasted_iota(jnp.int32, cot_ref.shape, 0)
    g = jnp.where(position < length[0], cot_ref[...].astype(f32), 0.0)
    inner = jnp.broadcast_to(jnp.sum(g * n2, axis=1, keepdims=True), (rows, 8)).T[0:1]
    onto = mm(par_ref[16:18].astype(bf16), g.astype(bf16), NT)
    onto = [onto[j : j + 1] for j in range(2)]
    named = named_ref[...]
    expert = lax.broadcasted_iota(jnp.int32, hot[0].shape, 0)
    local = {
        FFN_EXPERTS + 1: inner,
        FFN_EXPERTS + 2: alphas[0][0] * inner + alphas[0][1] * onto[0],
        FFN_EXPERTS + 3: alphas[1][0] * inner + alphas[1][1] * onto[1],
    }
    dgates = []
    for r in range(2):
        there = jnp.sum(jnp.where(hot[r][:FFN_EXPERTS], named, 0.0), axis=0, keepdims=True)
        for e, value in local.items():
            there = there + jnp.where(hot[r][e : e + 1], value, 0.0)
        dgates.append(there)
    mean = gates[0] * dgates[0] + gates[1] * dgates[1]
    dz = jnp.where(hot[0], gates[0] * (dgates[0] - mean), 0.0)
    dz = dz + jnp.where(hot[1], gates[1] * (dgates[1] - mean), 0.0)
    for j in range(2):
        da = weights[1 + j] * inner
        db = weights[1 + j] * onto[j]
        centre = alphas[j][0] * da + alphas[j][1] * db
        dz = dz + jnp.where(expert == EXPERTS + 2 * j, alphas[j][0] * (da - centre), 0.0)
        dz = dz + jnp.where(expert == EXPERTS + 2 * j + 1, alphas[j][1] * (db - centre), 0.0)
    scale, first_vec, second_vec = scales(alphas, weights)
    highest = lax.Precision.HIGHEST
    dn2 = dn_ref[...] + scale * g + sum(mm(part, par_ref[:16].astype(bf16), TN) for part in thirds(dz))
    q = dn2 * gain
    dres = g + inverse * (q - m * jnp.mean(q * m, axis=1, keepdims=True))
    dres_ref[...] = dres
    da = dres.astype(bf16)
    wo = wo_ref[...].reshape(-1, width)
    got_ref[...] = mm(wo, da, NT).astype(bf16).reshape(got_ref.shape)

    core = lax.rem((own + 1) // 2, 2)
    slot = 2 * (own // 4) + lax.rem(own, 4) // 2
    copies = []
    for target in range(nt):
        inside = jnp.logical_and(core == c, target == t)
        copy = remote(got_ref.at[target], heads_ref.at[slot], send_sem.at[target], recv_sem.at[slot], ctx=core, tp=target)
        copies.append((inside, copy, pltpu.make_async_copy(got_ref.at[target], heads_ref.at[slot], local_sem)))
    for inside, copy, kept in copies:

        @pl.when(jnp.logical_not(inside))
        def _():
            copy.start()

        @pl.when(inside)
        def _():
            kept.start()

    small_ref[0:16] = mm(dz, n2, NN, highest)
    small_ref[16:24] = jnp.zeros((8, width), f32)
    small_ref[16:17] = jnp.sum(first_vec * g, axis=0, keepdims=True)
    small_ref[17:18] = jnp.sum(second_vec * g, axis=0, keepdims=True)
    small_ref[18:19] = jnp.sum(dn2 * m, axis=0, keepdims=True)
    att = att_ref[...].reshape(-1, rows)
    gwo_ref[...] = mm(att, da).astype(bf16).reshape(gwo_ref.shape)
    for inside, copy, kept in copies:

        @pl.when(jnp.logical_not(inside))
        def _():
            copy.wait_send()

        @pl.when(inside)
        def _():
            kept.wait()

    for i in range(heads_ref.shape[0]):

        @pl.when(zig(c, i) != own)
        def _():
            remote(got_ref.at[0], heads_ref.at[i], send_sem.at[0], recv_sem.at[i], ctx=c, tp=t).wait_recv()


def turn(length, res, dn, named, cot, att, wo, small, prev, routes, count, number):
    rows, width = res.shape
    nt = lax.axis_size("tp")
    args = (res, dn, named, cot, att, wo, small, prev, routes)
    return pl.pallas_call(
        turn_kernel,
        grid_spec=pltpu.PrefetchScalarGridSpec(
            num_scalar_prefetch=1,
            grid=(1,),
            in_specs=[full(v.shape) for v in args],
            out_specs=[full((rows, width))] + anywhere(1) + [full(wo.shape), full((24, width))],
            scratch_shapes=[
                pltpu.VMEM(att.shape, bf16),
                pltpu.SemaphoreType.DMA((nt,)),
                pltpu.SemaphoreType.DMA((count,)),
                pltpu.SemaphoreType.DMA,
            ],
        ),
        out_shape=[
            jax.ShapeDtypeStruct((rows, width), f32),
            jax.ShapeDtypeStruct((count,) + att.shape[1:], bf16),
            jax.ShapeDtypeStruct(wo.shape, bf16),
            jax.ShapeDtypeStruct((24, width), f32),
        ],
        compiler_params=params(collective_id=number, has_side_effects=True),
        cost_estimate=cost(18),
        name="turn",
    )(length, *args)


def both_cores(own_ref, other_ref, targets):
    core = lax.axis_index("ctx")
    for k, target in enumerate(targets):
        for j in range(own_ref.shape[0]):
            mine, theirs = own_ref[j, k].astype(f32), other_ref[j, k].astype(f32)
            target[0, j] = jnp.where(core == 0, mine, theirs)
            target[1, j] = jnp.where(core == 0, theirs, mine)


def output_kernel(base_ref, feed_ref, length_ref, own_ref, other_ref, out_ref, *targets):
    both_cores(own_ref, other_ref, targets)
    rows = base_ref.shape[0]
    first = (lax.axis_index("ctx") * lax.axis_size("tp") + lax.axis_index("tp")) * pl.num_programs(0) + pl.program_id(0)
    position = first * rows + lax.broadcasted_iota(jnp.int32, base_ref.shape, 0)
    out_ref[...] = jnp.where(position < length_ref[0], base_ref[...] + feed_ref[...], 0.0).astype(bf16)


def steps_of(depth):
    return 4 if depth % 64 == 0 else 1


def output_rows(base, feed, length, own, other):
    rows, width = base.shape
    each, kinds, depth, hidden = own.shape
    steps = steps_of(depth)
    by_row = pl.BlockSpec((rows // steps, width), lambda i: (i, 0))
    pair = pl.BlockSpec((each, kinds, depth // steps, hidden), lambda i: (0, 0, i, 0))
    return pl.pallas_call(
        output_kernel,
        grid=(steps,),
        in_specs=[by_row, by_row, pl.BlockSpec(memory_space=pltpu.SMEM), pair, pair],
        out_specs=[by_row] + [pl.BlockSpec((2, each, depth // steps, hidden), lambda i: (0, 0, i, 0))] * 3,
        out_shape=[jax.ShapeDtypeStruct((rows, width), bf16)]
        + [jax.ShapeDtypeStruct((2, 2 * each, depth, hidden), f32)] * 3,
        compiler_params=params(),
        cost_estimate=cost(6),
        name="output_rows",
    )(base, feed, length, own, other)


def finish_kernel(x_ref, dn_ref, dres_ref, small_ref, gw_ref, gs_ref, top_ref, wq_ref, wk_ref, limit_ref, own_ref, other_ref, *refs):
    outs = refs[3:]
    gin_ref, targets = outs[0], outs[1:4]
    x = x_ref[...].astype(f32)
    inverse = lax.rsqrt(jnp.mean(x * x, axis=1, keepdims=True) + epsilon)
    m = x * inverse
    q = dn_ref[...] * small_ref[18:19]
    gin_ref[...] = dres_ref[...] + inverse * (q - m * jnp.mean(q * m, axis=1, keepdims=True))
    both_cores(own_ref, other_ref, targets)

    @pl.when(pl.program_id(0) == 0)
    def _():
        gq, gk, gv, go, gnorm, gmoe, grouter, gconst, gvec, fac_ref, cq_ref, ck_ref = outs[4:]
        width = wq_ref.shape[1]
        flat = gw_ref[...].reshape(4 * width, gw_ref.shape[2])
        for k, target in enumerate((gq, gk, gv)):
            target[...] = flat[k * width : (k + 1) * width].T
        go[...] = flat[3 * width :]
        sums = gs_ref[...]
        grouter[...] = sums[:EXPERTS]
        gconst[...] = sums[EXPERTS : EXPERTS + 4]
        gvec[...] = sums[16:18]
        gmoe[...] = sums[18:19]
        gnorm[...] = sums[19:20]
        factors = limit_ref[0] / jnp.maximum(top_ref[...], limit_ref[0])
        for h in range(fac_ref.shape[0]):
            fac_ref[h] = factors[h, 0]
        lane = lax.broadcasted_iota(jnp.int32, (1, width), 1)
        root = jnp.zeros((1, width), f32)
        for h in range(width // HEAD_DIM):
            root = jnp.where(lane // HEAD_DIM == h, jnp.sqrt(factors[h : h + 1, :1]), root)
        cq_ref[...] = (wq_ref[...].astype(f32) * root).astype(bf16)
        ck_ref[...] = (wk_ref[...].astype(f32) * root).astype(bf16)


def finish_rows(x, dn, dres, small, gw, gs, top, wq, wk, limit, own, other, finals):
    rows, width = x.shape
    each, kinds, depth, hidden = own.shape
    steps = steps_of(depth)
    tile, deep = rows // steps, depth // steps
    by_row = pl.BlockSpec((tile, width), lambda i: (i, 0))
    expert_out = pl.BlockSpec((2, each, deep, hidden), lambda i: (0, 1, i, 0))
    once = [
        jax.ShapeDtypeStruct(shape, f32)
        for shape in [wq.shape] * 3
        + [(wq.shape[1], depth), (1, depth), (1, depth), (EXPERTS, depth), (4, depth), (2, depth), (wq.shape[1] // HEAD_DIM,)]
    ] + [jax.ShapeDtypeStruct(wq.shape, bf16)] * 2
    return pl.pallas_call(
        finish_kernel,
        grid=(steps,),
        in_specs=[
            by_row,
            by_row,
            by_row,
            full(small.shape),
            full(gw.shape),
            full(gs.shape),
            full(top.shape),
            full(wq.shape),
            full(wk.shape),
            pl.BlockSpec(memory_space=pltpu.SMEM),
        ]
        + [pl.BlockSpec((each, kinds, deep, hidden), lambda i: (0, 0, i, 0))] * 2
        + anywhere(3),
        out_specs=[by_row, expert_out, expert_out, expert_out] + [full(v.shape) if v.ndim > 1 else pl.BlockSpec(memory_space=pltpu.SMEM) for v in once],
        out_shape=[
            jax.ShapeDtypeStruct((rows, width), f32),
        ]
        + [jax.ShapeDtypeStruct(v.shape, f32) for v in finals]
        + once,
        input_output_aliases={12: 1, 13: 2, 14: 3},
        compiler_params=params(),
        cost_estimate=cost(8),
        name="finish_rows",
    )(x, dn, dres, small, gw, gs, top, wq, wk, limit, own, other, *finals)


def pick_kernel(first, g_ref, u_ref, d_ref, out_ref):
    for k, source in enumerate((g_ref, u_ref, d_ref)):
        out_ref[0, k] = source[0]


def pick(first, start, some, gate, up, down):
    _, depth, hidden = gate.shape
    source = pl.BlockSpec((1, depth, hidden), lambda i, f: (f[0] + start + i, 0, 0))
    return pl.pallas_call(
        pick_kernel,
        grid_spec=pltpu.PrefetchScalarGridSpec(
            num_scalar_prefetch=1,
            grid=(some,),
            in_specs=[source] * 3,
            out_specs=pl.BlockSpec((1, 3, depth, hidden), lambda i, f: (i, 0, 0, 0)),
        ),
        out_shape=jax.ShapeDtypeStruct((some, 3, depth, hidden), gate.dtype),
        compiler_params=params(),
        cost_estimate=cost(2),
        name="pick",
    )(first, gate, up, down)


def expert_kernel(start, first, x_ref, g_ref, gate_ref, w_ref, feed_ref, back_ref, gw_ref):
    parts, _, _, depth, hidden = w_ref.shape
    width = parts * depth
    wg, wu, wd = [w_ref[:, 0, k].reshape(width, hidden) for k in range(3)]
    x, g, gate = x_ref[0], g_ref[0], gate_ref[0]
    gate_pre = mm(x, wg)
    up = mm(x, wu)
    sigmoid = 1.0 / (1.0 + jnp.exp(-gate_pre))
    activated = gate_pre * sigmoid
    inner = (activated * up).astype(bf16)
    g32 = g.astype(f32)
    dout = (gate * g32).astype(bf16)
    dinner = mm(dout, wd)
    out = mm(inner, wd, NT)
    feed_ref[0] = (gate * out).astype(bf16)
    dgate = jnp.sum(g32 * out, axis=1, keepdims=True)
    dpre = (dinner * up * sigmoid * (1.0 + gate_pre * (1.0 - sigmoid))).astype(bf16)
    dup = (dinner * activated).astype(bf16)
    back_ref[0, :, :width] = (mm(dpre, wg, NT) + mm(dup, wu, NT)).astype(bf16)
    lane = lax.broadcasted_iota(jnp.int32, (dgate.shape[0], back_ref.shape[2] - width), 1)
    coarse = dgate.astype(bf16).astype(f32)
    at = first[0] + start + pl.program_id(0)
    extra = jnp.where(lane == at, coarse, jnp.where(lane == at + 16, dgate - coarse, 0.0))
    back_ref[0, :, width:] = extra.astype(bf16)
    for k, (left, right) in enumerate(((x, dpre), (x, dup), (dout, inner))):
        gw_ref[:, 0, k] = mm(left, right, TN).reshape(parts, depth, hidden).astype(bf16)


def expert(start, first, x, g, gate, w):
    slots, width = x.shape[1:]
    parts, some, kinds, depth, hidden = w.shape
    pick = lambda i, f: (start + i, 0, 0)
    return pl.pallas_call(
        functools.partial(expert_kernel, start),
        grid_spec=pltpu.PrefetchScalarGridSpec(
            num_scalar_prefetch=1,
            grid=(some,),
            in_specs=[
                pl.BlockSpec((1, slots, width), pick),
                pl.BlockSpec((1, slots, width), pick),
                pl.BlockSpec((1, slots, 1), pick),
                pl.BlockSpec((parts, 1, kinds, depth, hidden), lambda i, f: (0, i, 0, 0, 0)),
            ],
            out_specs=[
                pl.BlockSpec((1, slots, width), lambda i, f: (i, 0, 0)),
                pl.BlockSpec((1, slots, width + EXTRA), lambda i, f: (i, 0, 0)),
                pl.BlockSpec((parts, 1, kinds, depth, hidden), lambda i, f: (0, i, 0, 0, 0)),
            ],
        ),
        out_shape=[
            jax.ShapeDtypeStruct((some, slots, width), bf16),
            jax.ShapeDtypeStruct((some, slots, width + EXTRA), bf16),
            jax.ShapeDtypeStruct(w.shape, bf16),
        ],
        compiler_params=params(),
        cost_estimate=cost(12 * some),
        name="expert",
    )(first, x, g, gate, w)


def shards(
    hidden_in,
    cotangent,
    lengths,
    routes,
    prev_logits,
    norm_attn,
    w_query,
    w_key,
    w_value,
    w_out,
    norm_moe,
    w_router,
    w_const,
    const_vec,
    w_gate,
    w_up,
    w_down,
    threshold,
):
    plane = ("ctx", "tp")
    core = lax.axis_index("ctx")
    nc, nt, ns = lax.axis_size("ctx"), lax.axis_size("tp"), lax.axis_size("shard")
    own, width = hidden_in.shape
    per = own * nt
    total = per * nc
    depth = w_gate.shape[1]
    heads = w_query.shape[1] // HEAD_DIM
    head_width = heads * HEAD_DIM
    local = FFN_EXPERTS // nc
    count = total // BLOCK // nc
    routes, prev = routes.T, prev_logits.T
    first = (core * local).astype(jnp.int32)[None]

    expert_w = []
    for start in range(0, local, 2):
        pieces = pick(first, start, 2, w_gate, w_up, w_down)
        expert_w.append(lax.all_gather(pieces, "shard", axis=0, tiled=False))
    rows_all, attention_w, small, routes_all = opening(
        hidden_in,
        (w_query, w_key, w_value, w_out),
        (w_router.T, w_const.T, const_vec, norm_attn[None], norm_moe[None]),
        routes,
        0,
    )
    rows_all = rows_all.reshape(total, width)
    cosine, sine = rope_tables(total)

    qt, kt, k, v, vt, wt, small, out_w = project(rows_all, attention_w, small, cosine, sine, heads, 8)
    ot, lse, top, cot_all = attend(lengths, qt, k, vt, cotangent, count, 1)
    att, res, base, x_slots, g_slots, gate_slots, row_at = route(
        ot, hidden_in, out_w, small, prev, routes_all, cot_all, local, 2
    )

    feeds, backs, grads = [], [], []
    for j, w in enumerate(expert_w):
        if grads:
            part = spread(row_at, feeds[0], local)
            x_slots, part = lax.optimization_barrier((x_slots, part))
        feed, back, raw = expert(2 * j, first, x_slots, g_slots, gate_slots, w)
        feeds.append(feed)
        backs.append(back)
        grads.append(lax.psum_scatter(raw, "shard", scatter_dimension=0, tiled=True)[0])
    back, feed, named = combine(row_at, backs, part, feeds[1], 3)

    dres, got, grad_out, gsmall = turn(
        lengths, res, back, named, cotangent, att, out_w, small, prev, routes_all, count, 4
    )
    dq, dk, dv, grad_out, feed = revisit(qt, k, kt, v, ot, got, lse, grad_out, feed, 5)
    early, dq = lax.optimization_barrier((grads[0], dq))
    output, *finals = output_rows(base, feed, lengths, early, swap(early, 6))
    dq, *finals = lax.optimization_barrier((dq, *finals))
    part, grad_w, gsmall, top = closing(dq, dk, dv, rows_all, cosine, sine, wt, small, grad_out, gsmall, top, 7)
    late, top = lax.optimization_barrier((grads[1], top))
    (grad_input, grad_gate, grad_up, grad_down, grad_q, grad_k, grad_v, grad_out, grad_norm_attn, grad_norm_moe,
     grad_router, grad_const, grad_vec, factors, clipped_query, clipped_key) = finish_rows(
        hidden_in, part, dres, small, grad_w, gsmall, top, w_query, w_key, threshold, late, swap(late, 9), finals
    )
    grad_gate, grad_up, grad_down = [v.reshape((-1,) + v.shape[2:]) for v in (grad_gate, grad_up, grad_down)]
    return (
        output,
        grad_input,
        grad_norm_attn[0],
        grad_q,
        grad_k,
        grad_v,
        grad_out,
        grad_norm_moe[0],
        grad_router.T,
        grad_const.T,
        grad_vec,
        grad_gate,
        grad_up,
        grad_down,
        factors,
        clipped_query,
        clipped_key,
    )


def solution(mesh):
    return jax.shard_map(
        shards,
        mesh=mesh,
        in_specs=(
            P(("shard", "ctx", "tp"), None),
            P(("shard", "ctx", "tp"), None),
            P("shard"),
            P(("shard", "ctx"), None),
            P(("shard", "ctx"), None),
            P("shard"),
            P("shard", "tp"),
            P("shard", "tp"),
            P("shard", "tp"),
            P("tp", "shard"),
            P("shard"),
            P("shard", None),
            P("shard", None),
            P(None, "shard"),
            P(None, "shard", "tp"),
            P(None, "shard", "tp"),
            P(None, "shard", "tp"),
            P(),
        ),
        out_specs=(
            P(("shard", "ctx", "tp"), None),
            P(("shard", "ctx", "tp"), None),
            P("shard"),
            P("shard", "tp"),
            P("shard", "tp"),
            P("shard", "tp"),
            P("tp", "shard"),
            P("shard"),
            P("shard", None),
            P("shard", None),
            P(None, "shard"),
            P(None, "shard", "tp"),
            P(None, "shard", "tp"),
            P(None, "shard", "tp"),
            P("tp"),
            P("shard", "tp"),
            P("shard", "tp"),
        ),
        check_vma=False,
    )
```

```python
import functools

import jax
import jax.numpy as jnp
import numpy as np
from jax import lax
from jax.experimental import pallas as pl
from jax.experimental.pallas import tpu as pltpu
from jax.sharding import PartitionSpec as P

HEAD_DIM = 64
EXPERTS = 12
FFN_EXPERTS = 8
CAP = 512
BLOCK = 512
EXTRA = 128
SMALL = 32
MESH = pl.DeviceIdType.MESH

epsilon = 1e-06
rope_base = 10000.0
bf16 = jnp.bfloat16
f32 = jnp.float32

NN = (((1,), (0,)), ((), ()))
NT = (((1,), (1,)), ((), ()))
TN = (((0,), (0,)), ((), ()))


def mm(left, right, dims=NN, precision=None):
    return lax.dot_general(
        left, right, dims, preferred_element_type=f32, precision=precision
    )


def params(mib=56, **more):
    return pltpu.CompilerParams(vmem_limit_bytes=mib * 1024 * 1024, **more)


def cost(us):
    return pl.CostEstimate(flops=int(us * 1e9), bytes_accessed=int(us * 3e6), transcendentals=0)


def full(shape):
    return pl.BlockSpec(shape, lambda *_: (0,) * len(shape))


def rope_tables(total):
    half = HEAD_DIM // 2
    freqs = np.float32(rope_base) ** (np.float32(-2.0) * np.arange(half, dtype=np.float32) / np.float32(HEAD_DIM))
    angles = freqs.astype(np.float32)[:, None] * np.arange(total, dtype=np.float32)[None, :]
    angles = angles.astype(np.float64)
    return jnp.asarray(np.cos(angles), f32), jnp.asarray(np.sin(angles), f32)


def zig(core, i):
    return 4 * (i // 2) + (core if i % 2 == 0 else 3 - core)


def anywhere(count):
    return [pl.BlockSpec(memory_space=pl.ANY)] * count


def spot():
    return lax.axis_index("shard"), lax.axis_index("ctx"), lax.axis_index("tp")


def across(t):
    return t + 1 - 2 * lax.rem(t, 2), lax.rem(t + 2, 4), 3 - t


def remote(source, target, sends, recvs, **where):
    return pltpu.make_async_remote_copy(
        src_ref=source,
        dst_ref=target,
        send_sem=sends,
        recv_sem=recvs,
        device_id=where,
        device_id_type=MESH,
    )


def greet(depth=True):
    z, c, t = spot()
    nc, nt, ns = lax.axis_size("ctx"), lax.axis_size("tp"), lax.axis_size("shard")
    barrier = pltpu.get_barrier_semaphore()
    for step in range(1, nc * nt):
        other = lax.rem(c * nt + t + step, nc * nt)
        pl.semaphore_signal(
            barrier,
            inc=1,
            device_id={"ctx": other // nt, "tp": lax.rem(other, nt)},
            device_id_type=MESH,
        )
    if depth:
        for step in range(1, ns):
            pl.semaphore_signal(
                barrier,
                inc=1,
                device_id={"shard": lax.rem(z + step, ns)},
                device_id_type=MESH,
            )
    pl.semaphore_wait(barrier, nc * nt - 1 + (ns - 1 if depth else 0))


class Gather:
    KINDS = 9

    def __init__(self, x, out, sends, recvs, own, cuts, stage=None, relative=False):
        z, c, t = spot()
        tx, ty, td = across(t)
        rows = x.shape[0] // cuts
        half = rows // 2
        self.cuts = cuts
        sib = {"ctx": 1 - c}
        px, py = {"tp": tx}, {"tp": ty}
        near = (t, tx, ty, td)
        if relative:
            here, there = list(range(8)), list(range(8))
            mine = (1, 2, 4)
            passed = ((1, 5), (1, 3), (2, 6), (2, 3), (3, 7), (3, 7))
        else:
            here = [4 * c + n for n in near] + [4 * (1 - c) + n for n in near]
            there = here[:4]
            mine = (here[0],) * 3
            passed = tuple((here[n], here[n]) for n in (1, 1, 2, 2, 3, 3))
        self.load = None if stage is None else pltpu.make_async_copy(x, stage, own.at[0])
        self.own = pltpu.make_async_copy(x if stage is None else stage, out.at[here[0]], own.at[1])

        def parts(s):
            whole = pl.ds(s * rows, rows)
            one, two = pl.ds(s * rows, half), pl.ds(s * rows + half, half)
            return whole, one, two

        def copies(s):
            whole, one, two = parts(s)
            made = [
                remote(x.at[whole], out.at[slot, whole], sends.at[s, k], recvs.at[s, k], **where)
                for k, (slot, where) in enumerate(zip(mine, (px, py, sib)))
            ]
            ways = ((whole, sib), (one, py), (whole, sib), (two, px), (one, sib), (two, sib))
            for k, ((source, target), (part, where)) in enumerate(zip(passed, ways)):
                made.append(
                    remote(out.at[source, part], out.at[target, part], sends.at[s, k + 3], recvs.at[s, k + 3], **where)
                )
            return made

        self.copies = [copies(s) for s in range(cuts)]

        def arrivals(s):
            whole, one, two = parts(s)
            where = [(1, whole), (2, whole), (4, whole), (5, whole), (3, one), (6, whole), (3, two), (7, one), (7, two)]
            return [
                remote(out.at[here[n], part], out.at[here[n], part], sends.at[s, k], recvs.at[s, k], **sib)
                for k, (n, part) in enumerate(where)
            ]

        self.arrivals = [arrivals(s) for s in range(cuts)]

    @staticmethod
    def scratch(cuts):
        return [
            pltpu.SemaphoreType.DMA((cuts, Gather.KINDS)),
            pltpu.SemaphoreType.DMA((cuts, Gather.KINDS)),
            pltpu.SemaphoreType.DMA((2,)),
        ]

    def first(self):
        for s in range(self.cuts):
            for k in (0, 1, 2):
                self.copies[s][k].start()
        (self.load or self.own).start()

    def second(self, s):
        if self.load is not None and s == 0:
            self.load.wait()
            self.own.start()
        self.arrivals[s][0].wait_recv()
        self.copies[s][4].start()
        self.copies[s][3].start()
        self.arrivals[s][1].wait_recv()
        self.copies[s][6].start()
        self.copies[s][5].start()

    def third(self, s):
        for k in (4, 6):
            self.arrivals[s][k].wait_recv()
            self.copies[s][7 if k == 4 else 8].start()

    def beside(self):
        for s in range(self.cuts):
            for k in (2, 3, 5):
                self.arrivals[s][k].wait_recv()

    def last(self, rest=False):
        for s in range(self.cuts):
            for k in (7, 8) if rest else (2, 3, 5, 7, 8):
                self.arrivals[s][k].wait_recv()
        for s in range(self.cuts):
            for k in range(self.KINDS):
                self.copies[s][k].wait_send()
        if not rest:
            self.own.wait()


class Sum:
    def __init__(self, p, held, came, across_in, across_out, sends, recvs, loads, stage=None):
        z, c, t = spot()
        self.t = t
        tx, ty, td = across(t)
        half = held.shape[1] // 2
        self.half = half
        self.one, self.two = pl.ds(0, half), pl.ds(half, half)
        self.order = (td, tx, ty, t)
        self.held, self.came, self.inn = held, came, across_in
        sib, px, py = {"ctx": 1 - c}, {"tp": tx}, {"tp": ty}
        self.core = []
        for k, o in enumerate(self.order):
            source = p.at[4 * (1 - c) + o] if stage is None else stage.at[k]
            self.core.append(remote(source, came.at[o], sends.at[k], recvs.at[k], **sib))
        self.loads = None
        if stage is None:
            self.loads = [pltpu.make_async_copy(p.at[4 * c + o], held.at[o], loads.at[k]) for k, o in enumerate(self.order)]

        def send(k, source, slot, where):
            return remote(source, across_in.at[slot], sends.at[k], recvs.at[k], **where)

        self.side = {
            "dx": send(4, held.at[td, self.one], 0, px),
            "dy": send(5, held.at[td, self.two], 1, py),
            "x": send(6, held.at[tx, self.one], 2, px),
            "y": send(7, held.at[ty, self.two], 3, py),
            "cy": send(8, across_out.at[0], 4, py),
            "cx": send(9, across_out.at[1], 5, px),
        }
        self.out = across_out
        self.near = (tx, ty, td)

    @staticmethod
    def scratch(rows, width):
        return [
            pltpu.VMEM((4, rows, width), bf16),
            pltpu.VMEM((4, rows, width), bf16),
            pltpu.VMEM((6, rows // 2, width), bf16),
            pltpu.VMEM((2, rows // 2, width), bf16),
            pltpu.SemaphoreType.DMA((10,)),
            pltpu.SemaphoreType.DMA((10,)),
            pltpu.SemaphoreType.DMA((4,)),
        ]

    def first(self):
        for k in range(4):
            self.core[k].start()
            self.loads[k].start()

    def add(self, k, mine):
        o = self.order[k]
        self.core[k].wait_recv()
        self.held[o] = (mine + self.came[o].astype(mine.dtype)).astype(bf16)
        for name in (("dx", "dy"), ("x",), ("y",), ())[k]:
            self.side[name].start()

    def second(self):
        for k, o in enumerate(self.order):
            self.loads[k].wait()
            self.add(k, self.held[o])

    def third(self):
        tx, ty, td = self.near
        self.side["dx"].wait_recv()
        self.out[0] = self.held[ty, self.one] + self.inn[0]
        self.side["cy"].start()
        self.side["dy"].wait_recv()
        self.out[1] = self.held[tx, self.two] + self.inn[1]
        self.side["cx"].start()

    def last(self):
        for k in ("x", "y", "cy", "cx"):
            self.side[k].wait_recv()
        for copy in self.core + list(self.side.values()):
            copy.wait_send()

    def total(self):
        def add(part, a, b):
            return self.held[self.t, part].astype(f32) + self.inn[a].astype(f32) + self.inn[b].astype(f32)

        return add(self.one, 2, 4), add(self.two, 3, 5)


def qkv_kernel(x_ref, w_ref, s_ref, cos_ref, sin_ref, qt_ref, kt_ref, k_ref, v_ref, vt_ref, wt_ref, small_ref, wo_ref, wo, send, recv, local):
    heads = qt_ref.shape[0]
    width = heads * HEAD_DIM
    half = HEAD_DIM // 2
    z, c, t = spot()
    nt = lax.axis_size("tp")
    mid = width // 2
    mine, theirs = pl.ds(c * mid, mid), pl.ds((1 - c) * mid, mid)
    away, came, onward, there = [], [], [], []
    for step in range(1, nt):
        back = lax.rem(t + nt - step, nt)
        away.append(remote(wo.at[mine], wo_ref.at[t, mine], send.at[step], recv.at[step], tp=lax.rem(t + step, nt)))
        ref = wo_ref.at[back, mine]
        came.append(remote(ref, ref, send.at[nt + step], recv.at[step], ctx=1 - c))
        onward.append(remote(ref, ref, send.at[nt + step], recv.at[nt + step], ctx=1 - c))
        ref = wo_ref.at[back, theirs]
        there.append(remote(ref, ref, send.at[nt + step], recv.at[nt + step], ctx=1 - c))
    own = pltpu.make_async_copy(wo, wo_ref.at[t], local)
    i = pl.program_id(0)

    @pl.when(i == 0)
    def _():
        def flat(v):
            return v.astype(f32).reshape(v.shape[0] * v.shape[1], v.shape[2])

        def whole(core, which):
            rest = flat(w_ref[core, :, 2])[:, which * (width - 128) : (which + 1) * (width - 128)]
            return jnp.concatenate([flat(w_ref[core, :, which]), rest], axis=1).T.astype(bf16)

        wo[...] = whole(1, 1)
        greet(False)
        for copy in away:
            copy.start()
        own.start()
        wt_ref[:width] = whole(0, 0)
        wt_ref[width : 2 * width] = whole(0, 1)
        wt_ref[2 * width :] = whole(1, 0)
        small_ref[...] = jnp.concatenate([s_ref[n].astype(f32) for n in range(s_ref.shape[0])], axis=1)

    x = x_ref[...].astype(f32)
    inverse = lax.rsqrt(jnp.mean(x * x, axis=1, keepdims=True) + epsilon)
    a = (x * inverse * small_ref[18:19]).astype(bf16)
    y = mm(wt_ref[...], a, NT)
    cosine, sine = cos_ref[...], sin_ref[...]

    def turned(first):
        u, w = y[first : first + half], y[first + half : first + HEAD_DIM]
        return jnp.concatenate([u * cosine - w * sine, w * cosine + u * sine], axis=0)

    for h in range(heads):
        at = h * HEAD_DIM
        qt_ref[h] = (turned(at) * HEAD_DIM**-0.5).astype(bf16)
        key = turned(width + at)
        kt_ref[h] = key.astype(bf16)
        k_ref[h] = key.T.astype(bf16)
        value = y[2 * width + at : 2 * width + at + HEAD_DIM]
        v_ref[h] = value.T.astype(bf16)
        vt_ref[h, :HEAD_DIM] = value.astype(bf16)
        vt_ref[h, HEAD_DIM:] = jnp.ones((16, value.shape[1]), bf16)

    @pl.when(i == pl.num_programs(0) - 2)
    def _():
        for copy, forth in zip(came, onward):
            copy.wait_recv()
            forth.start()

    @pl.when(i == pl.num_programs(0) - 1)
    def _():
        for copy in there:
            copy.wait_recv()
        for copy in away + onward:
            copy.wait_send()
        own.wait()


def project(rows, w, small, cosine, sine, heads, number):
    total, width = rows.shape
    tile = BLOCK
    out = heads * HEAD_DIM
    nt = lax.axis_size("tp")
    shapes = [
        jax.ShapeDtypeStruct((heads, HEAD_DIM, total), bf16),
        jax.ShapeDtypeStruct((heads, HEAD_DIM, total), bf16),
        jax.ShapeDtypeStruct((heads, total, HEAD_DIM), bf16),
        jax.ShapeDtypeStruct((heads, total, HEAD_DIM), bf16),
        jax.ShapeDtypeStruct((heads, HEAD_DIM + 16, total), bf16),
        jax.ShapeDtypeStruct((3 * out, width), bf16),
        jax.ShapeDtypeStruct((SMALL, width), f32),
        jax.ShapeDtypeStruct((nt, out, width), bf16),
    ]
    return pl.pallas_call(
        qkv_kernel,
        grid=(total // tile,),
        in_specs=[
            pl.BlockSpec((tile, width), lambda i: (i, 0)),
            full(w.shape),
            full(small.shape),
            pl.BlockSpec((HEAD_DIM // 2, tile), lambda i: (0, i)),
            pl.BlockSpec((HEAD_DIM // 2, tile), lambda i: (0, i)),
        ],
        out_specs=[
            pl.BlockSpec((heads, HEAD_DIM, tile), lambda i: (0, 0, i)),
            pl.BlockSpec((heads, HEAD_DIM, tile), lambda i: (0, 0, i)),
            pl.BlockSpec((heads, tile, HEAD_DIM), lambda i: (0, i, 0)),
            pl.BlockSpec((heads, tile, HEAD_DIM), lambda i: (0, i, 0)),
            pl.BlockSpec((heads, HEAD_DIM + 16, tile), lambda i: (0, 0, i)),
        ]
        + [full(v.shape) for v in shapes[5:7]]
        + anywhere(1),
        scratch_shapes=[
            pltpu.VMEM((out, width), bf16),
            pltpu.SemaphoreType.DMA((2 * nt,)),
            pltpu.SemaphoreType.DMA((2 * nt,)),
            pltpu.SemaphoreType.DMA,
        ],
        out_shape=shapes,
        compiler_params=params(collective_id=number, has_side_effects=True),
        cost_estimate=cost(14),
        name="project",
    )(rows, w, small, cosine, sine)


def dealt(core, i):
    return 4 * (i // 2) + jnp.where(lax.rem(i, 2) == 0, core, 3 - core)


def attend_kernel(cuts, length, qt_ref, k_ref, vt_ref, cot_ref, ot_ref, lse_ref, top_ref, cots_ref, mask_cot, *sems):
    z, c, t = spot()
    nt = lax.axis_size("tp")
    h, i = pl.program_id(0), pl.program_id(1)
    count = pl.num_programs(1)
    at_step = h * count + i
    last = pl.num_programs(0) * count - 1
    gather = Gather(mask_cot, cots_ref, *sems, cuts)

    @pl.when(at_step == 0)
    def _():
        rows = cot_ref.shape[0]
        position = (c * nt + t) * rows + lax.broadcasted_iota(jnp.int32, cot_ref.shape, 0)
        mask_cot[...] = jnp.where(position < length[0], cot_ref[...].astype(f32), 0.0).astype(bf16)
        greet(False)
        gather.first()

    index = dealt(c, i)
    columns = BLOCK
    qt = qt_ref[0, :, pl.ds(pl.multiple_of(index * BLOCK, BLOCK), BLOCK)]

    def step(at, carry, diagonal):
        peak, total = carry
        start = pl.multiple_of(at * BLOCK, BLOCK)
        scores = mm(k_ref[0, pl.ds(start, BLOCK), :], qt)
        if diagonal:
            keys = lax.broadcasted_iota(jnp.int32, scores.shape, 0)
            queries = lax.broadcasted_iota(jnp.int32, scores.shape, 1)
            scores = jnp.where(keys <= queries, scores, -1e30)
        higher = jnp.maximum(peak, jnp.max(scores, axis=0, keepdims=True))
        weights = jnp.exp(scores - higher).astype(bf16)
        total = total * jnp.exp(peak - higher) + mm(vt_ref[0, :, pl.ds(start, BLOCK)], weights)
        return higher, total

    start = (jnp.full((1, columns), -1e30, f32), jnp.zeros((HEAD_DIM + 16, columns), f32))
    carry = lax.fori_loop(0, index, lambda at, c: step(at, c, False), start)
    peak, total = step(index, carry, True)
    mass = total[HEAD_DIM : HEAD_DIM + 1]
    ot_ref[0] = (total[:HEAD_DIM] / mass).astype(bf16)
    lse_ref[0, 0] = peak + jnp.log(mass)
    position = index * BLOCK + lax.broadcasted_iota(jnp.int32, peak.shape, 1)
    top_ref[0, 0] = jnp.where(position < length[0], peak, -1e30)

    @pl.when(at_step == last - 3)
    def _():
        for s in range(cuts):
            gather.second(s)

    @pl.when(at_step == last)
    def _():
        for s in range(cuts):
            gather.third(s)
        gather.last()


def attend(length, qt, k, vt, cot, count, number):
    cuts = 1
    heads, _, total = qt.shape
    return pl.pallas_call(
        functools.partial(attend_kernel, cuts),
        grid_spec=pltpu.PrefetchScalarGridSpec(
            num_scalar_prefetch=1,
            grid=(heads, count),
            in_specs=[
                pl.BlockSpec((1, HEAD_DIM, total), lambda h, i, n: (h, 0, 0)),
                pl.BlockSpec((1, total, HEAD_DIM), lambda h, i, n: (h, 0, 0)),
                pl.BlockSpec((1, HEAD_DIM + 16, total), lambda h, i, n: (h, 0, 0)),
                full(cot.shape),
            ],
            out_specs=[
                pl.BlockSpec((1, HEAD_DIM, BLOCK), lambda h, i, n: (i, h, 0)),
                pl.BlockSpec((1, 1, 1, BLOCK), lambda h, i, n: (h, i, 0, 0)),
                pl.BlockSpec((1, 1, 1, BLOCK), lambda h, i, n: (h, i, 0, 0)),
            ]
            + anywhere(1),
            scratch_shapes=[
                pltpu.VMEM(cot.shape, bf16),
            ]
            + Gather.scratch(cuts),
        ),
        out_shape=[
            jax.ShapeDtypeStruct((count, heads * HEAD_DIM, BLOCK), bf16),
            jax.ShapeDtypeStruct((heads, count, 1, BLOCK), f32),
            jax.ShapeDtypeStruct((heads, count, 1, BLOCK), f32),
            jax.ShapeDtypeStruct((8,) + cot.shape, bf16),
        ],
        compiler_params=params(collective_id=number, has_side_effects=True),
        cost_estimate=cost(35),
        name="attend",
    )(length, qt, k, vt, cot)


def revisit_kernel(qt_ref, k_ref, kt_ref, v_ref, ot_ref, got_ref, lse_ref, go_ref, feed_ref, dq_ref, dk_ref, dv_ref, gos_ref, fed_ref, sum_k, sum_v, came_ref, w_send, w_recv, *scratch):
    z, c, t = spot()
    job = Sum(feed_ref, *scratch)
    nt = lax.axis_size("tp")
    h, i = pl.program_id(0), pl.program_id(1)
    count = pl.num_programs(1)
    index = dealt(c, i)
    here = pl.ds(pl.multiple_of(index * BLOCK, BLOCK), BLOCK)
    away = [
        remote(go_ref.at[lax.rem(t + step, nt)], came_ref.at[step], w_send.at[step], w_recv.at[step], tp=lax.rem(t + step, nt))
        for step in range(1, nt)
    ]

    at_step = h * count + i
    end = pl.num_programs(0) * count - 1

    @pl.when(at_step == 0)
    def _():
        greet(False)
        job.first()
        for copy in away:
            copy.start()

    @pl.when(at_step == 3)
    def _():
        job.second()

    @pl.when(at_step == end - 3)
    def _():
        job.third()

    qt, got = qt_ref[0, :, here], got_ref[0]
    lse = lse_ref[0, 0]
    centre = jnp.sum(ot_ref[0].astype(f32) * got.astype(f32), axis=0, keepdims=True)

    @pl.when(i == 0)
    def _():
        sum_k[...] = jnp.zeros_like(sum_k)
        sum_v[...] = jnp.zeros_like(sum_v)
        dq_ref[...] = jnp.zeros_like(dq_ref)

    def step(at, grad, diagonal):
        start = pl.multiple_of(at * BLOCK, BLOCK)
        here = pl.ds(start, BLOCK)
        scores = mm(k_ref[0, here, :], qt)
        probs = jnp.exp(scores - lse)
        if diagonal:
            keys = lax.broadcasted_iota(jnp.int32, scores.shape, 0)
            queries = lax.broadcasted_iota(jnp.int32, scores.shape, 1)
            probs = jnp.where(keys <= queries, probs, 0.0)
        grad_probs = mm(v_ref[0, here, :], got)
        grad_scores = (probs * (grad_probs - centre)).astype(bf16)
        sum_v[:, here] += mm(got, probs.astype(bf16), NT)
        sum_k[:, here] += mm(qt, grad_scores, NT)
        return grad + mm(kt_ref[0, :, here], grad_scores)

    grad = lax.fori_loop(0, index, lambda at, c: step(at, c, False), jnp.zeros(qt.shape, f32))
    dq_ref[0, :, here] = step(index, grad, True) * HEAD_DIM**-0.5

    @pl.when(i == count - 1)
    def _():
        dk_ref[0] = sum_k[...]
        dv_ref[0] = sum_v[...]

    @pl.when(at_step == end)
    def _():
        job.last()
        one, two = job.total()
        fed_ref[: job.half] = one
        fed_ref[job.half :] = two
        total = go_ref[t].astype(f32)
        for step, copy in enumerate(away):
            copy.wait_recv()
            total = total + came_ref[step + 1].astype(f32)
            copy.wait_send()
        gos_ref[...] = total.astype(bf16)


def revisit(qt, k, kt, v, ot, got, lse, go, feed, number):
    heads, _, total = qt.shape
    count = ot.shape[0]
    nt = lax.axis_size("tp")
    whole = pl.BlockSpec((1, HEAD_DIM, total), lambda h, i: (h, 0, 0))
    tall = pl.BlockSpec((1, total, HEAD_DIM), lambda h, i: (h, 0, 0))
    some = pl.BlockSpec((1, HEAD_DIM, BLOCK), lambda h, i: (i, h, 0))
    return pl.pallas_call(
        revisit_kernel,
        grid=(heads, count),
        in_specs=[
            whole,
            tall,
            whole,
            tall,
            some,
            some,
            pl.BlockSpec((1, 1, 1, BLOCK), lambda h, i: (h, i, 0, 0)),
            full(go.shape),
        ]
        + anywhere(1),
        out_specs=[whole, whole, whole, full(go.shape[1:]), full(feed.shape[1:])],
        scratch_shapes=[
            pltpu.VMEM((HEAD_DIM, total), f32),
            pltpu.VMEM((HEAD_DIM, total), f32),
            pltpu.VMEM(go.shape, bf16),
            pltpu.SemaphoreType.DMA((nt,)),
            pltpu.SemaphoreType.DMA((nt,)),
        ]
        + Sum.scratch(*feed.shape[1:]),
        out_shape=[jax.ShapeDtypeStruct((heads, HEAD_DIM, total), f32)] * 3
        + [jax.ShapeDtypeStruct(go.shape[1:], bf16), jax.ShapeDtypeStruct(feed.shape[1:], f32)],
        compiler_params=params(collective_id=number, has_side_effects=True),
        cost_estimate=cost(50),
        name="revisit",
    )(qt, k, kt, v, ot, got, lse, go, feed)


def opening_kernel(cuts, x_ref, wq_ref, wk_ref, wv_ref, wo_ref, wr_ref, wc_ref, vec_ref, na_ref, nm_ref, routes_ref, out_ref, ws_ref, smalls_ref, all_routes_ref, held, stage, small_ref, *sems):
    gather = Gather(x_ref, out_ref, *sems[:3], cuts, stage)
    sends, recvs, local = sems[3:]
    z, c, t = spot()
    ns = lax.axis_size("shard")
    one = jnp.where(c == 0, wq_ref[...].astype(f32), wv_ref[...].astype(f32))
    two = jnp.where(c == 0, wk_ref[...].astype(f32), wo_ref[...].astype(f32).T)
    held[0] = one[:, :128].astype(bf16)
    held[1] = two[:, :128].astype(bf16)
    parts = [v[...].astype(f32) for v in (wr_ref, wc_ref, vec_ref, na_ref, nm_ref)]
    used = sum(v.shape[0] for v in parts)
    parts.append(jnp.zeros((SMALL - used, parts[0].shape[1]), f32))
    small_ref[...] = jnp.concatenate(parts, axis=0).astype(bf16)
    held[2] = jnp.concatenate([one[:, 128:], two[:, 128:]], axis=1).astype(bf16)
    greet()
    started = []

    def go(k, source, target, **where):
        copy = remote(source, target, sends.at[k], recvs.at[k], **where)
        copy.start()
        started.append(copy)

    def came(k, ref):
        remote(ref, ref, sends.at[k], recvs.at[k], ctx=1 - c).wait_recv()

    for step in range(1, ns):
        go(step, held, ws_ref.at[c, z], shard=lax.rem(z + step, ns))
    gather.first()
    for step in range(1, ns):
        go(2 * ns + step, small_ref, smalls_ref.at[z], shard=lax.rem(z + step, ns))
    go(0, held, ws_ref.at[c, z], ctx=1 - c)
    go(ns, routes_ref, all_routes_ref.at[c], ctx=1 - c)
    mine = [
        pltpu.make_async_copy(held, ws_ref.at[c, z], local.at[0]),
        pltpu.make_async_copy(small_ref, smalls_ref.at[z], local.at[1]),
        pltpu.make_async_copy(routes_ref, all_routes_ref.at[c], local.at[2]),
    ]
    for copy in mine:
        copy.start()
    for s in range(cuts):
        gather.second(s)
    for s in range(cuts):
        gather.third(s)
    for step in range(1, ns):
        back = lax.rem(z + ns - step, ns)
        came(step, ws_ref.at[c, back])
        go(ns + step, ws_ref.at[c, back], ws_ref.at[c, back], ctx=1 - c)
    gather.last()
    came(0, ws_ref.at[1 - c, z])
    came(ns, all_routes_ref.at[1 - c])
    for step in range(1, ns):
        back = lax.rem(z + ns - step, ns)
        came(2 * ns + step, smalls_ref.at[back])
        came(ns + step, ws_ref.at[1 - c, back])
    for copy in started:
        copy.wait_send()
    for copy in mine:
        copy.wait()


def opening(x, weights, small, routes, number):
    cuts = 2
    ns = lax.axis_size("shard")
    depth = weights[0].shape[0]
    held = (3, depth, 128)
    vmem = pl.BlockSpec(memory_space=pltpu.VMEM)
    return pl.pallas_call(
        functools.partial(opening_kernel, cuts),
        in_specs=anywhere(1) + [vmem] * (len(weights) + len(small) + 1),
        out_specs=anywhere(4),
        out_shape=[
            jax.ShapeDtypeStruct((8,) + x.shape, x.dtype),
            jax.ShapeDtypeStruct((2, ns) + held, bf16),
            jax.ShapeDtypeStruct((ns, SMALL, depth), bf16),
            jax.ShapeDtypeStruct((2,) + routes.shape, routes.dtype),
        ],
        scratch_shapes=[pltpu.VMEM(held, bf16), pltpu.VMEM(x.shape, x.dtype), pltpu.VMEM((SMALL, depth), bf16)]
        + Gather.scratch(cuts)
        + [
            pltpu.SemaphoreType.DMA((3 * ns,)),
            pltpu.SemaphoreType.DMA((3 * ns,)),
            pltpu.SemaphoreType.DMA((3,)),
        ],
        compiler_params=params(collective_id=number, has_side_effects=True),
        cost_estimate=cost(30),
        name="opening",
    )(x, *weights, *small, routes)


def places(routes_ref, row_ref):
    one = lax.broadcasted_iota(jnp.int32, (BLOCK, BLOCK), 0)
    two = lax.broadcasted_iota(jnp.int32, (BLOCK, BLOCK), 1)
    before = (one < two).astype(bf16)
    blocks, _, per = routes_ref.shape
    for b in range(blocks):
        carry = jnp.zeros((16, 1), f32)
        for at in range(0, per, BLOCK):
            here = slice(at, at + BLOCK)
            expert = lax.broadcasted_iota(jnp.int32, (16, BLOCK), 0)
            member = (routes_ref[b, 0:1, here] == expert) | (routes_ref[b, 1:2, here] == expert)
            rank = mm(member.astype(bf16), before) + carry
            row_ref[:, b * per + at : b * per + at + BLOCK] = jnp.where(member, rank, -1.0)
            carry = carry + jnp.sum(member.astype(f32), axis=1, keepdims=True)


def route_kernel(cuts, o_ref, x_ref, wo_ref, small_ref, prev_ref, routes_ref, cots_ref,
                 att, res_out, base_out, x_out, g_out, gate_ref, row_ref,
                 x_in, wo_in, res, base, a, comb, rows, cots, combs, xs, gs,
                 o_send, o_recv, c_send, c_recv, local, out_sem, x_sem, g_sem, *sems):
    gather = Gather(a, rows, *sems, cuts, relative=True)
    z, c, t = spot()
    nt = lax.axis_size("tp")
    own = 4 * c + t
    near = (t,) + across(t)
    blocks, _, per = routes_ref.shape
    width = rows.shape[2]
    experts = xs.shape[0]
    here = pl.ds(pl.multiple_of(t * BLOCK, BLOCK), BLOCK)
    loads = [
        pltpu.make_async_copy(cots_ref, cots, local.at[0]),
        pltpu.make_async_copy(x_ref, x_in, local.at[1]),
        pltpu.make_async_copy(wo_ref, wo_in, local.at[2]),
    ]
    for copy in loads:
        copy.start()
    greet(False)

    copies = []
    for i in range(o_ref.shape[0]):
        block = zig(c, i)
        copy = remote(o_ref.at[i], att.at[t], o_send.at[i], o_recv.at[t], ctx=block // nt, tp=lax.rem(block, nt))
        copies.append((block == own, copy, pltpu.make_async_copy(o_ref.at[i], att.at[t], local.at[3])))
    for mine, copy, inside in copies:

        @pl.when(jnp.logical_not(mine))
        def _():
            copy.start()

        @pl.when(mine)
        def _():
            inside.start()

    each = per // nt

    def names(b, j, order):
        start = pl.multiple_of(b * per, per)
        mine = row_ref[pl.ds(experts * c + j, 1), pl.ds(start, per)] if order is None else jnp.concatenate(
            [row_ref[pl.ds(experts * c + j, 1), pl.ds(pl.multiple_of(start + o * each, each), each)] for o in order], axis=1
        )
        return lax.broadcasted_iota(jnp.int32, (CAP, mine.shape[1]), 0).astype(f32) == mine

    def fetch(n):
        b, j = n // experts, lax.rem(n, experts)
        here = pl.ds(pl.multiple_of(b * CAP, CAP), CAP)
        hot = names(b, j, None)
        gs[j, here] = mm(hot.astype(bf16), cots[pl.ds(4 * b, 4)].reshape(per, width)).astype(bf16)
        pltpu.make_async_copy(gs.at[j, here], g_out.at[j, here], g_sem.at[n]).start()

    def fetch_x(beside, j, which):
        b = 1 - c if beside else c
        here = pl.ds(pl.multiple_of(b * CAP, CAP), CAP)
        order = [near[k] for k in which]
        hot = names(b, j, order)
        first = 4 * beside + which[0]
        got = mm(hot.astype(bf16), rows[first : first + len(which)].reshape(len(which) * each, width)).astype(bf16)
        gate = jnp.zeros((CAP, 1), f32)
        for k, o in enumerate(order):
            weight = combs[4 * b + o, pl.ds(experts * c + j, 1)]
            gate = gate + jnp.sum(jnp.where(hot[:, k * each : (k + 1) * each], weight, 0.0), axis=1, keepdims=True)
        if which[0] == 0:
            xs[j, here] = got
            gate_ref[j, here] = gate
        else:
            xs[j, here] = xs[j, here] + got
            gate_ref[j, here] = gate_ref[j, here] + gate
            n = b * experts + j
            pltpu.make_async_copy(xs.at[j, here], x_out.at[j, here], x_sem.at[n]).start()

    def all_x(beside, which):
        @pl.loop(0, experts)
        def _(j):
            fetch_x(beside, j, which)

    def fetch_g(first, last):
        @pl.loop(first, last)
        def _(n):
            fetch(n)

    places(routes_ref, row_ref)
    for copy in loads:
        copy.wait()
    fetch_g(0, 2)
    for mine, copy, inside in copies:

        @pl.when(jnp.logical_not(mine))
        def _():
            copy.wait_send()

        @pl.when(mine)
        def _():
            inside.wait()

    mine = lax.rem((own + 1) // 2, 2) == c
    for source in range(nt):

        @pl.when(jnp.logical_or(jnp.logical_not(mine), source != t))
        def _():
            remote(o_ref.at[0], att.at[source], o_send.at[0], o_recv.at[source], ctx=c, tp=t).wait_recv()

    attended = att[...].reshape(-1, BLOCK)
    r = x_in[...].astype(f32) + mm(attended, wo_in[...].reshape(-1, width), TN)
    inverse = lax.rsqrt(jnp.mean(r * r, axis=1, keepdims=True) + epsilon)
    n2 = r * inverse * small_ref[19:20]
    a[...] = n2.astype(bf16)
    gather.first()
    res[...] = r
    _, _, combined, alphas, weights = mixing(n2, small_ref[:16], *laid(prev_ref[:, here], routes_ref[c, :, here]))
    comb[...] = combined
    pairs = []
    for step in range(1, 8):
        other, back = lax.rem(own + step, 8), lax.rem(own + 8 - step, 8)
        where = {"ctx": other // 4, "tp": lax.rem(other, 4)}
        copy = remote(comb, combs.at[own], c_send.at[step], c_recv.at[step], **where)
        copy.start()
        pairs.append((copy, remote(comb, combs.at[back], c_send.at[step], c_recv.at[step], **where)))
    combs[own] = comb[...]
    scale, one, two = scales(alphas, weights)
    base[...] = r + scale * n2 + one * small_ref[16:17] + two * small_ref[17:18]
    outs = [
        pltpu.make_async_copy(res, res_out, out_sem.at[0]),
        pltpu.make_async_copy(base, base_out, out_sem.at[1]),
    ]
    for copy in outs:
        copy.start()

    total = blocks * experts
    fetch_g(2, 4)
    gather.second(0)
    fetch_g(4, total)
    gather.second(1)
    gather.own.wait()
    for copy, came in pairs:
        came.wait_recv()
    all_x(0, (0, 1, 2))
    gather.third(0)
    gather.third(1)
    gather.beside()
    all_x(1, (0, 1, 2))
    all_x(0, (3,))
    gather.last(True)
    all_x(1, (3,))

    for copy, came in pairs:
        copy.wait_send()
    for copy in outs:
        copy.wait()

    @pl.loop(0, total)
    def _(n):
        b, j = n // experts, lax.rem(n, experts)
        here = pl.ds(pl.multiple_of(b * CAP, CAP), CAP)
        pltpu.make_async_copy(gs.at[j, here], g_out.at[j, here], g_sem.at[n]).wait()
        pltpu.make_async_copy(xs.at[j, here], x_out.at[j, here], x_sem.at[n]).wait()


def route(o, x, wo, small, prev, routes, cots, experts, number):
    cuts = 2
    own, width = x.shape
    nt = lax.axis_size("tp")
    blocks, _, per = routes.shape
    slots = jax.ShapeDtypeStruct((experts, blocks * CAP, width), bf16)
    vmem = pl.BlockSpec(memory_space=pltpu.VMEM)
    return pl.pallas_call(
        functools.partial(route_kernel, cuts),
        in_specs=anywhere(3) + [vmem, vmem, vmem] + anywhere(1),
        out_specs=[vmem] + anywhere(4) + [vmem, vmem],
        out_shape=[
            jax.ShapeDtypeStruct((nt,) + o.shape[1:], bf16),
            jax.ShapeDtypeStruct((own, width), f32),
            jax.ShapeDtypeStruct((own, width), f32),
            slots,
            slots,
            jax.ShapeDtypeStruct((experts, blocks * CAP, 1), f32),
            jax.ShapeDtypeStruct((16, blocks * per), f32),
        ],
        scratch_shapes=[
            pltpu.VMEM((own, width), bf16),
            pltpu.VMEM(wo.shape, bf16),
            pltpu.VMEM((own, width), f32),
            pltpu.VMEM((own, width), f32),
            pltpu.VMEM((own, width), bf16),
            pltpu.VMEM((16, own), f32),
            pltpu.VMEM((8, own, width), bf16),
            pltpu.VMEM((8, own, width), bf16),
            pltpu.VMEM((8, 16, own), f32),
            pltpu.VMEM(slots.shape, bf16),
            pltpu.VMEM(slots.shape, bf16),
            pltpu.SemaphoreType.DMA((o.shape[0],)),
            pltpu.SemaphoreType.DMA((nt,)),
            pltpu.SemaphoreType.DMA((8,)),
            pltpu.SemaphoreType.DMA((8,)),
            pltpu.SemaphoreType.DMA((4,)),
            pltpu.SemaphoreType.DMA((2,)),
            pltpu.SemaphoreType.DMA((blocks * experts,)),
            pltpu.SemaphoreType.DMA((blocks * experts,)),
        ]
        + Gather.scratch(cuts),
        compiler_params=params(collective_id=number, has_side_effects=True),
        cost_estimate=cost(65),
        name="route",
    )(o, x, wo, small, prev, routes, cots)


def spot_rows(place, c, experts, first, some, values, at):
    lane = lax.broadcasted_iota(jnp.int32, place.shape, 1)
    slot = lax.broadcasted_iota(jnp.int32, (place.shape[0], CAP), 1).astype(f32)
    total = None
    for j in range(some):
        mine = jnp.sum(jnp.where(lane == experts * c + first + j, place, 0.0), axis=1, keepdims=True)
        term = mm((slot == mine).astype(bf16), values[j, at])
        total = term if total is None else total + term
    return total


def combine_kernel(experts, row_ref, *refs):
    back_ref, feed_ref, out_ref, feed_out, gates_ref = refs[:5]
    backs, feeds, stage, staged, gsend, gcame, l_sem, o_sem, g_send, g_recv = refs[5:15]
    job = Sum(None, *refs[15:], stage=stage)
    z, c, t = spot()
    own = 4 * c + t
    width = stage.shape[2]
    loads = [pltpu.make_async_copy(back_ref, backs, l_sem.at[0])]
    more = [pltpu.make_async_copy(feed_ref, feeds, l_sem.at[1])]
    for copy in loads + more:
        copy.start()
    greet(False)

    def tile(values, owner):
        start = pl.multiple_of(owner * BLOCK, BLOCK)
        place = row_ref[:, pl.ds(start, BLOCK)].T
        here = pl.ds(pl.multiple_of(owner // 4 * CAP, CAP), CAP)
        count = values.shape[0]
        return spot_rows(place, c, experts, experts - count, count, values, here)

    def back(owner):
        got = tile(backs, owner)
        named = got[:, width:].T
        gsend[owner] = named[:FFN_EXPERTS] + named[16 : 16 + FFN_EXPERTS]
        return got[:, :width]

    for copy in loads:
        copy.wait()
    for k, o in enumerate(job.order):
        stage[k] = back(4 * (1 - c) + o).astype(bf16)
        job.core[k].start()
        job.add(k, back(4 * c + o))
    job.third()
    pairs = []
    for step in range(1, 8):
        other = lax.rem(own + step, 8)
        copy = remote(gsend.at[other], gcame.at[step], g_send.at[step], g_recv.at[step], ctx=other // 4, tp=lax.rem(other, 4))
        copy.start()
        pairs.append(copy)
    for copy in more:
        copy.wait()

    def feed(first, last):
        @pl.loop(first, last)
        def _(n):
            staged[n] = tile(feeds, n).astype(bf16)
            pltpu.make_async_copy(staged.at[n], feed_out.at[n], o_sem.at[n]).start()

    feed(0, 8)
    gates = gsend[own]
    for step, copy in enumerate(pairs):
        copy.wait_recv()
        gates = gates + gcame[step + 1]
        copy.wait_send()
    gates_ref[...] = gates
    job.last()
    one, two = job.total()
    out_ref[: job.half] = one
    out_ref[job.half :] = two

    @pl.loop(0, 8)
    def _(n):
        pltpu.make_async_copy(staged.at[n], feed_out.at[n], o_sem.at[n]).wait()


def combine(row, back, feed, number):
    experts, slots, width = feed.shape
    wide = back.shape[2]
    rows = row.shape[1] // 8
    vmem = pl.BlockSpec(memory_space=pltpu.VMEM)
    return pl.pallas_call(
        functools.partial(combine_kernel, experts),
        in_specs=[vmem] + anywhere(2),
        out_specs=[vmem] + anywhere(1) + [vmem],
        out_shape=[
            jax.ShapeDtypeStruct((rows, width), f32),
            jax.ShapeDtypeStruct((8, rows, width), bf16),
            jax.ShapeDtypeStruct((FFN_EXPERTS, rows), f32),
        ],
        scratch_shapes=[
            pltpu.VMEM((experts, slots, wide), bf16),
            pltpu.VMEM(feed.shape, bf16),
            pltpu.VMEM((4, rows, width), bf16),
            pltpu.VMEM((8, rows, width), bf16),
            pltpu.VMEM((8, FFN_EXPERTS, rows), f32),
            pltpu.VMEM((8, FFN_EXPERTS, rows), f32),
            pltpu.SemaphoreType.DMA((2,)),
            pltpu.SemaphoreType.DMA((8,)),
            pltpu.SemaphoreType.DMA((8,)),
            pltpu.SemaphoreType.DMA((8,)),
        ]
        + Sum.scratch(rows, width),
        compiler_params=params(collective_id=number, has_side_effects=True),
        cost_estimate=cost(45),
        name="combine",
    )(row, back, feed)


def closing_kernel(dq_ref, dk_ref, dv_ref, x_ref, cos_ref, sin_ref, wt_ref, par_ref, go_ref, small_ref, top_ref,
                   out_ref, gsum_ref, ssum_ref, tmax_ref,
                   dqs, dks, dvs, xs, total, row, gother, gcore, gline, gmine, smine, sline, splane, tline, mytop, stage, l_sem, *sems):
    job = Sum(None, *sems[:7], stage=stage)
    sends, recvs = sems[7:]
    z, c, t = spot()
    ns = lax.axis_size("shard")
    heads = dqs.shape[0]
    half = HEAD_DIM // 2
    own = 4 * c + t
    order = [4 * (1 - c) + o for o in job.order] + [4 * c + o for o in job.order]

    def lanes(o):
        return pl.ds(pl.multiple_of(o * BLOCK, BLOCK), BLOCK)

    loads = []
    for n, o in enumerate(order):
        here = lanes(o)
        loads.append(
            [
                pltpu.make_async_copy(dq_ref.at[:, :, here], dqs.at[:, :, here], l_sem.at[n, 0]),
                pltpu.make_async_copy(dk_ref.at[:, :, here], dks.at[:, :, here], l_sem.at[n, 1]),
                pltpu.make_async_copy(dv_ref.at[:, :, here], dvs.at[:, :, here], l_sem.at[n, 2]),
                pltpu.make_async_copy(x_ref.at[here], xs.at[here], l_sem.at[n, 3]),
            ]
        )
    for k in range(4):
        for copy in loads[k] + loads[4 + k]:
            copy.start()
    greet()
    started = []

    def go(k, source, target, **where):
        copy = remote(source, target, sends.at[k], recvs.at[k], **where)
        copy.start()
        started.append(copy)
        return copy

    line_row = lax.broadcasted_iota(jnp.int32, mytop.shape, 0)
    high = jnp.full(mytop.shape, -1e30, f32)
    for h in range(top_ref.shape[0]):
        best = jnp.max(jnp.max(top_ref[h], axis=0), axis=1, keepdims=True)
        high = jnp.where(line_row == h, best, high)
    mytop[...] = high
    tops = [go(3 + ns + s, mytop, tline.at[s], shard=lax.rem(z + s, ns)) for s in range(1, ns)]
    total[...] = jnp.zeros_like(total)
    row[...] = jnp.zeros_like(row)

    def tile(o):
        here = lanes(o)
        cosine, sine = cos_ref[:, here], sin_ref[:, here]

        def turned(g):
            u, w = g[:half], g[half:]
            return jnp.concatenate([u * cosine + w * sine, w * cosine - u * sine], axis=0)

        x = xs[here].astype(f32)
        m = x * lax.rsqrt(jnp.mean(x * x, axis=1, keepdims=True) + epsilon)
        a = (m * par_ref[18:19]).astype(bf16)
        pieces = [turned(dqs[h, :, here]) for h in range(heads)]
        pieces += [turned(dks[h, :, here]) for h in range(heads)]
        pieces += [dvs[h, :, here] for h in range(heads)]
        grads = jnp.concatenate(pieces, axis=0).astype(bf16)
        part = mm(grads, wt_ref[...], TN)
        row[...] += jnp.sum(part * m, axis=0, keepdims=True)
        total[...] += mm(grads, a)
        return part

    for k in range(4):
        for copy in loads[k] + loads[4 + k]:
            copy.wait()
        stage[k] = tile(order[k]).astype(bf16)
        job.core[k].start()
        job.add(k, tile(order[4 + k]))

    cut_rows, depth = gsum_ref.shape[1:]
    at = lax.broadcasted_iota(jnp.int32, small_ref.shape, 0)
    smalls = small_ref[...] + jnp.where(at == 19, row[...], 0.0)
    for s in range(ns):
        here = slice(s * depth, (s + 1) * depth)
        one = total[:cut_rows, here].astype(bf16)
        two = jnp.concatenate([total[cut_rows:, here].astype(bf16), go_ref[:, here]], axis=0)
        gmine[s] = packed(jnp.where(c == 0, one.astype(f32), two.astype(f32))).astype(bf16)
        gother[s] = packed(jnp.where(c == 0, two.astype(f32), one.astype(f32))).astype(bf16)
        smine[s] = smalls[:, here]
    core = go(0, gother, gcore, ctx=1 - c)
    small = [go(3 + s, smine.at[lax.rem(z + s, ns)], sline.at[s], shard=lax.rem(z + s, ns)) for s in range(1, ns)]
    core.wait_recv()
    gmine[...] = gmine[...] + gcore[...]
    line = [go(3 + 2 * ns + s, gmine.at[lax.rem(z + s, ns)], gline.at[s], shard=lax.rem(z + s, ns)) for s in range(1, ns)]
    job.third()
    for copy in small:
        copy.wait_recv()
    value = smine[z]
    for s in range(1, ns):
        value = value + sline[s]
    splane[0] = value
    plane = []
    for s in range(1, 8):
        other = lax.rem(own + s, 8)
        plane.append(go(3 + 3 * ns + s, splane.at[0], splane.at[s], ctx=other // 4, tp=lax.rem(other, 4)))
    for copy in tops:
        copy.wait_recv()
    high = mytop[...]
    for s in range(1, ns):
        high = jnp.maximum(high, tline[s])
    tline[0] = high
    pair = go(2, tline.at[0], tline.at[ns], ctx=1 - c)
    for copy in line:
        copy.wait_recv()
    value = gmine[z].astype(f32)
    for s in range(1, ns):
        value = value + gline[s].astype(f32)
    gsum_ref[c] = unpacked(value, depth)
    go(3, gsum_ref.at[c], gsum_ref.at[c], ctx=1 - c)
    for copy in plane:
        copy.wait_recv()
    value = splane[0]
    for s in range(1, 8):
        value = value + splane[s]
    ssum_ref[...] = value
    pair.wait_recv()
    tmax_ref[...] = jnp.maximum(tline[0], tline[ns])
    job.last()
    one, two = job.total()
    out_ref[: job.half] = one
    out_ref[job.half :] = two
    remote(gsum_ref.at[1 - c], gsum_ref.at[1 - c], sends.at[3], recvs.at[3], ctx=1 - c).wait_recv()
    for copy in started:
        copy.wait_send()


def closing(dq, dk, dv, x, cosine, sine, wt, par, go, small, top, number):
    heads, _, total = dq.shape
    width = x.shape[1]
    rows = total // 8
    ns = lax.axis_size("shard")
    depth = width // ns
    cut_rows = 2 * heads * HEAD_DIM
    pieces = (ns, cut_rows * 3 // 2, 128) if depth == 192 else (ns, cut_rows, depth)
    smalls = (ns,) + small.shape[:1] + (depth,)
    vmem = pl.BlockSpec(memory_space=pltpu.VMEM)
    return pl.pallas_call(
        closing_kernel,
        in_specs=anywhere(4) + [vmem] * 7,
        out_specs=[vmem] * 4,
        out_shape=[
            jax.ShapeDtypeStruct((rows, width), f32),
            jax.ShapeDtypeStruct((2, cut_rows, depth), f32),
            jax.ShapeDtypeStruct(smalls[1:], f32),
            jax.ShapeDtypeStruct((8, 128), f32),
        ],
        scratch_shapes=[
            pltpu.VMEM(dq.shape, f32),
            pltpu.VMEM(dq.shape, f32),
            pltpu.VMEM(dq.shape, f32),
            pltpu.VMEM(x.shape, bf16),
            pltpu.VMEM(wt.shape, f32),
            pltpu.VMEM((1, width), f32),
            pltpu.VMEM(pieces, bf16),
            pltpu.VMEM(pieces, bf16),
            pltpu.VMEM(pieces, bf16),
            pltpu.VMEM(pieces, bf16),
            pltpu.VMEM(smalls, f32),
            pltpu.VMEM(smalls, f32),
            pltpu.VMEM((8,) + smalls[1:], f32),
            pltpu.VMEM((ns + 1, 8, 128), f32),
            pltpu.VMEM((8, 128), f32),
            pltpu.VMEM((4, rows, width), bf16),
            pltpu.SemaphoreType.DMA((8, 4)),
        ]
        + Sum.scratch(rows, width)
        + [
            pltpu.SemaphoreType.DMA((3 * ns + 11,)),
            pltpu.SemaphoreType.DMA((3 * ns + 11,)),
        ],
        compiler_params=params(collective_id=number, has_side_effects=True),
        cost_estimate=cost(45),
        name="closing",
    )(dq, dk, dv, x, cosine, sine, wt, par, go, small, top)


def packed(v):
    rows, lanes = v.shape
    if lanes != 192:
        return v
    rest = jnp.concatenate([v[: rows // 2, 128:], v[rows // 2 :, 128:]], axis=1)
    return jnp.concatenate([v[:, :128], rest], axis=0)


def unpacked(v, lanes):
    if lanes != 192:
        return v
    rows = v.shape[0] // 3 * 2
    rest = jnp.concatenate([v[rows:, :64], v[rows:, 64:]], axis=0)
    return jnp.concatenate([v[:rows], rest], axis=1)


def swap_kernel(ge_ref, other_ref, send, recv):
    z, c, t = spot()
    greet_core()
    copy = remote(ge_ref, other_ref, send, recv, ctx=1 - c)
    copy.start()
    copy.wait()


def greet_core():
    z, c, t = spot()
    barrier = pltpu.get_barrier_semaphore()
    pl.semaphore_signal(barrier, inc=1, device_id={"ctx": 1 - c}, device_id_type=MESH)
    pl.semaphore_wait(barrier, 1)


def swap(ge, number):
    return pl.pallas_call(
        swap_kernel,
        in_specs=anywhere(1),
        out_specs=anywhere(1)[0],
        out_shape=jax.ShapeDtypeStruct(ge.shape, ge.dtype),
        scratch_shapes=[pltpu.SemaphoreType.DMA, pltpu.SemaphoreType.DMA],
        compiler_params=params(collective_id=number, has_side_effects=True),
        cost_estimate=cost(5),
        name="swap",
    )(ge)


def laid(previous, routes):
    count, rows = previous.shape
    return jnp.concatenate([previous, jnp.zeros((16 - count, rows), f32)], axis=0), routes.astype(f32)


def thirds(v):
    a = v.astype(bf16)
    rest = v - a.astype(f32)
    b = rest.astype(bf16)
    return a, b, (rest - b.astype(f32)).astype(bf16)


def mixing(n2, wrc, previous, routes):
    z = sum(mm(wrc.astype(bf16), part, NT) for part in thirds(n2))
    expert = lax.broadcasted_iota(jnp.int32, z.shape, 0).astype(f32)
    logits = z + previous
    hot = [expert == routes[r : r + 1] for r in range(2)]
    picked = [jnp.sum(jnp.where(hot[r], logits, 0.0), axis=0, keepdims=True) for r in range(2)]
    most = jnp.maximum(picked[0], picked[1])
    e = [jnp.exp(p - most) for p in picked]
    gates = [v / (e[0] + e[1]) for v in e]
    combine = jnp.where(hot[0], gates[0], 0.0) + jnp.where(hot[1], gates[1], 0.0)
    alphas = []
    for j in range(2):
        first, second = z[EXPERTS + 2 * j : EXPERTS + 2 * j + 1], z[EXPERTS + 2 * j + 1 : EXPERTS + 2 * j + 2]
        most = jnp.maximum(first, second)
        a, b = jnp.exp(first - most), jnp.exp(second - most)
        alphas.append((a / (a + b), b / (a + b)))
    weights = [combine[FFN_EXPERTS + 1 + j : FFN_EXPERTS + 2 + j] for j in range(3)]
    return hot, gates, combine, alphas, weights


def scales(alphas, weights):
    scale = weights[0] + weights[1] * alphas[0][0] + weights[2] * alphas[1][0]
    at = lax.broadcasted_iota(jnp.int32, (8, scale.shape[1]), 0)
    value = jnp.where(at == 0, scale, jnp.where(at == 1, weights[1] * alphas[0][1], weights[2] * alphas[1][1])).T
    return value[:, 0:1], value[:, 1:2], value[:, 2:3]


def turn_kernel(length, res_ref, dn_ref, named_ref, cot_ref, att_ref, wo_ref, par_ref, prev_ref, routes_ref,
                dres_ref, heads_ref, gwo_ref, small_ref, got_ref, send_sem, recv_sem, local_sem):
    z, c, t = spot()
    nt = lax.axis_size("tp")
    own = c * nt + t
    rows, width = res_ref.shape
    greet(False)
    here = pl.ds(pl.multiple_of(t * rows, rows), rows)
    res = res_ref[...]
    gain = par_ref[19:20]
    inverse = lax.rsqrt(jnp.mean(res * res, axis=1, keepdims=True) + epsilon)
    m = res * inverse
    n2 = m * gain
    previous, routes = laid(prev_ref[:, here], routes_ref[c, :, here])
    hot, gates, _, alphas, weights = mixing(n2, par_ref[:16], previous, routes)
    position = own * rows + lax.broadcasted_iota(jnp.int32, cot_ref.shape, 0)
    g = jnp.where(position < length[0], cot_ref[...].astype(f32), 0.0)
    inner = jnp.broadcast_to(jnp.sum(g * n2, axis=1, keepdims=True), (rows, 8)).T[0:1]
    onto = mm(par_ref[16:18].astype(bf16), g.astype(bf16), NT)
    onto = [onto[j : j + 1] for j in range(2)]
    named = named_ref[...]
    expert = lax.broadcasted_iota(jnp.int32, hot[0].shape, 0)
    local = {
        FFN_EXPERTS + 1: inner,
        FFN_EXPERTS + 2: alphas[0][0] * inner + alphas[0][1] * onto[0],
        FFN_EXPERTS + 3: alphas[1][0] * inner + alphas[1][1] * onto[1],
    }
    dgates = []
    for r in range(2):
        there = jnp.sum(jnp.where(hot[r][:FFN_EXPERTS], named, 0.0), axis=0, keepdims=True)
        for e, value in local.items():
            there = there + jnp.where(hot[r][e : e + 1], value, 0.0)
        dgates.append(there)
    mean = gates[0] * dgates[0] + gates[1] * dgates[1]
    dz = jnp.where(hot[0], gates[0] * (dgates[0] - mean), 0.0)
    dz = dz + jnp.where(hot[1], gates[1] * (dgates[1] - mean), 0.0)
    for j in range(2):
        da = weights[1 + j] * inner
        db = weights[1 + j] * onto[j]
        centre = alphas[j][0] * da + alphas[j][1] * db
        dz = dz + jnp.where(expert == EXPERTS + 2 * j, alphas[j][0] * (da - centre), 0.0)
        dz = dz + jnp.where(expert == EXPERTS + 2 * j + 1, alphas[j][1] * (db - centre), 0.0)
    scale, first_vec, second_vec = scales(alphas, weights)
    highest = lax.Precision.HIGHEST
    dn2 = dn_ref[...] + scale * g + sum(mm(part, par_ref[:16].astype(bf16), TN) for part in thirds(dz))
    q = dn2 * gain
    dres = g + inverse * (q - m * jnp.mean(q * m, axis=1, keepdims=True))
    dres_ref[...] = dres
    da = dres.astype(bf16)
    wo = wo_ref[...].reshape(-1, width)
    got_ref[...] = mm(wo, da, NT).astype(bf16).reshape(got_ref.shape)

    core = lax.rem((own + 1) // 2, 2)
    slot = 2 * (own // 4) + lax.rem(own, 4) // 2
    copies = []
    for target in range(nt):
        inside = jnp.logical_and(core == c, target == t)
        copy = remote(got_ref.at[target], heads_ref.at[slot], send_sem.at[target], recv_sem.at[slot], ctx=core, tp=target)
        copies.append((inside, copy, pltpu.make_async_copy(got_ref.at[target], heads_ref.at[slot], local_sem)))
    for inside, copy, kept in copies:

        @pl.when(jnp.logical_not(inside))
        def _():
            copy.start()

        @pl.when(inside)
        def _():
            kept.start()

    small_ref[0:16] = mm(dz, n2, NN, highest)
    small_ref[16:24] = jnp.zeros((8, width), f32)
    small_ref[16:17] = jnp.sum(first_vec * g, axis=0, keepdims=True)
    small_ref[17:18] = jnp.sum(second_vec * g, axis=0, keepdims=True)
    small_ref[18:19] = jnp.sum(dn2 * m, axis=0, keepdims=True)
    att = att_ref[...].reshape(-1, rows)
    gwo_ref[...] = mm(att, da).astype(bf16).reshape(gwo_ref.shape)
    for inside, copy, kept in copies:

        @pl.when(jnp.logical_not(inside))
        def _():
            copy.wait_send()

        @pl.when(inside)
        def _():
            kept.wait()

    for i in range(heads_ref.shape[0]):

        @pl.when(zig(c, i) != own)
        def _():
            remote(got_ref.at[0], heads_ref.at[i], send_sem.at[0], recv_sem.at[i], ctx=c, tp=t).wait_recv()


def turn(length, res, dn, named, cot, att, wo, small, prev, routes, count, number):
    rows, width = res.shape
    nt = lax.axis_size("tp")
    args = (res, dn, named, cot, att, wo, small, prev, routes)
    return pl.pallas_call(
        turn_kernel,
        grid_spec=pltpu.PrefetchScalarGridSpec(
            num_scalar_prefetch=1,
            grid=(1,),
            in_specs=[full(v.shape) for v in args],
            out_specs=[full((rows, width))] + anywhere(1) + [full(wo.shape), full((24, width))],
            scratch_shapes=[
                pltpu.VMEM(att.shape, bf16),
                pltpu.SemaphoreType.DMA((nt,)),
                pltpu.SemaphoreType.DMA((count,)),
                pltpu.SemaphoreType.DMA,
            ],
        ),
        out_shape=[
            jax.ShapeDtypeStruct((rows, width), f32),
            jax.ShapeDtypeStruct((count,) + att.shape[1:], bf16),
            jax.ShapeDtypeStruct(wo.shape, bf16),
            jax.ShapeDtypeStruct((24, width), f32),
        ],
        compiler_params=params(collective_id=number, has_side_effects=True),
        cost_estimate=cost(18),
        name="turn",
    )(length, *args)


def both_cores(own_ref, other_ref, targets):
    core = lax.axis_index("ctx")
    for k, target in enumerate(targets):
        for j in range(own_ref.shape[0]):
            mine, theirs = own_ref[j, k].astype(f32), other_ref[j, k].astype(f32)
            target[0, j] = jnp.where(core == 0, mine, theirs)
            target[1, j] = jnp.where(core == 0, theirs, mine)


def steps_of(depth):
    return 4 if depth % 64 == 0 else 1


def finish_kernel(x_ref, dn_ref, dres_ref, small_ref, gw_ref, gs_ref, top_ref, wq_ref, wk_ref, limit_ref, length_ref, base_ref, feed_ref, own_ref, other_ref, out_ref, *outs):
    gin_ref, targets = outs[0], outs[1:4]
    x = x_ref[...].astype(f32)
    inverse = lax.rsqrt(jnp.mean(x * x, axis=1, keepdims=True) + epsilon)
    m = x * inverse
    q = dn_ref[...] * small_ref[18:19]
    gin_ref[...] = dres_ref[...] + inverse * (q - m * jnp.mean(q * m, axis=1, keepdims=True))
    both_cores(own_ref, other_ref, targets)
    rows = x.shape[0]
    first = (lax.axis_index("ctx") * lax.axis_size("tp") + lax.axis_index("tp")) * pl.num_programs(0) + pl.program_id(0)
    position = first * rows + lax.broadcasted_iota(jnp.int32, x.shape, 0)
    out_ref[...] = jnp.where(position < length_ref[0], base_ref[...] + feed_ref[...], 0.0).astype(bf16)

    @pl.when(pl.program_id(0) == 0)
    def _():
        gq, gk, gv, go, gnorm, gmoe, grouter, gconst, gvec, fac_ref, cq_ref, ck_ref = outs[4:]
        width = wq_ref.shape[1]
        flat = gw_ref[...].reshape(4 * width, gw_ref.shape[2])
        for k, target in enumerate((gq, gk, gv)):
            target[...] = flat[k * width : (k + 1) * width].T
        go[...] = flat[3 * width :]
        sums = gs_ref[...]
        grouter[...] = sums[:EXPERTS]
        gconst[...] = sums[EXPERTS : EXPERTS + 4]
        gvec[...] = sums[16:18]
        gmoe[...] = sums[18:19]
        gnorm[...] = sums[19:20]
        factors = limit_ref[0] / jnp.maximum(top_ref[...], limit_ref[0])
        for h in range(fac_ref.shape[0]):
            fac_ref[h] = factors[h, 0]
        lane = lax.broadcasted_iota(jnp.int32, (1, width), 1)
        root = jnp.zeros((1, width), f32)
        for h in range(width // HEAD_DIM):
            root = jnp.where(lane // HEAD_DIM == h, jnp.sqrt(factors[h : h + 1, :1]), root)
        cq_ref[...] = (wq_ref[...].astype(f32) * root).astype(bf16)
        ck_ref[...] = (wk_ref[...].astype(f32) * root).astype(bf16)


def finish_rows(x, dn, dres, small, gw, gs, top, wq, wk, limit, length, base, feed, own, other):
    rows, width = x.shape
    each, kinds, depth, hidden = own.shape
    steps = steps_of(depth)
    tile, deep = rows // steps, depth // steps
    by_row = pl.BlockSpec((tile, width), lambda i: (i, 0))
    expert_out = pl.BlockSpec((2, each, deep, hidden), lambda i: (0, 0, i, 0))
    once = [
        jax.ShapeDtypeStruct(shape, f32)
        for shape in [wq.shape] * 3
        + [(wq.shape[1], depth), (1, depth), (1, depth), (EXPERTS, depth), (4, depth), (2, depth), (wq.shape[1] // HEAD_DIM,)]
    ] + [jax.ShapeDtypeStruct(wq.shape, bf16)] * 2
    return pl.pallas_call(
        finish_kernel,
        grid=(steps,),
        in_specs=[
            by_row,
            by_row,
            by_row,
            full(small.shape),
            full(gw.shape),
            full(gs.shape),
            full(top.shape),
            full(wq.shape),
            full(wk.shape),
            pl.BlockSpec(memory_space=pltpu.SMEM),
            pl.BlockSpec(memory_space=pltpu.SMEM),
            by_row,
            by_row,
        ]
        + [pl.BlockSpec((each, kinds, deep, hidden), lambda i: (0, 0, i, 0))] * 2,
        out_specs=[by_row, by_row, expert_out, expert_out, expert_out] + [full(v.shape) if v.ndim > 1 else pl.BlockSpec(memory_space=pltpu.SMEM) for v in once],
        out_shape=[
            jax.ShapeDtypeStruct((rows, width), bf16),
            jax.ShapeDtypeStruct((rows, width), f32),
        ]
        + [jax.ShapeDtypeStruct((2, each, depth, hidden), f32)] * 3
        + once,
        compiler_params=params(),
        cost_estimate=cost(8),
        name="finish_rows",
    )(x, dn, dres, small, gw, gs, top, wq, wk, limit, length, base, feed, own, other)


def pick_kernel(first, g_ref, u_ref, d_ref, out_ref):
    for k, source in enumerate((g_ref, u_ref, d_ref)):
        out_ref[0, k] = source[0]


def pick(first, start, some, gate, up, down):
    _, depth, hidden = gate.shape
    source = pl.BlockSpec((1, depth, hidden), lambda i, f: (f[0] + start + i, 0, 0))
    return pl.pallas_call(
        pick_kernel,
        grid_spec=pltpu.PrefetchScalarGridSpec(
            num_scalar_prefetch=1,
            grid=(some,),
            in_specs=[source] * 3,
            out_specs=pl.BlockSpec((1, 3, depth, hidden), lambda i, f: (i, 0, 0, 0)),
        ),
        out_shape=jax.ShapeDtypeStruct((some, 3, depth, hidden), gate.dtype),
        compiler_params=params(),
        cost_estimate=cost(2),
        name="pick",
    )(first, gate, up, down)


def expert_kernel(start, first, x_ref, g_ref, gate_ref, w_ref, *refs):
    feed_ref, back_ref, gw_ref = refs[-3:]
    parts, _, _, depth, hidden = w_ref.shape
    width = parts * depth
    wg, wu, wd = [w_ref[:, 0, k].reshape(width, hidden) for k in range(3)]
    x, g, gate = x_ref[0], g_ref[0], gate_ref[0]
    gate_pre = mm(x, wg)
    up = mm(x, wu)
    sigmoid = 1.0 / (1.0 + jnp.exp(-gate_pre))
    activated = gate_pre * sigmoid
    inner = (activated * up).astype(bf16)
    g32 = g.astype(f32)
    dout = (gate * g32).astype(bf16)
    dinner = mm(dout, wd)
    out = mm(inner, wd, NT)
    feed_ref[0] = (gate * out).astype(bf16)
    dgate = jnp.sum(g32 * out, axis=1, keepdims=True)
    dpre = (dinner * up * sigmoid * (1.0 + gate_pre * (1.0 - sigmoid))).astype(bf16)
    dup = (dinner * activated).astype(bf16)
    back_ref[0, :, :width] = (mm(dpre, wg, NT) + mm(dup, wu, NT)).astype(bf16)
    lane = lax.broadcasted_iota(jnp.int32, (dgate.shape[0], back_ref.shape[2] - width), 1)
    coarse = dgate.astype(bf16).astype(f32)
    at = first[0] + start + pl.program_id(0)
    extra = jnp.where(lane == at, coarse, jnp.where(lane == at + 16, dgate - coarse, 0.0))
    back_ref[0, :, width:] = extra.astype(bf16)
    for k, (left, right) in enumerate(((x, dpre), (x, dup), (dout, inner))):
        gw_ref[:, 0, k] = mm(left, right, TN).reshape(parts, depth, hidden).astype(bf16)


def expert(start, first, x, g, gate, w, into=()):
    local, slots, width = x.shape
    parts, some, kinds, depth, hidden = w.shape
    pick = lambda i, f: (start + i, 0, 0)
    return pl.pallas_call(
        functools.partial(expert_kernel, start),
        grid_spec=pltpu.PrefetchScalarGridSpec(
            num_scalar_prefetch=1,
            grid=(some,),
            in_specs=[
                pl.BlockSpec((1, slots, width), pick),
                pl.BlockSpec((1, slots, width), pick),
                pl.BlockSpec((1, slots, 1), pick),
                pl.BlockSpec((parts, 1, kinds, depth, hidden), lambda i, f: (0, i, 0, 0, 0)),
            ]
            + anywhere(len(into)),
            out_specs=[
                pl.BlockSpec((1, slots, width), pick),
                pl.BlockSpec((1, slots, width + EXTRA), pick),
                pl.BlockSpec((parts, 1, kinds, depth, hidden), lambda i, f: (0, start + i, 0, 0, 0)),
            ],
        ),
        out_shape=[
            jax.ShapeDtypeStruct((local, slots, width), bf16),
            jax.ShapeDtypeStruct((local, slots, width + EXTRA), bf16),
            jax.ShapeDtypeStruct((parts, local, kinds, depth, hidden), bf16),
        ],
        input_output_aliases={5 + n: n for n in range(len(into))},
        compiler_params=params(),
        cost_estimate=cost(10 * some),
        name="expert",
    )(first, x, g, gate, w, *into)


def shards(
    hidden_in,
    cotangent,
    lengths,
    routes,
    prev_logits,
    norm_attn,
    w_query,
    w_key,
    w_value,
    w_out,
    norm_moe,
    w_router,
    w_const,
    const_vec,
    w_gate,
    w_up,
    w_down,
    threshold,
):
    plane = ("ctx", "tp")
    core = lax.axis_index("ctx")
    nc, nt, ns = lax.axis_size("ctx"), lax.axis_size("tp"), lax.axis_size("shard")
    own, width = hidden_in.shape
    per = own * nt
    total = per * nc
    depth = w_gate.shape[1]
    heads = w_query.shape[1] // HEAD_DIM
    head_width = heads * HEAD_DIM
    local = FFN_EXPERTS // nc
    count = total // BLOCK // nc
    routes, prev = routes.T, prev_logits.T
    first = (core * local).astype(jnp.int32)[None]

    calls = ((0, local - 1), (local - 1, 1))
    expert_w = []
    for start, some in calls:
        pieces = pick(first, start, some, w_gate, w_up, w_down)
        expert_w.append(lax.all_gather(pieces, "shard", axis=0, tiled=False))
    rows_all, attention_w, small, routes_all = opening(
        hidden_in,
        (w_query, w_key, w_value, w_out),
        (w_router.T, w_const.T, const_vec, norm_attn[None], norm_moe[None]),
        routes,
        0,
    )
    rows_all = rows_all.reshape(total, width)
    cosine, sine = rope_tables(total)

    qt, kt, k, v, vt, wt, small, out_w = project(rows_all, attention_w, small, cosine, sine, heads, 8)
    ot, lse, top, cot_all = attend(lengths, qt, k, vt, cotangent, count, 1)
    att, res, base, x_slots, g_slots, gate_slots, row_at = route(
        ot, hidden_in, out_w, small, prev, routes_all, cot_all, local, 2
    )

    results = ()
    for (start, _), w in zip(calls, expert_w):
        results = expert(start, first, x_slots, g_slots, gate_slots, w, results)
    feed, back, grads = results
    grads = lax.psum_scatter(grads, "shard", scatter_dimension=0, tiled=True)[0]
    back, feed, named = combine(row_at, back, feed, 3)

    dres, got, grad_out, gsmall = turn(
        lengths, res, back, named, cotangent, att, out_w, small, prev, routes_all, count, 4
    )
    dq, dk, dv, grad_out, feed = revisit(qt, k, kt, v, ot, got, lse, grad_out, feed, 5)
    part, grad_w, gsmall, top = closing(dq, dk, dv, rows_all, cosine, sine, wt, small, grad_out, gsmall, top, 6)
    grads, top = lax.optimization_barrier((grads, top))
    (output, grad_input, grad_gate, grad_up, grad_down, grad_q, grad_k, grad_v, grad_out, grad_norm_attn, grad_norm_moe,
     grad_router, grad_const, grad_vec, factors, clipped_query, clipped_key) = finish_rows(
        hidden_in, part, dres, small, grad_w, gsmall, top, w_query, w_key, threshold, lengths, base, feed, grads, swap(grads, 7)
    )
    grad_gate, grad_up, grad_down = [v.reshape((-1,) + v.shape[2:]) for v in (grad_gate, grad_up, grad_down)]
    return (
        output,
        grad_input,
        grad_norm_attn[0],
        grad_q,
        grad_k,
        grad_v,
        grad_out,
        grad_norm_moe[0],
        grad_router.T,
        grad_const.T,
        grad_vec,
        grad_gate,
        grad_up,
        grad_down,
        factors,
        clipped_query,
        clipped_key,
    )


def solution(mesh):
    return jax.shard_map(
        shards,
        mesh=mesh,
        in_specs=(
            P(("shard", "ctx", "tp"), None),
            P(("shard", "ctx", "tp"), None),
            P("shard"),
            P(("shard", "ctx"), None),
            P(("shard", "ctx"), None),
            P("shard"),
            P("shard", "tp"),
            P("shard", "tp"),
            P("shard", "tp"),
            P("tp", "shard"),
            P("shard"),
            P("shard", None),
            P("shard", None),
            P(None, "shard"),
            P(None, "shard", "tp"),
            P(None, "shard", "tp"),
            P(None, "shard", "tp"),
            P(),
        ),
        out_specs=(
            P(("shard", "ctx", "tp"), None),
            P(("shard", "ctx", "tp"), None),
            P("shard"),
            P("shard", "tp"),
            P("shard", "tp"),
            P("shard", "tp"),
            P("tp", "shard"),
            P("shard"),
            P("shard", None),
            P("shard", None),
            P(None, "shard"),
            P(None, "shard", "tp"),
            P(None, "shard", "tp"),
            P(None, "shard", "tp"),
            P("tp"),
            P("shard", "tp"),
            P("shard", "tp"),
        ),
        check_vma=False,
    )
```

```python
import functools

import jax
import jax.numpy as jnp
import numpy as np
from jax import lax
from jax.experimental import pallas as pl
from jax.experimental.pallas import tpu as pltpu
from jax.sharding import PartitionSpec as P

HEAD_DIM = 64
EXPERTS = 12
FFN_EXPERTS = 8
CAP = 512
BLOCK = 512
EXTRA = 128
SMALL = 32
MESH = pl.DeviceIdType.MESH

epsilon = 1e-06
rope_base = 10000.0
bf16 = jnp.bfloat16
f32 = jnp.float32

NN = (((1,), (0,)), ((), ()))
NT = (((1,), (1,)), ((), ()))
TN = (((0,), (0,)), ((), ()))


def mm(left, right, dims=NN, precision=None):
    return lax.dot_general(
        left, right, dims, preferred_element_type=f32, precision=precision
    )


def params(mib=56, **more):
    return pltpu.CompilerParams(vmem_limit_bytes=mib * 1024 * 1024, **more)


def cost(us):
    return pl.CostEstimate(flops=int(us * 1e9), bytes_accessed=int(us * 3e6), transcendentals=0)


def full(shape):
    return pl.BlockSpec(shape, lambda *_: (0,) * len(shape))


def rope_tables(total):
    half = HEAD_DIM // 2
    freqs = np.float32(rope_base) ** (np.float32(-2.0) * np.arange(half, dtype=np.float32) / np.float32(HEAD_DIM))
    angles = freqs.astype(np.float32)[:, None] * np.arange(total, dtype=np.float32)[None, :]
    angles = angles.astype(np.float64)
    return jnp.asarray(np.cos(angles), f32), jnp.asarray(np.sin(angles), f32)


def zig(core, i):
    return 4 * (i // 2) + (core if i % 2 == 0 else 3 - core)


def anywhere(count):
    return [pl.BlockSpec(memory_space=pl.ANY)] * count


def spot():
    return lax.axis_index("shard"), lax.axis_index("ctx"), lax.axis_index("tp")


def across(t):
    return t + 1 - 2 * lax.rem(t, 2), lax.rem(t + 2, 4), 3 - t


def remote(source, target, sends, recvs, **where):
    return pltpu.make_async_remote_copy(
        src_ref=source,
        dst_ref=target,
        send_sem=sends,
        recv_sem=recvs,
        device_id=where,
        device_id_type=MESH,
    )


def greet(depth=True):
    z, c, t = spot()
    nc, nt, ns = lax.axis_size("ctx"), lax.axis_size("tp"), lax.axis_size("shard")
    barrier = pltpu.get_barrier_semaphore()
    for step in range(1, nc * nt):
        other = lax.rem(c * nt + t + step, nc * nt)
        pl.semaphore_signal(
            barrier,
            inc=1,
            device_id={"ctx": other // nt, "tp": lax.rem(other, nt)},
            device_id_type=MESH,
        )
    if depth:
        for step in range(1, ns):
            pl.semaphore_signal(
                barrier,
                inc=1,
                device_id={"shard": lax.rem(z + step, ns)},
                device_id_type=MESH,
            )
    pl.semaphore_wait(barrier, nc * nt - 1 + (ns - 1 if depth else 0))


class Gather:
    KINDS = 9

    def __init__(self, x, out, sends, recvs, own, cuts, stage=None, relative=False):
        z, c, t = spot()
        tx, ty, td = across(t)
        rows = x.shape[0] // cuts
        half = rows // 2
        self.cuts = cuts
        sib = {"ctx": 1 - c}
        px, py = {"tp": tx}, {"tp": ty}
        near = (t, tx, ty, td)
        if relative:
            here, there = list(range(8)), list(range(8))
            mine = (1, 2, 4)
            passed = ((1, 5), (1, 3), (2, 6), (2, 3), (3, 7), (3, 7))
        else:
            here = [4 * c + n for n in near] + [4 * (1 - c) + n for n in near]
            there = here[:4]
            mine = (here[0],) * 3
            passed = tuple((here[n], here[n]) for n in (1, 1, 2, 2, 3, 3))
        self.load = None if stage is None else pltpu.make_async_copy(x, stage, own.at[0])
        self.own = pltpu.make_async_copy(x if stage is None else stage, out.at[here[0]], own.at[1])

        def parts(s):
            whole = pl.ds(s * rows, rows)
            one, two = pl.ds(s * rows, half), pl.ds(s * rows + half, half)
            return whole, one, two

        def copies(s):
            whole, one, two = parts(s)
            made = [
                remote(x.at[whole], out.at[slot, whole], sends.at[s, k], recvs.at[s, k], **where)
                for k, (slot, where) in enumerate(zip(mine, (px, py, sib)))
            ]
            ways = ((whole, sib), (one, py), (whole, sib), (two, px), (one, sib), (two, sib))
            for k, ((source, target), (part, where)) in enumerate(zip(passed, ways)):
                made.append(
                    remote(out.at[source, part], out.at[target, part], sends.at[s, k + 3], recvs.at[s, k + 3], **where)
                )
            return made

        self.copies = [copies(s) for s in range(cuts)]

        def arrivals(s):
            whole, one, two = parts(s)
            where = [(1, whole), (2, whole), (4, whole), (5, whole), (3, one), (6, whole), (3, two), (7, one), (7, two)]
            return [
                remote(out.at[here[n], part], out.at[here[n], part], sends.at[s, k], recvs.at[s, k], **sib)
                for k, (n, part) in enumerate(where)
            ]

        self.arrivals = [arrivals(s) for s in range(cuts)]

    @staticmethod
    def scratch(cuts):
        return [
            pltpu.SemaphoreType.DMA((cuts, Gather.KINDS)),
            pltpu.SemaphoreType.DMA((cuts, Gather.KINDS)),
            pltpu.SemaphoreType.DMA((2,)),
        ]

    def first(self):
        for s in range(self.cuts):
            for k in (0, 1, 2):
                self.copies[s][k].start()
        (self.load or self.own).start()

    def second(self, s):
        if self.load is not None and s == 0:
            self.load.wait()
            self.own.start()
        self.arrivals[s][0].wait_recv()
        self.copies[s][4].start()
        self.copies[s][3].start()
        self.arrivals[s][1].wait_recv()
        self.copies[s][6].start()
        self.copies[s][5].start()

    def third(self, s):
        for k in (4, 6):
            self.arrivals[s][k].wait_recv()
            self.copies[s][7 if k == 4 else 8].start()

    def beside(self):
        for s in range(self.cuts):
            for k in (2, 3, 5):
                self.arrivals[s][k].wait_recv()

    def last(self, rest=False):
        for s in range(self.cuts):
            for k in (7, 8) if rest else (2, 3, 5, 7, 8):
                self.arrivals[s][k].wait_recv()
        for s in range(self.cuts):
            for k in range(self.KINDS):
                self.copies[s][k].wait_send()
        if not rest:
            self.own.wait()


class Sum:
    def __init__(self, p, held, came, across_in, across_out, sends, recvs, loads, stage=None):
        z, c, t = spot()
        self.t = t
        tx, ty, td = across(t)
        half = held.shape[1] // 2
        self.half = half
        self.one, self.two = pl.ds(0, half), pl.ds(half, half)
        self.order = (td, tx, ty, t)
        self.held, self.came, self.inn = held, came, across_in
        sib, px, py = {"ctx": 1 - c}, {"tp": tx}, {"tp": ty}
        self.core = []
        for k, o in enumerate(self.order):
            source = p.at[4 * (1 - c) + o] if stage is None else stage.at[k]
            self.core.append(remote(source, came.at[o], sends.at[k], recvs.at[k], **sib))
        self.loads = None
        if stage is None:
            self.loads = [pltpu.make_async_copy(p.at[4 * c + o], held.at[o], loads.at[k]) for k, o in enumerate(self.order)]

        def send(k, source, slot, where):
            return remote(source, across_in.at[slot], sends.at[k], recvs.at[k], **where)

        self.side = {
            "dx": send(4, held.at[td, self.one], 0, px),
            "dy": send(5, held.at[td, self.two], 1, py),
            "x": send(6, held.at[tx, self.one], 2, px),
            "y": send(7, held.at[ty, self.two], 3, py),
            "cy": send(8, across_out.at[0], 4, py),
            "cx": send(9, across_out.at[1], 5, px),
        }
        self.out = across_out
        self.near = (tx, ty, td)

    @staticmethod
    def scratch(rows, width):
        return [
            pltpu.VMEM((4, rows, width), bf16),
            pltpu.VMEM((4, rows, width), bf16),
            pltpu.VMEM((6, rows // 2, width), bf16),
            pltpu.VMEM((2, rows // 2, width), bf16),
            pltpu.SemaphoreType.DMA((10,)),
            pltpu.SemaphoreType.DMA((10,)),
            pltpu.SemaphoreType.DMA((4,)),
        ]

    def first(self):
        for k in range(4):
            self.core[k].start()
            self.loads[k].start()

    def add(self, k, mine):
        o = self.order[k]
        self.core[k].wait_recv()
        self.held[o] = (mine + self.came[o].astype(mine.dtype)).astype(bf16)
        for name in (("dx", "dy"), ("x",), ("y",), ())[k]:
            self.side[name].start()

    def second(self):
        for k, o in enumerate(self.order):
            self.loads[k].wait()
            self.add(k, self.held[o])

    def third(self):
        tx, ty, td = self.near
        self.side["dx"].wait_recv()
        self.out[0] = self.held[ty, self.one] + self.inn[0]
        self.side["cy"].start()
        self.side["dy"].wait_recv()
        self.out[1] = self.held[tx, self.two] + self.inn[1]
        self.side["cx"].start()

    def last(self):
        for k in ("x", "y", "cy", "cx"):
            self.side[k].wait_recv()
        for copy in self.core + list(self.side.values()):
            copy.wait_send()

    def total(self):
        def add(part, a, b):
            return self.held[self.t, part].astype(f32) + self.inn[a].astype(f32) + self.inn[b].astype(f32)

        return add(self.one, 2, 4), add(self.two, 3, 5)


def qkv_kernel(x_ref, w_ref, s_ref, cos_ref, sin_ref, qt_ref, kt_ref, k_ref, v_ref, vt_ref, wt_ref, small_ref, wo_ref, wo, send, recv, local):
    heads = qt_ref.shape[0]
    width = heads * HEAD_DIM
    half = HEAD_DIM // 2
    z, c, t = spot()
    nt = lax.axis_size("tp")
    mid = width // 2
    mine, theirs = pl.ds(c * mid, mid), pl.ds((1 - c) * mid, mid)
    away, came, onward, there = [], [], [], []
    for step in range(1, nt):
        back = lax.rem(t + nt - step, nt)
        away.append(remote(wo.at[mine], wo_ref.at[t, mine], send.at[step], recv.at[step], tp=lax.rem(t + step, nt)))
        ref = wo_ref.at[back, mine]
        came.append(remote(ref, ref, send.at[nt + step], recv.at[step], ctx=1 - c))
        onward.append(remote(ref, ref, send.at[nt + step], recv.at[nt + step], ctx=1 - c))
        ref = wo_ref.at[back, theirs]
        there.append(remote(ref, ref, send.at[nt + step], recv.at[nt + step], ctx=1 - c))
    own = pltpu.make_async_copy(wo, wo_ref.at[t], local)
    i = pl.program_id(0)

    @pl.when(i == 0)
    def _():
        def flat(v):
            return v.astype(f32).reshape(v.shape[0] * v.shape[1], v.shape[2])

        def whole(core, which):
            rest = flat(w_ref[core, :, 2])[:, which * (width - 128) : (which + 1) * (width - 128)]
            return jnp.concatenate([flat(w_ref[core, :, which]), rest], axis=1).T.astype(bf16)

        wo[...] = whole(1, 1)
        greet(False)
        for copy in away:
            copy.start()
        own.start()
        wt_ref[:width] = whole(0, 0)
        wt_ref[width : 2 * width] = whole(0, 1)
        wt_ref[2 * width :] = whole(1, 0)
        small_ref[...] = jnp.concatenate([s_ref[n].astype(f32) for n in range(s_ref.shape[0])], axis=1)

    x = x_ref[...].astype(f32)
    inverse = lax.rsqrt(jnp.mean(x * x, axis=1, keepdims=True) + epsilon)
    a = (x * inverse * small_ref[18:19]).astype(bf16)
    y = mm(wt_ref[...], a, NT)
    cosine, sine = cos_ref[...], sin_ref[...]

    def turned(first):
        u, w = y[first : first + half], y[first + half : first + HEAD_DIM]
        return jnp.concatenate([u * cosine - w * sine, w * cosine + u * sine], axis=0)

    for h in range(heads):
        at = h * HEAD_DIM
        qt_ref[h] = (turned(at) * HEAD_DIM**-0.5).astype(bf16)
        key = turned(width + at)
        kt_ref[h] = key.astype(bf16)
        k_ref[h] = key.T.astype(bf16)
        value = y[2 * width + at : 2 * width + at + HEAD_DIM]
        v_ref[h] = value.T.astype(bf16)
        vt_ref[h, :HEAD_DIM] = value.astype(bf16)
        vt_ref[h, HEAD_DIM:] = jnp.ones((16, value.shape[1]), bf16)

    @pl.when(i == pl.num_programs(0) - 2)
    def _():
        for copy, forth in zip(came, onward):
            copy.wait_recv()
            forth.start()

    @pl.when(i == pl.num_programs(0) - 1)
    def _():
        for copy in there:
            copy.wait_recv()
        for copy in away + onward:
            copy.wait_send()
        own.wait()


def project(rows, w, small, cosine, sine, heads, number):
    total, width = rows.shape
    tile = BLOCK
    out = heads * HEAD_DIM
    nt = lax.axis_size("tp")
    shapes = [
        jax.ShapeDtypeStruct((heads, HEAD_DIM, total), bf16),
        jax.ShapeDtypeStruct((heads, HEAD_DIM, total), bf16),
        jax.ShapeDtypeStruct((heads, total, HEAD_DIM), bf16),
        jax.ShapeDtypeStruct((heads, total, HEAD_DIM), bf16),
        jax.ShapeDtypeStruct((heads, HEAD_DIM + 16, total), bf16),
        jax.ShapeDtypeStruct((3 * out, width), bf16),
        jax.ShapeDtypeStruct((SMALL, width), f32),
        jax.ShapeDtypeStruct((nt, out, width), bf16),
    ]
    return pl.pallas_call(
        qkv_kernel,
        grid=(total // tile,),
        in_specs=[
            pl.BlockSpec((tile, width), lambda i: (i, 0)),
            full(w.shape),
            full(small.shape),
            pl.BlockSpec((HEAD_DIM // 2, tile), lambda i: (0, i)),
            pl.BlockSpec((HEAD_DIM // 2, tile), lambda i: (0, i)),
        ],
        out_specs=[
            pl.BlockSpec((heads, HEAD_DIM, tile), lambda i: (0, 0, i)),
            pl.BlockSpec((heads, HEAD_DIM, tile), lambda i: (0, 0, i)),
            pl.BlockSpec((heads, tile, HEAD_DIM), lambda i: (0, i, 0)),
            pl.BlockSpec((heads, tile, HEAD_DIM), lambda i: (0, i, 0)),
            pl.BlockSpec((heads, HEAD_DIM + 16, tile), lambda i: (0, 0, i)),
        ]
        + [full(v.shape) for v in shapes[5:7]]
        + anywhere(1),
        scratch_shapes=[
            pltpu.VMEM((out, width), bf16),
            pltpu.SemaphoreType.DMA((2 * nt,)),
            pltpu.SemaphoreType.DMA((2 * nt,)),
            pltpu.SemaphoreType.DMA,
        ],
        out_shape=shapes,
        compiler_params=params(collective_id=number, has_side_effects=True),
        cost_estimate=cost(14),
        name="project",
    )(rows, w, small, cosine, sine)


def dealt(core, i):
    return 4 * (i // 2) + jnp.where(lax.rem(i, 2) == 0, core, 3 - core)


def attend_kernel(cuts, length, qt_ref, k_ref, vt_ref, cot_ref, ot_ref, lse_ref, top_ref, cots_ref, mask_cot, *sems):
    z, c, t = spot()
    nt = lax.axis_size("tp")
    h, i = pl.program_id(0), pl.program_id(1)
    count = pl.num_programs(1)
    at_step = h * count + i
    last = pl.num_programs(0) * count - 1
    gather = Gather(mask_cot, cots_ref, *sems, cuts)

    @pl.when(at_step == 0)
    def _():
        rows = cot_ref.shape[0]
        position = (c * nt + t) * rows + lax.broadcasted_iota(jnp.int32, cot_ref.shape, 0)
        mask_cot[...] = jnp.where(position < length[0], cot_ref[...].astype(f32), 0.0).astype(bf16)
        greet(False)
        gather.first()

    index = dealt(c, i)
    columns = BLOCK
    qt = qt_ref[0, :, pl.ds(pl.multiple_of(index * BLOCK, BLOCK), BLOCK)]

    def step(at, carry, diagonal):
        peak, total = carry
        start = pl.multiple_of(at * BLOCK, BLOCK)
        scores = mm(k_ref[0, pl.ds(start, BLOCK), :], qt)
        if diagonal:
            keys = lax.broadcasted_iota(jnp.int32, scores.shape, 0)
            queries = lax.broadcasted_iota(jnp.int32, scores.shape, 1)
            scores = jnp.where(keys <= queries, scores, -1e30)
        higher = jnp.maximum(peak, jnp.max(scores, axis=0, keepdims=True))
        weights = jnp.exp(scores - higher).astype(bf16)
        total = total * jnp.exp(peak - higher) + mm(vt_ref[0, :, pl.ds(start, BLOCK)], weights)
        return higher, total

    start = (jnp.full((1, columns), -1e30, f32), jnp.zeros((HEAD_DIM + 16, columns), f32))
    carry = lax.fori_loop(0, index, lambda at, c: step(at, c, False), start)
    peak, total = step(index, carry, True)
    mass = total[HEAD_DIM : HEAD_DIM + 1]
    ot_ref[0] = (total[:HEAD_DIM] / mass).astype(bf16)
    lse_ref[0, 0] = peak + jnp.log(mass)
    position = index * BLOCK + lax.broadcasted_iota(jnp.int32, peak.shape, 1)
    top_ref[0, 0] = jnp.where(position < length[0], peak, -1e30)

    @pl.when(at_step == last - 3)
    def _():
        for s in range(cuts):
            gather.second(s)

    @pl.when(at_step == last)
    def _():
        for s in range(cuts):
            gather.third(s)
        gather.last()


def attend(length, qt, k, vt, cot, count, number):
    cuts = 1
    heads, _, total = qt.shape
    return pl.pallas_call(
        functools.partial(attend_kernel, cuts),
        grid_spec=pltpu.PrefetchScalarGridSpec(
            num_scalar_prefetch=1,
            grid=(heads, count),
            in_specs=[
                pl.BlockSpec((1, HEAD_DIM, total), lambda h, i, n: (h, 0, 0)),
                pl.BlockSpec((1, total, HEAD_DIM), lambda h, i, n: (h, 0, 0)),
                pl.BlockSpec((1, HEAD_DIM + 16, total), lambda h, i, n: (h, 0, 0)),
                full(cot.shape),
            ],
            out_specs=[
                pl.BlockSpec((1, HEAD_DIM, BLOCK), lambda h, i, n: (i, h, 0)),
                pl.BlockSpec((1, 1, 1, BLOCK), lambda h, i, n: (h, i, 0, 0)),
                pl.BlockSpec((1, 1, 1, BLOCK), lambda h, i, n: (h, i, 0, 0)),
            ]
            + anywhere(1),
            scratch_shapes=[
                pltpu.VMEM(cot.shape, bf16),
            ]
            + Gather.scratch(cuts),
        ),
        out_shape=[
            jax.ShapeDtypeStruct((count, heads * HEAD_DIM, BLOCK), bf16),
            jax.ShapeDtypeStruct((heads, count, 1, BLOCK), f32),
            jax.ShapeDtypeStruct((heads, count, 1, BLOCK), f32),
            jax.ShapeDtypeStruct((8,) + cot.shape, bf16),
        ],
        compiler_params=params(collective_id=number, has_side_effects=True),
        cost_estimate=cost(35),
        name="attend",
    )(length, qt, k, vt, cot)


def revisit_kernel(qt_ref, k_ref, kt_ref, v_ref, ot_ref, got_ref, lse_ref, go_ref, feed_ref, dq_ref, dk_ref, dv_ref, gos_ref, fed_ref, sum_k, sum_v, came_ref, w_send, w_recv, *scratch):
    z, c, t = spot()
    job = Sum(feed_ref, *scratch)
    nt = lax.axis_size("tp")
    h, i = pl.program_id(0), pl.program_id(1)
    count = pl.num_programs(1)
    index = dealt(c, i)
    here = pl.ds(pl.multiple_of(index * BLOCK, BLOCK), BLOCK)
    away = [
        remote(go_ref.at[lax.rem(t + step, nt)], came_ref.at[step], w_send.at[step], w_recv.at[step], tp=lax.rem(t + step, nt))
        for step in range(1, nt)
    ]

    at_step = h * count + i
    end = pl.num_programs(0) * count - 1

    @pl.when(at_step == 0)
    def _():
        greet(False)
        job.first()
        for copy in away:
            copy.start()

    @pl.when(at_step == 3)
    def _():
        job.second()

    @pl.when(at_step == end - 3)
    def _():
        job.third()

    qt, got = qt_ref[0, :, here], got_ref[0]
    lse = lse_ref[0, 0]
    centre = jnp.sum(ot_ref[0].astype(f32) * got.astype(f32), axis=0, keepdims=True)

    @pl.when(i == 0)
    def _():
        sum_k[...] = jnp.zeros_like(sum_k)
        sum_v[...] = jnp.zeros_like(sum_v)
        dq_ref[...] = jnp.zeros_like(dq_ref)

    def step(at, grad, diagonal):
        start = pl.multiple_of(at * BLOCK, BLOCK)
        here = pl.ds(start, BLOCK)
        scores = mm(k_ref[0, here, :], qt)
        probs = jnp.exp(scores - lse)
        if diagonal:
            keys = lax.broadcasted_iota(jnp.int32, scores.shape, 0)
            queries = lax.broadcasted_iota(jnp.int32, scores.shape, 1)
            probs = jnp.where(keys <= queries, probs, 0.0)
        grad_probs = mm(v_ref[0, here, :], got)
        grad_scores = (probs * (grad_probs - centre)).astype(bf16)
        sum_v[:, here] += mm(got, probs.astype(bf16), NT)
        sum_k[:, here] += mm(qt, grad_scores, NT)
        return grad + mm(kt_ref[0, :, here], grad_scores)

    grad = lax.fori_loop(0, index, lambda at, c: step(at, c, False), jnp.zeros(qt.shape, f32))
    dq_ref[0, :, here] = step(index, grad, True) * HEAD_DIM**-0.5

    @pl.when(i == count - 1)
    def _():
        dk_ref[0] = sum_k[...]
        dv_ref[0] = sum_v[...]

    @pl.when(at_step == end)
    def _():
        job.last()
        one, two = job.total()
        fed_ref[: job.half] = one
        fed_ref[job.half :] = two
        total = go_ref[t].astype(f32)
        for step, copy in enumerate(away):
            copy.wait_recv()
            total = total + came_ref[step + 1].astype(f32)
            copy.wait_send()
        gos_ref[...] = total.astype(bf16)


def revisit(qt, k, kt, v, ot, got, lse, go, feed, number):
    heads, _, total = qt.shape
    count = ot.shape[0]
    nt = lax.axis_size("tp")
    whole = pl.BlockSpec((1, HEAD_DIM, total), lambda h, i: (h, 0, 0))
    tall = pl.BlockSpec((1, total, HEAD_DIM), lambda h, i: (h, 0, 0))
    some = pl.BlockSpec((1, HEAD_DIM, BLOCK), lambda h, i: (i, h, 0))
    return pl.pallas_call(
        revisit_kernel,
        grid=(heads, count),
        in_specs=[
            whole,
            tall,
            whole,
            tall,
            some,
            some,
            pl.BlockSpec((1, 1, 1, BLOCK), lambda h, i: (h, i, 0, 0)),
            full(go.shape),
        ]
        + anywhere(1),
        out_specs=[whole, whole, whole, full(go.shape[1:]), full(feed.shape[1:])],
        scratch_shapes=[
            pltpu.VMEM((HEAD_DIM, total), f32),
            pltpu.VMEM((HEAD_DIM, total), f32),
            pltpu.VMEM(go.shape, bf16),
            pltpu.SemaphoreType.DMA((nt,)),
            pltpu.SemaphoreType.DMA((nt,)),
        ]
        + Sum.scratch(*feed.shape[1:]),
        out_shape=[jax.ShapeDtypeStruct((heads, HEAD_DIM, total), f32)] * 3
        + [jax.ShapeDtypeStruct(go.shape[1:], bf16), jax.ShapeDtypeStruct(feed.shape[1:], f32)],
        compiler_params=params(collective_id=number, has_side_effects=True),
        cost_estimate=cost(50),
        name="revisit",
    )(qt, k, kt, v, ot, got, lse, go, feed)


def opening_kernel(cuts, x_ref, wq_ref, wk_ref, wv_ref, wo_ref, wr_ref, wc_ref, vec_ref, na_ref, nm_ref, routes_ref, out_ref, ws_ref, smalls_ref, all_routes_ref, held, stage, small_ref, *sems):
    gather = Gather(x_ref, out_ref, *sems[:3], cuts, stage)
    sends, recvs, local = sems[3:]
    z, c, t = spot()
    ns = lax.axis_size("shard")
    one = jnp.where(c == 0, wq_ref[...].astype(f32), wv_ref[...].astype(f32))
    two = jnp.where(c == 0, wk_ref[...].astype(f32), wo_ref[...].astype(f32).T)
    held[0] = one[:, :128].astype(bf16)
    held[1] = two[:, :128].astype(bf16)
    parts = [v[...].astype(f32) for v in (wr_ref, wc_ref, vec_ref, na_ref, nm_ref)]
    used = sum(v.shape[0] for v in parts)
    parts.append(jnp.zeros((SMALL - used, parts[0].shape[1]), f32))
    small_ref[...] = jnp.concatenate(parts, axis=0).astype(bf16)
    held[2] = jnp.concatenate([one[:, 128:], two[:, 128:]], axis=1).astype(bf16)
    greet()
    started = []

    def go(k, source, target, **where):
        copy = remote(source, target, sends.at[k], recvs.at[k], **where)
        copy.start()
        started.append(copy)

    def came(k, ref):
        remote(ref, ref, sends.at[k], recvs.at[k], ctx=1 - c).wait_recv()

    for step in range(1, ns):
        go(step, held, ws_ref.at[c, z], shard=lax.rem(z + step, ns))
    gather.first()
    for step in range(1, ns):
        go(2 * ns + step, small_ref, smalls_ref.at[z], shard=lax.rem(z + step, ns))
    go(0, held, ws_ref.at[c, z], ctx=1 - c)
    go(ns, routes_ref, all_routes_ref.at[c], ctx=1 - c)
    mine = [
        pltpu.make_async_copy(held, ws_ref.at[c, z], local.at[0]),
        pltpu.make_async_copy(small_ref, smalls_ref.at[z], local.at[1]),
        pltpu.make_async_copy(routes_ref, all_routes_ref.at[c], local.at[2]),
    ]
    for copy in mine:
        copy.start()
    for s in range(cuts):
        gather.second(s)
    for s in range(cuts):
        gather.third(s)
    for step in range(1, ns):
        back = lax.rem(z + ns - step, ns)
        came(step, ws_ref.at[c, back])
        go(ns + step, ws_ref.at[c, back], ws_ref.at[c, back], ctx=1 - c)
    gather.last()
    came(0, ws_ref.at[1 - c, z])
    came(ns, all_routes_ref.at[1 - c])
    for step in range(1, ns):
        back = lax.rem(z + ns - step, ns)
        came(2 * ns + step, smalls_ref.at[back])
        came(ns + step, ws_ref.at[1 - c, back])
    for copy in started:
        copy.wait_send()
    for copy in mine:
        copy.wait()


def opening(x, weights, small, routes, number):
    cuts = 2
    ns = lax.axis_size("shard")
    depth = weights[0].shape[0]
    held = (3, depth, 128)
    vmem = pl.BlockSpec(memory_space=pltpu.VMEM)
    return pl.pallas_call(
        functools.partial(opening_kernel, cuts),
        in_specs=anywhere(1) + [vmem] * (len(weights) + len(small) + 1),
        out_specs=anywhere(4),
        out_shape=[
            jax.ShapeDtypeStruct((8,) + x.shape, x.dtype),
            jax.ShapeDtypeStruct((2, ns) + held, bf16),
            jax.ShapeDtypeStruct((ns, SMALL, depth), bf16),
            jax.ShapeDtypeStruct((2,) + routes.shape, routes.dtype),
        ],
        scratch_shapes=[pltpu.VMEM(held, bf16), pltpu.VMEM(x.shape, x.dtype), pltpu.VMEM((SMALL, depth), bf16)]
        + Gather.scratch(cuts)
        + [
            pltpu.SemaphoreType.DMA((3 * ns,)),
            pltpu.SemaphoreType.DMA((3 * ns,)),
            pltpu.SemaphoreType.DMA((3,)),
        ],
        compiler_params=params(collective_id=number, has_side_effects=True),
        cost_estimate=cost(30),
        name="opening",
    )(x, *weights, *small, routes)


def places(routes_ref, row_ref):
    one = lax.broadcasted_iota(jnp.int32, (BLOCK, BLOCK), 0)
    two = lax.broadcasted_iota(jnp.int32, (BLOCK, BLOCK), 1)
    before = (one < two).astype(bf16)
    blocks, _, per = routes_ref.shape
    for b in range(blocks):
        carry = jnp.zeros((16, 1), f32)
        for at in range(0, per, BLOCK):
            here = slice(at, at + BLOCK)
            expert = lax.broadcasted_iota(jnp.int32, (16, BLOCK), 0)
            member = (routes_ref[b, 0:1, here] == expert) | (routes_ref[b, 1:2, here] == expert)
            rank = mm(member.astype(bf16), before) + carry
            row_ref[:, b * per + at : b * per + at + BLOCK] = jnp.where(member, rank, -1.0)
            carry = carry + jnp.sum(member.astype(f32), axis=1, keepdims=True)


def route_kernel(cuts, o_ref, x_ref, wo_ref, small_ref, prev_ref, routes_ref, cots_ref,
                 att, res_out, base_out, x_out, g_out, gate_ref, row_ref,
                 x_in, wo_in, res, base, a, comb, rows, cots, combs, xs, gs,
                 o_send, o_recv, c_send, c_recv, local, out_sem, x_sem, g_sem, *sems):
    gather = Gather(a, rows, *sems, cuts, relative=True)
    z, c, t = spot()
    nt = lax.axis_size("tp")
    own = 4 * c + t
    near = (t,) + across(t)
    blocks, _, per = routes_ref.shape
    width = rows.shape[2]
    experts = xs.shape[0]
    here = pl.ds(pl.multiple_of(t * BLOCK, BLOCK), BLOCK)
    loads = [
        pltpu.make_async_copy(cots_ref, cots, local.at[0]),
        pltpu.make_async_copy(x_ref, x_in, local.at[1]),
        pltpu.make_async_copy(wo_ref, wo_in, local.at[2]),
    ]
    for copy in loads:
        copy.start()
    greet(False)

    copies = []
    for i in range(o_ref.shape[0]):
        block = zig(c, i)
        copy = remote(o_ref.at[i], att.at[t], o_send.at[i], o_recv.at[t], ctx=block // nt, tp=lax.rem(block, nt))
        copies.append((block == own, copy, pltpu.make_async_copy(o_ref.at[i], att.at[t], local.at[3])))
    for mine, copy, inside in copies:

        @pl.when(jnp.logical_not(mine))
        def _():
            copy.start()

        @pl.when(mine)
        def _():
            inside.start()

    each = per // nt

    def names(b, j, order):
        start = pl.multiple_of(b * per, per)
        mine = row_ref[pl.ds(experts * c + j, 1), pl.ds(start, per)] if order is None else jnp.concatenate(
            [row_ref[pl.ds(experts * c + j, 1), pl.ds(pl.multiple_of(start + o * each, each), each)] for o in order], axis=1
        )
        return lax.broadcasted_iota(jnp.int32, (CAP, mine.shape[1]), 0).astype(f32) == mine

    def fetch(n):
        b, j = n // experts, lax.rem(n, experts)
        here = pl.ds(pl.multiple_of(b * CAP, CAP), CAP)
        hot = names(b, j, None)
        gs[j, here] = mm(hot.astype(bf16), cots[pl.ds(4 * b, 4)].reshape(per, width)).astype(bf16)
        pltpu.make_async_copy(gs.at[j, here], g_out.at[j, here], g_sem.at[n]).start()

    def fetch_x(beside, j, which):
        b = 1 - c if beside else c
        here = pl.ds(pl.multiple_of(b * CAP, CAP), CAP)
        order = [near[k] for k in which]
        hot = names(b, j, order)
        first = 4 * beside + which[0]
        got = mm(hot.astype(bf16), rows[first : first + len(which)].reshape(len(which) * each, width)).astype(bf16)
        gate = jnp.zeros((CAP, 1), f32)
        for k, o in enumerate(order):
            weight = combs[4 * b + o, pl.ds(experts * c + j, 1)]
            gate = gate + jnp.sum(jnp.where(hot[:, k * each : (k + 1) * each], weight, 0.0), axis=1, keepdims=True)
        if which[0] == 0:
            xs[j, here] = got
            gate_ref[j, here] = gate
        else:
            xs[j, here] = xs[j, here] + got
            gate_ref[j, here] = gate_ref[j, here] + gate
            n = b * experts + j
            pltpu.make_async_copy(xs.at[j, here], x_out.at[j, here], x_sem.at[n]).start()

    def all_x(beside, which):
        @pl.loop(0, experts)
        def _(j):
            fetch_x(beside, j, which)

    def fetch_g(first, last):
        @pl.loop(first, last)
        def _(n):
            fetch(n)

    places(routes_ref, row_ref)
    for copy in loads:
        copy.wait()
    fetch_g(0, 2)
    for mine, copy, inside in copies:

        @pl.when(jnp.logical_not(mine))
        def _():
            copy.wait_send()

        @pl.when(mine)
        def _():
            inside.wait()

    mine = lax.rem((own + 1) // 2, 2) == c
    for source in range(nt):

        @pl.when(jnp.logical_or(jnp.logical_not(mine), source != t))
        def _():
            remote(o_ref.at[0], att.at[source], o_send.at[0], o_recv.at[source], ctx=c, tp=t).wait_recv()

    attended = att[...].reshape(-1, BLOCK)
    r = x_in[...].astype(f32) + mm(attended, wo_in[...].reshape(-1, width), TN)
    inverse = lax.rsqrt(jnp.mean(r * r, axis=1, keepdims=True) + epsilon)
    n2 = r * inverse * small_ref[19:20]
    a[...] = n2.astype(bf16)
    gather.first()
    res[...] = r
    _, _, combined, alphas, weights = mixing(n2, small_ref[:16], *laid(prev_ref[:, here], routes_ref[c, :, here]))
    comb[...] = combined
    pairs = []
    for step in range(1, 8):
        other, back = lax.rem(own + step, 8), lax.rem(own + 8 - step, 8)
        where = {"ctx": other // 4, "tp": lax.rem(other, 4)}
        copy = remote(comb, combs.at[own], c_send.at[step], c_recv.at[step], **where)
        copy.start()
        pairs.append((copy, remote(comb, combs.at[back], c_send.at[step], c_recv.at[step], **where)))
    combs[own] = comb[...]
    scale, one, two = scales(alphas, weights)
    base[...] = r + scale * n2 + one * small_ref[16:17] + two * small_ref[17:18]
    outs = [
        pltpu.make_async_copy(res, res_out, out_sem.at[0]),
        pltpu.make_async_copy(base, base_out, out_sem.at[1]),
    ]
    for copy in outs:
        copy.start()

    total = blocks * experts
    fetch_g(2, 4)
    gather.second(0)
    fetch_g(4, total)
    gather.second(1)
    gather.own.wait()
    for copy, came in pairs:
        came.wait_recv()
    all_x(0, (0, 1, 2))
    gather.third(0)
    gather.third(1)
    gather.beside()
    all_x(1, (0, 1, 2))
    all_x(0, (3,))
    gather.last(True)
    all_x(1, (3,))

    for copy, came in pairs:
        copy.wait_send()
    for copy in outs:
        copy.wait()

    @pl.loop(0, total)
    def _(n):
        b, j = n // experts, lax.rem(n, experts)
        here = pl.ds(pl.multiple_of(b * CAP, CAP), CAP)
        pltpu.make_async_copy(gs.at[j, here], g_out.at[j, here], g_sem.at[n]).wait()
        pltpu.make_async_copy(xs.at[j, here], x_out.at[j, here], x_sem.at[n]).wait()


def route(o, x, wo, small, prev, routes, cots, experts, number):
    cuts = 2
    own, width = x.shape
    nt = lax.axis_size("tp")
    blocks, _, per = routes.shape
    slots = jax.ShapeDtypeStruct((experts, blocks * CAP, width), bf16)
    vmem = pl.BlockSpec(memory_space=pltpu.VMEM)
    return pl.pallas_call(
        functools.partial(route_kernel, cuts),
        in_specs=anywhere(3) + [vmem, vmem, vmem] + anywhere(1),
        out_specs=[vmem] + anywhere(4) + [vmem, vmem],
        out_shape=[
            jax.ShapeDtypeStruct((nt,) + o.shape[1:], bf16),
            jax.ShapeDtypeStruct((own, width), f32),
            jax.ShapeDtypeStruct((own, width), f32),
            slots,
            slots,
            jax.ShapeDtypeStruct((experts, blocks * CAP, 1), f32),
            jax.ShapeDtypeStruct((16, blocks * per), f32),
        ],
        scratch_shapes=[
            pltpu.VMEM((own, width), bf16),
            pltpu.VMEM(wo.shape, bf16),
            pltpu.VMEM((own, width), f32),
            pltpu.VMEM((own, width), f32),
            pltpu.VMEM((own, width), bf16),
            pltpu.VMEM((16, own), f32),
            pltpu.VMEM((8, own, width), bf16),
            pltpu.VMEM((8, own, width), bf16),
            pltpu.VMEM((8, 16, own), f32),
            pltpu.VMEM(slots.shape, bf16),
            pltpu.VMEM(slots.shape, bf16),
            pltpu.SemaphoreType.DMA((o.shape[0],)),
            pltpu.SemaphoreType.DMA((nt,)),
            pltpu.SemaphoreType.DMA((8,)),
            pltpu.SemaphoreType.DMA((8,)),
            pltpu.SemaphoreType.DMA((4,)),
            pltpu.SemaphoreType.DMA((2,)),
            pltpu.SemaphoreType.DMA((blocks * experts,)),
            pltpu.SemaphoreType.DMA((blocks * experts,)),
        ]
        + Gather.scratch(cuts),
        compiler_params=params(collective_id=number, has_side_effects=True),
        cost_estimate=cost(65),
        name="route",
    )(o, x, wo, small, prev, routes, cots)


def spot_rows(place, c, experts, first, some, values, at):
    lane = lax.broadcasted_iota(jnp.int32, place.shape, 1)
    slot = lax.broadcasted_iota(jnp.int32, (place.shape[0], CAP), 1).astype(f32)
    total = None
    for j in range(some):
        mine = jnp.sum(jnp.where(lane == experts * c + first + j, place, 0.0), axis=1, keepdims=True)
        term = mm((slot == mine).astype(bf16), values[j, at])
        total = term if total is None else total + term
    return total


def combine_kernel(experts, row_ref, *refs):
    back_ref, feed_ref, out_ref, feed_out, gates_ref = refs[:5]
    backs, feeds, stage, staged, gsend, gcame, l_sem, o_sem, g_send, g_recv = refs[5:15]
    job = Sum(None, *refs[15:], stage=stage)
    z, c, t = spot()
    own = 4 * c + t
    width = stage.shape[2]
    loads = [pltpu.make_async_copy(back_ref, backs, l_sem.at[0])]
    more = [pltpu.make_async_copy(feed_ref, feeds, l_sem.at[1])]
    for copy in loads + more:
        copy.start()
    greet(False)

    def tile(values, owner):
        start = pl.multiple_of(owner * BLOCK, BLOCK)
        place = row_ref[:, pl.ds(start, BLOCK)].T
        here = pl.ds(pl.multiple_of(owner // 4 * CAP, CAP), CAP)
        count = values.shape[0]
        return spot_rows(place, c, experts, experts - count, count, values, here)

    def back(owner):
        got = tile(backs, owner)
        named = got[:, width:].T
        gsend[owner] = named[:FFN_EXPERTS] + named[16 : 16 + FFN_EXPERTS]
        return got[:, :width]

    for copy in loads:
        copy.wait()
    for k, o in enumerate(job.order):
        stage[k] = back(4 * (1 - c) + o).astype(bf16)
        job.core[k].start()
        job.add(k, back(4 * c + o))
    job.third()
    pairs = []
    for step in range(1, 8):
        other = lax.rem(own + step, 8)
        copy = remote(gsend.at[other], gcame.at[step], g_send.at[step], g_recv.at[step], ctx=other // 4, tp=lax.rem(other, 4))
        copy.start()
        pairs.append(copy)
    for copy in more:
        copy.wait()

    def feed(first, last):
        @pl.loop(first, last)
        def _(n):
            staged[n] = tile(feeds, n).astype(bf16)
            pltpu.make_async_copy(staged.at[n], feed_out.at[n], o_sem.at[n]).start()

    feed(0, 8)
    gates = gsend[own]
    for step, copy in enumerate(pairs):
        copy.wait_recv()
        gates = gates + gcame[step + 1]
        copy.wait_send()
    gates_ref[...] = gates
    job.last()
    one, two = job.total()
    out_ref[: job.half] = one
    out_ref[job.half :] = two

    @pl.loop(0, 8)
    def _(n):
        pltpu.make_async_copy(staged.at[n], feed_out.at[n], o_sem.at[n]).wait()


def combine(row, back, feed, number):
    experts, slots, width = feed.shape
    wide = back.shape[2]
    rows = row.shape[1] // 8
    vmem = pl.BlockSpec(memory_space=pltpu.VMEM)
    return pl.pallas_call(
        functools.partial(combine_kernel, experts),
        in_specs=[vmem] + anywhere(2),
        out_specs=[vmem] + anywhere(1) + [vmem],
        out_shape=[
            jax.ShapeDtypeStruct((rows, width), f32),
            jax.ShapeDtypeStruct((8, rows, width), bf16),
            jax.ShapeDtypeStruct((FFN_EXPERTS, rows), f32),
        ],
        scratch_shapes=[
            pltpu.VMEM((experts, slots, wide), bf16),
            pltpu.VMEM(feed.shape, bf16),
            pltpu.VMEM((4, rows, width), bf16),
            pltpu.VMEM((8, rows, width), bf16),
            pltpu.VMEM((8, FFN_EXPERTS, rows), f32),
            pltpu.VMEM((8, FFN_EXPERTS, rows), f32),
            pltpu.SemaphoreType.DMA((2,)),
            pltpu.SemaphoreType.DMA((8,)),
            pltpu.SemaphoreType.DMA((8,)),
            pltpu.SemaphoreType.DMA((8,)),
        ]
        + Sum.scratch(rows, width),
        compiler_params=params(collective_id=number, has_side_effects=True),
        cost_estimate=cost(45),
        name="combine",
    )(row, back, feed)


def closing_kernel(dq_ref, dk_ref, dv_ref, x_ref, cos_ref, sin_ref, wt_ref, par_ref, go_ref, small_ref, top_ref,
                   out_ref, gsum_ref, ssum_ref, tmax_ref,
                   dqs, dks, dvs, xs, total, row, gother, gcore, gline, gmine, smine, sline, splane, tline, mytop, stage, l_sem, *sems):
    job = Sum(None, *sems[:7], stage=stage)
    sends, recvs = sems[7:]
    z, c, t = spot()
    ns = lax.axis_size("shard")
    heads = dqs.shape[0]
    half = HEAD_DIM // 2
    own = 4 * c + t
    order = [4 * (1 - c) + o for o in job.order] + [4 * c + o for o in job.order]

    def lanes(o):
        return pl.ds(pl.multiple_of(o * BLOCK, BLOCK), BLOCK)

    loads = []
    for n, o in enumerate(order):
        here = lanes(o)
        loads.append(
            [
                pltpu.make_async_copy(dq_ref.at[:, :, here], dqs.at[:, :, here], l_sem.at[n, 0]),
                pltpu.make_async_copy(dk_ref.at[:, :, here], dks.at[:, :, here], l_sem.at[n, 1]),
                pltpu.make_async_copy(dv_ref.at[:, :, here], dvs.at[:, :, here], l_sem.at[n, 2]),
                pltpu.make_async_copy(x_ref.at[here], xs.at[here], l_sem.at[n, 3]),
            ]
        )
    for k in range(4):
        for copy in loads[k] + loads[4 + k]:
            copy.start()
    greet()
    started = []

    def go(k, source, target, **where):
        copy = remote(source, target, sends.at[k], recvs.at[k], **where)
        copy.start()
        started.append(copy)
        return copy

    line_row = lax.broadcasted_iota(jnp.int32, mytop.shape, 0)
    high = jnp.full(mytop.shape, -1e30, f32)
    for h in range(top_ref.shape[0]):
        best = jnp.max(jnp.max(top_ref[h], axis=0), axis=1, keepdims=True)
        high = jnp.where(line_row == h, best, high)
    mytop[...] = high
    tops = [go(3 + ns + s, mytop, tline.at[s], shard=lax.rem(z + s, ns)) for s in range(1, ns)]
    total[...] = jnp.zeros_like(total)
    row[...] = jnp.zeros_like(row)

    def tile(o):
        here = lanes(o)
        cosine, sine = cos_ref[:, here], sin_ref[:, here]

        def turned(g):
            u, w = g[:half], g[half:]
            return jnp.concatenate([u * cosine + w * sine, w * cosine - u * sine], axis=0)

        x = xs[here].astype(f32)
        m = x * lax.rsqrt(jnp.mean(x * x, axis=1, keepdims=True) + epsilon)
        a = (m * par_ref[18:19]).astype(bf16)
        pieces = [turned(dqs[h, :, here]) for h in range(heads)]
        pieces += [turned(dks[h, :, here]) for h in range(heads)]
        pieces += [dvs[h, :, here] for h in range(heads)]
        grads = jnp.concatenate(pieces, axis=0).astype(bf16)
        part = mm(grads, wt_ref[...], TN)
        row[...] += jnp.sum(part * m, axis=0, keepdims=True)
        total[...] += mm(grads, a)
        return part

    for k in range(4):
        for copy in loads[k] + loads[4 + k]:
            copy.wait()
        stage[k] = tile(order[k]).astype(bf16)
        job.core[k].start()
        job.add(k, tile(order[4 + k]))

    cut_rows, depth = gsum_ref.shape[1:]
    at = lax.broadcasted_iota(jnp.int32, small_ref.shape, 0)
    smalls = small_ref[...] + jnp.where(at == 19, row[...], 0.0)
    for s in range(ns):
        here = slice(s * depth, (s + 1) * depth)
        one = total[:cut_rows, here].astype(bf16)
        two = jnp.concatenate([total[cut_rows:, here].astype(bf16), go_ref[:, here]], axis=0)
        gmine[s] = packed(jnp.where(c == 0, one.astype(f32), two.astype(f32))).astype(bf16)
        gother[s] = packed(jnp.where(c == 0, two.astype(f32), one.astype(f32))).astype(bf16)
        smine[s] = smalls[:, here]
    core = go(0, gother, gcore, ctx=1 - c)
    small = [go(3 + s, smine.at[lax.rem(z + s, ns)], sline.at[s], shard=lax.rem(z + s, ns)) for s in range(1, ns)]
    core.wait_recv()
    gmine[...] = gmine[...] + gcore[...]
    line = [go(3 + 2 * ns + s, gmine.at[lax.rem(z + s, ns)], gline.at[s], shard=lax.rem(z + s, ns)) for s in range(1, ns)]
    job.third()
    for copy in small:
        copy.wait_recv()
    value = smine[z]
    for s in range(1, ns):
        value = value + sline[s]
    splane[0] = value
    plane = []
    for s in range(1, 8):
        other = lax.rem(own + s, 8)
        plane.append(go(3 + 3 * ns + s, splane.at[0], splane.at[s], ctx=other // 4, tp=lax.rem(other, 4)))
    for copy in tops:
        copy.wait_recv()
    high = mytop[...]
    for s in range(1, ns):
        high = jnp.maximum(high, tline[s])
    tline[0] = high
    pair = go(2, tline.at[0], tline.at[ns], ctx=1 - c)
    for copy in line:
        copy.wait_recv()
    value = gmine[z].astype(f32)
    for s in range(1, ns):
        value = value + gline[s].astype(f32)
    gsum_ref[c] = unpacked(value, depth)
    go(3, gsum_ref.at[c], gsum_ref.at[c], ctx=1 - c)
    for copy in plane:
        copy.wait_recv()
    value = splane[0]
    for s in range(1, 8):
        value = value + splane[s]
    ssum_ref[...] = value
    pair.wait_recv()
    tmax_ref[...] = jnp.maximum(tline[0], tline[ns])
    job.last()
    one, two = job.total()
    out_ref[: job.half] = one
    out_ref[job.half :] = two
    remote(gsum_ref.at[1 - c], gsum_ref.at[1 - c], sends.at[3], recvs.at[3], ctx=1 - c).wait_recv()
    for copy in started:
        copy.wait_send()


def closing(dq, dk, dv, x, cosine, sine, wt, par, go, small, top, number):
    heads, _, total = dq.shape
    width = x.shape[1]
    rows = total // 8
    ns = lax.axis_size("shard")
    depth = width // ns
    cut_rows = 2 * heads * HEAD_DIM
    pieces = (ns, cut_rows * 3 // 2, 128) if depth == 192 else (ns, cut_rows, depth)
    smalls = (ns,) + small.shape[:1] + (depth,)
    vmem = pl.BlockSpec(memory_space=pltpu.VMEM)
    return pl.pallas_call(
        closing_kernel,
        in_specs=anywhere(4) + [vmem] * 7,
        out_specs=[vmem] * 4,
        out_shape=[
            jax.ShapeDtypeStruct((rows, width), f32),
            jax.ShapeDtypeStruct((2, cut_rows, depth), f32),
            jax.ShapeDtypeStruct(smalls[1:], f32),
            jax.ShapeDtypeStruct((8, 128), f32),
        ],
        scratch_shapes=[
            pltpu.VMEM(dq.shape, f32),
            pltpu.VMEM(dq.shape, f32),
            pltpu.VMEM(dq.shape, f32),
            pltpu.VMEM(x.shape, bf16),
            pltpu.VMEM(wt.shape, f32),
            pltpu.VMEM((1, width), f32),
            pltpu.VMEM(pieces, bf16),
            pltpu.VMEM(pieces, bf16),
            pltpu.VMEM(pieces, bf16),
            pltpu.VMEM(pieces, bf16),
            pltpu.VMEM(smalls, f32),
            pltpu.VMEM(smalls, f32),
            pltpu.VMEM((8,) + smalls[1:], f32),
            pltpu.VMEM((ns + 1, 8, 128), f32),
            pltpu.VMEM((8, 128), f32),
            pltpu.VMEM((4, rows, width), bf16),
            pltpu.SemaphoreType.DMA((8, 4)),
        ]
        + Sum.scratch(rows, width)
        + [
            pltpu.SemaphoreType.DMA((3 * ns + 11,)),
            pltpu.SemaphoreType.DMA((3 * ns + 11,)),
        ],
        compiler_params=params(collective_id=number, has_side_effects=True),
        cost_estimate=cost(45),
        name="closing",
    )(dq, dk, dv, x, cosine, sine, wt, par, go, small, top)


def packed(v):
    rows, lanes = v.shape
    if lanes != 192:
        return v
    rest = jnp.concatenate([v[: rows // 2, 128:], v[rows // 2 :, 128:]], axis=1)
    return jnp.concatenate([v[:, :128], rest], axis=0)


def unpacked(v, lanes):
    if lanes != 192:
        return v
    rows = v.shape[0] // 3 * 2
    rest = jnp.concatenate([v[rows:, :64], v[rows:, 64:]], axis=0)
    return jnp.concatenate([v[:rows], rest], axis=1)


def swap_kernel(ge_ref, other_ref, send, recv):
    z, c, t = spot()
    greet_core()
    copy = remote(ge_ref, other_ref, send, recv, ctx=1 - c)
    copy.start()
    copy.wait()


def greet_core():
    z, c, t = spot()
    barrier = pltpu.get_barrier_semaphore()
    pl.semaphore_signal(barrier, inc=1, device_id={"ctx": 1 - c}, device_id_type=MESH)
    pl.semaphore_wait(barrier, 1)


def swap(ge, number):
    return pl.pallas_call(
        swap_kernel,
        in_specs=anywhere(1),
        out_specs=anywhere(1)[0],
        out_shape=jax.ShapeDtypeStruct(ge.shape, ge.dtype),
        scratch_shapes=[pltpu.SemaphoreType.DMA, pltpu.SemaphoreType.DMA],
        compiler_params=params(collective_id=number, has_side_effects=True),
        cost_estimate=cost(5),
        name="swap",
    )(ge)


def laid(previous, routes):
    count, rows = previous.shape
    return jnp.concatenate([previous, jnp.zeros((16 - count, rows), f32)], axis=0), routes.astype(f32)


def thirds(v):
    a = v.astype(bf16)
    rest = v - a.astype(f32)
    b = rest.astype(bf16)
    return a, b, (rest - b.astype(f32)).astype(bf16)


def mixing(n2, wrc, previous, routes):
    z = sum(mm(wrc.astype(bf16), part, NT) for part in thirds(n2))
    expert = lax.broadcasted_iota(jnp.int32, z.shape, 0).astype(f32)
    logits = z + previous
    hot = [expert == routes[r : r + 1] for r in range(2)]
    picked = [jnp.sum(jnp.where(hot[r], logits, 0.0), axis=0, keepdims=True) for r in range(2)]
    most = jnp.maximum(picked[0], picked[1])
    e = [jnp.exp(p - most) for p in picked]
    gates = [v / (e[0] + e[1]) for v in e]
    combine = jnp.where(hot[0], gates[0], 0.0) + jnp.where(hot[1], gates[1], 0.0)
    alphas = []
    for j in range(2):
        first, second = z[EXPERTS + 2 * j : EXPERTS + 2 * j + 1], z[EXPERTS + 2 * j + 1 : EXPERTS + 2 * j + 2]
        most = jnp.maximum(first, second)
        a, b = jnp.exp(first - most), jnp.exp(second - most)
        alphas.append((a / (a + b), b / (a + b)))
    weights = [combine[FFN_EXPERTS + 1 + j : FFN_EXPERTS + 2 + j] for j in range(3)]
    return hot, gates, combine, alphas, weights


def scales(alphas, weights):
    scale = weights[0] + weights[1] * alphas[0][0] + weights[2] * alphas[1][0]
    at = lax.broadcasted_iota(jnp.int32, (8, scale.shape[1]), 0)
    value = jnp.where(at == 0, scale, jnp.where(at == 1, weights[1] * alphas[0][1], weights[2] * alphas[1][1])).T
    return value[:, 0:1], value[:, 1:2], value[:, 2:3]


def turn_kernel(length, res_ref, dn_ref, named_ref, cot_ref, att_ref, wo_ref, par_ref, prev_ref, routes_ref,
                dres_ref, heads_ref, gwo_ref, small_ref, got_ref, send_sem, recv_sem, local_sem):
    z, c, t = spot()
    nt = lax.axis_size("tp")
    own = c * nt + t
    rows, width = res_ref.shape
    greet(False)
    here = pl.ds(pl.multiple_of(t * rows, rows), rows)
    res = res_ref[...]
    gain = par_ref[19:20]
    inverse = lax.rsqrt(jnp.mean(res * res, axis=1, keepdims=True) + epsilon)
    m = res * inverse
    n2 = m * gain
    previous, routes = laid(prev_ref[:, here], routes_ref[c, :, here])
    hot, gates, _, alphas, weights = mixing(n2, par_ref[:16], previous, routes)
    position = own * rows + lax.broadcasted_iota(jnp.int32, cot_ref.shape, 0)
    g = jnp.where(position < length[0], cot_ref[...].astype(f32), 0.0)
    inner = jnp.broadcast_to(jnp.sum(g * n2, axis=1, keepdims=True), (rows, 8)).T[0:1]
    onto = mm(par_ref[16:18].astype(bf16), g.astype(bf16), NT)
    onto = [onto[j : j + 1] for j in range(2)]
    named = named_ref[...]
    expert = lax.broadcasted_iota(jnp.int32, hot[0].shape, 0)
    local = {
        FFN_EXPERTS + 1: inner,
        FFN_EXPERTS + 2: alphas[0][0] * inner + alphas[0][1] * onto[0],
        FFN_EXPERTS + 3: alphas[1][0] * inner + alphas[1][1] * onto[1],
    }
    dgates = []
    for r in range(2):
        there = jnp.sum(jnp.where(hot[r][:FFN_EXPERTS], named, 0.0), axis=0, keepdims=True)
        for e, value in local.items():
            there = there + jnp.where(hot[r][e : e + 1], value, 0.0)
        dgates.append(there)
    mean = gates[0] * dgates[0] + gates[1] * dgates[1]
    dz = jnp.where(hot[0], gates[0] * (dgates[0] - mean), 0.0)
    dz = dz + jnp.where(hot[1], gates[1] * (dgates[1] - mean), 0.0)
    for j in range(2):
        da = weights[1 + j] * inner
        db = weights[1 + j] * onto[j]
        centre = alphas[j][0] * da + alphas[j][1] * db
        dz = dz + jnp.where(expert == EXPERTS + 2 * j, alphas[j][0] * (da - centre), 0.0)
        dz = dz + jnp.where(expert == EXPERTS + 2 * j + 1, alphas[j][1] * (db - centre), 0.0)
    scale, first_vec, second_vec = scales(alphas, weights)
    highest = lax.Precision.HIGHEST
    dn2 = dn_ref[...] + scale * g + sum(mm(part, par_ref[:16].astype(bf16), TN) for part in thirds(dz))
    q = dn2 * gain
    dres = g + inverse * (q - m * jnp.mean(q * m, axis=1, keepdims=True))
    dres_ref[...] = dres
    da = dres.astype(bf16)
    wo = wo_ref[...].reshape(-1, width)
    got_ref[...] = mm(wo, da, NT).astype(bf16).reshape(got_ref.shape)

    core = lax.rem((own + 1) // 2, 2)
    slot = 2 * (own // 4) + lax.rem(own, 4) // 2
    copies = []
    for target in range(nt):
        inside = jnp.logical_and(core == c, target == t)
        copy = remote(got_ref.at[target], heads_ref.at[slot], send_sem.at[target], recv_sem.at[slot], ctx=core, tp=target)
        copies.append((inside, copy, pltpu.make_async_copy(got_ref.at[target], heads_ref.at[slot], local_sem)))
    for inside, copy, kept in copies:

        @pl.when(jnp.logical_not(inside))
        def _():
            copy.start()

        @pl.when(inside)
        def _():
            kept.start()

    small_ref[0:16] = mm(dz, n2, NN, highest)
    small_ref[16:24] = jnp.zeros((8, width), f32)
    small_ref[16:17] = jnp.sum(first_vec * g, axis=0, keepdims=True)
    small_ref[17:18] = jnp.sum(second_vec * g, axis=0, keepdims=True)
    small_ref[18:19] = jnp.sum(dn2 * m, axis=0, keepdims=True)
    att = att_ref[...].reshape(-1, rows)
    gwo_ref[...] = mm(att, da).astype(bf16).reshape(gwo_ref.shape)
    for inside, copy, kept in copies:

        @pl.when(jnp.logical_not(inside))
        def _():
            copy.wait_send()

        @pl.when(inside)
        def _():
            kept.wait()

    for i in range(heads_ref.shape[0]):

        @pl.when(zig(c, i) != own)
        def _():
            remote(got_ref.at[0], heads_ref.at[i], send_sem.at[0], recv_sem.at[i], ctx=c, tp=t).wait_recv()


def turn(length, res, dn, named, cot, att, wo, small, prev, routes, count, number):
    rows, width = res.shape
    nt = lax.axis_size("tp")
    args = (res, dn, named, cot, att, wo, small, prev, routes)
    return pl.pallas_call(
        turn_kernel,
        grid_spec=pltpu.PrefetchScalarGridSpec(
            num_scalar_prefetch=1,
            grid=(1,),
            in_specs=[full(v.shape) for v in args],
            out_specs=[full((rows, width))] + anywhere(1) + [full(wo.shape), full((24, width))],
            scratch_shapes=[
                pltpu.VMEM(att.shape, bf16),
                pltpu.SemaphoreType.DMA((nt,)),
                pltpu.SemaphoreType.DMA((count,)),
                pltpu.SemaphoreType.DMA,
            ],
        ),
        out_shape=[
            jax.ShapeDtypeStruct((rows, width), f32),
            jax.ShapeDtypeStruct((count,) + att.shape[1:], bf16),
            jax.ShapeDtypeStruct(wo.shape, bf16),
            jax.ShapeDtypeStruct((24, width), f32),
        ],
        compiler_params=params(collective_id=number, has_side_effects=True),
        cost_estimate=cost(18),
        name="turn",
    )(length, *args)


def both_cores(own_ref, other_ref, targets):
    core = lax.axis_index("ctx")
    for k, target in enumerate(targets):
        for j in range(own_ref.shape[0]):
            mine, theirs = own_ref[j, k].astype(f32), other_ref[j, k].astype(f32)
            target[0, j] = jnp.where(core == 0, mine, theirs)
            target[1, j] = jnp.where(core == 0, theirs, mine)


def output_kernel(base_ref, feed_ref, length_ref, own_ref, other_ref, out_ref, *targets):
    both_cores(own_ref, other_ref, targets)
    rows = base_ref.shape[0]
    first = (lax.axis_index("ctx") * lax.axis_size("tp") + lax.axis_index("tp")) * pl.num_programs(0) + pl.program_id(0)
    position = first * rows + lax.broadcasted_iota(jnp.int32, base_ref.shape, 0)
    out_ref[...] = jnp.where(position < length_ref[0], base_ref[...] + feed_ref[...], 0.0).astype(bf16)


def steps_of(depth):
    return 4 if depth % 64 == 0 else 1


def output_rows(base, feed, length, own, other, local):
    rows, width = base.shape
    each, kinds, depth, hidden = own.shape
    steps = steps_of(depth)
    by_row = pl.BlockSpec((rows // steps, width), lambda i: (i, 0))
    pair = pl.BlockSpec((each, kinds, depth // steps, hidden), lambda i: (0, 0, i, 0))
    return pl.pallas_call(
        output_kernel,
        grid=(steps,),
        in_specs=[by_row, by_row, pl.BlockSpec(memory_space=pltpu.SMEM), pair, pair],
        out_specs=[by_row] + [pl.BlockSpec((2, each, depth // steps, hidden), lambda i: (0, 0, i, 0))] * 3,
        out_shape=[jax.ShapeDtypeStruct((rows, width), bf16)]
        + [jax.ShapeDtypeStruct((2, local, depth, hidden), f32)] * 3,
        compiler_params=params(),
        cost_estimate=cost(6),
        name="output_rows",
    )(base, feed, length, own, other)


def finish_kernel(x_ref, dn_ref, dres_ref, small_ref, gw_ref, gs_ref, top_ref, wq_ref, wk_ref, limit_ref, own_ref, other_ref, *refs):
    outs = refs[3:]
    gin_ref, targets = outs[0], outs[1:4]
    x = x_ref[...].astype(f32)
    inverse = lax.rsqrt(jnp.mean(x * x, axis=1, keepdims=True) + epsilon)
    m = x * inverse
    q = dn_ref[...] * small_ref[18:19]
    gin_ref[...] = dres_ref[...] + inverse * (q - m * jnp.mean(q * m, axis=1, keepdims=True))
    both_cores(own_ref, other_ref, targets)

    @pl.when(pl.program_id(0) == 0)
    def _():
        gq, gk, gv, go, gnorm, gmoe, grouter, gconst, gvec, fac_ref, cq_ref, ck_ref = outs[4:]
        width = wq_ref.shape[1]
        flat = gw_ref[...].reshape(4 * width, gw_ref.shape[2])
        for k, target in enumerate((gq, gk, gv)):
            target[...] = flat[k * width : (k + 1) * width].T
        go[...] = flat[3 * width :]
        sums = gs_ref[...]
        grouter[...] = sums[:EXPERTS]
        gconst[...] = sums[EXPERTS : EXPERTS + 4]
        gvec[...] = sums[16:18]
        gmoe[...] = sums[18:19]
        gnorm[...] = sums[19:20]
        factors = limit_ref[0] / jnp.maximum(top_ref[...], limit_ref[0])
        for h in range(fac_ref.shape[0]):
            fac_ref[h] = factors[h, 0]
        lane = lax.broadcasted_iota(jnp.int32, (1, width), 1)
        root = jnp.zeros((1, width), f32)
        for h in range(width // HEAD_DIM):
            root = jnp.where(lane // HEAD_DIM == h, jnp.sqrt(factors[h : h + 1, :1]), root)
        cq_ref[...] = (wq_ref[...].astype(f32) * root).astype(bf16)
        ck_ref[...] = (wk_ref[...].astype(f32) * root).astype(bf16)


def finish_rows(x, dn, dres, small, gw, gs, top, wq, wk, limit, own, other, finals):
    rows, width = x.shape
    each, kinds, depth, hidden = own.shape
    steps = steps_of(depth)
    tile, deep = rows // steps, depth // steps
    by_row = pl.BlockSpec((tile, width), lambda i: (i, 0))
    expert_out = pl.BlockSpec((2, each, deep, hidden), lambda i: (0, finals[0].shape[1] // each - 1, i, 0))
    once = [
        jax.ShapeDtypeStruct(shape, f32)
        for shape in [wq.shape] * 3
        + [(wq.shape[1], depth), (1, depth), (1, depth), (EXPERTS, depth), (4, depth), (2, depth), (wq.shape[1] // HEAD_DIM,)]
    ] + [jax.ShapeDtypeStruct(wq.shape, bf16)] * 2
    return pl.pallas_call(
        finish_kernel,
        grid=(steps,),
        in_specs=[
            by_row,
            by_row,
            by_row,
            full(small.shape),
            full(gw.shape),
            full(gs.shape),
            full(top.shape),
            full(wq.shape),
            full(wk.shape),
            pl.BlockSpec(memory_space=pltpu.SMEM),
        ]
        + [pl.BlockSpec((each, kinds, deep, hidden), lambda i: (0, 0, i, 0))] * 2
        + anywhere(3),
        out_specs=[by_row, expert_out, expert_out, expert_out] + [full(v.shape) if v.ndim > 1 else pl.BlockSpec(memory_space=pltpu.SMEM) for v in once],
        out_shape=[
            jax.ShapeDtypeStruct((rows, width), f32),
        ]
        + [jax.ShapeDtypeStruct(v.shape, f32) for v in finals]
        + once,
        input_output_aliases={12: 1, 13: 2, 14: 3},
        compiler_params=params(),
        cost_estimate=cost(8),
        name="finish_rows",
    )(x, dn, dres, small, gw, gs, top, wq, wk, limit, own, other, *finals)


def pick_kernel(first, g_ref, u_ref, d_ref, out_ref):
    for k, source in enumerate((g_ref, u_ref, d_ref)):
        out_ref[0, k] = source[0]


def pick(first, start, some, gate, up, down):
    _, depth, hidden = gate.shape
    source = pl.BlockSpec((1, depth, hidden), lambda i, f: (f[0] + start + i, 0, 0))
    return pl.pallas_call(
        pick_kernel,
        grid_spec=pltpu.PrefetchScalarGridSpec(
            num_scalar_prefetch=1,
            grid=(some,),
            in_specs=[source] * 3,
            out_specs=pl.BlockSpec((1, 3, depth, hidden), lambda i, f: (i, 0, 0, 0)),
        ),
        out_shape=jax.ShapeDtypeStruct((some, 3, depth, hidden), gate.dtype),
        compiler_params=params(),
        cost_estimate=cost(2),
        name="pick",
    )(first, gate, up, down)


def expert_kernel(start, first, x_ref, g_ref, gate_ref, w_ref, *refs):
    feed_ref, back_ref, gw_ref = refs[-3:]
    parts, _, _, depth, hidden = w_ref.shape
    width = parts * depth
    wg, wu, wd = [w_ref[:, 0, k].reshape(width, hidden) for k in range(3)]
    x, g, gate = x_ref[0], g_ref[0], gate_ref[0]
    gate_pre = mm(x, wg)
    up = mm(x, wu)
    sigmoid = 1.0 / (1.0 + jnp.exp(-gate_pre))
    activated = gate_pre * sigmoid
    inner = (activated * up).astype(bf16)
    g32 = g.astype(f32)
    dout = (gate * g32).astype(bf16)
    dinner = mm(dout, wd)
    out = mm(inner, wd, NT)
    feed_ref[0] = (gate * out).astype(bf16)
    dgate = jnp.sum(g32 * out, axis=1, keepdims=True)
    dpre = (dinner * up * sigmoid * (1.0 + gate_pre * (1.0 - sigmoid))).astype(bf16)
    dup = (dinner * activated).astype(bf16)
    back_ref[0, :, :width] = (mm(dpre, wg, NT) + mm(dup, wu, NT)).astype(bf16)
    lane = lax.broadcasted_iota(jnp.int32, (dgate.shape[0], back_ref.shape[2] - width), 1)
    coarse = dgate.astype(bf16).astype(f32)
    at = first[0] + start + pl.program_id(0)
    extra = jnp.where(lane == at, coarse, jnp.where(lane == at + 16, dgate - coarse, 0.0))
    back_ref[0, :, width:] = extra.astype(bf16)
    for k, (left, right) in enumerate(((x, dpre), (x, dup), (dout, inner))):
        gw_ref[:, 0, k] = mm(left, right, TN).reshape(parts, depth, hidden).astype(bf16)


def expert(start, first, x, g, gate, w, into=()):
    local, slots, width = x.shape
    parts, some, kinds, depth, hidden = w.shape
    pick = lambda i, f: (start + i, 0, 0)
    return pl.pallas_call(
        functools.partial(expert_kernel, start),
        grid_spec=pltpu.PrefetchScalarGridSpec(
            num_scalar_prefetch=1,
            grid=(some,),
            in_specs=[
                pl.BlockSpec((1, slots, width), pick),
                pl.BlockSpec((1, slots, width), pick),
                pl.BlockSpec((1, slots, 1), pick),
                pl.BlockSpec((parts, 1, kinds, depth, hidden), lambda i, f: (0, i, 0, 0, 0)),
            ]
            + anywhere(len(into)),
            out_specs=[
                pl.BlockSpec((1, slots, width), pick),
                pl.BlockSpec((1, slots, width + EXTRA), pick),
                pl.BlockSpec((parts, 1, kinds, depth, hidden), lambda i, f: (0, i, 0, 0, 0)),
            ],
        ),
        out_shape=[
            jax.ShapeDtypeStruct((local, slots, width), bf16),
            jax.ShapeDtypeStruct((local, slots, width + EXTRA), bf16),
            jax.ShapeDtypeStruct(w.shape, bf16),
        ],
        input_output_aliases={5 + n: n for n in range(len(into))},
        compiler_params=params(),
        cost_estimate=cost(10 * some),
        name="expert",
    )(first, x, g, gate, w, *into)


def shards(
    hidden_in,
    cotangent,
    lengths,
    routes,
    prev_logits,
    norm_attn,
    w_query,
    w_key,
    w_value,
    w_out,
    norm_moe,
    w_router,
    w_const,
    const_vec,
    w_gate,
    w_up,
    w_down,
    threshold,
):
    plane = ("ctx", "tp")
    core = lax.axis_index("ctx")
    nc, nt, ns = lax.axis_size("ctx"), lax.axis_size("tp"), lax.axis_size("shard")
    own, width = hidden_in.shape
    per = own * nt
    total = per * nc
    depth = w_gate.shape[1]
    heads = w_query.shape[1] // HEAD_DIM
    head_width = heads * HEAD_DIM
    local = FFN_EXPERTS // nc
    count = total // BLOCK // nc
    routes, prev = routes.T, prev_logits.T
    first = (core * local).astype(jnp.int32)[None]

    calls = ((0, local - 1), (local - 1, 1))
    expert_w = []
    for start, some in calls:
        pieces = pick(first, start, some, w_gate, w_up, w_down)
        expert_w.append(lax.all_gather(pieces, "shard", axis=0, tiled=False))
    rows_all, attention_w, small, routes_all = opening(
        hidden_in,
        (w_query, w_key, w_value, w_out),
        (w_router.T, w_const.T, const_vec, norm_attn[None], norm_moe[None]),
        routes,
        0,
    )
    rows_all = rows_all.reshape(total, width)
    cosine, sine = rope_tables(total)

    qt, kt, k, v, vt, wt, small, out_w = project(rows_all, attention_w, small, cosine, sine, heads, 8)
    ot, lse, top, cot_all = attend(lengths, qt, k, vt, cotangent, count, 1)
    att, res, base, x_slots, g_slots, gate_slots, row_at = route(
        ot, hidden_in, out_w, small, prev, routes_all, cot_all, local, 2
    )

    results, grads = (), []
    for (start, _), w in zip(calls, expert_w):
        *results, grad = expert(start, first, x_slots, g_slots, gate_slots, w, results)
        grads.append(lax.psum_scatter(grad, "shard", scatter_dimension=0, tiled=True)[0])
    feed, back = results
    back, feed, named = combine(row_at, back, feed, 3)

    dres, got, grad_out, gsmall = turn(
        lengths, res, back, named, cotangent, att, out_w, small, prev, routes_all, count, 4
    )
    dq, dk, dv, grad_out, feed = revisit(qt, k, kt, v, ot, got, lse, grad_out, feed, 5)
    early, dq = lax.optimization_barrier((grads[0], dq))
    output, *finals = output_rows(base, feed, lengths, early, swap(early, 6), local)
    dq, *finals = lax.optimization_barrier((dq, *finals))
    part, grad_w, gsmall, top = closing(dq, dk, dv, rows_all, cosine, sine, wt, small, grad_out, gsmall, top, 7)
    late, top = lax.optimization_barrier((grads[1], top))
    (grad_input, grad_gate, grad_up, grad_down, grad_q, grad_k, grad_v, grad_out, grad_norm_attn, grad_norm_moe,
     grad_router, grad_const, grad_vec, factors, clipped_query, clipped_key) = finish_rows(
        hidden_in, part, dres, small, grad_w, gsmall, top, w_query, w_key, threshold, late, swap(late, 9), finals
    )
    grad_gate, grad_up, grad_down = [v.reshape((-1,) + v.shape[2:]) for v in (grad_gate, grad_up, grad_down)]
    return (
        output,
        grad_input,
        grad_norm_attn[0],
        grad_q,
        grad_k,
        grad_v,
        grad_out,
        grad_norm_moe[0],
        grad_router.T,
        grad_const.T,
        grad_vec,
        grad_gate,
        grad_up,
        grad_down,
        factors,
        clipped_query,
        clipped_key,
    )


def solution(mesh):
    return jax.shard_map(
        shards,
        mesh=mesh,
        in_specs=(
            P(("shard", "ctx", "tp"), None),
            P(("shard", "ctx", "tp"), None),
            P("shard"),
            P(("shard", "ctx"), None),
            P(("shard", "ctx"), None),
            P("shard"),
            P("shard", "tp"),
            P("shard", "tp"),
            P("shard", "tp"),
            P("tp", "shard"),
            P("shard"),
            P("shard", None),
            P("shard", None),
            P(None, "shard"),
            P(None, "shard", "tp"),
            P(None, "shard", "tp"),
            P(None, "shard", "tp"),
            P(),
        ),
        out_specs=(
            P(("shard", "ctx", "tp"), None),
            P(("shard", "ctx", "tp"), None),
            P("shard"),
            P("shard", "tp"),
            P("shard", "tp"),
            P("shard", "tp"),
            P("tp", "shard"),
            P("shard"),
            P("shard", None),
            P("shard", None),
            P(None, "shard"),
            P(None, "shard", "tp"),
            P(None, "shard", "tp"),
            P(None, "shard", "tp"),
            P("tp"),
            P("shard", "tp"),
            P("shard", "tp"),
        ),
        check_vma=False,
    )
```

```python
import functools

import jax
import jax.numpy as jnp
import numpy as np
from jax import lax
from jax.experimental import pallas as pl
from jax.experimental.pallas import tpu as pltpu
from jax.sharding import PartitionSpec as P

HEAD_DIM = 64
EXPERTS = 12
FFN_EXPERTS = 8
CAP = 512
BLOCK = 512
EXTRA = 128
SMALL = 32
MESH = pl.DeviceIdType.MESH

epsilon = 1e-06
rope_base = 10000.0
bf16 = jnp.bfloat16
f32 = jnp.float32

NN = (((1,), (0,)), ((), ()))
NT = (((1,), (1,)), ((), ()))
TN = (((0,), (0,)), ((), ()))


def mm(left, right, dims=NN, precision=None):
    return lax.dot_general(
        left, right, dims, preferred_element_type=f32, precision=precision
    )


def params(mib=56, **more):
    return pltpu.CompilerParams(vmem_limit_bytes=mib * 1024 * 1024, **more)


def cost(us):
    return pl.CostEstimate(flops=int(us * 1e9), bytes_accessed=int(us * 3e6), transcendentals=0)


def full(shape):
    return pl.BlockSpec(shape, lambda *_: (0,) * len(shape))


def rope_tables(total):
    half = HEAD_DIM // 2
    freqs = np.float32(rope_base) ** (np.float32(-2.0) * np.arange(half, dtype=np.float32) / np.float32(HEAD_DIM))
    angles = freqs.astype(np.float32)[:, None] * np.arange(total, dtype=np.float32)[None, :]
    angles = angles.astype(np.float64)
    return jnp.asarray(np.cos(angles), f32), jnp.asarray(np.sin(angles), f32)


def zig(core, i):
    return 4 * (i // 2) + (core if i % 2 == 0 else 3 - core)


def anywhere(count):
    return [pl.BlockSpec(memory_space=pl.ANY)] * count


def spot():
    return lax.axis_index("shard"), lax.axis_index("ctx"), lax.axis_index("tp")


def across(t):
    return t + 1 - 2 * lax.rem(t, 2), lax.rem(t + 2, 4), 3 - t


def remote(source, target, sends, recvs, **where):
    return pltpu.make_async_remote_copy(
        src_ref=source,
        dst_ref=target,
        send_sem=sends,
        recv_sem=recvs,
        device_id=where,
        device_id_type=MESH,
    )


def greet(depth=True):
    z, c, t = spot()
    nc, nt, ns = lax.axis_size("ctx"), lax.axis_size("tp"), lax.axis_size("shard")
    barrier = pltpu.get_barrier_semaphore()
    for step in range(1, nc * nt):
        other = lax.rem(c * nt + t + step, nc * nt)
        pl.semaphore_signal(
            barrier,
            inc=1,
            device_id={"ctx": other // nt, "tp": lax.rem(other, nt)},
            device_id_type=MESH,
        )
    if depth:
        for step in range(1, ns):
            pl.semaphore_signal(
                barrier,
                inc=1,
                device_id={"shard": lax.rem(z + step, ns)},
                device_id_type=MESH,
            )
    pl.semaphore_wait(barrier, nc * nt - 1 + (ns - 1 if depth else 0))


class Gather:
    KINDS = 9

    def __init__(self, x, out, sends, recvs, own, cuts, stage=None, relative=False):
        z, c, t = spot()
        tx, ty, td = across(t)
        rows = x.shape[0] // cuts
        half = rows // 2
        self.cuts = cuts
        sib = {"ctx": 1 - c}
        px, py = {"tp": tx}, {"tp": ty}
        near = (t, tx, ty, td)
        if relative:
            here, there = list(range(8)), list(range(8))
            mine = (1, 2, 4)
            passed = ((1, 5), (1, 3), (2, 6), (2, 3), (3, 7), (3, 7))
        else:
            here = [4 * c + n for n in near] + [4 * (1 - c) + n for n in near]
            there = here[:4]
            mine = (here[0],) * 3
            passed = tuple((here[n], here[n]) for n in (1, 1, 2, 2, 3, 3))
        self.load = None if stage is None else pltpu.make_async_copy(x, stage, own.at[0])
        self.own = pltpu.make_async_copy(x if stage is None else stage, out.at[here[0]], own.at[1])

        def parts(s):
            whole = pl.ds(s * rows, rows)
            one, two = pl.ds(s * rows, half), pl.ds(s * rows + half, half)
            return whole, one, two

        def copies(s):
            whole, one, two = parts(s)
            made = [
                remote(x.at[whole], out.at[slot, whole], sends.at[s, k], recvs.at[s, k], **where)
                for k, (slot, where) in enumerate(zip(mine, (px, py, sib)))
            ]
            ways = ((whole, sib), (one, py), (whole, sib), (two, px), (one, sib), (two, sib))
            for k, ((source, target), (part, where)) in enumerate(zip(passed, ways)):
                made.append(
                    remote(out.at[source, part], out.at[target, part], sends.at[s, k + 3], recvs.at[s, k + 3], **where)
                )
            return made

        self.copies = [copies(s) for s in range(cuts)]

        def arrivals(s):
            whole, one, two = parts(s)
            where = [(1, whole), (2, whole), (4, whole), (5, whole), (3, one), (6, whole), (3, two), (7, one), (7, two)]
            return [
                remote(out.at[here[n], part], out.at[here[n], part], sends.at[s, k], recvs.at[s, k], **sib)
                for k, (n, part) in enumerate(where)
            ]

        self.arrivals = [arrivals(s) for s in range(cuts)]

    @staticmethod
    def scratch(cuts):
        return [
            pltpu.SemaphoreType.DMA((cuts, Gather.KINDS)),
            pltpu.SemaphoreType.DMA((cuts, Gather.KINDS)),
            pltpu.SemaphoreType.DMA((2,)),
        ]

    def first(self):
        for s in range(self.cuts):
            for k in (0, 1, 2):
                self.copies[s][k].start()
        (self.load or self.own).start()

    def second(self, s):
        if self.load is not None and s == 0:
            self.load.wait()
            self.own.start()
        self.arrivals[s][0].wait_recv()
        self.copies[s][4].start()
        self.copies[s][3].start()
        self.arrivals[s][1].wait_recv()
        self.copies[s][6].start()
        self.copies[s][5].start()

    def third(self, s):
        for k in (4, 6):
            self.arrivals[s][k].wait_recv()
            self.copies[s][7 if k == 4 else 8].start()

    def beside(self):
        for s in range(self.cuts):
            for k in (2, 3, 5):
                self.arrivals[s][k].wait_recv()

    def last(self, rest=False):
        for s in range(self.cuts):
            for k in (7, 8) if rest else (2, 3, 5, 7, 8):
                self.arrivals[s][k].wait_recv()
        for s in range(self.cuts):
            for k in range(self.KINDS):
                self.copies[s][k].wait_send()
        if not rest:
            self.own.wait()


class Sum:
    def __init__(self, p, held, came, across_in, across_out, sends, recvs, loads, stage=None):
        z, c, t = spot()
        self.t = t
        tx, ty, td = across(t)
        half = held.shape[1] // 2
        self.half = half
        self.one, self.two = pl.ds(0, half), pl.ds(half, half)
        self.order = (td, tx, ty, t)
        self.held, self.came, self.inn = held, came, across_in
        sib, px, py = {"ctx": 1 - c}, {"tp": tx}, {"tp": ty}
        self.core = []
        for k, o in enumerate(self.order):
            source = p.at[4 * (1 - c) + o] if stage is None else stage.at[k]
            self.core.append(remote(source, came.at[o], sends.at[k], recvs.at[k], **sib))
        self.loads = None
        if stage is None:
            self.loads = [pltpu.make_async_copy(p.at[4 * c + o], held.at[o], loads.at[k]) for k, o in enumerate(self.order)]

        def send(k, source, slot, where):
            return remote(source, across_in.at[slot], sends.at[k], recvs.at[k], **where)

        self.side = {
            "dx": send(4, held.at[td, self.one], 0, px),
            "dy": send(5, held.at[td, self.two], 1, py),
            "x": send(6, held.at[tx, self.one], 2, px),
            "y": send(7, held.at[ty, self.two], 3, py),
            "cy": send(8, across_out.at[0], 4, py),
            "cx": send(9, across_out.at[1], 5, px),
        }
        self.out = across_out
        self.near = (tx, ty, td)

    @staticmethod
    def scratch(rows, width):
        return [
            pltpu.VMEM((4, rows, width), bf16),
            pltpu.VMEM((4, rows, width), bf16),
            pltpu.VMEM((6, rows // 2, width), bf16),
            pltpu.VMEM((2, rows // 2, width), bf16),
            pltpu.SemaphoreType.DMA((10,)),
            pltpu.SemaphoreType.DMA((10,)),
            pltpu.SemaphoreType.DMA((4,)),
        ]

    def first(self):
        for k in range(4):
            self.core[k].start()
            self.loads[k].start()

    def add(self, k, mine):
        o = self.order[k]
        self.core[k].wait_recv()
        self.held[o] = (mine + self.came[o].astype(mine.dtype)).astype(bf16)
        for name in (("dx", "dy"), ("x",), ("y",), ())[k]:
            self.side[name].start()

    def second(self):
        for k, o in enumerate(self.order):
            self.loads[k].wait()
            self.add(k, self.held[o])

    def third(self):
        tx, ty, td = self.near
        self.side["dx"].wait_recv()
        self.out[0] = self.held[ty, self.one] + self.inn[0]
        self.side["cy"].start()
        self.side["dy"].wait_recv()
        self.out[1] = self.held[tx, self.two] + self.inn[1]
        self.side["cx"].start()

    def last(self):
        for k in ("x", "y", "cy", "cx"):
            self.side[k].wait_recv()
        for copy in self.core + list(self.side.values()):
            copy.wait_send()

    def total(self):
        def add(part, a, b):
            return self.held[self.t, part].astype(f32) + self.inn[a].astype(f32) + self.inn[b].astype(f32)

        return add(self.one, 2, 4), add(self.two, 3, 5)


def qkv_kernel(x_ref, w_ref, s_ref, cos_ref, sin_ref, qt_ref, kt_ref, k_ref, v_ref, vt_ref, wt_ref, small_ref, wo_ref, wo, send, recv, local):
    heads = qt_ref.shape[0]
    width = heads * HEAD_DIM
    half = HEAD_DIM // 2
    z, c, t = spot()
    nt = lax.axis_size("tp")
    mid = width // 2
    mine, theirs = pl.ds(c * mid, mid), pl.ds((1 - c) * mid, mid)
    away, came, onward, there = [], [], [], []
    for step in range(1, nt):
        back = lax.rem(t + nt - step, nt)
        away.append(remote(wo.at[mine], wo_ref.at[t, mine], send.at[step], recv.at[step], tp=lax.rem(t + step, nt)))
        ref = wo_ref.at[back, mine]
        came.append(remote(ref, ref, send.at[nt + step], recv.at[step], ctx=1 - c))
        onward.append(remote(ref, ref, send.at[nt + step], recv.at[nt + step], ctx=1 - c))
        ref = wo_ref.at[back, theirs]
        there.append(remote(ref, ref, send.at[nt + step], recv.at[nt + step], ctx=1 - c))
    own = pltpu.make_async_copy(wo, wo_ref.at[t], local)
    i = pl.program_id(0)

    @pl.when(i == 0)
    def _():
        def flat(v):
            return v.astype(f32).reshape(v.shape[0] * v.shape[1], v.shape[2])

        def whole(core, which):
            rest = flat(w_ref[core, :, 2])[:, which * (width - 128) : (which + 1) * (width - 128)]
            return jnp.concatenate([flat(w_ref[core, :, which]), rest], axis=1).T.astype(bf16)

        wo[...] = whole(1, 1)
        greet(False)
        for copy in away:
            copy.start()
        own.start()
        wt_ref[:width] = whole(0, 0)
        wt_ref[width : 2 * width] = whole(0, 1)
        wt_ref[2 * width :] = whole(1, 0)
        small_ref[...] = jnp.concatenate([s_ref[n].astype(f32) for n in range(s_ref.shape[0])], axis=1)

    x = x_ref[...].astype(f32)
    inverse = lax.rsqrt(jnp.mean(x * x, axis=1, keepdims=True) + epsilon)
    a = (x * inverse * small_ref[18:19]).astype(bf16)
    y = mm(wt_ref[...], a, NT)
    cosine, sine = cos_ref[...], sin_ref[...]

    def turned(first):
        u, w = y[first : first + half], y[first + half : first + HEAD_DIM]
        return jnp.concatenate([u * cosine - w * sine, w * cosine + u * sine], axis=0)

    for h in range(heads):
        at = h * HEAD_DIM
        qt_ref[h] = (turned(at) * HEAD_DIM**-0.5).astype(bf16)
        key = turned(width + at)
        kt_ref[h] = key.astype(bf16)
        k_ref[h] = key.T.astype(bf16)
        value = y[2 * width + at : 2 * width + at + HEAD_DIM]
        v_ref[h] = value.T.astype(bf16)
        vt_ref[h, :HEAD_DIM] = value.astype(bf16)
        vt_ref[h, HEAD_DIM:] = jnp.ones((16, value.shape[1]), bf16)

    @pl.when(i == pl.num_programs(0) - 2)
    def _():
        for copy, forth in zip(came, onward):
            copy.wait_recv()
            forth.start()

    @pl.when(i == pl.num_programs(0) - 1)
    def _():
        for copy in there:
            copy.wait_recv()
        for copy in away + onward:
            copy.wait_send()
        own.wait()


def project(rows, w, small, cosine, sine, heads, number):
    total, width = rows.shape
    tile = BLOCK
    out = heads * HEAD_DIM
    nt = lax.axis_size("tp")
    shapes = [
        jax.ShapeDtypeStruct((heads, HEAD_DIM, total), bf16),
        jax.ShapeDtypeStruct((heads, HEAD_DIM, total), bf16),
        jax.ShapeDtypeStruct((heads, total, HEAD_DIM), bf16),
        jax.ShapeDtypeStruct((heads, total, HEAD_DIM), bf16),
        jax.ShapeDtypeStruct((heads, HEAD_DIM + 16, total), bf16),
        jax.ShapeDtypeStruct((3 * out, width), bf16),
        jax.ShapeDtypeStruct((SMALL, width), f32),
        jax.ShapeDtypeStruct((nt, out, width), bf16),
    ]
    return pl.pallas_call(
        qkv_kernel,
        grid=(total // tile,),
        in_specs=[
            pl.BlockSpec((tile, width), lambda i: (i, 0)),
            full(w.shape),
            full(small.shape),
            pl.BlockSpec((HEAD_DIM // 2, tile), lambda i: (0, i)),
            pl.BlockSpec((HEAD_DIM // 2, tile), lambda i: (0, i)),
        ],
        out_specs=[
            pl.BlockSpec((heads, HEAD_DIM, tile), lambda i: (0, 0, i)),
            pl.BlockSpec((heads, HEAD_DIM, tile), lambda i: (0, 0, i)),
            pl.BlockSpec((heads, tile, HEAD_DIM), lambda i: (0, i, 0)),
            pl.BlockSpec((heads, tile, HEAD_DIM), lambda i: (0, i, 0)),
            pl.BlockSpec((heads, HEAD_DIM + 16, tile), lambda i: (0, 0, i)),
        ]
        + [full(v.shape) for v in shapes[5:7]]
        + anywhere(1),
        scratch_shapes=[
            pltpu.VMEM((out, width), bf16),
            pltpu.SemaphoreType.DMA((2 * nt,)),
            pltpu.SemaphoreType.DMA((2 * nt,)),
            pltpu.SemaphoreType.DMA,
        ],
        out_shape=shapes,
        compiler_params=params(collective_id=number, has_side_effects=True),
        cost_estimate=cost(14),
        name="project",
    )(rows, w, small, cosine, sine)


def dealt(core, i):
    return 4 * (i // 2) + jnp.where(lax.rem(i, 2) == 0, core, 3 - core)


def attend_kernel(cuts, length, qt_ref, k_ref, vt_ref, cot_ref, ot_ref, lse_ref, top_ref, cots_ref, mask_cot, *sems):
    z, c, t = spot()
    nt = lax.axis_size("tp")
    h, i = pl.program_id(0), pl.program_id(1)
    count = pl.num_programs(1)
    at_step = h * count + i
    last = pl.num_programs(0) * count - 1
    gather = Gather(mask_cot, cots_ref, *sems, cuts)

    @pl.when(at_step == 0)
    def _():
        rows = cot_ref.shape[0]
        position = (c * nt + t) * rows + lax.broadcasted_iota(jnp.int32, cot_ref.shape, 0)
        mask_cot[...] = jnp.where(position < length[0], cot_ref[...].astype(f32), 0.0).astype(bf16)
        greet(False)
        gather.first()

    index = dealt(c, i)
    columns = BLOCK
    qt = qt_ref[0, :, pl.ds(pl.multiple_of(index * BLOCK, BLOCK), BLOCK)]

    def step(at, carry, diagonal):
        peak, total = carry
        start = pl.multiple_of(at * BLOCK, BLOCK)
        scores = mm(k_ref[0, pl.ds(start, BLOCK), :], qt)
        if diagonal:
            keys = lax.broadcasted_iota(jnp.int32, scores.shape, 0)
            queries = lax.broadcasted_iota(jnp.int32, scores.shape, 1)
            scores = jnp.where(keys <= queries, scores, -1e30)
        higher = jnp.maximum(peak, jnp.max(scores, axis=0, keepdims=True))
        weights = jnp.exp(scores - higher).astype(bf16)
        total = total * jnp.exp(peak - higher) + mm(vt_ref[0, :, pl.ds(start, BLOCK)], weights)
        return higher, total

    start = (jnp.full((1, columns), -1e30, f32), jnp.zeros((HEAD_DIM + 16, columns), f32))
    carry = lax.fori_loop(0, index, lambda at, c: step(at, c, False), start)
    peak, total = step(index, carry, True)
    mass = total[HEAD_DIM : HEAD_DIM + 1]
    ot_ref[0] = (total[:HEAD_DIM] / mass).astype(bf16)
    lse_ref[0, 0] = peak + jnp.log(mass)
    position = index * BLOCK + lax.broadcasted_iota(jnp.int32, peak.shape, 1)
    top_ref[0, 0] = jnp.where(position < length[0], peak, -1e30)

    @pl.when(at_step == last - 3)
    def _():
        for s in range(cuts):
            gather.second(s)

    @pl.when(at_step == last)
    def _():
        for s in range(cuts):
            gather.third(s)
        gather.last()


def attend(length, qt, k, vt, cot, count, number):
    cuts = 1
    heads, _, total = qt.shape
    return pl.pallas_call(
        functools.partial(attend_kernel, cuts),
        grid_spec=pltpu.PrefetchScalarGridSpec(
            num_scalar_prefetch=1,
            grid=(heads, count),
            in_specs=[
                pl.BlockSpec((1, HEAD_DIM, total), lambda h, i, n: (h, 0, 0)),
                pl.BlockSpec((1, total, HEAD_DIM), lambda h, i, n: (h, 0, 0)),
                pl.BlockSpec((1, HEAD_DIM + 16, total), lambda h, i, n: (h, 0, 0)),
                full(cot.shape),
            ],
            out_specs=[
                pl.BlockSpec((1, HEAD_DIM, BLOCK), lambda h, i, n: (i, h, 0)),
                pl.BlockSpec((1, 1, 1, BLOCK), lambda h, i, n: (h, i, 0, 0)),
                pl.BlockSpec((1, 1, 1, BLOCK), lambda h, i, n: (h, i, 0, 0)),
            ]
            + anywhere(1),
            scratch_shapes=[
                pltpu.VMEM(cot.shape, bf16),
            ]
            + Gather.scratch(cuts),
        ),
        out_shape=[
            jax.ShapeDtypeStruct((count, heads * HEAD_DIM, BLOCK), bf16),
            jax.ShapeDtypeStruct((heads, count, 1, BLOCK), f32),
            jax.ShapeDtypeStruct((heads, count, 1, BLOCK), f32),
            jax.ShapeDtypeStruct((8,) + cot.shape, bf16),
        ],
        compiler_params=params(collective_id=number, has_side_effects=True),
        cost_estimate=cost(35),
        name="attend",
    )(length, qt, k, vt, cot)


def revisit_kernel(qt_ref, k_ref, kt_ref, v_ref, ot_ref, got_ref, lse_ref, go_ref, feed_ref, dq_ref, dk_ref, dv_ref, gos_ref, fed_ref, sum_k, sum_v, came_ref, w_send, w_recv, *scratch):
    z, c, t = spot()
    job = Sum(feed_ref, *scratch)
    nt = lax.axis_size("tp")
    h, i = pl.program_id(0), pl.program_id(1)
    count = pl.num_programs(1)
    index = dealt(c, i)
    here = pl.ds(pl.multiple_of(index * BLOCK, BLOCK), BLOCK)
    away = [
        remote(go_ref.at[lax.rem(t + step, nt)], came_ref.at[step], w_send.at[step], w_recv.at[step], tp=lax.rem(t + step, nt))
        for step in range(1, nt)
    ]

    at_step = h * count + i
    end = pl.num_programs(0) * count - 1

    @pl.when(at_step == 0)
    def _():
        greet(False)
        job.first()
        for copy in away:
            copy.start()

    @pl.when(at_step == 3)
    def _():
        job.second()

    @pl.when(at_step == end - 3)
    def _():
        job.third()

    qt, got = qt_ref[0, :, here], got_ref[0]
    lse = lse_ref[0, 0]
    centre = jnp.sum(ot_ref[0].astype(f32) * got.astype(f32), axis=0, keepdims=True)

    @pl.when(i == 0)
    def _():
        sum_k[...] = jnp.zeros_like(sum_k)
        sum_v[...] = jnp.zeros_like(sum_v)
        dq_ref[...] = jnp.zeros_like(dq_ref)

    def step(at, grad, diagonal):
        start = pl.multiple_of(at * BLOCK, BLOCK)
        here = pl.ds(start, BLOCK)
        scores = mm(k_ref[0, here, :], qt)
        probs = jnp.exp(scores - lse)
        if diagonal:
            keys = lax.broadcasted_iota(jnp.int32, scores.shape, 0)
            queries = lax.broadcasted_iota(jnp.int32, scores.shape, 1)
            probs = jnp.where(keys <= queries, probs, 0.0)
        grad_probs = mm(v_ref[0, here, :], got)
        grad_scores = (probs * (grad_probs - centre)).astype(bf16)
        sum_v[:, here] += mm(got, probs.astype(bf16), NT)
        sum_k[:, here] += mm(qt, grad_scores, NT)
        return grad + mm(kt_ref[0, :, here], grad_scores)

    grad = lax.fori_loop(0, index, lambda at, c: step(at, c, False), jnp.zeros(qt.shape, f32))
    dq_ref[0, :, here] = step(index, grad, True) * HEAD_DIM**-0.5

    @pl.when(i == count - 1)
    def _():
        dk_ref[0] = sum_k[...]
        dv_ref[0] = sum_v[...]

    @pl.when(at_step == end)
    def _():
        job.last()
        one, two = job.total()
        fed_ref[: job.half] = one
        fed_ref[job.half :] = two
        total = go_ref[t].astype(f32)
        for step, copy in enumerate(away):
            copy.wait_recv()
            total = total + came_ref[step + 1].astype(f32)
            copy.wait_send()
        gos_ref[...] = total.astype(bf16)


def revisit(qt, k, kt, v, ot, got, lse, go, feed, number):
    heads, _, total = qt.shape
    count = ot.shape[0]
    nt = lax.axis_size("tp")
    whole = pl.BlockSpec((1, HEAD_DIM, total), lambda h, i: (h, 0, 0))
    tall = pl.BlockSpec((1, total, HEAD_DIM), lambda h, i: (h, 0, 0))
    some = pl.BlockSpec((1, HEAD_DIM, BLOCK), lambda h, i: (i, h, 0))
    return pl.pallas_call(
        revisit_kernel,
        grid=(heads, count),
        in_specs=[
            whole,
            tall,
            whole,
            tall,
            some,
            some,
            pl.BlockSpec((1, 1, 1, BLOCK), lambda h, i: (h, i, 0, 0)),
            full(go.shape),
        ]
        + anywhere(1),
        out_specs=[whole, whole, whole, full(go.shape[1:]), full(feed.shape[1:])],
        scratch_shapes=[
            pltpu.VMEM((HEAD_DIM, total), f32),
            pltpu.VMEM((HEAD_DIM, total), f32),
            pltpu.VMEM(go.shape, bf16),
            pltpu.SemaphoreType.DMA((nt,)),
            pltpu.SemaphoreType.DMA((nt,)),
        ]
        + Sum.scratch(*feed.shape[1:]),
        out_shape=[jax.ShapeDtypeStruct((heads, HEAD_DIM, total), f32)] * 3
        + [jax.ShapeDtypeStruct(go.shape[1:], bf16), jax.ShapeDtypeStruct(feed.shape[1:], f32)],
        compiler_params=params(collective_id=number, has_side_effects=True),
        cost_estimate=cost(50),
        name="revisit",
    )(qt, k, kt, v, ot, got, lse, go, feed)


def opening_kernel(cuts, x_ref, wq_ref, wk_ref, wv_ref, wo_ref, wr_ref, wc_ref, vec_ref, na_ref, nm_ref, routes_ref, out_ref, ws_ref, smalls_ref, all_routes_ref, held, stage, small_ref, *sems):
    gather = Gather(x_ref, out_ref, *sems[:3], cuts, stage)
    sends, recvs, local = sems[3:]
    z, c, t = spot()
    ns = lax.axis_size("shard")
    one = jnp.where(c == 0, wq_ref[...].astype(f32), wv_ref[...].astype(f32))
    two = jnp.where(c == 0, wk_ref[...].astype(f32), wo_ref[...].astype(f32).T)
    held[0] = one[:, :128].astype(bf16)
    held[1] = two[:, :128].astype(bf16)
    parts = [v[...].astype(f32) for v in (wr_ref, wc_ref, vec_ref, na_ref, nm_ref)]
    used = sum(v.shape[0] for v in parts)
    parts.append(jnp.zeros((SMALL - used, parts[0].shape[1]), f32))
    small_ref[...] = jnp.concatenate(parts, axis=0).astype(bf16)
    held[2] = jnp.concatenate([one[:, 128:], two[:, 128:]], axis=1).astype(bf16)
    greet()
    started = []

    def go(k, source, target, **where):
        copy = remote(source, target, sends.at[k], recvs.at[k], **where)
        copy.start()
        started.append(copy)

    def came(k, ref):
        remote(ref, ref, sends.at[k], recvs.at[k], ctx=1 - c).wait_recv()

    for step in range(1, ns):
        go(step, held, ws_ref.at[c, z], shard=lax.rem(z + step, ns))
    gather.first()
    for step in range(1, ns):
        go(2 * ns + step, small_ref, smalls_ref.at[z], shard=lax.rem(z + step, ns))
    go(0, held, ws_ref.at[c, z], ctx=1 - c)
    go(ns, routes_ref, all_routes_ref.at[c], ctx=1 - c)
    mine = [
        pltpu.make_async_copy(held, ws_ref.at[c, z], local.at[0]),
        pltpu.make_async_copy(small_ref, smalls_ref.at[z], local.at[1]),
        pltpu.make_async_copy(routes_ref, all_routes_ref.at[c], local.at[2]),
    ]
    for copy in mine:
        copy.start()
    for s in range(cuts):
        gather.second(s)
    for s in range(cuts):
        gather.third(s)
    for step in range(1, ns):
        back = lax.rem(z + ns - step, ns)
        came(step, ws_ref.at[c, back])
        go(ns + step, ws_ref.at[c, back], ws_ref.at[c, back], ctx=1 - c)
    gather.last()
    came(0, ws_ref.at[1 - c, z])
    came(ns, all_routes_ref.at[1 - c])
    for step in range(1, ns):
        back = lax.rem(z + ns - step, ns)
        came(2 * ns + step, smalls_ref.at[back])
        came(ns + step, ws_ref.at[1 - c, back])
    for copy in started:
        copy.wait_send()
    for copy in mine:
        copy.wait()


def opening(x, weights, small, routes, number):
    cuts = 2
    ns = lax.axis_size("shard")
    depth = weights[0].shape[0]
    held = (3, depth, 128)
    vmem = pl.BlockSpec(memory_space=pltpu.VMEM)
    return pl.pallas_call(
        functools.partial(opening_kernel, cuts),
        in_specs=anywhere(1) + [vmem] * (len(weights) + len(small) + 1),
        out_specs=anywhere(4),
        out_shape=[
            jax.ShapeDtypeStruct((8,) + x.shape, x.dtype),
            jax.ShapeDtypeStruct((2, ns) + held, bf16),
            jax.ShapeDtypeStruct((ns, SMALL, depth), bf16),
            jax.ShapeDtypeStruct((2,) + routes.shape, routes.dtype),
        ],
        scratch_shapes=[pltpu.VMEM(held, bf16), pltpu.VMEM(x.shape, x.dtype), pltpu.VMEM((SMALL, depth), bf16)]
        + Gather.scratch(cuts)
        + [
            pltpu.SemaphoreType.DMA((3 * ns,)),
            pltpu.SemaphoreType.DMA((3 * ns,)),
            pltpu.SemaphoreType.DMA((3,)),
        ],
        compiler_params=params(collective_id=number, has_side_effects=True),
        cost_estimate=cost(30),
        name="opening",
    )(x, *weights, *small, routes)


def places(routes_ref, row_ref):
    one = lax.broadcasted_iota(jnp.int32, (BLOCK, BLOCK), 0)
    two = lax.broadcasted_iota(jnp.int32, (BLOCK, BLOCK), 1)
    before = (one < two).astype(bf16)
    blocks, _, per = routes_ref.shape
    for b in range(blocks):
        carry = jnp.zeros((16, 1), f32)
        for at in range(0, per, BLOCK):
            here = slice(at, at + BLOCK)
            expert = lax.broadcasted_iota(jnp.int32, (16, BLOCK), 0)
            member = (routes_ref[b, 0:1, here] == expert) | (routes_ref[b, 1:2, here] == expert)
            rank = mm(member.astype(bf16), before) + carry
            row_ref[:, b * per + at : b * per + at + BLOCK] = jnp.where(member, rank, -1.0)
            carry = carry + jnp.sum(member.astype(f32), axis=1, keepdims=True)


def route_kernel(cuts, o_ref, x_ref, wo_ref, small_ref, prev_ref, routes_ref, cots_ref,
                 att, res_out, base_out, x_out, g_out, gate_ref, row_ref,
                 x_in, wo_in, res, base, a, comb, rows, cots, combs, xs, gs,
                 o_send, o_recv, c_send, c_recv, local, out_sem, x_sem, g_sem, *sems):
    gather = Gather(a, rows, *sems, cuts, relative=True)
    z, c, t = spot()
    nt = lax.axis_size("tp")
    own = 4 * c + t
    near = (t,) + across(t)
    blocks, _, per = routes_ref.shape
    width = rows.shape[2]
    experts = xs.shape[0]
    here = pl.ds(pl.multiple_of(t * BLOCK, BLOCK), BLOCK)
    loads = [
        pltpu.make_async_copy(cots_ref, cots, local.at[0]),
        pltpu.make_async_copy(x_ref, x_in, local.at[1]),
        pltpu.make_async_copy(wo_ref, wo_in, local.at[2]),
    ]
    for copy in loads:
        copy.start()
    greet(False)

    copies = []
    for i in range(o_ref.shape[0]):
        block = zig(c, i)
        copy = remote(o_ref.at[i], att.at[t], o_send.at[i], o_recv.at[t], ctx=block // nt, tp=lax.rem(block, nt))
        copies.append((block == own, copy, pltpu.make_async_copy(o_ref.at[i], att.at[t], local.at[3])))
    for mine, copy, inside in copies:

        @pl.when(jnp.logical_not(mine))
        def _():
            copy.start()

        @pl.when(mine)
        def _():
            inside.start()

    each = per // nt

    def names(b, j, order):
        start = pl.multiple_of(b * per, per)
        mine = row_ref[pl.ds(experts * c + j, 1), pl.ds(start, per)] if order is None else jnp.concatenate(
            [row_ref[pl.ds(experts * c + j, 1), pl.ds(pl.multiple_of(start + o * each, each), each)] for o in order], axis=1
        )
        return lax.broadcasted_iota(jnp.int32, (CAP, mine.shape[1]), 0).astype(f32) == mine

    def fetch(n):
        b, j = n // experts, lax.rem(n, experts)
        here = pl.ds(pl.multiple_of(b * CAP, CAP), CAP)
        hot = names(b, j, None)
        gs[j, here] = mm(hot.astype(bf16), cots[pl.ds(4 * b, 4)].reshape(per, width)).astype(bf16)
        pltpu.make_async_copy(gs.at[j, here], g_out.at[j, here], g_sem.at[n]).start()

    def fetch_x(beside, j, which):
        b = 1 - c if beside else c
        here = pl.ds(pl.multiple_of(b * CAP, CAP), CAP)
        order = [near[k] for k in which]
        hot = names(b, j, order)
        first = 4 * beside + which[0]
        got = mm(hot.astype(bf16), rows[first : first + len(which)].reshape(len(which) * each, width)).astype(bf16)
        gate = jnp.zeros((CAP, 1), f32)
        for k, o in enumerate(order):
            weight = combs[4 * b + o, pl.ds(experts * c + j, 1)]
            gate = gate + jnp.sum(jnp.where(hot[:, k * each : (k + 1) * each], weight, 0.0), axis=1, keepdims=True)
        if which[0] == 0:
            xs[j, here] = got
            gate_ref[j, here] = gate
        else:
            xs[j, here] = xs[j, here] + got
            gate_ref[j, here] = gate_ref[j, here] + gate
            n = b * experts + j
            pltpu.make_async_copy(xs.at[j, here], x_out.at[j, here], x_sem.at[n]).start()

    def all_x(beside, which):
        @pl.loop(0, experts)
        def _(j):
            fetch_x(beside, j, which)

    def fetch_g(first, last):
        @pl.loop(first, last)
        def _(n):
            fetch(n)

    places(routes_ref, row_ref)
    for copy in loads:
        copy.wait()
    fetch_g(0, 2)
    for mine, copy, inside in copies:

        @pl.when(jnp.logical_not(mine))
        def _():
            copy.wait_send()

        @pl.when(mine)
        def _():
            inside.wait()

    mine = lax.rem((own + 1) // 2, 2) == c
    for source in range(nt):

        @pl.when(jnp.logical_or(jnp.logical_not(mine), source != t))
        def _():
            remote(o_ref.at[0], att.at[source], o_send.at[0], o_recv.at[source], ctx=c, tp=t).wait_recv()

    attended = att[...].reshape(-1, BLOCK)
    r = x_in[...].astype(f32) + mm(attended, wo_in[...].reshape(-1, width), TN)
    inverse = lax.rsqrt(jnp.mean(r * r, axis=1, keepdims=True) + epsilon)
    n2 = r * inverse * small_ref[19:20]
    a[...] = n2.astype(bf16)
    gather.first()
    res[...] = r
    _, _, combined, alphas, weights = mixing(n2, small_ref[:16], *laid(prev_ref[:, here], routes_ref[c, :, here]))
    comb[...] = combined
    pairs = []
    for step in range(1, 8):
        other, back = lax.rem(own + step, 8), lax.rem(own + 8 - step, 8)
        where = {"ctx": other // 4, "tp": lax.rem(other, 4)}
        copy = remote(comb, combs.at[own], c_send.at[step], c_recv.at[step], **where)
        copy.start()
        pairs.append((copy, remote(comb, combs.at[back], c_send.at[step], c_recv.at[step], **where)))
    combs[own] = comb[...]
    scale, one, two = scales(alphas, weights)
    base[...] = r + scale * n2 + one * small_ref[16:17] + two * small_ref[17:18]
    outs = [
        pltpu.make_async_copy(res, res_out, out_sem.at[0]),
        pltpu.make_async_copy(base, base_out, out_sem.at[1]),
    ]
    for copy in outs:
        copy.start()

    total = blocks * experts
    fetch_g(2, 4)
    gather.second(0)
    fetch_g(4, total)
    gather.second(1)
    gather.own.wait()
    for copy, came in pairs:
        came.wait_recv()
    all_x(0, (0, 1, 2))
    gather.third(0)
    gather.third(1)
    gather.beside()
    all_x(1, (0, 1, 2))
    all_x(0, (3,))
    gather.last(True)
    all_x(1, (3,))

    for copy, came in pairs:
        copy.wait_send()
    for copy in outs:
        copy.wait()

    @pl.loop(0, total)
    def _(n):
        b, j = n // experts, lax.rem(n, experts)
        here = pl.ds(pl.multiple_of(b * CAP, CAP), CAP)
        pltpu.make_async_copy(gs.at[j, here], g_out.at[j, here], g_sem.at[n]).wait()
        pltpu.make_async_copy(xs.at[j, here], x_out.at[j, here], x_sem.at[n]).wait()


def route(o, x, wo, small, prev, routes, cots, experts, number):
    cuts = 2
    own, width = x.shape
    nt = lax.axis_size("tp")
    blocks, _, per = routes.shape
    slots = jax.ShapeDtypeStruct((experts, blocks * CAP, width), bf16)
    vmem = pl.BlockSpec(memory_space=pltpu.VMEM)
    return pl.pallas_call(
        functools.partial(route_kernel, cuts),
        in_specs=anywhere(3) + [vmem, vmem, vmem] + anywhere(1),
        out_specs=[vmem] + anywhere(4) + [vmem, vmem],
        out_shape=[
            jax.ShapeDtypeStruct((nt,) + o.shape[1:], bf16),
            jax.ShapeDtypeStruct((own, width), f32),
            jax.ShapeDtypeStruct((own, width), f32),
            slots,
            slots,
            jax.ShapeDtypeStruct((experts, blocks * CAP, 1), f32),
            jax.ShapeDtypeStruct((16, blocks * per), f32),
        ],
        scratch_shapes=[
            pltpu.VMEM((own, width), bf16),
            pltpu.VMEM(wo.shape, bf16),
            pltpu.VMEM((own, width), f32),
            pltpu.VMEM((own, width), f32),
            pltpu.VMEM((own, width), bf16),
            pltpu.VMEM((16, own), f32),
            pltpu.VMEM((8, own, width), bf16),
            pltpu.VMEM((8, own, width), bf16),
            pltpu.VMEM((8, 16, own), f32),
            pltpu.VMEM(slots.shape, bf16),
            pltpu.VMEM(slots.shape, bf16),
            pltpu.SemaphoreType.DMA((o.shape[0],)),
            pltpu.SemaphoreType.DMA((nt,)),
            pltpu.SemaphoreType.DMA((8,)),
            pltpu.SemaphoreType.DMA((8,)),
            pltpu.SemaphoreType.DMA((4,)),
            pltpu.SemaphoreType.DMA((2,)),
            pltpu.SemaphoreType.DMA((blocks * experts,)),
            pltpu.SemaphoreType.DMA((blocks * experts,)),
        ]
        + Gather.scratch(cuts),
        compiler_params=params(collective_id=number, has_side_effects=True),
        cost_estimate=cost(65),
        name="route",
    )(o, x, wo, small, prev, routes, cots)


def spot_rows(place, c, experts, first, some, values, at):
    lane = lax.broadcasted_iota(jnp.int32, place.shape, 1)
    slot = lax.broadcasted_iota(jnp.int32, (place.shape[0], CAP), 1).astype(f32)
    total = None
    for j in range(some):
        mine = jnp.sum(jnp.where(lane == experts * c + first + j, place, 0.0), axis=1, keepdims=True)
        term = mm((slot == mine).astype(bf16), values[j, at])
        total = term if total is None else total + term
    return total


def combine_kernel(experts, row_ref, *refs):
    back_ref, feed_ref, out_ref, feed_out, gates_ref = refs[:5]
    backs, feeds, stage, staged, gsend, gcame, l_sem, o_sem, g_send, g_recv = refs[5:15]
    job = Sum(None, *refs[15:], stage=stage)
    z, c, t = spot()
    own = 4 * c + t
    width = stage.shape[2]
    loads = [pltpu.make_async_copy(back_ref, backs, l_sem.at[0])]
    more = [pltpu.make_async_copy(feed_ref, feeds, l_sem.at[1])]
    for copy in loads + more:
        copy.start()
    greet(False)

    def tile(values, owner):
        start = pl.multiple_of(owner * BLOCK, BLOCK)
        place = row_ref[:, pl.ds(start, BLOCK)].T
        here = pl.ds(pl.multiple_of(owner // 4 * CAP, CAP), CAP)
        count = values.shape[0]
        return spot_rows(place, c, experts, experts - count, count, values, here)

    def back(owner):
        got = tile(backs, owner)
        named = got[:, width:].T
        gsend[owner] = named[:FFN_EXPERTS] + named[16 : 16 + FFN_EXPERTS]
        return got[:, :width]

    for copy in loads:
        copy.wait()
    for k, o in enumerate(job.order):
        stage[k] = back(4 * (1 - c) + o).astype(bf16)
        job.core[k].start()
        job.add(k, back(4 * c + o))
    job.third()
    pairs = []
    for step in range(1, 8):
        other = lax.rem(own + step, 8)
        copy = remote(gsend.at[other], gcame.at[step], g_send.at[step], g_recv.at[step], ctx=other // 4, tp=lax.rem(other, 4))
        copy.start()
        pairs.append(copy)
    for copy in more:
        copy.wait()

    def feed(first, last):
        @pl.loop(first, last)
        def _(n):
            staged[n] = tile(feeds, n).astype(bf16)
            pltpu.make_async_copy(staged.at[n], feed_out.at[n], o_sem.at[n]).start()

    feed(0, 8)
    gates = gsend[own]
    for step, copy in enumerate(pairs):
        copy.wait_recv()
        gates = gates + gcame[step + 1]
        copy.wait_send()
    gates_ref[...] = gates
    job.last()
    one, two = job.total()
    out_ref[: job.half] = one
    out_ref[job.half :] = two

    @pl.loop(0, 8)
    def _(n):
        pltpu.make_async_copy(staged.at[n], feed_out.at[n], o_sem.at[n]).wait()


def combine(row, back, feed, number):
    experts, slots, width = feed.shape
    wide = back.shape[2]
    rows = row.shape[1] // 8
    vmem = pl.BlockSpec(memory_space=pltpu.VMEM)
    return pl.pallas_call(
        functools.partial(combine_kernel, experts),
        in_specs=[vmem] + anywhere(2),
        out_specs=[vmem] + anywhere(1) + [vmem],
        out_shape=[
            jax.ShapeDtypeStruct((rows, width), f32),
            jax.ShapeDtypeStruct((8, rows, width), bf16),
            jax.ShapeDtypeStruct((FFN_EXPERTS, rows), f32),
        ],
        scratch_shapes=[
            pltpu.VMEM((experts, slots, wide), bf16),
            pltpu.VMEM(feed.shape, bf16),
            pltpu.VMEM((4, rows, width), bf16),
            pltpu.VMEM((8, rows, width), bf16),
            pltpu.VMEM((8, FFN_EXPERTS, rows), f32),
            pltpu.VMEM((8, FFN_EXPERTS, rows), f32),
            pltpu.SemaphoreType.DMA((2,)),
            pltpu.SemaphoreType.DMA((8,)),
            pltpu.SemaphoreType.DMA((8,)),
            pltpu.SemaphoreType.DMA((8,)),
        ]
        + Sum.scratch(rows, width),
        compiler_params=params(collective_id=number, has_side_effects=True),
        cost_estimate=cost(45),
        name="combine",
    )(row, back, feed)


def closing_kernel(dq_ref, dk_ref, dv_ref, x_ref, cos_ref, sin_ref, wt_ref, par_ref, go_ref, small_ref, top_ref,
                   out_ref, gsum_ref, ssum_ref, tmax_ref,
                   dqs, dks, dvs, xs, total, row, gother, gcore, gline, gmine, smine, sline, splane, tline, mytop, stage, l_sem, *sems):
    job = Sum(None, *sems[:7], stage=stage)
    sends, recvs = sems[7:]
    z, c, t = spot()
    ns = lax.axis_size("shard")
    heads = dqs.shape[0]
    half = HEAD_DIM // 2
    own = 4 * c + t
    order = [4 * (1 - c) + o for o in job.order] + [4 * c + o for o in job.order]

    def lanes(o):
        return pl.ds(pl.multiple_of(o * BLOCK, BLOCK), BLOCK)

    loads = []
    for n, o in enumerate(order):
        here = lanes(o)
        loads.append(
            [
                pltpu.make_async_copy(dq_ref.at[:, :, here], dqs.at[:, :, here], l_sem.at[n, 0]),
                pltpu.make_async_copy(dk_ref.at[:, :, here], dks.at[:, :, here], l_sem.at[n, 1]),
                pltpu.make_async_copy(dv_ref.at[:, :, here], dvs.at[:, :, here], l_sem.at[n, 2]),
                pltpu.make_async_copy(x_ref.at[here], xs.at[here], l_sem.at[n, 3]),
            ]
        )
    for k in range(4):
        for copy in loads[k] + loads[4 + k]:
            copy.start()
    greet()
    started = []

    def go(k, source, target, **where):
        copy = remote(source, target, sends.at[k], recvs.at[k], **where)
        copy.start()
        started.append(copy)
        return copy

    line_row = lax.broadcasted_iota(jnp.int32, mytop.shape, 0)
    high = jnp.full(mytop.shape, -1e30, f32)
    for h in range(top_ref.shape[0]):
        best = jnp.max(jnp.max(top_ref[h], axis=0), axis=1, keepdims=True)
        high = jnp.where(line_row == h, best, high)
    mytop[...] = high
    tops = [go(3 + ns + s, mytop, tline.at[s], shard=lax.rem(z + s, ns)) for s in range(1, ns)]
    total[...] = jnp.zeros_like(total)
    row[...] = jnp.zeros_like(row)

    def tile(o):
        here = lanes(o)
        cosine, sine = cos_ref[:, here], sin_ref[:, here]

        def turned(g):
            u, w = g[:half], g[half:]
            return jnp.concatenate([u * cosine + w * sine, w * cosine - u * sine], axis=0)

        x = xs[here].astype(f32)
        m = x * lax.rsqrt(jnp.mean(x * x, axis=1, keepdims=True) + epsilon)
        a = (m * par_ref[18:19]).astype(bf16)
        pieces = [turned(dqs[h, :, here]) for h in range(heads)]
        pieces += [turned(dks[h, :, here]) for h in range(heads)]
        pieces += [dvs[h, :, here] for h in range(heads)]
        grads = jnp.concatenate(pieces, axis=0).astype(bf16)
        part = mm(grads, wt_ref[...], TN)
        row[...] += jnp.sum(part * m, axis=0, keepdims=True)
        total[...] += mm(grads, a)
        return part

    for k in range(4):
        for copy in loads[k] + loads[4 + k]:
            copy.wait()
        stage[k] = tile(order[k]).astype(bf16)
        job.core[k].start()
        job.add(k, tile(order[4 + k]))

    cut_rows, depth = gsum_ref.shape[1:]
    at = lax.broadcasted_iota(jnp.int32, small_ref.shape, 0)
    smalls = small_ref[...] + jnp.where(at == 19, row[...], 0.0)
    for s in range(ns):
        here = slice(s * depth, (s + 1) * depth)
        one = total[:cut_rows, here].astype(bf16)
        two = jnp.concatenate([total[cut_rows:, here].astype(bf16), go_ref[:, here]], axis=0)
        gmine[s] = packed(jnp.where(c == 0, one.astype(f32), two.astype(f32))).astype(bf16)
        gother[s] = packed(jnp.where(c == 0, two.astype(f32), one.astype(f32))).astype(bf16)
        smine[s] = smalls[:, here]
    core = go(0, gother, gcore, ctx=1 - c)
    small = [go(3 + s, smine.at[lax.rem(z + s, ns)], sline.at[s], shard=lax.rem(z + s, ns)) for s in range(1, ns)]
    core.wait_recv()
    gmine[...] = gmine[...] + gcore[...]
    line = [go(3 + 2 * ns + s, gmine.at[lax.rem(z + s, ns)], gline.at[s], shard=lax.rem(z + s, ns)) for s in range(1, ns)]
    job.third()
    for copy in small:
        copy.wait_recv()
    value = smine[z]
    for s in range(1, ns):
        value = value + sline[s]
    splane[0] = value
    plane = []
    for s in range(1, 8):
        other = lax.rem(own + s, 8)
        plane.append(go(3 + 3 * ns + s, splane.at[0], splane.at[s], ctx=other // 4, tp=lax.rem(other, 4)))
    for copy in tops:
        copy.wait_recv()
    high = mytop[...]
    for s in range(1, ns):
        high = jnp.maximum(high, tline[s])
    tline[0] = high
    pair = go(2, tline.at[0], tline.at[ns], ctx=1 - c)
    for copy in line:
        copy.wait_recv()
    value = gmine[z].astype(f32)
    for s in range(1, ns):
        value = value + gline[s].astype(f32)
    gsum_ref[c] = unpacked(value, depth)
    go(3, gsum_ref.at[c], gsum_ref.at[c], ctx=1 - c)
    for copy in plane:
        copy.wait_recv()
    value = splane[0]
    for s in range(1, 8):
        value = value + splane[s]
    ssum_ref[...] = value
    pair.wait_recv()
    tmax_ref[...] = jnp.maximum(tline[0], tline[ns])
    job.last()
    one, two = job.total()
    out_ref[: job.half] = one
    out_ref[job.half :] = two
    remote(gsum_ref.at[1 - c], gsum_ref.at[1 - c], sends.at[3], recvs.at[3], ctx=1 - c).wait_recv()
    for copy in started:
        copy.wait_send()


def closing(dq, dk, dv, x, cosine, sine, wt, par, go, small, top, number):
    heads, _, total = dq.shape
    width = x.shape[1]
    rows = total // 8
    ns = lax.axis_size("shard")
    depth = width // ns
    cut_rows = 2 * heads * HEAD_DIM
    pieces = (ns, cut_rows * 3 // 2, 128) if depth == 192 else (ns, cut_rows, depth)
    smalls = (ns,) + small.shape[:1] + (depth,)
    vmem = pl.BlockSpec(memory_space=pltpu.VMEM)
    return pl.pallas_call(
        closing_kernel,
        in_specs=anywhere(4) + [vmem] * 7,
        out_specs=[vmem] * 4,
        out_shape=[
            jax.ShapeDtypeStruct((rows, width), f32),
            jax.ShapeDtypeStruct((2, cut_rows, depth), f32),
            jax.ShapeDtypeStruct(smalls[1:], f32),
            jax.ShapeDtypeStruct((8, 128), f32),
        ],
        scratch_shapes=[
            pltpu.VMEM(dq.shape, f32),
            pltpu.VMEM(dq.shape, f32),
            pltpu.VMEM(dq.shape, f32),
            pltpu.VMEM(x.shape, bf16),
            pltpu.VMEM(wt.shape, f32),
            pltpu.VMEM((1, width), f32),
            pltpu.VMEM(pieces, bf16),
            pltpu.VMEM(pieces, bf16),
            pltpu.VMEM(pieces, bf16),
            pltpu.VMEM(pieces, bf16),
            pltpu.VMEM(smalls, f32),
            pltpu.VMEM(smalls, f32),
            pltpu.VMEM((8,) + smalls[1:], f32),
            pltpu.VMEM((ns + 1, 8, 128), f32),
            pltpu.VMEM((8, 128), f32),
            pltpu.VMEM((4, rows, width), bf16),
            pltpu.SemaphoreType.DMA((8, 4)),
        ]
        + Sum.scratch(rows, width)
        + [
            pltpu.SemaphoreType.DMA((3 * ns + 11,)),
            pltpu.SemaphoreType.DMA((3 * ns + 11,)),
        ],
        compiler_params=params(collective_id=number, has_side_effects=True),
        cost_estimate=cost(45),
        name="closing",
    )(dq, dk, dv, x, cosine, sine, wt, par, go, small, top)


def packed(v):
    rows, lanes = v.shape
    if lanes != 192:
        return v
    rest = jnp.concatenate([v[: rows // 2, 128:], v[rows // 2 :, 128:]], axis=1)
    return jnp.concatenate([v[:, :128], rest], axis=0)


def unpacked(v, lanes):
    if lanes != 192:
        return v
    rows = v.shape[0] // 3 * 2
    rest = jnp.concatenate([v[rows:, :64], v[rows:, 64:]], axis=0)
    return jnp.concatenate([v[:rows], rest], axis=1)


def swap_kernel(ge_ref, other_ref, send, recv):
    z, c, t = spot()
    greet_core()
    copy = remote(ge_ref, other_ref, send, recv, ctx=1 - c)
    copy.start()
    copy.wait()


def greet_core():
    z, c, t = spot()
    barrier = pltpu.get_barrier_semaphore()
    pl.semaphore_signal(barrier, inc=1, device_id={"ctx": 1 - c}, device_id_type=MESH)
    pl.semaphore_wait(barrier, 1)


def swap(ge, number):
    return pl.pallas_call(
        swap_kernel,
        in_specs=anywhere(1),
        out_specs=anywhere(1)[0],
        out_shape=jax.ShapeDtypeStruct(ge.shape, ge.dtype),
        scratch_shapes=[pltpu.SemaphoreType.DMA, pltpu.SemaphoreType.DMA],
        compiler_params=params(collective_id=number, has_side_effects=True),
        cost_estimate=cost(5),
        name="swap",
    )(ge)


def laid(previous, routes):
    count, rows = previous.shape
    return jnp.concatenate([previous, jnp.zeros((16 - count, rows), f32)], axis=0), routes.astype(f32)


def thirds(v):
    a = v.astype(bf16)
    rest = v - a.astype(f32)
    b = rest.astype(bf16)
    return a, b, (rest - b.astype(f32)).astype(bf16)


def mixing(n2, wrc, previous, routes):
    z = sum(mm(wrc.astype(bf16), part, NT) for part in thirds(n2))
    expert = lax.broadcasted_iota(jnp.int32, z.shape, 0).astype(f32)
    logits = z + previous
    hot = [expert == routes[r : r + 1] for r in range(2)]
    picked = [jnp.sum(jnp.where(hot[r], logits, 0.0), axis=0, keepdims=True) for r in range(2)]
    most = jnp.maximum(picked[0], picked[1])
    e = [jnp.exp(p - most) for p in picked]
    gates = [v / (e[0] + e[1]) for v in e]
    combine = jnp.where(hot[0], gates[0], 0.0) + jnp.where(hot[1], gates[1], 0.0)
    alphas = []
    for j in range(2):
        first, second = z[EXPERTS + 2 * j : EXPERTS + 2 * j + 1], z[EXPERTS + 2 * j + 1 : EXPERTS + 2 * j + 2]
        most = jnp.maximum(first, second)
        a, b = jnp.exp(first - most), jnp.exp(second - most)
        alphas.append((a / (a + b), b / (a + b)))
    weights = [combine[FFN_EXPERTS + 1 + j : FFN_EXPERTS + 2 + j] for j in range(3)]
    return hot, gates, combine, alphas, weights


def scales(alphas, weights):
    scale = weights[0] + weights[1] * alphas[0][0] + weights[2] * alphas[1][0]
    at = lax.broadcasted_iota(jnp.int32, (8, scale.shape[1]), 0)
    value = jnp.where(at == 0, scale, jnp.where(at == 1, weights[1] * alphas[0][1], weights[2] * alphas[1][1])).T
    return value[:, 0:1], value[:, 1:2], value[:, 2:3]


def turn_kernel(length, res_ref, dn_ref, named_ref, cot_ref, att_ref, wo_ref, par_ref, prev_ref, routes_ref,
                dres_ref, heads_ref, gwo_ref, small_ref, got_ref, send_sem, recv_sem, local_sem):
    z, c, t = spot()
    nt = lax.axis_size("tp")
    own = c * nt + t
    rows, width = res_ref.shape
    greet(False)
    here = pl.ds(pl.multiple_of(t * rows, rows), rows)
    res = res_ref[...]
    gain = par_ref[19:20]
    inverse = lax.rsqrt(jnp.mean(res * res, axis=1, keepdims=True) + epsilon)
    m = res * inverse
    n2 = m * gain
    previous, routes = laid(prev_ref[:, here], routes_ref[c, :, here])
    hot, gates, _, alphas, weights = mixing(n2, par_ref[:16], previous, routes)
    position = own * rows + lax.broadcasted_iota(jnp.int32, cot_ref.shape, 0)
    g = jnp.where(position < length[0], cot_ref[...].astype(f32), 0.0)
    inner = jnp.broadcast_to(jnp.sum(g * n2, axis=1, keepdims=True), (rows, 8)).T[0:1]
    onto = mm(par_ref[16:18].astype(bf16), g.astype(bf16), NT)
    onto = [onto[j : j + 1] for j in range(2)]
    named = named_ref[...]
    expert = lax.broadcasted_iota(jnp.int32, hot[0].shape, 0)
    local = {
        FFN_EXPERTS + 1: inner,
        FFN_EXPERTS + 2: alphas[0][0] * inner + alphas[0][1] * onto[0],
        FFN_EXPERTS + 3: alphas[1][0] * inner + alphas[1][1] * onto[1],
    }
    dgates = []
    for r in range(2):
        there = jnp.sum(jnp.where(hot[r][:FFN_EXPERTS], named, 0.0), axis=0, keepdims=True)
        for e, value in local.items():
            there = there + jnp.where(hot[r][e : e + 1], value, 0.0)
        dgates.append(there)
    mean = gates[0] * dgates[0] + gates[1] * dgates[1]
    dz = jnp.where(hot[0], gates[0] * (dgates[0] - mean), 0.0)
    dz = dz + jnp.where(hot[1], gates[1] * (dgates[1] - mean), 0.0)
    for j in range(2):
        da = weights[1 + j] * inner
        db = weights[1 + j] * onto[j]
        centre = alphas[j][0] * da + alphas[j][1] * db
        dz = dz + jnp.where(expert == EXPERTS + 2 * j, alphas[j][0] * (da - centre), 0.0)
        dz = dz + jnp.where(expert == EXPERTS + 2 * j + 1, alphas[j][1] * (db - centre), 0.0)
    scale, first_vec, second_vec = scales(alphas, weights)
    highest = lax.Precision.HIGHEST
    dn2 = dn_ref[...] + scale * g + sum(mm(part, par_ref[:16].astype(bf16), TN) for part in thirds(dz))
    q = dn2 * gain
    dres = g + inverse * (q - m * jnp.mean(q * m, axis=1, keepdims=True))
    dres_ref[...] = dres
    da = dres.astype(bf16)
    wo = wo_ref[...].reshape(-1, width)
    got_ref[...] = mm(wo, da, NT).astype(bf16).reshape(got_ref.shape)

    core = lax.rem((own + 1) // 2, 2)
    slot = 2 * (own // 4) + lax.rem(own, 4) // 2
    copies = []
    for target in range(nt):
        inside = jnp.logical_and(core == c, target == t)
        copy = remote(got_ref.at[target], heads_ref.at[slot], send_sem.at[target], recv_sem.at[slot], ctx=core, tp=target)
        copies.append((inside, copy, pltpu.make_async_copy(got_ref.at[target], heads_ref.at[slot], local_sem)))
    for inside, copy, kept in copies:

        @pl.when(jnp.logical_not(inside))
        def _():
            copy.start()

        @pl.when(inside)
        def _():
            kept.start()

    small_ref[0:16] = mm(dz, n2, NN, highest)
    small_ref[16:24] = jnp.zeros((8, width), f32)
    small_ref[16:17] = jnp.sum(first_vec * g, axis=0, keepdims=True)
    small_ref[17:18] = jnp.sum(second_vec * g, axis=0, keepdims=True)
    small_ref[18:19] = jnp.sum(dn2 * m, axis=0, keepdims=True)
    att = att_ref[...].reshape(-1, rows)
    gwo_ref[...] = mm(att, da).astype(bf16).reshape(gwo_ref.shape)
    for inside, copy, kept in copies:

        @pl.when(jnp.logical_not(inside))
        def _():
            copy.wait_send()

        @pl.when(inside)
        def _():
            kept.wait()

    for i in range(heads_ref.shape[0]):

        @pl.when(zig(c, i) != own)
        def _():
            remote(got_ref.at[0], heads_ref.at[i], send_sem.at[0], recv_sem.at[i], ctx=c, tp=t).wait_recv()


def turn(length, res, dn, named, cot, att, wo, small, prev, routes, count, number):
    rows, width = res.shape
    nt = lax.axis_size("tp")
    args = (res, dn, named, cot, att, wo, small, prev, routes)
    return pl.pallas_call(
        turn_kernel,
        grid_spec=pltpu.PrefetchScalarGridSpec(
            num_scalar_prefetch=1,
            grid=(1,),
            in_specs=[full(v.shape) for v in args],
            out_specs=[full((rows, width))] + anywhere(1) + [full(wo.shape), full((24, width))],
            scratch_shapes=[
                pltpu.VMEM(att.shape, bf16),
                pltpu.SemaphoreType.DMA((nt,)),
                pltpu.SemaphoreType.DMA((count,)),
                pltpu.SemaphoreType.DMA,
            ],
        ),
        out_shape=[
            jax.ShapeDtypeStruct((rows, width), f32),
            jax.ShapeDtypeStruct((count,) + att.shape[1:], bf16),
            jax.ShapeDtypeStruct(wo.shape, bf16),
            jax.ShapeDtypeStruct((24, width), f32),
        ],
        compiler_params=params(collective_id=number, has_side_effects=True),
        cost_estimate=cost(18),
        name="turn",
    )(length, *args)


def both_cores(own_ref, other_ref, targets):
    core = lax.axis_index("ctx")
    for k, target in enumerate(targets):
        for j in range(own_ref.shape[0]):
            mine, theirs = own_ref[j, k].astype(f32), other_ref[j, k].astype(f32)
            target[0, j] = jnp.where(core == 0, mine, theirs)
            target[1, j] = jnp.where(core == 0, theirs, mine)


def output_kernel(base_ref, feed_ref, length_ref, own_ref, other_ref, out_ref, *targets):
    both_cores(own_ref, other_ref, targets)
    rows = base_ref.shape[0]
    first = (lax.axis_index("ctx") * lax.axis_size("tp") + lax.axis_index("tp")) * pl.num_programs(0) + pl.program_id(0)
    position = first * rows + lax.broadcasted_iota(jnp.int32, base_ref.shape, 0)
    out_ref[...] = jnp.where(position < length_ref[0], base_ref[...] + feed_ref[...], 0.0).astype(bf16)


def steps_of(depth):
    return 4 if depth % 64 == 0 else 1


def output_rows(base, feed, length, own, other, local):
    rows, width = base.shape
    each, kinds, depth, hidden = own.shape
    steps = steps_of(depth)
    by_row = pl.BlockSpec((rows // steps, width), lambda i: (i, 0))
    pair = pl.BlockSpec((each, kinds, depth // steps, hidden), lambda i: (0, 0, i, 0))
    return pl.pallas_call(
        output_kernel,
        grid=(steps,),
        in_specs=[by_row, by_row, pl.BlockSpec(memory_space=pltpu.SMEM), pair, pair],
        out_specs=[by_row] + [pl.BlockSpec((2, each, depth // steps, hidden), lambda i: (0, 0, i, 0))] * 3,
        out_shape=[jax.ShapeDtypeStruct((rows, width), bf16)]
        + [jax.ShapeDtypeStruct((2, local, depth, hidden), f32)] * 3,
        compiler_params=params(),
        cost_estimate=cost(6),
        name="output_rows",
    )(base, feed, length, own, other)


def finish_kernel(x_ref, dn_ref, dres_ref, small_ref, gw_ref, gs_ref, top_ref, wq_ref, wk_ref, limit_ref, own_ref, other_ref, *refs):
    outs = refs[3:]
    gin_ref, targets = outs[0], outs[1:4]
    x = x_ref[...].astype(f32)
    inverse = lax.rsqrt(jnp.mean(x * x, axis=1, keepdims=True) + epsilon)
    m = x * inverse
    q = dn_ref[...] * small_ref[18:19]
    gin_ref[...] = dres_ref[...] + inverse * (q - m * jnp.mean(q * m, axis=1, keepdims=True))
    both_cores(own_ref, other_ref, targets)

    @pl.when(pl.program_id(0) == 0)
    def _():
        gq, gk, gv, go, gnorm, gmoe, grouter, gconst, gvec, fac_ref, cq_ref, ck_ref = outs[4:]
        width = wq_ref.shape[1]
        flat = gw_ref[...].reshape(4 * width, gw_ref.shape[2])
        for k, target in enumerate((gq, gk, gv)):
            target[...] = flat[k * width : (k + 1) * width].T
        go[...] = flat[3 * width :]
        sums = gs_ref[...]
        grouter[...] = sums[:EXPERTS]
        gconst[...] = sums[EXPERTS : EXPERTS + 4]
        gvec[...] = sums[16:18]
        gmoe[...] = sums[18:19]
        gnorm[...] = sums[19:20]
        factors = limit_ref[0] / jnp.maximum(top_ref[...], limit_ref[0])
        for h in range(fac_ref.shape[0]):
            fac_ref[h] = factors[h, 0]
        lane = lax.broadcasted_iota(jnp.int32, (1, width), 1)
        root = jnp.zeros((1, width), f32)
        for h in range(width // HEAD_DIM):
            root = jnp.where(lane // HEAD_DIM == h, jnp.sqrt(factors[h : h + 1, :1]), root)
        cq_ref[...] = (wq_ref[...].astype(f32) * root).astype(bf16)
        ck_ref[...] = (wk_ref[...].astype(f32) * root).astype(bf16)


def finish_rows(x, dn, dres, small, gw, gs, top, wq, wk, limit, own, other, finals):
    rows, width = x.shape
    each, kinds, depth, hidden = own.shape
    steps = steps_of(depth)
    tile, deep = rows // steps, depth // steps
    by_row = pl.BlockSpec((tile, width), lambda i: (i, 0))
    expert_out = pl.BlockSpec((2, each, deep, hidden), lambda i: (0, finals[0].shape[1] // each - 1, i, 0))
    once = [
        jax.ShapeDtypeStruct(shape, f32)
        for shape in [wq.shape] * 3
        + [(wq.shape[1], depth), (1, depth), (1, depth), (EXPERTS, depth), (4, depth), (2, depth), (wq.shape[1] // HEAD_DIM,)]
    ] + [jax.ShapeDtypeStruct(wq.shape, bf16)] * 2
    return pl.pallas_call(
        finish_kernel,
        grid=(steps,),
        in_specs=[
            by_row,
            by_row,
            by_row,
            full(small.shape),
            full(gw.shape),
            full(gs.shape),
            full(top.shape),
            full(wq.shape),
            full(wk.shape),
            pl.BlockSpec(memory_space=pltpu.SMEM),
        ]
        + [pl.BlockSpec((each, kinds, deep, hidden), lambda i: (0, 0, i, 0))] * 2
        + anywhere(3),
        out_specs=[by_row, expert_out, expert_out, expert_out] + [full(v.shape) if v.ndim > 1 else pl.BlockSpec(memory_space=pltpu.SMEM) for v in once],
        out_shape=[
            jax.ShapeDtypeStruct((rows, width), f32),
        ]
        + [jax.ShapeDtypeStruct(v.shape, f32) for v in finals]
        + once,
        input_output_aliases={12: 1, 13: 2, 14: 3},
        compiler_params=params(),
        cost_estimate=cost(8),
        name="finish_rows",
    )(x, dn, dres, small, gw, gs, top, wq, wk, limit, own, other, *finals)


def pick_kernel(first, g_ref, u_ref, d_ref, out_ref):
    for k, source in enumerate((g_ref, u_ref, d_ref)):
        out_ref[0, k] = source[0]


def pick(first, start, some, gate, up, down):
    _, depth, hidden = gate.shape
    source = pl.BlockSpec((1, depth, hidden), lambda i, f: (f[0] + start + i, 0, 0))
    return pl.pallas_call(
        pick_kernel,
        grid_spec=pltpu.PrefetchScalarGridSpec(
            num_scalar_prefetch=1,
            grid=(some,),
            in_specs=[source] * 3,
            out_specs=pl.BlockSpec((1, 3, depth, hidden), lambda i, f: (i, 0, 0, 0)),
        ),
        out_shape=jax.ShapeDtypeStruct((some, 3, depth, hidden), gate.dtype),
        compiler_params=params(),
        cost_estimate=cost(2),
        name="pick",
    )(first, gate, up, down)


def expert_kernel(start, first, x_ref, g_ref, gate_ref, w_ref, *refs):
    feed_ref, back_ref, gw_ref = refs[-3:]
    parts, _, _, depth, hidden = w_ref.shape
    width = parts * depth
    wg, wu, wd = [w_ref[:, 0, k].reshape(width, hidden) for k in range(3)]
    x, g, gate = x_ref[0], g_ref[0], gate_ref[0]
    gate_pre = mm(x, wg)
    up = mm(x, wu)
    sigmoid = 1.0 / (1.0 + jnp.exp(-gate_pre))
    activated = gate_pre * sigmoid
    inner = (activated * up).astype(bf16)
    g32 = g.astype(f32)
    dout = (gate * g32).astype(bf16)
    dinner = mm(dout, wd)
    out = mm(inner, wd, NT)
    feed_ref[0] = (gate * out).astype(bf16)
    dgate = jnp.sum(g32 * out, axis=1, keepdims=True)
    dpre = (dinner * up * sigmoid * (1.0 + gate_pre * (1.0 - sigmoid))).astype(bf16)
    dup = (dinner * activated).astype(bf16)
    back_ref[0, :, :width] = (mm(dpre, wg, NT) + mm(dup, wu, NT)).astype(bf16)
    lane = lax.broadcasted_iota(jnp.int32, (dgate.shape[0], back_ref.shape[2] - width), 1)
    coarse = dgate.astype(bf16).astype(f32)
    at = first[0] + start + pl.program_id(0)
    extra = jnp.where(lane == at, coarse, jnp.where(lane == at + 16, dgate - coarse, 0.0))
    back_ref[0, :, width:] = extra.astype(bf16)
    for k, (left, right) in enumerate(((x, dpre), (x, dup), (dout, inner))):
        gw_ref[:, 0, k] = mm(left, right, TN).reshape(parts, depth, hidden).astype(bf16)


def expert(start, some, first, x, g, gate, w, at, into=()):
    local, slots, width = x.shape
    parts, _, kinds, depth, hidden = w.shape
    pick = lambda i, f: (start + i, 0, 0)
    return pl.pallas_call(
        functools.partial(expert_kernel, start),
        grid_spec=pltpu.PrefetchScalarGridSpec(
            num_scalar_prefetch=1,
            grid=(some,),
            in_specs=[
                pl.BlockSpec((1, slots, width), pick),
                pl.BlockSpec((1, slots, width), pick),
                pl.BlockSpec((1, slots, 1), pick),
                pl.BlockSpec((parts, 1, kinds, depth, hidden), lambda i, f: (0, at + i, 0, 0, 0)),
            ]
            + anywhere(len(into)),
            out_specs=[
                pl.BlockSpec((1, slots, width), pick),
                pl.BlockSpec((1, slots, width + EXTRA), pick),
                pl.BlockSpec((parts, 1, kinds, depth, hidden), lambda i, f: (0, start % 2 + i, 0, 0, 0)),
            ],
        ),
        out_shape=[
            jax.ShapeDtypeStruct((local, slots, width), bf16),
            jax.ShapeDtypeStruct((local, slots, width + EXTRA), bf16),
            jax.ShapeDtypeStruct((parts, 2, kinds, depth, hidden), bf16),
        ],
        input_output_aliases={5 + n: n for n in range(len(into))},
        compiler_params=params(),
        cost_estimate=cost(10 * some),
        name="expert",
    )(first, x, g, gate, w, *into)


def shards(
    hidden_in,
    cotangent,
    lengths,
    routes,
    prev_logits,
    norm_attn,
    w_query,
    w_key,
    w_value,
    w_out,
    norm_moe,
    w_router,
    w_const,
    const_vec,
    w_gate,
    w_up,
    w_down,
    threshold,
):
    plane = ("ctx", "tp")
    core = lax.axis_index("ctx")
    nc, nt, ns = lax.axis_size("ctx"), lax.axis_size("tp"), lax.axis_size("shard")
    own, width = hidden_in.shape
    per = own * nt
    total = per * nc
    depth = w_gate.shape[1]
    heads = w_query.shape[1] // HEAD_DIM
    head_width = heads * HEAD_DIM
    local = FFN_EXPERTS // nc
    count = total // BLOCK // nc
    routes, prev = routes.T, prev_logits.T
    first = (core * local).astype(jnp.int32)[None]

    calls = ((0, local - 1), (local - 1, 1))
    expert_w = []
    for start, some in calls:
        pieces = pick(first, start, some, w_gate, w_up, w_down)
        expert_w.append(lax.all_gather(pieces, "shard", axis=0, tiled=False))
    rows_all, attention_w, small, routes_all = opening(
        hidden_in,
        (w_query, w_key, w_value, w_out),
        (w_router.T, w_const.T, const_vec, norm_attn[None], norm_moe[None]),
        routes,
        0,
    )
    rows_all = rows_all.reshape(total, width)
    cosine, sine = rope_tables(total)

    qt, kt, k, v, vt, wt, small, out_w = project(rows_all, attention_w, small, cosine, sine, heads, 8)
    ot, lse, top, cot_all = attend(lengths, qt, k, vt, cotangent, count, 1)
    att, res, base, x_slots, g_slots, gate_slots, row_at = route(
        ot, hidden_in, out_w, small, prev, routes_all, cot_all, local, 2
    )

    slots = (first, x_slots, g_slots, gate_slots)
    *results, pair = expert(0, 2, *slots, expert_w[0], 0)
    grads = [pair]
    *results, pair = expert(2, 1, *slots, expert_w[0], 2, results)
    *results, pair = expert(3, 1, *slots, expert_w[1], 0, (*results, pair))
    grads = [lax.psum_scatter(g, "shard", scatter_dimension=0, tiled=True)[0] for g in (*grads, pair)]
    feed, back = results
    back, feed, named = combine(row_at, back, feed, 3)

    dres, got, grad_out, gsmall = turn(
        lengths, res, back, named, cotangent, att, out_w, small, prev, routes_all, count, 4
    )
    dq, dk, dv, grad_out, feed = revisit(qt, k, kt, v, ot, got, lse, grad_out, feed, 5)
    early, dq = lax.optimization_barrier((grads[0], dq))
    output, *finals = output_rows(base, feed, lengths, early, swap(early, 6), local)
    dq, *finals = lax.optimization_barrier((dq, *finals))
    part, grad_w, gsmall, top = closing(dq, dk, dv, rows_all, cosine, sine, wt, small, grad_out, gsmall, top, 7)
    late, top = lax.optimization_barrier((grads[1], top))
    (grad_input, grad_gate, grad_up, grad_down, grad_q, grad_k, grad_v, grad_out, grad_norm_attn, grad_norm_moe,
     grad_router, grad_const, grad_vec, factors, clipped_query, clipped_key) = finish_rows(
        hidden_in, part, dres, small, grad_w, gsmall, top, w_query, w_key, threshold, late, swap(late, 9), finals
    )
    grad_gate, grad_up, grad_down = [v.reshape((-1,) + v.shape[2:]) for v in (grad_gate, grad_up, grad_down)]
    return (
        output,
        grad_input,
        grad_norm_attn[0],
        grad_q,
        grad_k,
        grad_v,
        grad_out,
        grad_norm_moe[0],
        grad_router.T,
        grad_const.T,
        grad_vec,
        grad_gate,
        grad_up,
        grad_down,
        factors,
        clipped_query,
        clipped_key,
    )


def solution(mesh):
    return jax.shard_map(
        shards,
        mesh=mesh,
        in_specs=(
            P(("shard", "ctx", "tp"), None),
            P(("shard", "ctx", "tp"), None),
            P("shard"),
            P(("shard", "ctx"), None),
            P(("shard", "ctx"), None),
            P("shard"),
            P("shard", "tp"),
            P("shard", "tp"),
            P("shard", "tp"),
            P("tp", "shard"),
            P("shard"),
            P("shard", None),
            P("shard", None),
            P(None, "shard"),
            P(None, "shard", "tp"),
            P(None, "shard", "tp"),
            P(None, "shard", "tp"),
            P(),
        ),
        out_specs=(
            P(("shard", "ctx", "tp"), None),
            P(("shard", "ctx", "tp"), None),
            P("shard"),
            P("shard", "tp"),
            P("shard", "tp"),
            P("shard", "tp"),
            P("tp", "shard"),
            P("shard"),
            P("shard", None),
            P("shard", None),
            P(None, "shard"),
            P(None, "shard", "tp"),
            P(None, "shard", "tp"),
            P(None, "shard", "tp"),
            P("tp"),
            P("shard", "tp"),
            P("shard", "tp"),
        ),
        check_vma=False,
    )
```
